32 devices in a mesh: dp: 8 (over y, x, core), tensor: 4 (over z).
Axes of the slice: x: 2, y: 2, z: 4, core: 2. Of those that a mesh axis runs over, the one named last changes fastest.
Arguments:
- hidden_in: bfloat16 [4096, 2048], P(('dp', 'tensor')), may hold values from -6 to 6
- teacher: bfloat16 [4096, 2048], P(('dp', 'tensor')), may hold values from -6 to 6
- lengths: int32 [8], replicated, may hold values from 128 to 512, as said below
- routes: int32 [4096, 8], P('dp'), may hold values from 0 to 15, all different within a row; in each aligned block of 128 rows (0 to 127, 128 to 255, ...) at most 68 rows name the same one
- attn_norm_gain: bfloat16 [2048], replicated, may hold values from 0.5 to 1.5
- ffn_norm_gain: bfloat16 [2048], replicated, may hold values from 0.5 to 1.5
- q_weight: bfloat16 [2048, 2048], P('dp', 'tensor'), may hold values from -0.125 to 0.125
- k_weight: bfloat16 [2048, 2048], P('dp', 'tensor'), may hold values from -0.125 to 0.125
- v_weight: bfloat16 [2048, 2048], P('dp', 'tensor'), may hold values from -0.125 to 0.125
- q_gain: bfloat16 [16, 128], P('tensor', 'dp'), may hold values from 0.5 to 1.5
- k_gain: bfloat16 [16, 128], P('tensor', 'dp'), may hold values from 0.5 to 1.5
- o_weight: bfloat16 [2048, 2048], P('tensor', 'dp'), may hold values from -2 to 2
- router_weight: bfloat16 [2048, 16], replicated, may hold values from -0.0625 to 0.0625
- gate_weight: bfloat16 [16, 2048, 1024], P(None, 'dp', 'tensor'), may hold values from -0.125 to 0.125
- up_weight: bfloat16 [16, 2048, 1024], P(None, 'dp', 'tensor'), may hold values from -0.125 to 0.125
- down_weight: bfloat16 [16, 1024, 2048], P(None, 'tensor', 'dp'), may hold values from -3 to 3
Outputs:
- loss_parts: float32 [8], P('dp')
- grad_in: float32 [4096, 2048], P(('dp', 'tensor'))
- grad_attn_gain: float32 [2048], P(('dp', 'tensor'))
- grad_ffn_gain: float32 [2048], P(('dp', 'tensor'))
- grad_q: float32 [2048, 2048], P('dp', 'tensor')
- grad_k: float32 [2048, 2048], P('dp', 'tensor')
- grad_v: float32 [2048, 2048], P('dp', 'tensor')
- grad_q_gain: float32 [16, 128], P('tensor', 'dp')
- grad_k_gain: float32 [16, 128], P('tensor', 'dp')
- grad_o: float32 [2048, 2048], P('tensor', 'dp')
- grad_router: float32 [2048, 16], P(('dp', 'tensor'))
- grad_gate: float32 [16, 2048, 1024], P(None, 'dp', 'tensor')
- grad_up: float32 [16, 2048, 1024], P(None, 'dp', 'tensor')
- grad_down: float32 [16, 1024, 2048], P(None, 'tensor', 'dp')
The draws below stay inside these ranges and needn't reach their ends.
Inputs may be any that keep to these rules, and one draw needn't show every extreme that they name: `lengths`: each sequence has at least 128 valid tokens; in every draw at least one sequence is valid to its end. `routes`: within the 128 rows of one device (aligned blocks), no expert is named by more than 68 rows, and that bound is reached.
All inputs are finite; a program needn't handle non-finite values.
Results may differ from the reference program's by a relative error of at most 0.022.
Values may be sent and summed in bfloat16 or wider, within the bound.
A program may use at most 320 MiB of HBM per device.

```python
import math
import jax
import jax.numpy as jnp
import numpy as np
from jax import lax

D = 2048
H = 16
HD = 128
FF = 1024
TOPK = 8
E = 16
TOK_DEV = 128
SEQ = 512
TOKENS = 4096
CAP = 68
N_DP = 8


def draw_lengths(key, part):
    first_key, second_key = jax.random.split(key)
    drawn = jax.random.randint(first_key, (N_DP,), SEQ // 4, SEQ + 1)
    full_index = jax.random.randint(second_key, (), 0, N_DP)
    return jnp.where(jnp.arange(N_DP) == full_index, SEQ, drawn).astype(jnp.int32)


def steps_of(rng, extent, cuts, low, top_value):
    factor_of, own = 1.0, jax.random.fold_in(rng, 6)
    for position, blocks in cuts:
        steps = jnp.exp(jax.random.uniform(jax.random.fold_in(own, position), (blocks,), jnp.float32, low / len(cuts), top_value / len(cuts)))
        factor_of = factor_of * jnp.repeat(steps, extent[position] // blocks).reshape([-1 if axis == position else 1 for axis in range(len(extent))])
    return factor_of


def assign_block(key, own, number, rows, count, top, most, slope):
    ranking = jax.random.permutation(key, count)
    packed, usual = load_shares(count, rows * top, most, slope, True), load_shares(count, rows * top, most, slope, False)
    places = jnp.arange(count)

    def named(sizes, turn):
        used = int((sizes > 0).sum())
        fixed = max(1, used // 4)
        shifted = fixed + (places - fixed + turn * (used - fixed)) % max(1, count - fixed)
        return jnp.zeros((count,), jnp.int32).at[ranking[jnp.where(places < fixed, places, shifted)]].set(jnp.asarray(sizes, jnp.int32))

    sizes = jnp.where(number % 4 == 0, named(packed, number // 4), named(usual, number - number // 4 - 1))
    mixed = jax.random.permutation(jax.random.fold_in(own, 3), count)
    source_of, taker = mixed[0:count // 2 * 2:2], mixed[1:count // 2 * 2:2]
    slack = jnp.minimum(sizes[source_of] - 1, most - sizes[taker]) // 2
    slack = jnp.where((source_of == ranking[0]) | (taker == ranking[0]) | (sizes[taker] == 0), 0, jnp.maximum(slack, 0))
    shifted = jax.random.randint(jax.random.fold_in(own, 4), (count // 2,), 0, 1 << 20) % (slack + 1)
    sizes = sizes.at[source_of].add(-shifted).at[taker].add(shifted)
    items = jnp.searchsorted(jnp.cumsum(sizes), jnp.arange(rows * top), side="right").astype(jnp.int32)
    table = items.reshape(top, rows).T
    table = table[jax.random.permutation(jax.random.fold_in(own, 1), rows)]
    turn = jax.random.randint(jax.random.fold_in(own, 2), (rows, 1), 0, top)
    return jnp.take_along_axis(table, (jnp.arange(top)[None, :] + turn) % top, axis=1)


def load_shares(amount, total, bound, skew, full):
    loads = [(1 << 20) // math.isqrt(grade ** skew) + 1 for grade in range(1, amount + 1)]
    largest = bound if full else min(bound, max(-(-total // amount), total * loads[0] // sum(loads)))
    least = 1 if total - largest >= amount - 1 else 0
    holding, surplus = [largest] + [least] * (amount - 1), total - largest - least * (amount - 1)
    while surplus > 0:
        candidates = [i for i in range(1, amount) if holding[i] < largest] or [i for i in range(1, amount) if holding[i] < bound]
        pool, left = sum([loads[i] for i in candidates]), surplus
        for i in candidates:
            extra = min(bound - holding[i], max(1, left * loads[i] // pool), surplus)
            holding[i] = holding[i] + extra
            surplus = surplus - extra
    return np.array(holding)


def noise(stream_key, extent, scale, bound, pieces=(), kind=jnp.bfloat16):
    loudness = steps_of(stream_key, extent, pieces, -0.22, 0.18) if pieces else 1.0
    array = jax.random.normal(stream_key, extent, jnp.float32) * scale * loudness
    return jnp.minimum(jnp.maximum(array, -bound), bound).astype(kind)


def setup_inputs(seed: int = 0) -> dict:
    streams_of = jax.random.split(jax.random.key(seed), 17)
    hidden_in = noise(streams_of[0], (TOKENS, D), 1.0, 6.0, ((0, 32),))
    teacher = noise(streams_of[1], (TOKENS, D), 1.0, 6.0, ((0, 32),))
    lengths = draw_lengths(jax.random.fold_in(streams_of[16], 71), 0)
    routes_keys = jax.random.split(jax.random.fold_in(streams_of[3], 1), TOKENS // TOK_DEV)
    routes_turns = jax.random.permutation(jax.random.fold_in(streams_of[3], 3), TOKENS // TOK_DEV)
    routes = jax.vmap(lambda own, number: assign_block(jax.random.fold_in(streams_of[3], 2), own, number, TOK_DEV, E, TOPK, CAP, 0))(routes_keys, routes_turns).reshape((TOKENS, TOPK))
    attn_norm_gain = jnp.clip(1.0 + 0.1 * jax.random.normal(streams_of[4], (D,), jnp.float32), 0.5, 1.5).astype(jnp.bfloat16)
    ffn_norm_gain = jnp.clip(1.0 + 0.1 * jax.random.normal(streams_of[5], (D,), jnp.float32), 0.5, 1.5).astype(jnp.bfloat16)
    q_weight = noise(streams_of[6], (D, D), D ** -0.5, 0.125, ((0, 8), (1, 4)))
    k_weight = noise(streams_of[7], (D, D), D ** -0.5, 0.125, ((0, 8), (1, 4)))
    v_weight = noise(streams_of[8], (D, D), D ** -0.5, 0.125, ((0, 8), (1, 4)))
    q_gain = jnp.clip(1.0 + 0.1 * jax.random.normal(streams_of[9], (H, HD), jnp.float32), 0.5, 1.5).astype(jnp.bfloat16)
    k_gain = jnp.clip(1.0 + 0.1 * jax.random.normal(streams_of[10], (H, HD), jnp.float32), 0.5, 1.5).astype(jnp.bfloat16)
    o_weight = noise(streams_of[11], (D, D), (max(D // 256, 1)) ** -0.5, 2.0, ((0, 4), (1, 8)))
    router_weight = noise(streams_of[12], (D, E), (4 * D) ** -0.5, 0.0625)
    gate_weight = noise(streams_of[13], (E, D, FF), D ** -0.5, 0.125, ((1, 8), (2, 4)))
    up_weight = noise(streams_of[14], (E, D, FF), D ** -0.5, 0.125, ((1, 8), (2, 4)))
    down_weight = noise(streams_of[15], (E, FF, D), (max(FF // 256, 1)) ** -0.5, 3.0, ((1, 4), (2, 8)))
    return dict(hidden_in=hidden_in, teacher=teacher, lengths=lengths, routes=routes, attn_norm_gain=attn_norm_gain, ffn_norm_gain=ffn_norm_gain, q_weight=q_weight, k_weight=k_weight, v_weight=v_weight, q_gain=q_gain, k_gain=k_gain, o_weight=o_weight, router_weight=router_weight, gate_weight=gate_weight, up_weight=up_weight, down_weight=down_weight)


EPSILON = 1e-05
THETA = 10000.0
HIGHEST = lax.Precision.HIGHEST

@jax.custom_vjp
def low(v):
    return lax.optimization_barrier(v.astype(jnp.bfloat16)).astype(jnp.float32)

@jax.custom_vjp
def low_back(v):
    return v

def low_keep(v):
    return (low(v), None)

def low_pass(kept, grad):
    return (grad,)

def back_keep(v):
    return (v, None)

def back_low(kept, grad):
    return (low(grad),)
low.defvjp(low_keep, low_pass)
low_back.defvjp(back_keep, back_low)

def rounded_both(value):
    return low(low_back(value))

def inverse_rms(value):
    return lax.rsqrt(lax.optimization_barrier(jnp.mean(value * value, axis=-1, keepdims=True)) + EPSILON)

def rotate(value, cosine, sine):
    middle_index = value.shape[-1] // 2
    leading = value[..., :middle_index]
    trailing = value[..., middle_index:]
    return jnp.concatenate([leading * cosine - trailing * sine, trailing * cosine + leading * sine], axis=-1)

def layer(params, hidden, target, length, route_ids, total_count):
    attn_gain, ffn_gain, q_proj, k_proj, v_proj, q_scale, k_scale, o_proj, router, gate_proj, up_proj, down_proj = params
    seq_len = hidden.shape[0]
    normed = low(hidden * inverse_rms(hidden) * attn_gain)
    query_raw = low_back(jnp.dot(normed, q_proj, precision=HIGHEST))
    key_raw = low_back(jnp.dot(normed, k_proj, precision=HIGHEST))
    value_all = rounded_both(jnp.dot(normed, v_proj, precision=HIGHEST)).reshape(seq_len, H, HD)
    query_norm = query_raw * inverse_rms(query_raw) * q_scale.reshape(-1)
    key_norm = key_raw * inverse_rms(key_raw) * k_scale.reshape(-1)
    positions = jnp.arange(seq_len)
    frequency = THETA ** (-jnp.arange(HD // 2).astype(jnp.float32) / (HD // 2))
    angles = positions.astype(jnp.float32)[:, None] * frequency[None, :]
    cosine = jnp.cos(angles)[:, None, :]
    sinus_table = jnp.sin(angles)[:, None, :]
    queries = low(rotate(query_norm.reshape(seq_len, H, HD), cosine, sinus_table))
    key_rows = low(rotate(key_norm.reshape(seq_len, H, HD), cosine, sinus_table))
    block_rows = min(512, seq_len)

    def attend(start):
        query_block = lax.dynamic_slice_in_dim(queries, start, block_rows, 0)
        scores = low_back(jnp.einsum('qhd,khd->hqk', query_block, key_rows, precision=HIGHEST) / math.sqrt(HD))
        query_pos = start + jnp.arange(block_rows)
        allowed = (positions[None, :] <= query_pos[:, None]) & (positions[None, :] < length)
        scores = jnp.where(allowed[None], scores, -1e+30)
        weights = low(jax.nn.softmax(scores, axis=-1))
        return rounded_both(jnp.einsum('hqk,khd->qhd', weights, value_all, precision=HIGHEST))
    starts = jnp.arange(seq_len // block_rows) * block_rows
    mixed = lax.map(jax.checkpoint(attend), starts).reshape(seq_len, D)
    middle = hidden + low_back(jnp.dot(mixed, o_proj, precision=HIGHEST))
    ffn_in = low(middle * inverse_rms(middle) * ffn_gain)
    gate_probs = jax.nn.softmax(jnp.dot(ffn_in, router, precision=HIGHEST), axis=-1)
    chosen = lax.optimization_barrier(jnp.sum(jax.nn.one_hot(route_ids, E, dtype=jnp.float32), axis=1))
    coeffs = gate_probs * chosen

    def expert(running, inputs):
        gate_matrix, up_matrix, down_matrix, coeff_column = inputs
        gate_value = low_back(jnp.dot(ffn_in, gate_matrix, precision=HIGHEST))
        up_value = low_back(jnp.dot(ffn_in, up_matrix, precision=HIGHEST))
        active = low(coeff_column[:, None] * jax.nn.silu(gate_value) * up_value)
        return (running + jnp.dot(active, down_matrix, precision=HIGHEST), None)
    expert_sum, _ = lax.scan(jax.checkpoint(expert), jnp.zeros((seq_len, D), jnp.float32), (gate_proj, up_proj, down_proj, coeffs.T))
    output = middle + low_back(expert_sum)
    valid = (positions < length)[:, None]
    mismatch = output - target
    return jnp.sum(jnp.where(valid, mismatch * mismatch, 0.0)) / (2.0 * D * total_count)

def reference(hidden_in, teacher, lengths, routes, attn_norm_gain, ffn_norm_gain, q_weight, k_weight, v_weight, q_gain, k_gain, o_weight, router_weight, gate_weight, up_weight, down_weight):
    params = tuple((weight.astype(jnp.float32) for weight in (attn_norm_gain, ffn_norm_gain, q_weight, k_weight, v_weight, q_gain, k_gain, o_weight, router_weight, gate_weight, up_weight, down_weight)))
    total_count = jnp.sum(lengths).astype(jnp.float32)
    hiddens = hidden_in.astype(jnp.float32).reshape(N_DP, SEQ, D)
    targets = teacher.astype(jnp.float32).reshape(N_DP, SEQ, D)
    route_sets = routes.reshape(N_DP, SEQ, TOPK)

    def per_sequence(totals, inputs):
        hidden, target, length, route_ids = inputs

        def loss_of(weights, states):
            return layer(weights, states, target, length, route_ids, total_count)
        part, pull = jax.vjp(loss_of, params, hidden)
        weight_grads, input_grad = pull(jnp.ones_like(part) * (TOKENS * D))
        return (jax.tree.map(jnp.add, totals, weight_grads), (part, input_grad))
    zeros = jax.tree.map(jnp.zeros_like, params)
    totals, (parts, input_grads) = lax.scan(per_sequence, zeros, (hiddens, targets, lengths, route_sets))
    return (parts, input_grads.reshape(TOKENS, D), totals[0], totals[1], totals[2], totals[3], totals[4], totals[5], totals[6], totals[7], totals[8], totals[9], totals[10], totals[11])
```

```python
import functools
import math

import jax
import jax.numpy as jnp
from jax import lax
from jax.experimental import pallas as pl
from jax.experimental.pallas import tpu as pltpu
from jax.sharding import PartitionSpec as P

HD = 128
TOK_DEV = 128
CAP = 68


EPSILON = 1e-05
THETA = 10000.0
HIGHEST = lax.Precision.HIGHEST


def inverse_rms(value):
    return lax.rsqrt(jnp.mean(value * value, axis=-1, keepdims=True) + EPSILON)


def rotate(value, cosine, sinus_table, direction):
    middle_index = value.shape[-1] // 2
    leading = value[..., :middle_index]
    trailing = value[..., middle_index:]
    return jnp.concatenate(
        [
            leading * cosine - direction * trailing * sinus_table,
            trailing * cosine + direction * leading * sinus_table,
        ],
        axis=-1,
    )


def norm_backward(grad_norm, unit_rows, inverse_rows, gain_row):
    scaled = grad_norm * gain_row
    return inverse_rows * (
        scaled - unit_rows * jnp.mean(scaled * unit_rows, axis=-1, keepdims=True)
    )


def fetch_attention(q_weight, k_weight, v_weight, o_weight, q_gain, k_gain):
    return (
        lax.all_gather(q_weight, "dp", axis=0, tiled=True),
        lax.all_gather(k_weight, "dp", axis=0, tiled=True),
        lax.all_gather(v_weight, "dp", axis=0, tiled=True),
        lax.all_gather(o_weight, "dp", axis=1, tiled=True),
        lax.all_gather(q_gain, "dp", axis=1, tiled=True),
        lax.all_gather(k_gain, "dp", axis=1, tiled=True),
    )


def fetch_experts(gate_weight, up_weight, down_weight):
    return (
        lax.all_gather(gate_weight, "dp", axis=1, tiled=True),
        lax.all_gather(up_weight, "dp", axis=1, tiled=True),
        lax.all_gather(down_weight, "dp", axis=2, tiled=True),
    )


def per_device(
    hidden_in,
    teacher,
    lengths,
    routes,
    attn_norm_gain,
    ffn_norm_gain,
    q_weight,
    k_weight,
    v_weight,
    q_gain,
    k_gain,
    o_weight,
    router_weight,
    gate_weight,
    up_weight,
    down_weight,
):
    dp_count = lax.axis_size("dp")
    tp_count = lax.axis_size("tensor")
    group_index = lax.axis_index("dp")
    member = lax.axis_index("tensor")
    row_count, model_width = hidden_in.shape
    seq_len = row_count * tp_count
    all_tokens = seq_len * dp_count
    length = lengths[group_index]
    total_count = jnp.sum(lengths).astype(jnp.float32)
    attn_gain = attn_norm_gain.astype(jnp.float32)
    ffn_gain = ffn_norm_gain.astype(jnp.float32)
    root_size = math.sqrt(HD)
    q_full, k_full, v_full, o_full, qgain_full, kgain_full = fetch_attention(
        q_weight, k_weight, v_weight, o_weight, q_gain, k_gain
    )
    local_heads = q_full.shape[1] // HD
    hidden_all = lax.all_gather(hidden_in, "tensor", axis=0, tiled=True).astype(jnp.float32)
    inverse_one = inverse_rms(hidden_all)
    unit_one = hidden_all * inverse_one
    normed = (unit_one * attn_gain).astype(jnp.bfloat16)
    query_raw = jnp.dot(normed, q_full, preferred_element_type=jnp.float32)
    key_raw = jnp.dot(normed, k_full, preferred_element_type=jnp.float32)
    value_low = jnp.dot(normed, v_full, preferred_element_type=jnp.float32).astype(jnp.bfloat16)
    query_sq, key_sq = lax.psum(
        (jnp.sum(query_raw * query_raw, axis=1), jnp.sum(key_raw * key_raw, axis=1)), "tensor"
    )
    query_inv = lax.rsqrt(query_sq / model_width + EPSILON)[:, None]
    key_inv = lax.rsqrt(key_sq / model_width + EPSILON)[:, None]
    query_unit = query_raw * query_inv
    key_unit = key_raw * key_inv
    query_gain = qgain_full.astype(jnp.float32).reshape(-1)
    key_gain = kgain_full.astype(jnp.float32).reshape(-1)
    positions = jnp.arange(seq_len)
    frequency = THETA ** (-jnp.arange(HD // 2).astype(jnp.float32) / (HD // 2))
    angles = positions.astype(jnp.float32)[:, None] * frequency[None, :]
    cosine = jnp.cos(angles)[:, None, :]
    sinus_table = jnp.sin(angles)[:, None, :]
    queries = rotate(
        (query_unit * query_gain).reshape(seq_len, local_heads, HD), cosine, sinus_table, 1.0
    ).astype(jnp.bfloat16)
    key_rows = rotate(
        (key_unit * key_gain).reshape(seq_len, local_heads, HD), cosine, sinus_table, 1.0
    ).astype(jnp.bfloat16)
    value_rows = value_low.reshape(seq_len, local_heads, HD)
    block_rows = min(512, seq_len)
    starts = jnp.arange(seq_len // block_rows) * block_rows

    def block_scores(start):
        query_block = lax.dynamic_slice_in_dim(queries, start, block_rows, 0)
        scores = (
            jnp.einsum("qhd,khd->hqk", query_block, key_rows, preferred_element_type=jnp.float32)
            / root_size
        )
        query_pos = start + jnp.arange(block_rows)
        allowed = (positions[None, :] <= query_pos[:, None]) & (positions[None, :] < length)
        return (query_block, jnp.where(allowed[None], scores, -1e30))

    def attend(start):
        unused_block, scores = block_scores(start)
        row_top = jnp.max(scores, axis=-1, keepdims=True)
        exponent = jnp.exp(scores - row_top)
        row_total = jnp.sum(exponent, axis=-1, keepdims=True)
        weights = (exponent / row_total).astype(jnp.bfloat16)
        mixed_block = jnp.einsum(
            "hqk,khd->qhd", weights, value_rows, preferred_element_type=jnp.float32
        )
        return (mixed_block.astype(jnp.bfloat16), (row_top + jnp.log(row_total))[..., 0])

    mixed_blocks, log_totals = lax.map(attend, starts)
    mixed = mixed_blocks.reshape(seq_len, local_heads * HD)
    attn_own = lax.psum_scatter(
        jnp.dot(mixed, o_full, preferred_element_type=jnp.float32).astype(jnp.bfloat16),
        "tensor",
        scatter_dimension=0,
        tiled=True,
    ).astype(jnp.float32)
    middle = hidden_in.astype(jnp.float32) + attn_own
    inverse_two = inverse_rms(middle)
    unit_two = middle * inverse_two
    ffn_own = (unit_two * ffn_gain).astype(jnp.bfloat16)
    gate_full, up_full, down_full = fetch_experts(gate_weight, up_weight, down_weight)
    ffn_all = lax.all_gather(ffn_own, "tensor", axis=0, tiled=True)
    expert_count = router_weight.shape[1]
    route_width = routes.shape[1]
    gate_probs = jax.nn.softmax(
        jnp.dot(ffn_all, router_weight, preferred_element_type=jnp.float32), axis=-1
    )
    picked = routes[:, :, None] == jnp.arange(expert_count)[None, None, :]
    route_gates = jnp.sum(jnp.where(picked, gate_probs[:, None, :], 0.0), axis=-1)
    block_count = seq_len // TOK_DEV
    per_expert = block_count * CAP
    picked_ints = picked.reshape(block_count, TOK_DEV * route_width, expert_count).astype(jnp.int32)
    slot_ranks = jnp.sum((jnp.cumsum(picked_ints, axis=1) - 1) * picked_ints, axis=-1).reshape(
        seq_len, route_width
    )
    block_ids = (positions // TOK_DEV)[:, None]
    slot_ids = (routes * per_expert + block_ids * CAP + slot_ranks).reshape(-1)
    slot_total = expert_count * per_expert
    token_ids = jnp.repeat(positions, route_width)
    group_width = 4
    turn_count = expert_count // group_width
    sources = (
        jnp.full((slot_total,), seq_len, jnp.int32)
        .at[slot_ids]
        .set(token_ids)
        .reshape(turn_count, group_width, per_expert)
    )
    slot_gates = (
        jnp.zeros((slot_total,), jnp.float32)
        .at[slot_ids]
        .set(route_gates.reshape(-1))
        .reshape(turn_count, group_width, per_expert, 1)
    )
    ffn_padded = jnp.concatenate([ffn_all, jnp.zeros((1, model_width), jnp.bfloat16)], axis=0)
    expert_running = jnp.zeros((seq_len + 1, model_width), jnp.float32)
    kept_values = []
    for turn_index in range(turn_count):
        lower = turn_index * group_width
        upper = lower + group_width
        expert_inputs = ffn_padded[sources[turn_index]]
        gate_value = jnp.einsum(
            "gpd,gdf->gpf",
            expert_inputs,
            gate_full[lower:upper],
            preferred_element_type=jnp.float32,
        )
        up_value = jnp.einsum(
            "gpd,gdf->gpf", expert_inputs, up_full[lower:upper], preferred_element_type=jnp.float32
        )
        active = (slot_gates[turn_index] * jax.nn.silu(gate_value) * up_value).astype(jnp.bfloat16)
        expert_outputs = jnp.einsum(
            "gpf,gfd->gpd", active, down_full[lower:upper], preferred_element_type=jnp.float32
        )
        expert_running = expert_running.at[sources[turn_index].reshape(-1)].add(
            expert_outputs.reshape(-1, model_width)
        )
        kept_values.append((gate_value, up_value, active))
    expert_own = lax.psum_scatter(
        expert_running[:seq_len].astype(jnp.bfloat16), "tensor", scatter_dimension=0, tiled=True
    ).astype(jnp.float32)
    output = middle + expert_own
    own_positions = member * row_count + jnp.arange(row_count)
    valid_rows = (own_positions < length)[:, None]
    mismatch = output - teacher.astype(jnp.float32)
    loss_own = jnp.sum(jnp.where(valid_rows, mismatch * mismatch, 0.0)) / (
        2.0 * model_width * total_count
    )
    grad_output = jnp.where(valid_rows, mismatch * (all_tokens / total_count), 0.0)
    grad_rows = lax.all_gather(grad_output.astype(jnp.bfloat16), "tensor", axis=0, tiled=True)
    gate_full, up_full, down_full = fetch_experts(gate_weight, up_weight, down_weight)
    grad_padded = jnp.concatenate([grad_rows, jnp.zeros((1, model_width), jnp.bfloat16)], axis=0)
    ffn_grad_running = jnp.zeros((seq_len + 1, model_width), jnp.float32)
    gate_grads = []
    up_grads = []
    down_grads = []
    slot_grads = []
    for turn_index in range(turn_count):
        gate_value, up_value, active = kept_values[turn_index]
        lower = turn_index * group_width
        upper = lower + group_width
        source_rows = sources[turn_index]
        expert_inputs = ffn_padded[source_rows]
        incoming = grad_padded[source_rows]
        grad_active = jnp.einsum(
            "gpd,gfd->gpf", incoming, down_full[lower:upper], preferred_element_type=jnp.float32
        )
        down_turn = jnp.einsum("gpf,gpd->gfd", active, incoming, preferred_element_type=jnp.float32)
        sigmoid_value = jax.nn.sigmoid(gate_value)
        silu_value = gate_value * sigmoid_value
        slot_grads.append(jnp.sum(grad_active * silu_value * up_value, axis=-1))
        grad_inner = grad_active * slot_gates[turn_index]
        grad_gate_value = (
            grad_inner * up_value * sigmoid_value * (1.0 + gate_value * (1.0 - sigmoid_value))
        ).astype(jnp.bfloat16)
        grad_up_value = (grad_inner * silu_value).astype(jnp.bfloat16)
        gate_turn = jnp.einsum(
            "gpd,gpf->gdf", expert_inputs, grad_gate_value, preferred_element_type=jnp.float32
        )
        up_turn = jnp.einsum(
            "gpd,gpf->gdf", expert_inputs, grad_up_value, preferred_element_type=jnp.float32
        )
        gate_grads.append(gate_turn)
        up_grads.append(up_turn)
        down_grads.append(down_turn)
        grad_inputs = jnp.einsum(
            "gpf,gdf->gpd",
            grad_gate_value,
            gate_full[lower:upper],
            preferred_element_type=jnp.float32,
        )
        grad_inputs = grad_inputs + jnp.einsum(
            "gpf,gdf->gpd", grad_up_value, up_full[lower:upper], preferred_element_type=jnp.float32
        )
        ffn_grad_running = ffn_grad_running.at[source_rows.reshape(-1)].add(
            grad_inputs.reshape(-1, model_width)
        )
    slot_grad_all = jnp.concatenate([entry.reshape(-1) for entry in slot_grads])
    route_grads = slot_grad_all[slot_ids].reshape(seq_len, route_width)
    grad_probs = jnp.sum(jnp.where(picked, route_grads[:, :, None], 0.0), axis=1)
    grad_logits = gate_probs * (
        grad_probs - jnp.sum(grad_probs * gate_probs, axis=-1, keepdims=True)
    )
    router_float = router_weight.astype(jnp.float32)
    ffn_grad_part = ffn_grad_running[:seq_len] + jnp.einsum(
        "se,de->sd", grad_logits, router_float, precision=HIGHEST
    )
    router_part = jnp.einsum(
        "sd,se->de", ffn_all, grad_logits, precision=HIGHEST, preferred_element_type=jnp.float32
    )
    ffn_grad_own = lax.psum_scatter(
        ffn_grad_part.astype(jnp.bfloat16), "tensor", scatter_dimension=0, tiled=True
    ).astype(jnp.float32)
    ffn_gain_part = jnp.sum(ffn_grad_own * unit_two, axis=0)
    grad_middle = grad_output + norm_backward(ffn_grad_own, unit_two, inverse_two, ffn_gain)
    attn_grad_rows = lax.all_gather(grad_middle.astype(jnp.bfloat16), "tensor", axis=0, tiled=True)
    q_full, k_full, v_full, o_full, qgain_full, kgain_full = fetch_attention(
        q_weight, k_weight, v_weight, o_weight, q_gain, k_gain
    )
    grad_o = jnp.einsum("sa,sb->ab", mixed, attn_grad_rows, preferred_element_type=jnp.float32)
    grad_mixed = (
        jnp.einsum("sb,ab->sa", attn_grad_rows, o_full, preferred_element_type=jnp.float32)
        .astype(jnp.bfloat16)
        .reshape(seq_len, local_heads, HD)
    )

    def attend_back(carry, inputs):
        key_running, value_running = carry
        start, log_total = inputs
        query_block, scores = block_scores(start)
        probs_float = jnp.exp(scores - log_total[..., None])
        probs_low = probs_float.astype(jnp.bfloat16)
        grad_block = lax.dynamic_slice_in_dim(grad_mixed, start, block_rows, 0)
        value_running = value_running + jnp.einsum(
            "hqk,qhd->khd", probs_low, grad_block, preferred_element_type=jnp.float32
        )
        grad_weights = jnp.einsum(
            "qhd,khd->hqk", grad_block, value_rows, preferred_element_type=jnp.float32
        )
        grad_scores = (
            probs_float
            * (grad_weights - jnp.sum(grad_weights * probs_float, axis=-1, keepdims=True))
        ).astype(jnp.bfloat16)
        query_grad_block = (
            jnp.einsum("hqk,khd->qhd", grad_scores, key_rows, preferred_element_type=jnp.float32)
            / root_size
        )
        key_running = (
            key_running
            + jnp.einsum(
                "hqk,qhd->khd", grad_scores, query_block, preferred_element_type=jnp.float32
            )
            / root_size
        )
        return ((key_running, value_running), query_grad_block)

    zero_heads = jnp.zeros((seq_len, local_heads, HD), jnp.float32)
    (key_grad_rot, value_grad), query_grad_blocks = lax.scan(
        attend_back, (zero_heads, zero_heads), (starts, log_totals)
    )
    query_grad = rotate(
        query_grad_blocks.reshape(seq_len, local_heads, HD), cosine, sinus_table, -1.0
    ).reshape(seq_len, local_heads * HD)
    key_grad = rotate(key_grad_rot, cosine, sinus_table, -1.0).reshape(seq_len, local_heads * HD)
    query_scaled = query_grad * query_gain
    key_scaled = key_grad * key_gain
    qgain_part = jnp.sum(query_grad * query_unit, axis=0)
    kgain_part = jnp.sum(key_grad * key_unit, axis=0)
    query_dot, key_dot, loss_group = lax.psum(
        (
            jnp.sum(query_scaled * query_unit, axis=1),
            jnp.sum(key_scaled * key_unit, axis=1),
            loss_own,
        ),
        "tensor",
    )
    query_raw_grad = (
        query_inv * (query_scaled - query_unit * (query_dot / model_width)[:, None])
    ).astype(jnp.bfloat16)
    key_raw_grad = (key_inv * (key_scaled - key_unit * (key_dot / model_width)[:, None])).astype(
        jnp.bfloat16
    )
    value_raw_grad = value_grad.reshape(seq_len, local_heads * HD).astype(jnp.bfloat16)
    grad_q = jnp.einsum("sd,sa->da", normed, query_raw_grad, preferred_element_type=jnp.float32)
    grad_k = jnp.einsum("sd,sa->da", normed, key_raw_grad, preferred_element_type=jnp.float32)
    grad_v = jnp.einsum("sd,sa->da", normed, value_raw_grad, preferred_element_type=jnp.float32)
    normed_grad = jnp.einsum(
        "sa,da->sd", query_raw_grad, q_full, preferred_element_type=jnp.float32
    )
    normed_grad = normed_grad + jnp.einsum(
        "sa,da->sd", key_raw_grad, k_full, preferred_element_type=jnp.float32
    )
    normed_grad = normed_grad + jnp.einsum(
        "sa,da->sd", value_raw_grad, v_full, preferred_element_type=jnp.float32
    )
    attn_gain_part = jnp.sum(normed_grad * unit_one, axis=0)
    input_part = norm_backward(normed_grad, unit_one, inverse_one, attn_gain)
    split_width = model_width // (dp_count * tp_count)
    input_own, attn_gain_share, ffn_gain_share, router_share = (
        lax.psum_scatter(
            input_part.astype(jnp.bfloat16), "tensor", scatter_dimension=0, tiled=True
        ).astype(jnp.float32),
        lax.psum_scatter(
            attn_gain_part.reshape(dp_count, tp_count, split_width).astype(jnp.bfloat16),
            "tensor",
            scatter_dimension=1,
            tiled=True,
        ).astype(jnp.float32),
        lax.psum_scatter(
            ffn_gain_part.reshape(dp_count, tp_count, split_width).astype(jnp.bfloat16),
            "tensor",
            scatter_dimension=1,
            tiled=True,
        ).astype(jnp.float32),
        lax.psum_scatter(
            router_part.reshape(dp_count, tp_count, split_width, expert_count).astype(jnp.bfloat16),
            "tensor",
            scatter_dimension=1,
            tiled=True,
        ).astype(jnp.float32),
    )
    grad_in = grad_middle + input_own
    (
        grad_q,
        grad_k,
        grad_v,
        grad_o,
        grad_qgain,
        grad_kgain,
        attn_gain_sum,
        ffn_gain_sum,
        router_sum,
    ) = (
        lax.psum_scatter(grad_q.astype(jnp.bfloat16), "dp", scatter_dimension=0, tiled=True).astype(
            jnp.float32
        ),
        lax.psum_scatter(grad_k.astype(jnp.bfloat16), "dp", scatter_dimension=0, tiled=True).astype(
            jnp.float32
        ),
        lax.psum_scatter(grad_v.astype(jnp.bfloat16), "dp", scatter_dimension=0, tiled=True).astype(
            jnp.float32
        ),
        lax.psum_scatter(grad_o.astype(jnp.bfloat16), "dp", scatter_dimension=1, tiled=True).astype(
            jnp.float32
        ),
        lax.psum_scatter(
            qgain_part.reshape(local_heads, HD).astype(jnp.bfloat16),
            "dp",
            scatter_dimension=1,
            tiled=True,
        ).astype(jnp.float32),
        lax.psum_scatter(
            kgain_part.reshape(local_heads, HD).astype(jnp.bfloat16),
            "dp",
            scatter_dimension=1,
            tiled=True,
        ).astype(jnp.float32),
        lax.psum_scatter(
            attn_gain_share.astype(jnp.bfloat16), "dp", scatter_dimension=0, tiled=True
        ).astype(jnp.float32),
        lax.psum_scatter(
            ffn_gain_share.astype(jnp.bfloat16), "dp", scatter_dimension=0, tiled=True
        ).astype(jnp.float32),
        lax.psum_scatter(
            router_share.astype(jnp.bfloat16), "dp", scatter_dimension=0, tiled=True
        ).astype(jnp.float32),
    )
    grad_gate, grad_up, grad_down = (
        lax.psum_scatter(
            jnp.concatenate(gate_grads, axis=0).astype(jnp.bfloat16),
            "dp",
            scatter_dimension=1,
            tiled=True,
        ).astype(jnp.float32),
        lax.psum_scatter(
            jnp.concatenate(up_grads, axis=0).astype(jnp.bfloat16),
            "dp",
            scatter_dimension=1,
            tiled=True,
        ).astype(jnp.float32),
        lax.psum_scatter(
            jnp.concatenate(down_grads, axis=0).astype(jnp.bfloat16),
            "dp",
            scatter_dimension=2,
            tiled=True,
        ).astype(jnp.float32),
    )
    return (
        loss_group.reshape(1),
        grad_in,
        attn_gain_sum.reshape(-1),
        ffn_gain_sum.reshape(-1),
        grad_q,
        grad_k,
        grad_v,
        grad_qgain,
        grad_kgain,
        grad_o,
        router_sum.reshape(-1, expert_count),
        grad_gate,
        grad_up,
        grad_down,
    )


MESH = pl.DeviceIdType.MESH
BF = jnp.bfloat16
F32 = jnp.float32
VMEM_LIMIT = 60 * 1024 * 1024
ANY = pl.BlockSpec(memory_space=pl.ANY)
VM = pl.BlockSpec(memory_space=pltpu.VMEM)


def flip(index, bits):
    for bit in (1, 2, 4):
        if bits & bit:
            index = index + bit * (1 - 2 * ((index // bit) % 2))
    return index


def both(first, second):
    return jnp.logical_and(first, second)


def under(condition, action):
    if condition is None:
        action()
    else:
        pl.when(condition)(action)


class Wire:
    def __init__(self, send_sem, recv_sem):
        self.send_sem, self.recv_sem, self.count, self.sent = send_sem, recv_sem, 0, []

    def slot(self):
        self.count += 1
        return self.count - 1

    def start(self, slot, source, target, device, condition=None):
        copy = pltpu.make_async_remote_copy(
            src_ref=source(),
            dst_ref=target(),
            send_sem=self.send_sem.at[slot],
            recv_sem=self.recv_sem.at[slot],
            device_id=device,
            device_id_type=MESH,
        )
        under(condition, lambda: copy.start())
        self.sent.append((condition, copy))

    def arrive(self, slot, region, device, condition=None):
        copy = pltpu.make_async_remote_copy(
            src_ref=region(),
            dst_ref=region(),
            send_sem=self.send_sem.at[slot],
            recv_sem=self.recv_sem.at[slot],
            device_id=device,
            device_id_type=MESH,
        )
        under(condition, lambda: copy.wait_recv())

    def finish(self):
        for condition, copy in self.sent:
            under(condition, lambda copy=copy: copy.wait_send())
        self.sent = []


class Local:
    def __init__(self, sem):
        self.sem, self.count = sem, 0

    def start(self, source, target):
        copy = pltpu.make_async_copy(source, target, self.sem.at[self.count])
        self.count += 1
        copy.start()
        return copy


def greet(devices):
    barrier = pltpu.get_barrier_semaphore()
    for condition, device in devices:
        under(
            condition,
            lambda device=device: pl.semaphore_signal(
                barrier, inc=1, device_id=device, device_id_type=MESH
            ),
        )
    amount = sum(1 for condition, device in devices if condition is None)
    for condition, device in devices:
        if condition is not None:
            amount = amount + jnp.where(condition, 1, 0)
    pl.semaphore_wait(barrier, amount)


def line_devices(d, t, extent):
    return [(t < extent - 1, (d, t + 1)), (t > 0, (d, t - 1))]


def rows_loop(rows, step, body):
    def run(index, carry):
        body(pl.multiple_of(index * step, step))
        return carry

    lax.fori_loop(0, rows // step, run, 0)


def add_into(target, source, rows):
    def body(start):
        part = pl.ds(start, 16)
        target[part] = (target[part].astype(F32) + source[part].astype(F32)).astype(BF)

    rows_loop(rows, 16, body)


def gather_line(wire, d, t, extent, own, place, on_block):
    up = [wire.slot() for unused in range(extent - 1)]
    down = [wire.slot() for unused in range(extent - 1)]
    up_device, down_device = (d, t + 1), (d, t - 1)
    wire.start(up[0], own, lambda: place(t), up_device, t < extent - 1)
    wire.start(down[0], own, lambda: place(t), down_device, t > 0)
    on_block(0, 0, t, None)
    for step in range(1, extent):
        wire.arrive(up[step - 1], lambda step=step: place(t - step), down_device, t >= step)
        if step < extent - 1:
            wire.start(
                up[step],
                lambda step=step: place(t - step),
                lambda step=step: place(t - step),
                up_device,
                both(t >= step, t < extent - 1),
            )
        wire.arrive(
            down[step - 1], lambda step=step: place(t + step), up_device, t <= extent - 1 - step
        )
        if step < extent - 1:
            wire.start(
                down[step],
                lambda step=step: place(t + step),
                lambda step=step: place(t + step),
                down_device,
                both(t <= extent - 1 - step, t > 0),
            )
        on_block(step, 0, t - step, t >= step)
        on_block(step, 1, t + step, t <= extent - 1 - step)


class LineSum:
    def __init__(self, wire, d, t, extent, block, up_in, down_in, rows, parts):
        self.wire, self.d, self.t, self.extent = wire, d, t, extent
        self.block, self.up_in, self.down_in = block, up_in, down_in
        self.rows, self.parts = rows // parts, parts
        self.up = [[wire.slot() for p in range(parts)] for s in range(extent - 1)]
        self.down = [[wire.slot() for p in range(parts)] for s in range(extent - 1)]

    def cut(self, ref, part):
        return ref.at[pl.ds(part * self.rows, self.rows)]

    def flow(self, step, part, near, index, slots, buffers, to_device, from_device):
        wire, extent = self.wire, self.extent
        block = lambda: self.cut(self.block(index), part)
        if step >= 1:
            source = lambda: self.cut(buffers.at[step - 1], part)
            active = both(both(near <= step, near < extent - 1), near >= 1)
            wire.arrive(slots[step - 1][part], source, from_device, active)
            under(active, lambda: add_into(block(), source(), self.rows))
        wire.start(
            slots[step][part],
            block,
            lambda: self.cut(buffers.at[step], part),
            to_device,
            both(near <= step, near < extent - 1),
        )

    def step(self, step):
        d, t, extent = self.d, self.t, self.extent
        for part in range(self.parts):
            self.flow(
                step,
                part,
                t,
                extent - 1 - step + t,
                self.up,
                self.up_in,
                (d, t + 1),
                (d, t - 1),
            )
            self.flow(
                step,
                part,
                extent - 1 - t,
                step + t - (extent - 1),
                self.down,
                self.down_in,
                (d, t - 1),
                (d, t + 1),
            )

    def last(self):
        d, t, extent = self.d, self.t, self.extent
        for ready, missing, slots, buffers, device in (
            (t > 0, t == 0, self.up, self.up_in, (d, t - 1)),
            (t < extent - 1, t == extent - 1, self.down, self.down_in, (d, t + 1)),
        ):
            buffer = buffers.at[extent - 2]
            for part in range(self.parts):
                self.wire.arrive(
                    slots[extent - 2][part],
                    lambda part=part, buffer=buffer: self.cut(buffer, part),
                    device,
                    ready,
                )

            def clear(buffer=buffer):
                buffer[...] = jnp.zeros(buffer.shape, BF)

            under(missing, clear)


def own_sum(block, up_in, down_in, part, columns):
    return (
        block[part, columns].astype(F32)
        + up_in[part, columns].astype(F32)
        + down_in[part, columns].astype(F32)
    )


def gather_plane(wire, d, t, extent, own, place, half):
    dx, dy, dxy, dc = flip(d, 2), flip(d, 4), flip(d, 6), flip(d, 1)
    to_x, to_y, to_c = (dx, t), (dy, t), (dc, t)
    events = []

    def cut(ref, which):
        return ref.at[pl.ds(which * half, half)]

    def on_block(step, side, index, condition):
        source = own if step == 0 else (lambda: place(d, index))
        event = dict(index=index, condition=condition, slots={})
        for name, device, which in (
            ("x0", to_x, 0),
            ("y1", to_y, 1),
            ("x1", to_x, 1),
            ("y0", to_y, 0),
        ):
            slot = wire.slot()
            event["slots"][name] = slot
            wire.start(
                slot,
                lambda which=which: cut(source(), which),
                lambda which=which: cut(place(d, index), which),
                device,
                condition,
            )
        slot = wire.slot()
        event["slots"]["c"] = slot
        wire.start(slot, source, lambda: place(d, index), to_c, condition)
        events.append(event)
        if step >= 1 and side == 1:
            for earlier in events[:-2]:
                relay(earlier)

    def relay(event):
        if "relayed" in event:
            return
        event["relayed"] = True
        index, condition, slots = event["index"], event["condition"], event["slots"]
        x_part = lambda which: (lambda: cut(place(dx, index), which))
        y_part = lambda which: (lambda: cut(place(dy, index), which))
        wire.arrive(slots["x0"], x_part(0), to_x, condition)
        slots["fy"] = wire.slot()
        wire.start(slots["fy"], x_part(0), x_part(0), to_y, condition)
        wire.arrive(slots["y1"], y_part(1), to_y, condition)
        slots["fx"] = wire.slot()
        wire.start(slots["fx"], y_part(1), y_part(1), to_x, condition)
        wire.arrive(slots["x1"], x_part(1), to_x, condition)
        slots["cx"] = wire.slot()
        wire.start(slots["cx"], lambda: place(dx, index), lambda: place(dx, index), to_c, condition)
        wire.arrive(slots["y0"], y_part(0), to_y, condition)
        slots["cy"] = wire.slot()
        wire.start(slots["cy"], lambda: place(dy, index), lambda: place(dy, index), to_c, condition)

    gather_line(wire, d, t, extent, own, lambda index: place(d, index), on_block)
    for event in events:
        relay(event)
    for event in events:
        index, condition, slots = event["index"], event["condition"], event["slots"]
        wire.arrive(slots["fy"], lambda: cut(place(dxy, index), 0), to_y, condition)
        wire.arrive(slots["fx"], lambda: cut(place(dxy, index), 1), to_x, condition)
        slots["cd"] = wire.slot()
        wire.start(
            slots["cd"], lambda: place(dxy, index), lambda: place(dxy, index), to_c, condition
        )
    for event in events:
        index, condition, slots = event["index"], event["condition"], event["slots"]
        for name, bits in (("c", 1), ("cx", 3), ("cy", 5), ("cd", 7)):
            wire.arrive(
                slots[name], lambda bits=bits: place(flip(d, bits), index), to_c, condition
            )


def plane_order(t):
    top = t // 2
    inner = ((t + 1) // 2) % 2
    return (
        3 - 3 * top,
        2 - top,
        (1 - inner) * (1 - top) + (2 + inner) * top,
        inner * (1 - top) + (3 - inner) * top,
    )


def sum_plane(wire, local, d, t, extent, partial, work, core_in, a_in, b_in, up_in, down_in, half):
    order = plane_order(t)
    to_x, to_y, to_c = (flip(d, 2), t), (flip(d, 4), t), (flip(d, 1), t)
    turns = (3, 1, 2, 0)
    slots_c, slots_a, slots_b, loads = {}, {}, {}, {}

    def cut(ref, which):
        return ref.at[pl.ds(which * half, half)]

    for k in range(extent):
        for i in turns:
            slots_c[k, i] = wire.slot()
            wire.start(
                slots_c[k, i],
                lambda k=k, i=i: partial.at[flip(d, 1 + 2 * i) * extent + order[k]],
                lambda k=k, i=i: core_in.at[k, i],
                to_c,
            )
            loads[k, i] = local.start(
                partial.at[flip(d, 2 * i) * extent + order[k]], work.at[k, i]
            )

    def inverse(index):
        where = jnp.int32(0)
        for k in range(1, extent):
            where = where + k * jnp.where(order[k] == index, 1, 0)
        return where

    line = LineSum(
        wire,
        d,
        t,
        extent,
        lambda index: work.at[inverse(index), 0],
        up_in,
        down_in,
        2 * half,
        1,
    )
    routes_a = ((to_x, 1, 0, 0, 0), (to_y, 2, 0, 1, 1), (to_x, 3, 2, 0, 2), (to_y, 3, 1, 1, 3))
    routes_b = ((to_y, 2, 0, 0), (to_x, 1, 1, 1))
    for turn in range(extent + 2):
        if turn < extent:
            k = turn
            for i in turns:
                loads[k, i].wait()
                wire.arrive(slots_c[k, i], lambda k=k, i=i: core_in.at[k, i], to_c)
                add_into(work.at[k, i], core_in.at[k, i], 2 * half)
            for device, source, target, which, row in (
                routes_a[2],
                routes_a[3],
                routes_a[0],
                routes_a[1],
            ):
                slots_a[k, row] = wire.slot()
                wire.start(
                    slots_a[k, row],
                    lambda k=k, source=source, which=which: cut(work.at[k, source], which),
                    lambda k=k, row=row: a_in.at[k, row],
                    device,
                )
        if 1 <= turn <= extent:
            k = turn - 1
            for device, source, target, which, row in (
                routes_a[2],
                routes_a[3],
                routes_a[0],
                routes_a[1],
            ):
                wire.arrive(slots_a[k, row], lambda k=k, row=row: a_in.at[k, row], device)
                add_into(cut(work.at[k, target], which), a_in.at[k, row], half)
                if row >= 2:
                    to, origin, part, b_row = routes_b[row - 2]
                    slots_b[k, b_row] = wire.slot()
                    wire.start(
                        slots_b[k, b_row],
                        lambda k=k, origin=origin, part=part: cut(work.at[k, origin], part),
                        lambda k=k, b_row=b_row: b_in.at[k, b_row],
                        to,
                    )
        if turn >= 2:
            k = turn - 2
            for device, source, which, row in routes_b:
                wire.arrive(slots_b[k, row], lambda k=k, row=row: b_in.at[k, row], device)
                add_into(cut(work.at[k, 0], which), b_in.at[k, row], half)
            if k < extent - 1:
                line.step(k)
    line.last()
    return work.at[extent - 1, 0]


def plane_devices(d, t, extent):
    return line_devices(d, t, extent) + [(None, (flip(d, bits), t)) for bits in (1, 2, 4)]


def kernel_params(number):
    return pltpu.CompilerParams(
        collective_id=number, has_side_effects=True, vmem_limit_bytes=VMEM_LIMIT
    )


def dma_pair(count):
    return [pltpu.SemaphoreType.DMA((count,)), pltpu.SemaphoreType.DMA((count,))]


def fetch_kernel(
    extent,
    hid,
    qkv,
    o,
    gains,
    gate,
    up,
    down,
    hid_all,
    qkv_all,
    o_all,
    gains_all,
    *rest,
):
    pieces, (stage, send_sem, recv_sem, local_sem) = rest[:8], rest[8:]
    d, t = lax.axis_index("dp"), lax.axis_index("tensor")
    rows = hid.shape[0]
    depth, o_rows = qkv.shape[0], o.shape[0]
    width = o.shape[1]
    greet(line_devices(d, t, extent) + [(None, (flip(d, bits), t)) for bits in range(1, 8)])
    wire, local = Wire(send_sem, recv_sem), Local(local_sem)
    dx, dy, dxy, dc = flip(d, 2), flip(d, 4), flip(d, 6), flip(d, 1)
    to_x, to_y, to_c = (dx, t), (dy, t), (dc, t)

    def region(device, which):
        start = pl.multiple_of(device * width, width)
        if which is None:
            return [qkv_all.at[pl.ds(device * depth, depth)], o_all.at[:, pl.ds(start, width)]]
        return [
            qkv_all.at[pl.ds(device * depth + which * (depth // 2), depth // 2)],
            o_all.at[pl.ds(which * (o_rows // 2), o_rows // 2), pl.ds(start, width)],
        ]

    def own(which):
        if which is None:
            return [qkv, o]
        return [
            qkv.at[pl.ds(which * (depth // 2), depth // 2)],
            o.at[pl.ds(which * (o_rows // 2), o_rows // 2)],
        ]

    def send(device, sources, targets):
        slots = []
        for source, target in zip(sources, targets):
            slot = wire.slot()
            wire.start(slot, lambda: source, lambda: target, device)
            slots.append(slot)
        return slots

    def arrive(slots, regions, device):
        for slot, part in zip(slots, regions):
            wire.arrive(slot, lambda: part, device)

    def block(index):
        return hid_all.at[pl.ds(index * rows, rows)]

    x_slots, y_slots, c_slots = {}, {}, {}
    for which, other in ((0, 1), (1, 0)):
        x_slots[which] = send(to_x, own(which), region(d, which))
        y_slots[other] = send(to_y, own(other), region(d, other))
    c_slots[1] = send(to_c, own(None), region(d, None))
    passed = {}
    loads, copies = [], []
    for place, weight in enumerate((gate, up, down)):
        loads.append(local.start(weight, stage.at[place]))

    def store_pieces():
        for load in loads:
            load.wait()
        for bits in range(8):
            first = 2 * flip(d, bits)
            for place in range(3):
                copies.append(
                    local.start(stage.at[place, pl.ds(first, 2)], pieces[bits].at[place])
                )

    def on_block(step, side, index, condition):
        if side == 1 or step == 0:
            return
        if step == 1:
            store_pieces()
            arrive(x_slots[0], region(dx, 0), to_x)
            passed["y"] = send(to_y, region(dx, 0), region(dx, 0))
            arrive(y_slots[1], region(dy, 1), to_y)
            passed["x"] = send(to_x, region(dy, 1), region(dy, 1))
        if step == 2:
            arrive(x_slots[1], region(dx, 1), to_x)
            c_slots[3] = send(to_c, region(dx, None), region(dx, None))
            arrive(y_slots[0], region(dy, 0), to_y)
            c_slots[5] = send(to_c, region(dy, None), region(dy, None))

    copies.append(local.start(hid, block(t)))
    for source, target in zip(own(None), region(d, None)):
        copies.append(local.start(source, target))
    gather_line(wire, d, t, extent, lambda: hid, block, on_block)
    gain_slots = {}
    for bits in range(1, 8):
        gain_slots[bits] = wire.slot()
        wire.start(
            gain_slots[bits],
            lambda: gains,
            lambda bits=bits: gains_all.at[bits],
            (flip(d, bits), t),
        )
    copies.append(local.start(gains, gains_all.at[0]))
    arrive(passed["y"], region(dxy, 0), to_y)
    arrive(passed["x"], region(dxy, 1), to_x)
    c_slots[7] = send(to_c, region(dxy, None), region(dxy, None))
    for bits in (1, 3, 5, 7):
        arrive(c_slots[bits], region(flip(d, bits), None), to_c)
    for bits in range(1, 8):
        wire.arrive(
            gain_slots[bits], lambda bits=bits: gains_all.at[bits], (flip(d, bits), t)
        )
    for copy in copies:
        copy.wait()
    wire.finish()


def fetch(extent, hid, qkv, o, gains, gate, up, down):
    rows, model_width = hid.shape
    piece = jax.ShapeDtypeStruct((3, 2) + gate.shape[1:], BF)
    return pl.pallas_call(
        functools.partial(fetch_kernel, extent),
        out_shape=[
            jax.ShapeDtypeStruct((rows * extent, model_width), BF),
            jax.ShapeDtypeStruct((8 * qkv.shape[0], qkv.shape[1]), BF),
            jax.ShapeDtypeStruct((o.shape[0], 8 * o.shape[1]), BF),
            jax.ShapeDtypeStruct((8,) + gains.shape, F32),
        ]
        + [piece] * 8,
        in_specs=[VM] * 4 + [ANY] * 3,
        out_specs=[ANY] * 12,
        scratch_shapes=[pltpu.VMEM((3,) + gate.shape, BF)]
        + dma_pair(64) + [pltpu.SemaphoreType.DMA((40,))],
        compiler_params=kernel_params(1),
        cost_estimate=pl.CostEstimate(flops=0, bytes_accessed=100_000_000, transcendentals=0),
    )(hid, qkv, o, gains, gate, up, down)


def line_total_kernel(extent, value, total, inbox, send_sem, recv_sem):
    d, t = lax.axis_index("dp"), lax.axis_index("tensor")
    peers = [(d, (t + k) % extent) for k in range(1, extent)]
    greet([(None, peer) for peer in peers])
    wire = Wire(send_sem, recv_sem)
    slots = []
    for k, peer in enumerate(peers):
        slot = wire.slot()
        slots.append(slot)
        wire.start(slot, lambda: value, lambda k=k: inbox.at[k], peer)
    result = value[...]
    for k, peer in enumerate(peers):
        wire.arrive(slots[k], lambda k=k: inbox.at[k], peer)
        result = result + inbox[k]
    total[...] = result
    wire.finish()


def line_total(extent, number, value):
    return pl.pallas_call(
        functools.partial(line_total_kernel, extent),
        out_shape=jax.ShapeDtypeStruct(value.shape, F32),
        in_specs=[VM],
        out_specs=VM,
        scratch_shapes=[pltpu.VMEM((extent - 1,) + value.shape, F32)] + dma_pair(extent - 1),
        compiler_params=kernel_params(number),
        cost_estimate=pl.CostEstimate(flops=0, bytes_accessed=10_000_000, transcendentals=0),
    )(value)


def enter_kernel(
    extent,
    partial,
    hid,
    gain,
    router,
    chosen,
    middle,
    gates,
    ffn_own,
    tokens,
    work,
    up_in,
    down_in,
    packet,
    send_sem,
    recv_sem,
    local_sem,
):
    d, t = lax.axis_index("dp"), lax.axis_index("tensor")
    rows, width = hid.shape
    greet(plane_devices(d, t, extent))
    wire, local = Wire(send_sem, recv_sem), Local(local_sem)
    local.start(partial, work).wait()
    line = LineSum(
        wire, d, t, extent, lambda index: work.at[index], up_in, down_in, rows, 2
    )
    for step in range(extent - 1):
        line.step(step)
    line.last()
    mine = work.at[t]
    everything = pl.ds(0, width)

    def body(start):
        part = pl.ds(start, 16)
        value = hid[part].astype(F32) + own_sum(
            mine, up_in.at[extent - 2], down_in.at[extent - 2], part, everything
        )
        middle[part] = value
        unit = value * lax.rsqrt(jnp.mean(value * value, axis=-1, keepdims=True) + EPSILON)
        packet[part, 0:width] = (unit * gain[...]).astype(BF)

    rows_loop(rows, 16, body)
    ffn_own[...] = packet[:, 0:width]
    logits = jnp.dot(packet[:, 0:width], router[...], preferred_element_type=F32)
    lane = lax.broadcasted_iota(jnp.int32, logits.shape, 1)
    top = jnp.max(jnp.where(lane < 16, logits, -1e30), axis=-1, keepdims=True)
    powers = jnp.where(lane < 32, jnp.exp(logits - top), 0.0)
    probs = powers / jnp.sum(jnp.where(lane < 16, powers, 0.0), axis=-1, keepdims=True)
    gates[...] = probs
    coeff = probs * chosen[...]
    high = coeff.astype(BF).astype(F32)
    packet[:, width : width + 128] = jnp.where(lane < 16, high, coeff - high).astype(BF)

    def place(device, index):
        return tokens.at[device * extent + index]

    copy = local.start(packet, place(d, t))
    gather_plane(wire, d, t, extent, lambda: packet, place, rows // 2)
    copy.wait()
    wire.finish()


def enter(extent, partial, hid, gain, router, chosen):
    rows, width = hid.shape
    return pl.pallas_call(
        functools.partial(enter_kernel, extent),
        out_shape=[
            jax.ShapeDtypeStruct((rows, width), F32),
            jax.ShapeDtypeStruct((rows, 128), F32),
            jax.ShapeDtypeStruct((rows, width), BF),
            jax.ShapeDtypeStruct((8 * extent, rows, width + 128), BF),
        ],
        in_specs=[ANY, VM, VM, VM, VM],
        out_specs=[VM, VM, VM, ANY],
        scratch_shapes=[
            pltpu.VMEM((extent, rows, width), BF),
            pltpu.VMEM((extent - 1, rows, width), BF),
            pltpu.VMEM((extent - 1, rows, width), BF),
            pltpu.VMEM((rows, width + 128), BF),
        ]
        + dma_pair(100)
        + [pltpu.SemaphoreType.DMA((2,))],
        compiler_params=kernel_params(3),
        cost_estimate=pl.CostEstimate(flops=0, bytes_accessed=300_000_000, transcendentals=0),
    )(partial, hid, gain, router, chosen)


def sum_scratch(extent, rows, width):
    return [
        pltpu.VMEM((extent, 4, rows, width), BF),
        pltpu.VMEM((extent, 4, rows, width), BF),
        pltpu.VMEM((extent, 4, rows // 2, width), BF),
        pltpu.VMEM((extent, 2, rows // 2, width), BF),
        pltpu.VMEM((extent - 1, rows, width), BF),
        pltpu.VMEM((extent - 1, rows, width), BF),
    ]


def turn_kernel(
    extent,
    partial,
    middle,
    teacher,
    weight,
    grad_output,
    row_loss,
    grads,
    work,
    core_in,
    a_in,
    b_in,
    up_in,
    down_in,
    packet,
    send_sem,
    recv_sem,
    local_sem,
):
    d, t = lax.axis_index("dp"), lax.axis_index("tensor")
    rows, width = middle.shape
    greet(plane_devices(d, t, extent))
    wire, local = Wire(send_sem, recv_sem), Local(local_sem)
    mine = sum_plane(
        wire, local, d, t, extent, partial, work, core_in, a_in, b_in, up_in, down_in, rows // 2
    )
    everything = pl.ds(0, width)

    def body(start):
        part = pl.ds(start, 16)
        output = middle[part] + own_sum(
            mine, up_in.at[extent - 2], down_in.at[extent - 2], part, everything
        )
        mismatch = output - teacher[part].astype(F32)
        scaled = mismatch * weight[part, 0:1]
        grad_output[part] = scaled
        packet[part] = scaled.astype(BF)
        row_loss[part] = jnp.broadcast_to(
            jnp.sum(scaled * mismatch, axis=-1, keepdims=True), (16, 128)
        )

    rows_loop(rows, 16, body)

    def place(device, index):
        return grads.at[device * extent + index]

    copy = local.start(packet, place(d, t))
    gather_plane(wire, d, t, extent, lambda: packet, place, rows // 2)
    copy.wait()
    wire.finish()


def turn(extent, partial, middle, teacher, weight):
    rows, width = middle.shape
    return pl.pallas_call(
        functools.partial(turn_kernel, extent),
        out_shape=[
            jax.ShapeDtypeStruct((rows, width), F32),
            jax.ShapeDtypeStruct((rows, 128), F32),
            jax.ShapeDtypeStruct((8 * extent, rows, width), BF),
        ],
        in_specs=[ANY, VM, VM, VM],
        out_specs=[VM, VM, ANY],
        scratch_shapes=sum_scratch(extent, rows, width)
        + [pltpu.VMEM((rows, width), BF)]
        + dma_pair(150)
        + [pltpu.SemaphoreType.DMA((20,))],
        compiler_params=kernel_params(4),
        cost_estimate=pl.CostEstimate(flops=0, bytes_accessed=450_000_000, transcendentals=0),
    )(partial, middle, teacher, weight)


def leave_kernel(
    extent,
    partial,
    middle,
    grad_output,
    gates,
    chosen,
    gain,
    router_t,
    grad_middle,
    grad_logits,
    gain_part,
    grads,
    work,
    core_in,
    a_in,
    b_in,
    up_in,
    down_in,
    packet,
    extra,
    send_sem,
    recv_sem,
    local_sem,
):
    d, t = lax.axis_index("dp"), lax.axis_index("tensor")
    rows, width = middle.shape
    greet(plane_devices(d, t, extent))
    wire, local = Wire(send_sem, recv_sem), Local(local_sem)
    mine = sum_plane(
        wire, local, d, t, extent, partial, work, core_in, a_in, b_in, up_in, down_in, rows // 2
    )
    up_last, down_last = up_in.at[extent - 2], down_in.at[extent - 2]
    coeff_grad = (
        own_sum(mine, up_last, down_last, pl.ds(0, rows), pl.ds(width, 128)) * chosen[...]
    )
    lane = lax.broadcasted_iota(jnp.int32, coeff_grad.shape, 1)
    probs = jnp.where(lane < 16, gates[...], 0.0)
    coeff_grad = jnp.where(lane < 16, coeff_grad, 0.0)
    logit_grad = probs * (coeff_grad - jnp.sum(coeff_grad * probs, axis=-1, keepdims=True))
    grad_logits[...] = logit_grad
    high = logit_grad.astype(BF)
    low_part = (logit_grad - high.astype(F32)).astype(BF)
    for begin in range(0, width, 512):
        columns = slice(begin, begin + 512)
        extra[:, columns] = jnp.dot(
            high, router_t[:, columns], preferred_element_type=F32
        ) + jnp.dot(low_part, router_t[:, columns], preferred_element_type=F32)
    gain_part[...] = jnp.zeros(gain_part.shape, F32)

    def body(start):
        part = pl.ds(start, 16)
        grad = own_sum(mine, up_last, down_last, part, pl.ds(0, width)) + extra[part]
        value = middle[part]
        inverse = lax.rsqrt(jnp.mean(value * value, axis=-1, keepdims=True) + EPSILON)
        unit = value * inverse
        product = grad * unit
        gain_part[...] += product[0:8] + product[8:16]
        scaled = grad * gain[...]
        result = grad_output[part] + inverse * (
            scaled - unit * jnp.mean(scaled * unit, axis=-1, keepdims=True)
        )
        grad_middle[part] = result
        packet[part] = result.astype(BF)

    rows_loop(rows, 16, body)

    def place(index):
        return grads.at[index]

    copy = local.start(packet, place(t))
    gather_line(wire, d, t, extent, lambda: packet, place, lambda *unused: None)
    copy.wait()
    wire.finish()


def leave(extent, partial, middle, grad_output, gates, chosen, gain, router_t):
    rows, width = middle.shape
    return pl.pallas_call(
        functools.partial(leave_kernel, extent),
        out_shape=[
            jax.ShapeDtypeStruct((rows, width), F32),
            jax.ShapeDtypeStruct((rows, 128), F32),
            jax.ShapeDtypeStruct((8, width), F32),
            jax.ShapeDtypeStruct((extent, rows, width), BF),
        ],
        in_specs=[ANY, VM, VM, VM, VM, VM, VM],
        out_specs=[VM, VM, VM, ANY],
        scratch_shapes=sum_scratch(extent, rows, width + 128)
        + [pltpu.VMEM((rows, width), BF), pltpu.VMEM((rows, width), F32)]
        + dma_pair(80)
        + [pltpu.SemaphoreType.DMA((20,))],
        compiler_params=kernel_params(5),
        cost_estimate=pl.CostEstimate(flops=0, bytes_accessed=350_000_000, transcendentals=0),
    )(partial, middle, grad_output, gates, chosen, gain, router_t)


def close_kernel(
    extent,
    partial,
    grad_middle,
    grad_qkv,
    grad_o,
    small,
    gains,
    grad_in,
    qkv_out,
    o_out,
    small_out,
    work,
    up_in,
    down_in,
    q_work,
    q_core,
    q_a,
    q_b,
    o_work,
    o_core,
    o_a,
    o_b,
    small_in,
    small_sum,
    small_last,
    send_sem,
    recv_sem,
    local_sem,
):
    d, t = lax.axis_index("dp"), lax.axis_index("tensor")
    rows, width = grad_middle.shape
    depth, o_width = qkv_out.shape[0], o_out.shape[1]
    line_peers = [(d, (t + k) % extent) for k in range(1, extent)]
    greet(
        [(None, peer) for peer in line_peers]
        + [(None, (flip(d, bits), t)) for bits in range(1, 8)]
    )
    wire, local = Wire(send_sem, recv_sem), Local(local_sem)
    to_x, to_y, to_c = (flip(d, 2), t), (flip(d, 4), t), (flip(d, 1), t)

    def slices(device):
        start = pl.multiple_of(device * o_width, o_width)
        return [
            grad_qkv.at[pl.ds(device * depth, depth)],
            grad_o.at[:, pl.ds(start, o_width)],
        ]

    turns = (3, 1, 2, 0)
    c_slots, loads = {}, {}
    work_load = local.start(partial, work)
    small_slots = []
    for k, peer in enumerate(line_peers):
        slot = wire.slot()
        small_slots.append(slot)
        wire.start(
            slot,
            lambda k=k: small.at[(t + k + 1) % extent],
            lambda k=k: small_in.at[k],
            peer,
        )
    for i in turns:
        sources = slices(flip(d, 1 + 2 * i))
        c_slots[i] = [wire.slot(), wire.slot()]
        wire.start(c_slots[i][0], lambda: sources[0], lambda i=i: q_core.at[i], to_c)
        wire.start(c_slots[i][1], lambda: sources[1], lambda i=i: o_core.at[i], to_c)
        mine = slices(flip(d, 2 * i))
        loads[i] = [local.start(mine[0], q_work.at[i]), local.start(mine[1], o_work.at[i])]
    work_load.wait()
    line = LineSum(
        wire, d, t, extent, lambda index: work.at[index], up_in, down_in, rows, 2
    )
    line.step(0)

    def cut(ref, which):
        half = ref.shape[0] // 2
        return ref.at[pl.ds(which * half, half)]

    a_slots, b_slots = {}, {}
    routes_a = ((to_x, 3, 2, 0, 0), (to_y, 3, 1, 1, 1), (to_x, 1, 0, 0, 2), (to_y, 2, 0, 1, 3))
    routes_b = ((to_y, 2, 0, 0), (to_x, 1, 1, 1))

    def core_add(i):
        for load in loads[i]:
            load.wait()
        wire.arrive(c_slots[i][0], lambda: q_core.at[i], to_c)
        wire.arrive(c_slots[i][1], lambda: o_core.at[i], to_c)
        add_into(q_work.at[i], q_core.at[i], q_work.shape[1])
        add_into(o_work.at[i], o_core.at[i], o_work.shape[1])

    def a_send(route):
        device, source, target, which, row = route
        a_slots[row] = [wire.slot(), wire.slot()]
        wire.start(
            a_slots[row][0], lambda: cut(q_work.at[source], which), lambda: q_a.at[row], device
        )
        wire.start(
            a_slots[row][1], lambda: cut(o_work.at[source], which), lambda: o_a.at[row], device
        )

    core_add(3)
    a_send(routes_a[0])
    a_send(routes_a[1])
    core_add(1)
    a_send(routes_a[2])
    core_add(2)
    a_send(routes_a[3])
    core_add(0)
    line.step(1)
    for device, source, target, which, row in routes_a:
        wire.arrive(a_slots[row][0], lambda: q_a.at[row], device)
        wire.arrive(a_slots[row][1], lambda: o_a.at[row], device)
        add_into(cut(q_work.at[target], which), q_a.at[row], q_a.shape[1])
        add_into(cut(o_work.at[target], which), o_a.at[row], o_a.shape[1])
        if row < 2:
            to, origin, part, b_row = routes_b[row]
            b_slots[b_row] = [wire.slot(), wire.slot()]
            wire.start(
                b_slots[b_row][0],
                lambda: cut(q_work.at[origin], part),
                lambda: q_b.at[b_row],
                to,
            )
            wire.start(
                b_slots[b_row][1],
                lambda: cut(o_work.at[origin], part),
                lambda: o_b.at[b_row],
                to,
            )
    for k, peer in enumerate(line_peers):
        wire.arrive(small_slots[k], lambda k=k: small_in.at[k], peer)
    total = small[t] + small_in[0]
    for k in range(1, extent - 1):
        total = total + small_in[k]
    small_sum[:, 0:16] = total
    small_sum[:, 16:24] = jnp.broadcast_to(gains[...][None], (8, 8, 128))
    last_slots = {}
    for bits in range(1, 8):
        last_slots[bits] = wire.slot()
        wire.start(
            last_slots[bits],
            lambda bits=bits: small_sum.at[flip(d, bits)],
            lambda bits=bits: small_last.at[bits],
            (flip(d, bits), t),
        )
    line.step(2)
    for device, source, which, row in routes_b:
        wire.arrive(b_slots[row][0], lambda: q_b.at[row], device)
        wire.arrive(b_slots[row][1], lambda: o_b.at[row], device)
        for kept, came, result in (
            (cut(q_work.at[0], which), q_b.at[row], cut(qkv_out, which)),
            (cut(o_work.at[0], which), o_b.at[row], cut(o_out, which)),
        ):

            def body(start, kept=kept, came=came, result=result):
                part = pl.ds(start, 16)
                result[part] = kept[part].astype(F32) + came[part].astype(F32)

            rows_loop(kept.shape[0], 16, body)
    line.last()
    mine = work.at[t]

    def body(start):
        part = pl.ds(start, 16)
        grad_in[part] = grad_middle[part] + own_sum(
            mine, up_in.at[extent - 2], down_in.at[extent - 2], part, pl.ds(0, width)
        )

    rows_loop(rows, 16, body)
    total = small_sum[d]
    for bits in range(1, 8):
        wire.arrive(
            last_slots[bits], lambda bits=bits: small_last.at[bits], (flip(d, bits), t)
        )
        total = total + small_last[bits]
    small_out[...] = total
    wire.finish()


def close(extent, partial, grad_middle, grad_qkv, grad_o, small, gains):
    rows, width = grad_middle.shape
    depth, q_width = grad_qkv.shape[0] // 8, grad_qkv.shape[1]
    o_rows, o_width = grad_o.shape[0], grad_o.shape[1] // 8
    scratch = [
        pltpu.VMEM((extent, rows, width), BF),
        pltpu.VMEM((extent - 1, rows, width), BF),
        pltpu.VMEM((extent - 1, rows, width), BF),
    ]
    for tall, wide in ((depth, q_width), (o_rows, o_width)):
        scratch += [
            pltpu.VMEM((4, tall, wide), BF),
            pltpu.VMEM((4, tall, wide), BF),
            pltpu.VMEM((4, tall // 2, wide), BF),
            pltpu.VMEM((2, tall // 2, wide), BF),
        ]
    scratch += [
        pltpu.VMEM((extent - 1, 8, 16, 128), F32),
        pltpu.VMEM((8, 24, 128), F32),
        pltpu.VMEM((8, 24, 128), F32),
    ]
    return pl.pallas_call(
        functools.partial(close_kernel, extent),
        out_shape=[
            jax.ShapeDtypeStruct((rows, width), F32),
            jax.ShapeDtypeStruct((depth, q_width), F32),
            jax.ShapeDtypeStruct((o_rows, o_width), F32),
            jax.ShapeDtypeStruct((24, 128), F32),
        ],
        in_specs=[ANY, VM, ANY, ANY, VM, VM],
        out_specs=[VM] * 4,
        scratch_shapes=scratch + dma_pair(64) + [pltpu.SemaphoreType.DMA((16,))],
        compiler_params=kernel_params(7),
        cost_estimate=pl.CostEstimate(flops=0, bytes_accessed=150_000_000, transcendentals=0),
    )(partial, grad_middle, grad_qkv, grad_o, small, gains)


def assemble(pieces, in_weight, out_weight, sem, d):
    copies = []
    slab = pieces[0].shape[2]
    for bits in range(8):
        start = pl.multiple_of(flip(d, bits) * slab, slab)
        for place in range(3):
            for e in range(2):
                if place < 2:
                    column = (2 * place + e) * slab
                    target = in_weight.at[pl.ds(start, slab), pl.ds(column, slab)]
                else:
                    target = out_weight.at[pl.ds(e * slab, slab), pl.ds(start, slab)]
                copies.append(
                    pltpu.make_async_copy(
                        pieces[bits].at[place, e], target, sem.at[bits * 6 + place * 2 + e]
                    )
                )
    for copy in copies:
        copy.start()
    for copy in copies:
        copy.wait()


def coefficients(columns, d, slab):
    values = columns.astype(F32)
    lane = lax.broadcasted_iota(jnp.int32, values.shape, 1)
    parts = []
    for e in range(2):
        wanted = jnp.logical_or(lane == 2 * d + e, lane == 16 + 2 * d + e)
        one = jnp.sum(jnp.where(wanted, values, 0.0), axis=-1, keepdims=True)
        parts.append(jnp.broadcast_to(one, (values.shape[0], slab)))
    return jnp.concatenate(parts, axis=1)


def experts_kernel(tile, tokens, *rest):
    pieces, (hidden, out, in_weight, out_weight, sem) = rest[:8], rest[8:]
    d = lax.axis_index("dp")
    width = out.shape[1]
    units = out_weight.shape[0]

    @pl.when(pl.program_id(0) == 0)
    def _():
        assemble(pieces, in_weight, out_weight, sem, d)

    def body(start):
        part = pl.ds(start, tile)
        both_values = jnp.dot(
            tokens[part, 0:width], in_weight[...], preferred_element_type=F32
        )
        hidden[part] = both_values.astype(BF)
        gate_value, up_value = both_values[:, :units], both_values[:, units:]
        coeff = coefficients(tokens[part, width : width + 128], d, units // 2)
        active = (coeff * (gate_value * jax.nn.sigmoid(gate_value)) * up_value).astype(BF)
        out[part] = jnp.dot(active, out_weight[...], preferred_element_type=F32).astype(BF)

    rows_loop(tokens.shape[0], tile, body)


def experts(tokens, pieces):
    count, wide = tokens.shape
    width = wide - 128
    slab = pieces[0].shape[2]
    block = 512
    return pl.pallas_call(
        functools.partial(experts_kernel, 256),
        grid=(count // block,),
        out_shape=[
            jax.ShapeDtypeStruct((count, 4 * slab), BF),
            jax.ShapeDtypeStruct((count, width), BF),
        ],
        in_specs=[pl.BlockSpec((block, wide), lambda i: (i, 0))] + [ANY] * 8,
        out_specs=[
            pl.BlockSpec((block, 4 * slab), lambda i: (i, 0)),
            pl.BlockSpec((block, width), lambda i: (i, 0)),
        ],
        scratch_shapes=[
            pltpu.VMEM((width, 4 * slab), BF),
            pltpu.VMEM((2 * slab, width), BF),
            pltpu.SemaphoreType.DMA((48,)),
        ],
        compiler_params=pltpu.CompilerParams(vmem_limit_bytes=VMEM_LIMIT),
        cost_estimate=pl.CostEstimate(
            flops=2 * count * width * 6 * slab, bytes_accessed=50_000_000, transcendentals=0
        ),
    )(tokens, *pieces)


def experts_back_kernel(tile, grads, tokens, hidden, *rest):
    pieces, (out, *others) = rest[:8], rest[8:]
    results, (in_weight, out_weight, in_total, out_total, sem) = others[:8], others[8:]
    d = lax.axis_index("dp")
    width = grads.shape[1]
    units, slab = out_weight.shape[0], out_weight.shape[0] // 2

    @pl.when(pl.program_id(0) == 0)
    def _():
        assemble(pieces, in_weight, out_weight, sem, d)
        in_total[...] = jnp.zeros(in_total.shape, F32)
        out_total[...] = jnp.zeros(out_total.shape, F32)

    def body(start):
        part = pl.ds(start, tile)
        incoming = grads[part]
        grad_active = lax.dot_general(
            incoming, out_weight[...], (((1,), (1,)), ((), ())), preferred_element_type=F32
        )
        gate_value = hidden[part, 0:units].astype(F32)
        up_value = hidden[part, units : 2 * units].astype(F32)
        coeff = coefficients(tokens[part, width : width + 128], d, slab)
        sigmoid_value = jax.nn.sigmoid(gate_value)
        silu_value = gate_value * sigmoid_value
        inner = grad_active * coeff
        direct = silu_value * up_value
        active = (coeff * direct).astype(BF)
        product = grad_active * direct
        lane = lax.broadcasted_iota(jnp.int32, (tile, 128), 1)
        sums = jnp.zeros((tile, 128), F32)
        for e in range(2):
            one = jnp.sum(product[:, e * slab : (e + 1) * slab], axis=-1, keepdims=True)
            sums = sums + jnp.where(lane == 2 * d + e, one, 0.0)
        grad_gate = inner * up_value * sigmoid_value * (1.0 + gate_value * (1.0 - sigmoid_value))
        grad_hidden = jnp.concatenate([grad_gate, inner * silu_value], axis=1).astype(BF)
        out[part, 0:width] = lax.dot_general(
            grad_hidden, in_weight[...], (((1,), (1,)), ((), ())), preferred_element_type=F32
        ).astype(BF)
        out[part, width : width + 128] = sums.astype(BF)
        out_total[...] += lax.dot_general(
            active, incoming, (((0,), (0,)), ((), ())), preferred_element_type=F32
        )
        in_total[...] += lax.dot_general(
            tokens[part, 0:width],
            grad_hidden,
            (((0,), (0,)), ((), ())),
            preferred_element_type=F32,
        )

    rows_loop(grads.shape[0], tile, body)

    @pl.when(pl.program_id(0) == pl.num_programs(0) - 1)
    def _():
        in_weight[...] = in_total[...].astype(BF)
        out_weight[...] = out_total[...].astype(BF)
        copies = []
        for bits in range(8):
            start = pl.multiple_of(flip(d, bits) * slab, slab)
            for place in range(3):
                for e in range(2):
                    if place < 2:
                        column = (2 * place + e) * slab
                        source = in_weight.at[pl.ds(start, slab), pl.ds(column, slab)]
                    else:
                        source = out_weight.at[pl.ds(e * slab, slab), pl.ds(start, slab)]
                    copies.append(
                        pltpu.make_async_copy(
                            source, results[bits].at[place, e], sem.at[bits * 6 + place * 2 + e]
                        )
                    )
        for copy in copies:
            copy.start()
        for copy in copies:
            copy.wait()


def experts_back(grads, tokens, hidden, pieces):
    count, wide = tokens.shape
    width = wide - 128
    slab = pieces[0].shape[2]
    block = 256
    return pl.pallas_call(
        functools.partial(experts_back_kernel, 256),
        grid=(count // block,),
        out_shape=[jax.ShapeDtypeStruct((count, wide), BF)]
        + [jax.ShapeDtypeStruct(pieces[0].shape, BF)] * 8,
        in_specs=[
            pl.BlockSpec((block, width), lambda i: (i, 0)),
            pl.BlockSpec((block, wide), lambda i: (i, 0)),
            pl.BlockSpec((block, 4 * slab), lambda i: (i, 0)),
        ]
        + [ANY] * 8,
        out_specs=[pl.BlockSpec((block, wide), lambda i: (i, 0))] + [ANY] * 8,
        scratch_shapes=[
            pltpu.VMEM((width, 4 * slab), BF),
            pltpu.VMEM((2 * slab, width), BF),
            pltpu.VMEM((width, 4 * slab), F32),
            pltpu.VMEM((2 * slab, width), F32),
            pltpu.SemaphoreType.DMA((48,)),
        ],
        compiler_params=pltpu.CompilerParams(vmem_limit_bytes=VMEM_LIMIT),
        cost_estimate=pl.CostEstimate(
            flops=2 * count * width * 12 * slab, bytes_accessed=80_000_000, transcendentals=0
        ),
    )(grads, tokens, hidden, *pieces)


def spread_kernel(*refs):
    pieces, outs = refs[:8], refs[8:]
    d = lax.axis_index("dp")
    for bits in range(8):
        first = 2 * flip(d, bits)
        for place in range(3):
            for e in range(2):
                outs[place][first + e] = pieces[bits][place, e].astype(F32)


def spread(pieces):
    shape = (16,) + pieces[0].shape[2:]
    return pl.pallas_call(
        spread_kernel,
        out_shape=[jax.ShapeDtypeStruct(shape, F32)] * 3,
        in_specs=[VM] * 8,
        out_specs=[VM] * 3,
        compiler_params=pltpu.CompilerParams(vmem_limit_bytes=VMEM_LIMIT),
        cost_estimate=pl.CostEstimate(flops=0, bytes_accessed=20_000_000, transcendentals=0),
    )(*pieces)


def exchange(value, bits):
    if bits == 0:
        return value
    return lax.ppermute(value, "dp", [(i, i ^ bits) for i in range(8)])


def per_device_block(
    hidden_in,
    teacher,
    lengths,
    routes,
    attn_norm_gain,
    ffn_norm_gain,
    q_weight,
    k_weight,
    v_weight,
    q_gain,
    k_gain,
    o_weight,
    router_weight,
    gate_weight,
    up_weight,
    down_weight,
):
    dp_count = lax.axis_size("dp")
    extent = lax.axis_size("tensor")
    d = lax.axis_index("dp")
    t = lax.axis_index("tensor")
    rows, width = hidden_in.shape
    seq_len = rows * extent
    all_tokens = seq_len * dp_count
    length = lengths[d]
    total_count = jnp.sum(lengths).astype(F32)
    attn_gain = attn_norm_gain.astype(F32)
    ffn_gain = ffn_norm_gain.astype(F32)[None, :]
    root_size = math.sqrt(HD)
    expert_count = router_weight.shape[1]
    head_width = q_gain.shape[1]
    local_heads = q_gain.shape[0]
    columns = local_heads * HD

    qkv_own = jnp.concatenate([q_weight, k_weight, v_weight], axis=1)
    gains_own = lax.dynamic_update_slice(
        jnp.zeros((2 * local_heads, HD), F32),
        jnp.concatenate([q_gain, k_gain], axis=0).astype(F32),
        (0, d * head_width),
    )
    hidden_bf, qkv_full, o_full, gains_all, *sent = fetch(
        extent, hidden_in, qkv_own, o_weight, gains_own, gate_weight, up_weight, down_weight
    )
    pieces = [exchange(piece, bits) for bits, piece in enumerate(sent)]
    gains_full = jnp.sum(gains_all, axis=0)
    query_gain = gains_full[:local_heads].reshape(-1)
    key_gain = gains_full[local_heads:].reshape(-1)

    hidden_all = hidden_bf.astype(F32)
    inverse_one = inverse_rms(hidden_all)
    unit_one = hidden_all * inverse_one
    normed = (unit_one * attn_gain).astype(BF)
    qkv = jnp.dot(normed, qkv_full, preferred_element_type=F32)
    query_raw, key_raw = qkv[:, :columns], qkv[:, columns : 2 * columns]
    value_low = qkv[:, 2 * columns :].astype(BF)
    squares = jnp.stack(
        [jnp.sum(query_raw * query_raw, axis=1), jnp.sum(key_raw * key_raw, axis=1)]
    )
    squares = line_total(extent, 2, squares.reshape(-1, 128)).reshape(2, seq_len)
    query_inv = lax.rsqrt(squares[0] / width + EPSILON)[:, None]
    key_inv = lax.rsqrt(squares[1] / width + EPSILON)[:, None]
    query_unit = query_raw * query_inv
    key_unit = key_raw * key_inv
    positions = jnp.arange(seq_len)
    frequency = THETA ** (-jnp.arange(HD // 2).astype(F32) / (HD // 2))
    angles = positions.astype(F32)[:, None] * frequency[None, :]
    cosine = jnp.cos(angles)[:, None, :]
    sinus_table = jnp.sin(angles)[:, None, :]
    queries = rotate(
        (query_unit * query_gain).reshape(seq_len, local_heads, HD), cosine, sinus_table, 1.0
    ).astype(BF)
    key_rows = rotate(
        (key_unit * key_gain).reshape(seq_len, local_heads, HD), cosine, sinus_table, 1.0
    ).astype(BF)
    value_rows = value_low.reshape(seq_len, local_heads, HD)
    scores = (
        jnp.einsum("qhd,khd->hqk", queries, key_rows, preferred_element_type=F32) / root_size
    )
    allowed = (positions[None, :] <= positions[:, None]) & (positions[None, :] < length)
    scores = jnp.where(allowed[None], scores, -1e30)
    row_top = jnp.max(scores, axis=-1, keepdims=True)
    exponent = jnp.exp(scores - row_top)
    probs_float = exponent / jnp.sum(exponent, axis=-1, keepdims=True)
    probs_low = probs_float.astype(BF)
    mixed = (
        jnp.einsum("hqk,khd->qhd", probs_low, value_rows, preferred_element_type=F32)
        .astype(BF)
        .reshape(seq_len, columns)
    )
    attn_partial = jnp.dot(mixed, o_full, preferred_element_type=F32).astype(BF)

    lane = jnp.arange(128)
    lane_expert = jnp.where(lane < 2 * expert_count, lane % expert_count, -1)
    routes_own = lax.dynamic_slice_in_dim(routes, t * rows, rows, 0)
    chosen = jnp.any(routes_own[:, :, None] == lane_expert[None, None, :], axis=1).astype(F32)
    blank = jnp.zeros((width, 128 - 2 * expert_count), BF)
    router_wide = jnp.concatenate([router_weight, router_weight, blank], axis=1)
    router_t = jnp.concatenate(
        [router_weight.T, jnp.zeros((128 - expert_count, width), BF)], axis=0
    )
    middle, gates, ffn_own, tokens = enter(
        extent,
        attn_partial.reshape(extent, rows, width),
        hidden_in,
        ffn_gain,
        router_wide,
        chosen,
    )
    tokens = tokens.reshape(all_tokens, width + 128)
    hidden, expert_partial = experts(tokens, pieces)
    own_positions = t * rows + jnp.arange(rows)
    row_scale = jnp.where(own_positions < length, all_tokens / total_count, 0.0)
    grad_output, row_loss, grads = turn(
        extent,
        expert_partial.reshape(dp_count * extent, rows, width),
        middle,
        teacher,
        jnp.broadcast_to(row_scale[:, None], (rows, 128)),
    )
    loss_own = jnp.sum(row_loss[:, 0]) / (2.0 * width * all_tokens)
    ffn_grad_partial, *expert_grads = experts_back(
        grads.reshape(all_tokens, width), tokens, hidden, pieces
    )
    expert_grads = [exchange(piece, bits) for bits, piece in enumerate(expert_grads)]
    grad_middle, grad_logits, ffn_gain_part, attn_grad_rows = leave(
        extent,
        ffn_grad_partial.reshape(dp_count * extent, rows, width + 128),
        middle,
        grad_output,
        gates,
        chosen,
        ffn_gain,
        router_t,
    )
    attn_grad_rows = attn_grad_rows.reshape(seq_len, width)
    router_part = jnp.einsum(
        "sd,se->de",
        ffn_own,
        grad_logits[:, :expert_count],
        precision=HIGHEST,
        preferred_element_type=F32,
    )
    grad_o = jnp.einsum("sa,sb->ab", mixed, attn_grad_rows, preferred_element_type=F32)
    grad_mixed = (
        jnp.einsum("sb,ab->sa", attn_grad_rows, o_full, preferred_element_type=F32)
        .astype(BF)
        .reshape(seq_len, local_heads, HD)
    )
    value_grad = jnp.einsum("hqk,qhd->khd", probs_low, grad_mixed, preferred_element_type=F32)
    grad_weights = jnp.einsum(
        "qhd,khd->hqk", grad_mixed, value_rows, preferred_element_type=F32
    )
    grad_scores = (
        probs_float
        * (grad_weights - jnp.sum(grad_weights * probs_float, axis=-1, keepdims=True))
    ).astype(BF)
    query_grad_rot = (
        jnp.einsum("hqk,khd->qhd", grad_scores, key_rows, preferred_element_type=F32) / root_size
    )
    key_grad_rot = (
        jnp.einsum("hqk,qhd->khd", grad_scores, queries, preferred_element_type=F32) / root_size
    )
    query_grad = rotate(query_grad_rot, cosine, sinus_table, -1.0).reshape(seq_len, columns)
    key_grad = rotate(key_grad_rot, cosine, sinus_table, -1.0).reshape(seq_len, columns)
    query_scaled = query_grad * query_gain
    key_scaled = key_grad * key_gain
    qgain_part = jnp.sum(query_grad * query_unit, axis=0)
    kgain_part = jnp.sum(key_grad * key_unit, axis=0)
    dots = jnp.concatenate(
        [
            jnp.sum(query_scaled * query_unit, axis=1),
            jnp.sum(key_scaled * key_unit, axis=1),
            jnp.full((1024,), loss_own, F32),
        ]
    )
    dots = line_total(extent, 6, dots.reshape(-1, 128)).reshape(-1)
    query_dot, key_dot, loss_group = (
        dots[:seq_len],
        dots[seq_len : 2 * seq_len],
        dots[2 * seq_len : 2 * seq_len + 1],
    )
    query_raw_grad = query_inv * (query_scaled - query_unit * (query_dot / width)[:, None])
    key_raw_grad = key_inv * (key_scaled - key_unit * (key_dot / width)[:, None])
    raw_grad = jnp.concatenate(
        [
            query_raw_grad.astype(BF),
            key_raw_grad.astype(BF),
            value_grad.reshape(seq_len, columns).astype(BF),
        ],
        axis=1,
    )
    grad_qkv = jnp.einsum("sd,sa->da", normed, raw_grad, preferred_element_type=F32)
    normed_grad = jnp.einsum("sa,da->sd", raw_grad, qkv_full, preferred_element_type=F32)
    attn_gain_part = jnp.sum(normed_grad * unit_one, axis=0)
    input_part = norm_backward(normed_grad, unit_one, inverse_one, attn_gain).astype(BF)

    split = width // (dp_count * extent)
    small = jnp.concatenate(
        [
            jnp.concatenate(
                [
                    attn_gain_part.reshape(dp_count, extent, 1, split),
                    jnp.sum(ffn_gain_part, axis=0).reshape(dp_count, extent, 1, split),
                ],
                axis=3,
            ),
            router_part.reshape(dp_count, extent, split * expert_count // 128, 128),
            jnp.zeros((dp_count, extent, 15 - split * expert_count // 128, 128), F32),
        ],
        axis=2,
    ).transpose(1, 0, 2, 3)
    gains_part = jnp.concatenate([qgain_part, kgain_part]).reshape(2 * local_heads, HD)
    grad_in, qkv_out, o_out, small_out = close(
        extent,
        input_part.reshape(extent, rows, width),
        grad_middle,
        grad_qkv.astype(BF),
        grad_o.astype(BF),
        small,
        gains_part,
    )
    grad_gate, grad_up, grad_down = spread(expert_grads)
    router_out = small_out[1 : 1 + split * expert_count // 128].reshape(split, expert_count)
    gain_out = lax.dynamic_slice(small_out, (16, d * head_width), (2 * local_heads, head_width))
    return (
        loss_group,
        grad_in,
        small_out[0, :split],
        small_out[0, split : 2 * split],
        qkv_out[:, :columns],
        qkv_out[:, columns : 2 * columns],
        qkv_out[:, 2 * columns :],
        gain_out[:local_heads],
        gain_out[local_heads:],
        o_out,
        router_out,
        grad_gate,
        grad_up,
        grad_down,
    )


def solution(mesh):
    placed = (
        P(("dp", "tensor"), None),
        P(("dp", "tensor"), None),
        P(),
        P("dp", None),
        P(),
        P(),
        P("dp", "tensor"),
        P("dp", "tensor"),
        P("dp", "tensor"),
        P("tensor", "dp"),
        P("tensor", "dp"),
        P("tensor", "dp"),
        P(),
        P(None, "dp", "tensor"),
        P(None, "dp", "tensor"),
        P(None, "tensor", "dp"),
    )
    block = mesh.shape["dp"] == 8 and mesh.shape["tensor"] == 4
    return jax.shard_map(
        per_device_block if block else per_device,
        mesh=mesh,
        in_specs=placed,
        out_specs=(
            P("dp"),
            P(("dp", "tensor"), None),
            P(("dp", "tensor")),
            P(("dp", "tensor")),
            P("dp", "tensor"),
            P("dp", "tensor"),
            P("dp", "tensor"),
            P("tensor", "dp"),
            P("tensor", "dp"),
            P("tensor", "dp"),
            P(("dp", "tensor"), None),
            P(None, "dp", "tensor"),
            P(None, "dp", "tensor"),
            P(None, "tensor", "dp"),
        ),
        check_vma=False,
    )
```

```python
import functools
import math

import jax
import jax.numpy as jnp
from jax import lax
from jax.experimental import pallas as pl
from jax.experimental.pallas import tpu as pltpu
from jax.sharding import PartitionSpec as P

HD = 128
TOK_DEV = 128
CAP = 68


EPSILON = 1e-05
THETA = 10000.0
HIGHEST = lax.Precision.HIGHEST


def inverse_rms(value):
    return lax.rsqrt(jnp.mean(value * value, axis=-1, keepdims=True) + EPSILON)


def rotate(value, cosine, sinus_table, direction):
    middle_index = value.shape[-1] // 2
    leading = value[..., :middle_index]
    trailing = value[..., middle_index:]
    return jnp.concatenate(
        [
            leading * cosine - direction * trailing * sinus_table,
            trailing * cosine + direction * leading * sinus_table,
        ],
        axis=-1,
    )


def norm_backward(grad_norm, unit_rows, inverse_rows, gain_row):
    scaled = grad_norm * gain_row
    return inverse_rows * (
        scaled - unit_rows * jnp.mean(scaled * unit_rows, axis=-1, keepdims=True)
    )


def fetch_attention(q_weight, k_weight, v_weight, o_weight, q_gain, k_gain):
    return (
        lax.all_gather(q_weight, "dp", axis=0, tiled=True),
        lax.all_gather(k_weight, "dp", axis=0, tiled=True),
        lax.all_gather(v_weight, "dp", axis=0, tiled=True),
        lax.all_gather(o_weight, "dp", axis=1, tiled=True),
        lax.all_gather(q_gain, "dp", axis=1, tiled=True),
        lax.all_gather(k_gain, "dp", axis=1, tiled=True),
    )


def fetch_experts(gate_weight, up_weight, down_weight):
    return (
        lax.all_gather(gate_weight, "dp", axis=1, tiled=True),
        lax.all_gather(up_weight, "dp", axis=1, tiled=True),
        lax.all_gather(down_weight, "dp", axis=2, tiled=True),
    )


def per_device(
    hidden_in,
    teacher,
    lengths,
    routes,
    attn_norm_gain,
    ffn_norm_gain,
    q_weight,
    k_weight,
    v_weight,
    q_gain,
    k_gain,
    o_weight,
    router_weight,
    gate_weight,
    up_weight,
    down_weight,
):
    dp_count = lax.axis_size("dp")
    tp_count = lax.axis_size("tensor")
    group_index = lax.axis_index("dp")
    member = lax.axis_index("tensor")
    row_count, model_width = hidden_in.shape
    seq_len = row_count * tp_count
    all_tokens = seq_len * dp_count
    length = lengths[group_index]
    total_count = jnp.sum(lengths).astype(jnp.float32)
    attn_gain = attn_norm_gain.astype(jnp.float32)
    ffn_gain = ffn_norm_gain.astype(jnp.float32)
    root_size = math.sqrt(HD)
    q_full, k_full, v_full, o_full, qgain_full, kgain_full = fetch_attention(
        q_weight, k_weight, v_weight, o_weight, q_gain, k_gain
    )
    local_heads = q_full.shape[1] // HD
    hidden_all = lax.all_gather(hidden_in, "tensor", axis=0, tiled=True).astype(jnp.float32)
    inverse_one = inverse_rms(hidden_all)
    unit_one = hidden_all * inverse_one
    normed = (unit_one * attn_gain).astype(jnp.bfloat16)
    query_raw = jnp.dot(normed, q_full, preferred_element_type=jnp.float32)
    key_raw = jnp.dot(normed, k_full, preferred_element_type=jnp.float32)
    value_low = jnp.dot(normed, v_full, preferred_element_type=jnp.float32).astype(jnp.bfloat16)
    query_sq, key_sq = lax.psum(
        (jnp.sum(query_raw * query_raw, axis=1), jnp.sum(key_raw * key_raw, axis=1)), "tensor"
    )
    query_inv = lax.rsqrt(query_sq / model_width + EPSILON)[:, None]
    key_inv = lax.rsqrt(key_sq / model_width + EPSILON)[:, None]
    query_unit = query_raw * query_inv
    key_unit = key_raw * key_inv
    query_gain = qgain_full.astype(jnp.float32).reshape(-1)
    key_gain = kgain_full.astype(jnp.float32).reshape(-1)
    positions = jnp.arange(seq_len)
    frequency = THETA ** (-jnp.arange(HD // 2).astype(jnp.float32) / (HD // 2))
    angles = positions.astype(jnp.float32)[:, None] * frequency[None, :]
    cosine = jnp.cos(angles)[:, None, :]
    sinus_table = jnp.sin(angles)[:, None, :]
    queries = rotate(
        (query_unit * query_gain).reshape(seq_len, local_heads, HD), cosine, sinus_table, 1.0
    ).astype(jnp.bfloat16)
    key_rows = rotate(
        (key_unit * key_gain).reshape(seq_len, local_heads, HD), cosine, sinus_table, 1.0
    ).astype(jnp.bfloat16)
    value_rows = value_low.reshape(seq_len, local_heads, HD)
    block_rows = min(512, seq_len)
    starts = jnp.arange(seq_len // block_rows) * block_rows

    def block_scores(start):
        query_block = lax.dynamic_slice_in_dim(queries, start, block_rows, 0)
        scores = (
            jnp.einsum("qhd,khd->hqk", query_block, key_rows, preferred_element_type=jnp.float32)
            / root_size
        )
        query_pos = start + jnp.arange(block_rows)
        allowed = (positions[None, :] <= query_pos[:, None]) & (positions[None, :] < length)
        return (query_block, jnp.where(allowed[None], scores, -1e30))

    def attend(start):
        unused_block, scores = block_scores(start)
        row_top = jnp.max(scores, axis=-1, keepdims=True)
        exponent = jnp.exp(scores - row_top)
        row_total = jnp.sum(exponent, axis=-1, keepdims=True)
        weights = (exponent / row_total).astype(jnp.bfloat16)
        mixed_block = jnp.einsum(
            "hqk,khd->qhd", weights, value_rows, preferred_element_type=jnp.float32
        )
        return (mixed_block.astype(jnp.bfloat16), (row_top + jnp.log(row_total))[..., 0])

    mixed_blocks, log_totals = lax.map(attend, starts)
    mixed = mixed_blocks.reshape(seq_len, local_heads * HD)
    attn_own = lax.psum_scatter(
        jnp.dot(mixed, o_full, preferred_element_type=jnp.float32).astype(jnp.bfloat16),
        "tensor",
        scatter_dimension=0,
        tiled=True,
    ).astype(jnp.float32)
    middle = hidden_in.astype(jnp.float32) + attn_own
    inverse_two = inverse_rms(middle)
    unit_two = middle * inverse_two
    ffn_own = (unit_two * ffn_gain).astype(jnp.bfloat16)
    gate_full, up_full, down_full = fetch_experts(gate_weight, up_weight, down_weight)
    ffn_all = lax.all_gather(ffn_own, "tensor", axis=0, tiled=True)
    expert_count = router_weight.shape[1]
    route_width = routes.shape[1]
    gate_probs = jax.nn.softmax(
        jnp.dot(ffn_all, router_weight, preferred_element_type=jnp.float32), axis=-1
    )
    picked = routes[:, :, None] == jnp.arange(expert_count)[None, None, :]
    route_gates = jnp.sum(jnp.where(picked, gate_probs[:, None, :], 0.0), axis=-1)
    block_count = seq_len // TOK_DEV
    per_expert = block_count * CAP
    picked_ints = picked.reshape(block_count, TOK_DEV * route_width, expert_count).astype(jnp.int32)
    slot_ranks = jnp.sum((jnp.cumsum(picked_ints, axis=1) - 1) * picked_ints, axis=-1).reshape(
        seq_len, route_width
    )
    block_ids = (positions // TOK_DEV)[:, None]
    slot_ids = (routes * per_expert + block_ids * CAP + slot_ranks).reshape(-1)
    slot_total = expert_count * per_expert
    token_ids = jnp.repeat(positions, route_width)
    group_width = 4
    turn_count = expert_count // group_width
    sources = (
        jnp.full((slot_total,), seq_len, jnp.int32)
        .at[slot_ids]
        .set(token_ids)
        .reshape(turn_count, group_width, per_expert)
    )
    slot_gates = (
        jnp.zeros((slot_total,), jnp.float32)
        .at[slot_ids]
        .set(route_gates.reshape(-1))
        .reshape(turn_count, group_width, per_expert, 1)
    )
    ffn_padded = jnp.concatenate([ffn_all, jnp.zeros((1, model_width), jnp.bfloat16)], axis=0)
    expert_running = jnp.zeros((seq_len + 1, model_width), jnp.float32)
    kept_values = []
    for turn_index in range(turn_count):
        lower = turn_index * group_width
        upper = lower + group_width
        expert_inputs = ffn_padded[sources[turn_index]]
        gate_value = jnp.einsum(
            "gpd,gdf->gpf",
            expert_inputs,
            gate_full[lower:upper],
            preferred_element_type=jnp.float32,
        )
        up_value = jnp.einsum(
            "gpd,gdf->gpf", expert_inputs, up_full[lower:upper], preferred_element_type=jnp.float32
        )
        active = (slot_gates[turn_index] * jax.nn.silu(gate_value) * up_value).astype(jnp.bfloat16)
        expert_outputs = jnp.einsum(
            "gpf,gfd->gpd", active, down_full[lower:upper], preferred_element_type=jnp.float32
        )
        expert_running = expert_running.at[sources[turn_index].reshape(-1)].add(
            expert_outputs.reshape(-1, model_width)
        )
        kept_values.append((gate_value, up_value, active))
    expert_own = lax.psum_scatter(
        expert_running[:seq_len].astype(jnp.bfloat16), "tensor", scatter_dimension=0, tiled=True
    ).astype(jnp.float32)
    output = middle + expert_own
    own_positions = member * row_count + jnp.arange(row_count)
    valid_rows = (own_positions < length)[:, None]
    mismatch = output - teacher.astype(jnp.float32)
    loss_own = jnp.sum(jnp.where(valid_rows, mismatch * mismatch, 0.0)) / (
        2.0 * model_width * total_count
    )
    grad_output = jnp.where(valid_rows, mismatch * (all_tokens / total_count), 0.0)
    grad_rows = lax.all_gather(grad_output.astype(jnp.bfloat16), "tensor", axis=0, tiled=True)
    gate_full, up_full, down_full = fetch_experts(gate_weight, up_weight, down_weight)
    grad_padded = jnp.concatenate([grad_rows, jnp.zeros((1, model_width), jnp.bfloat16)], axis=0)
    ffn_grad_running = jnp.zeros((seq_len + 1, model_width), jnp.float32)
    gate_grads = []
    up_grads = []
    down_grads = []
    slot_grads = []
    for turn_index in range(turn_count):
        gate_value, up_value, active = kept_values[turn_index]
        lower = turn_index * group_width
        upper = lower + group_width
        source_rows = sources[turn_index]
        expert_inputs = ffn_padded[source_rows]
        incoming = grad_padded[source_rows]
        grad_active = jnp.einsum(
            "gpd,gfd->gpf", incoming, down_full[lower:upper], preferred_element_type=jnp.float32
        )
        down_turn = jnp.einsum("gpf,gpd->gfd", active, incoming, preferred_element_type=jnp.float32)
        sigmoid_value = jax.nn.sigmoid(gate_value)
        silu_value = gate_value * sigmoid_value
        slot_grads.append(jnp.sum(grad_active * silu_value * up_value, axis=-1))
        grad_inner = grad_active * slot_gates[turn_index]
        grad_gate_value = (
            grad_inner * up_value * sigmoid_value * (1.0 + gate_value * (1.0 - sigmoid_value))
        ).astype(jnp.bfloat16)
        grad_up_value = (grad_inner * silu_value).astype(jnp.bfloat16)
        gate_turn = jnp.einsum(
            "gpd,gpf->gdf", expert_inputs, grad_gate_value, preferred_element_type=jnp.float32
        )
        up_turn = jnp.einsum(
            "gpd,gpf->gdf", expert_inputs, grad_up_value, preferred_element_type=jnp.float32
        )
        gate_grads.append(gate_turn)
        up_grads.append(up_turn)
        down_grads.append(down_turn)
        grad_inputs = jnp.einsum(
            "gpf,gdf->gpd",
            grad_gate_value,
            gate_full[lower:upper],
            preferred_element_type=jnp.float32,
        )
        grad_inputs = grad_inputs + jnp.einsum(
            "gpf,gdf->gpd", grad_up_value, up_full[lower:upper], preferred_element_type=jnp.float32
        )
        ffn_grad_running = ffn_grad_running.at[source_rows.reshape(-1)].add(
            grad_inputs.reshape(-1, model_width)
        )
    slot_grad_all = jnp.concatenate([entry.reshape(-1) for entry in slot_grads])
    route_grads = slot_grad_all[slot_ids].reshape(seq_len, route_width)
    grad_probs = jnp.sum(jnp.where(picked, route_grads[:, :, None], 0.0), axis=1)
    grad_logits = gate_probs * (
        grad_probs - jnp.sum(grad_probs * gate_probs, axis=-1, keepdims=True)
    )
    router_float = router_weight.astype(jnp.float32)
    ffn_grad_part = ffn_grad_running[:seq_len] + jnp.einsum(
        "se,de->sd", grad_logits, router_float, precision=HIGHEST
    )
    router_part = jnp.einsum(
        "sd,se->de", ffn_all, grad_logits, precision=HIGHEST, preferred_element_type=jnp.float32
    )
    ffn_grad_own = lax.psum_scatter(
        ffn_grad_part.astype(jnp.bfloat16), "tensor", scatter_dimension=0, tiled=True
    ).astype(jnp.float32)
    ffn_gain_part = jnp.sum(ffn_grad_own * unit_two, axis=0)
    grad_middle = grad_output + norm_backward(ffn_grad_own, unit_two, inverse_two, ffn_gain)
    attn_grad_rows = lax.all_gather(grad_middle.astype(jnp.bfloat16), "tensor", axis=0, tiled=True)
    q_full, k_full, v_full, o_full, qgain_full, kgain_full = fetch_attention(
        q_weight, k_weight, v_weight, o_weight, q_gain, k_gain
    )
    grad_o = jnp.einsum("sa,sb->ab", mixed, attn_grad_rows, preferred_element_type=jnp.float32)
    grad_mixed = (
        jnp.einsum("sb,ab->sa", attn_grad_rows, o_full, preferred_element_type=jnp.float32)
        .astype(jnp.bfloat16)
        .reshape(seq_len, local_heads, HD)
    )

    def attend_back(carry, inputs):
        key_running, value_running = carry
        start, log_total = inputs
        query_block, scores = block_scores(start)
        probs_float = jnp.exp(scores - log_total[..., None])
        probs_low = probs_float.astype(jnp.bfloat16)
        grad_block = lax.dynamic_slice_in_dim(grad_mixed, start, block_rows, 0)
        value_running = value_running + jnp.einsum(
            "hqk,qhd->khd", probs_low, grad_block, preferred_element_type=jnp.float32
        )
        grad_weights = jnp.einsum(
            "qhd,khd->hqk", grad_block, value_rows, preferred_element_type=jnp.float32
        )
        grad_scores = (
            probs_float
            * (grad_weights - jnp.sum(grad_weights * probs_float, axis=-1, keepdims=True))
        ).astype(jnp.bfloat16)
        query_grad_block = (
            jnp.einsum("hqk,khd->qhd", grad_scores, key_rows, preferred_element_type=jnp.float32)
            / root_size
        )
        key_running = (
            key_running
            + jnp.einsum(
                "hqk,qhd->khd", grad_scores, query_block, preferred_element_type=jnp.float32
            )
            / root_size
        )
        return ((key_running, value_running), query_grad_block)

    zero_heads = jnp.zeros((seq_len, local_heads, HD), jnp.float32)
    (key_grad_rot, value_grad), query_grad_blocks = lax.scan(
        attend_back, (zero_heads, zero_heads), (starts, log_totals)
    )
    query_grad = rotate(
        query_grad_blocks.reshape(seq_len, local_heads, HD), cosine, sinus_table, -1.0
    ).reshape(seq_len, local_heads * HD)
    key_grad = rotate(key_grad_rot, cosine, sinus_table, -1.0).reshape(seq_len, local_heads * HD)
    query_scaled = query_grad * query_gain
    key_scaled = key_grad * key_gain
    qgain_part = jnp.sum(query_grad * query_unit, axis=0)
    kgain_part = jnp.sum(key_grad * key_unit, axis=0)
    query_dot, key_dot, loss_group = lax.psum(
        (
            jnp.sum(query_scaled * query_unit, axis=1),
            jnp.sum(key_scaled * key_unit, axis=1),
            loss_own,
        ),
        "tensor",
    )
    query_raw_grad = (
        query_inv * (query_scaled - query_unit * (query_dot / model_width)[:, None])
    ).astype(jnp.bfloat16)
    key_raw_grad = (key_inv * (key_scaled - key_unit * (key_dot / model_width)[:, None])).astype(
        jnp.bfloat16
    )
    value_raw_grad = value_grad.reshape(seq_len, local_heads * HD).astype(jnp.bfloat16)
    grad_q = jnp.einsum("sd,sa->da", normed, query_raw_grad, preferred_element_type=jnp.float32)
    grad_k = jnp.einsum("sd,sa->da", normed, key_raw_grad, preferred_element_type=jnp.float32)
    grad_v = jnp.einsum("sd,sa->da", normed, value_raw_grad, preferred_element_type=jnp.float32)
    normed_grad = jnp.einsum(
        "sa,da->sd", query_raw_grad, q_full, preferred_element_type=jnp.float32
    )
    normed_grad = normed_grad + jnp.einsum(
        "sa,da->sd", key_raw_grad, k_full, preferred_element_type=jnp.float32
    )
    normed_grad = normed_grad + jnp.einsum(
        "sa,da->sd", value_raw_grad, v_full, preferred_element_type=jnp.float32
    )
    attn_gain_part = jnp.sum(normed_grad * unit_one, axis=0)
    input_part = norm_backward(normed_grad, unit_one, inverse_one, attn_gain)
    split_width = model_width // (dp_count * tp_count)
    input_own, attn_gain_share, ffn_gain_share, router_share = (
        lax.psum_scatter(
            input_part.astype(jnp.bfloat16), "tensor", scatter_dimension=0, tiled=True
        ).astype(jnp.float32),
        lax.psum_scatter(
            attn_gain_part.reshape(dp_count, tp_count, split_width).astype(jnp.bfloat16),
            "tensor",
            scatter_dimension=1,
            tiled=True,
        ).astype(jnp.float32),
        lax.psum_scatter(
            ffn_gain_part.reshape(dp_count, tp_count, split_width).astype(jnp.bfloat16),
            "tensor",
            scatter_dimension=1,
            tiled=True,
        ).astype(jnp.float32),
        lax.psum_scatter(
            router_part.reshape(dp_count, tp_count, split_width, expert_count).astype(jnp.bfloat16),
            "tensor",
            scatter_dimension=1,
            tiled=True,
        ).astype(jnp.float32),
    )
    grad_in = grad_middle + input_own
    (
        grad_q,
        grad_k,
        grad_v,
        grad_o,
        grad_qgain,
        grad_kgain,
        attn_gain_sum,
        ffn_gain_sum,
        router_sum,
    ) = (
        lax.psum_scatter(grad_q.astype(jnp.bfloat16), "dp", scatter_dimension=0, tiled=True).astype(
            jnp.float32
        ),
        lax.psum_scatter(grad_k.astype(jnp.bfloat16), "dp", scatter_dimension=0, tiled=True).astype(
            jnp.float32
        ),
        lax.psum_scatter(grad_v.astype(jnp.bfloat16), "dp", scatter_dimension=0, tiled=True).astype(
            jnp.float32
        ),
        lax.psum_scatter(grad_o.astype(jnp.bfloat16), "dp", scatter_dimension=1, tiled=True).astype(
            jnp.float32
        ),
        lax.psum_scatter(
            qgain_part.reshape(local_heads, HD).astype(jnp.bfloat16),
            "dp",
            scatter_dimension=1,
            tiled=True,
        ).astype(jnp.float32),
        lax.psum_scatter(
            kgain_part.reshape(local_heads, HD).astype(jnp.bfloat16),
            "dp",
            scatter_dimension=1,
            tiled=True,
        ).astype(jnp.float32),
        lax.psum_scatter(
            attn_gain_share.astype(jnp.bfloat16), "dp", scatter_dimension=0, tiled=True
        ).astype(jnp.float32),
        lax.psum_scatter(
            ffn_gain_share.astype(jnp.bfloat16), "dp", scatter_dimension=0, tiled=True
        ).astype(jnp.float32),
        lax.psum_scatter(
            router_share.astype(jnp.bfloat16), "dp", scatter_dimension=0, tiled=True
        ).astype(jnp.float32),
    )
    grad_gate, grad_up, grad_down = (
        lax.psum_scatter(
            jnp.concatenate(gate_grads, axis=0).astype(jnp.bfloat16),
            "dp",
            scatter_dimension=1,
            tiled=True,
        ).astype(jnp.float32),
        lax.psum_scatter(
            jnp.concatenate(up_grads, axis=0).astype(jnp.bfloat16),
            "dp",
            scatter_dimension=1,
            tiled=True,
        ).astype(jnp.float32),
        lax.psum_scatter(
            jnp.concatenate(down_grads, axis=0).astype(jnp.bfloat16),
            "dp",
            scatter_dimension=2,
            tiled=True,
        ).astype(jnp.float32),
    )
    return (
        loss_group.reshape(1),
        grad_in,
        attn_gain_sum.reshape(-1),
        ffn_gain_sum.reshape(-1),
        grad_q,
        grad_k,
        grad_v,
        grad_qgain,
        grad_kgain,
        grad_o,
        router_sum.reshape(-1, expert_count),
        grad_gate,
        grad_up,
        grad_down,
    )


MESH = pl.DeviceIdType.MESH
BF = jnp.bfloat16
F32 = jnp.float32
VMEM_LIMIT = 62 * 1024 * 1024
ANY = pl.BlockSpec(memory_space=pl.ANY)
VM = pl.BlockSpec(memory_space=pltpu.VMEM)


def flip(index, bits):
    for bit in (1, 2, 4):
        if bits & bit:
            index = index + bit * (1 - 2 * ((index // bit) % 2))
    return index


def both(first, second):
    return jnp.logical_and(first, second)


def under(condition, action):
    if condition is None:
        action()
    else:
        pl.when(condition)(action)


class Wire:
    def __init__(self, send_sem, recv_sem):
        self.send_sem, self.recv_sem, self.count, self.sent = send_sem, recv_sem, 0, []

    def slot(self):
        self.count += 1
        return self.count - 1

    def start(self, slot, source, target, device, condition=None):
        def make():
            return pltpu.make_async_remote_copy(
                src_ref=source(),
                dst_ref=target(),
                send_sem=self.send_sem.at[slot],
                recv_sem=self.recv_sem.at[slot],
                device_id=device,
                device_id_type=MESH,
            )

        under(condition, lambda: make().start())
        self.sent.append((condition, make))

    def arrive(self, slot, region, device, condition=None):
        copy = pltpu.make_async_remote_copy(
            src_ref=region(),
            dst_ref=region(),
            send_sem=self.send_sem.at[slot],
            recv_sem=self.recv_sem.at[slot],
            device_id=device,
            device_id_type=MESH,
        )
        under(condition, lambda: copy.wait_recv())

    def finish(self):
        for condition, make in self.sent:
            under(condition, lambda make=make: make().wait_send())
        self.sent = []


class Local:
    def __init__(self, sem):
        self.sem, self.count = sem, 0

    def start(self, source, target):
        copy = pltpu.make_async_copy(source, target, self.sem.at[self.count])
        self.count += 1
        copy.start()
        return copy


def greet(devices):
    barrier = pltpu.get_barrier_semaphore()
    for condition, device in devices:
        under(
            condition,
            lambda device=device: pl.semaphore_signal(
                barrier, inc=1, device_id=device, device_id_type=MESH
            ),
        )
    amount = sum(1 for condition, device in devices if condition is None)
    for condition, device in devices:
        if condition is not None:
            amount = amount + jnp.where(condition, 1, 0)
    pl.semaphore_wait(barrier, amount)


def line_devices(d, t, extent):
    return [(t < extent - 1, (d, t + 1)), (t > 0, (d, t - 1))]


def rows_loop(rows, step, body):
    def run(index, carry):
        body(pl.multiple_of(index * step, step))
        return carry

    lax.fori_loop(0, rows // step, run, 0)


def add_into(target, source, rows):
    def body(start):
        part = pl.ds(start, 16)
        target[part] = (target[part].astype(F32) + source[part].astype(F32)).astype(BF)

    rows_loop(rows, 16, body)


class LineGather:
    def __init__(self, wire, d, t, extent, own, place):
        self.wire, self.extent = wire, extent
        up = [wire.slot() for unused in range(extent - 1)]
        down = [wire.slot() for unused in range(extent - 1)]
        last = extent - 1
        above, below = (d, t + 1), (d, t - 1)
        wire.start(up[0], own, lambda: place(t), above, t < last)
        wire.start(down[0], own, lambda: place(t), below, t > 0)
        self.steps = {}
        for step in range(1, extent):
            from_below, from_above = t >= step, t <= last - step
            lower, upper = t - step, t + step
            self.steps[step] = (
                (
                    up,
                    lambda index=lower: place(index),
                    from_below,
                    both(from_below, t < last),
                    above,
                    below,
                ),
                (
                    down,
                    lambda index=upper: place(index),
                    from_above,
                    both(from_above, t > 0),
                    below,
                    above,
                ),
            )

    def step(self, step):
        for slots, region, valid, onward, to, source in self.steps[step]:
            self.wire.arrive(slots[step - 1], region, source, valid)
            if step < self.extent - 1:
                self.wire.start(slots[step], region, region, to, onward)


def arrival(t, turn):
    near = t - 1 + 2 * (1 - (t + 3) // 4)
    far = 3 * (1 - t // 2)
    choices = (t, near, 6 - t - near - far, far)
    if isinstance(turn, int):
        return choices[turn]
    result = choices[0]
    for number in range(1, 4):
        result = jnp.where(turn == number, choices[number], result)
    return result


class PlaneGather:
    def __init__(self, wire, d, t, extent, own, place, half):
        self.wire, self.place, self.half, self.own = wire, place, half, own
        self.to_x, self.to_y, self.to_c = (flip(d, 2), t), (flip(d, 4), t), (flip(d, 1), t)
        self.index = [arrival(t, turn) for turn in range(extent)]
        self.slots = {}
        self.line = LineGather(wire, d, t, extent, own, lambda j: place(j, 0, 0))

    def send(self, name, turn, source, target, device):
        slot = self.wire.slot()
        self.slots[name, turn] = slot
        self.wire.start(slot, source, target, device)

    def wait(self, name, turn, region, device):
        self.wire.arrive(self.slots[name, turn], region, device)

    def spot(self, turn, c, i, which=None):
        def region():
            ref = self.place(self.index[turn], c, i)
            return ref if which is None else ref.at[pl.ds(which * self.half, self.half)]

        return region

    def source(self, turn, which=None):
        def region():
            ref = self.own() if turn == 0 else self.place(self.index[turn], 0, 0)
            return ref if which is None else ref.at[pl.ds(which * self.half, self.half)]

        return region

    def stage(self, turn):
        source, spot = self.source, self.spot
        self.send("x0", turn, source(turn, 0), spot(turn, 0, 1, 0), self.to_x)
        self.send("y1", turn, source(turn, 1), spot(turn, 0, 2, 1), self.to_y)
        self.send("x1", turn, source(turn, 1), spot(turn, 0, 1, 1), self.to_x)
        self.send("y0", turn, source(turn, 0), spot(turn, 0, 2, 0), self.to_y)
        self.send("c0", turn, source(turn), spot(turn, 1, 0), self.to_c)

    def relay(self, turn):
        spot = self.spot
        self.wait("x0", turn, spot(turn, 0, 1, 0), self.to_x)
        self.send("fy", turn, spot(turn, 0, 1, 0), spot(turn, 0, 3, 0), self.to_y)
        self.wait("y1", turn, spot(turn, 0, 2, 1), self.to_y)
        self.send("fx", turn, spot(turn, 0, 2, 1), spot(turn, 0, 3, 1), self.to_x)
        self.wait("x1", turn, spot(turn, 0, 1, 1), self.to_x)
        self.send("c1", turn, spot(turn, 0, 1), spot(turn, 1, 1), self.to_c)
        self.wait("y0", turn, spot(turn, 0, 2, 0), self.to_y)
        self.send("c2", turn, spot(turn, 0, 2), spot(turn, 1, 2), self.to_c)

    def corner(self, turn):
        spot = self.spot
        self.wait("fy", turn, spot(turn, 0, 3, 0), self.to_y)
        self.wait("fx", turn, spot(turn, 0, 3, 1), self.to_x)
        self.send("c3", turn, spot(turn, 0, 3), spot(turn, 1, 3), self.to_c)

    def other(self, turn):
        for i in range(4):
            self.wait("c%d" % i, turn, self.spot(turn, 1, i), self.to_c)

    def actions(self):
        line, stage, relay, corner, other = (
            self.line.step,
            self.stage,
            self.relay,
            self.corner,
            self.other,
        )
        return (
            ((line, 1), (stage, 1), (relay, 0), (line, 2), (stage, 2), (corner, 0)),
            ((relay, 1), (line, 3), (stage, 3), (other, 0)),
            ((relay, 2), (corner, 1)),
            ((other, 1),),
            ((relay, 3), (corner, 2)),
            ((other, 2),),
            ((corner, 3),),
            ((other, 3),),
        )


class LineSum:
    def __init__(self, wire, d, t, extent, block, up_in, down_in, rows, parts):
        self.wire, self.d, self.t, self.extent = wire, d, t, extent
        self.block, self.up_in, self.down_in = block, up_in, down_in
        self.rows, self.parts = rows // parts, parts
        self.up = [[wire.slot() for p in range(parts)] for s in range(extent - 1)]
        self.down = [[wire.slot() for p in range(parts)] for s in range(extent - 1)]

    def cut(self, ref, part):
        return ref.at[pl.ds(part * self.rows, self.rows)]

    def flow(self, step, part, near, index, slots, buffers, to_device, from_device):
        wire, extent = self.wire, self.extent
        block = lambda: self.cut(self.block(index), part)
        if step >= 1:
            source = lambda: self.cut(buffers.at[step - 1], part)
            active = both(both(near <= step, near < extent - 1), near >= 1)
            wire.arrive(slots[step - 1][part], source, from_device, active)
            under(active, lambda: add_into(block(), source(), self.rows))
        wire.start(
            slots[step][part],
            block,
            lambda: self.cut(buffers.at[step], part),
            to_device,
            both(near <= step, near < extent - 1),
        )

    def step(self, step):
        d, t, extent = self.d, self.t, self.extent
        for part in range(self.parts):
            self.flow(
                step,
                part,
                t,
                extent - 1 - step + t,
                self.up,
                self.up_in,
                (d, t + 1),
                (d, t - 1),
            )
            self.flow(
                step,
                part,
                extent - 1 - t,
                step + t - (extent - 1),
                self.down,
                self.down_in,
                (d, t - 1),
                (d, t + 1),
            )

    def last(self):
        d, t, extent = self.d, self.t, self.extent
        for ready, missing, slots, buffers, device in (
            (t > 0, t == 0, self.up, self.up_in, (d, t - 1)),
            (t < extent - 1, t == extent - 1, self.down, self.down_in, (d, t + 1)),
        ):
            buffer = buffers.at[extent - 2]
            for part in range(self.parts):
                self.wire.arrive(
                    slots[extent - 2][part],
                    lambda part=part, buffer=buffer: self.cut(buffer, part),
                    device,
                    ready,
                )

            def clear(buffer=buffer):
                buffer[...] = jnp.zeros(buffer.shape, BF)

            under(missing, clear)


def own_sum(block, up_in, down_in, part, columns):
    return (
        block[part, columns].astype(F32)
        + up_in[part, columns].astype(F32)
        + down_in[part, columns].astype(F32)
    )


def plane_order(t):
    top = t // 2
    inner = ((t + 1) // 2) % 2
    return (
        3 - 3 * top,
        2 - top,
        (1 - inner) * (1 - top) + (2 + inner) * top,
        inner * (1 - top) + (3 - inner) * top,
    )


def sum_plane(wire, local, d, t, extent, partial, work, core_in, a_in, b_in, up_in, down_in, half):
    order = plane_order(t)
    to_x, to_y, to_c = (flip(d, 2), t), (flip(d, 4), t), (flip(d, 1), t)
    turns = (3, 1, 2, 0)
    slots_c, slots_a, slots_b, loads = {}, {}, {}, {}

    def cut(ref, which):
        return ref.at[pl.ds(which * half, half)]

    def begin(k):
        for i in turns:
            rows = pl.ds(i * 2 * half, 2 * half)
            slots_c[k, i] = wire.slot()
            wire.start(
                slots_c[k, i],
                lambda rows=rows: partial.at[order[k], 1, rows],
                lambda i=i: core_in.at[k, i],
                to_c,
            )
            loads[k, i] = local.start(partial.at[order[k], 0, rows], work.at[k, i])

    begin(0)

    def inverse(index):
        where = jnp.int32(0)
        for k in range(1, extent):
            where = where + k * jnp.where(order[k] == index, 1, 0)
        return where

    line = LineSum(
        wire,
        d,
        t,
        extent,
        lambda index: work.at[inverse(index), 0],
        up_in,
        down_in,
        2 * half,
        1,
    )
    routes_a = ((to_x, 1, 0, 0, 0), (to_y, 2, 0, 1, 1), (to_x, 3, 2, 0, 2), (to_y, 3, 1, 1, 3))
    routes_b = ((to_y, 2, 0, 0), (to_x, 1, 1, 1))
    for turn in range(extent + 2):
        if turn + 1 < extent:
            begin(turn + 1)
        if turn < extent:
            k = turn
            for i in turns:
                loads[k, i].wait()
                wire.arrive(slots_c[k, i], lambda k=k, i=i: core_in.at[k, i], to_c)
                add_into(work.at[k, i], core_in.at[k, i], 2 * half)
            for device, source, target, which, row in (
                routes_a[2],
                routes_a[3],
                routes_a[0],
                routes_a[1],
            ):
                slots_a[k, row] = wire.slot()
                wire.start(
                    slots_a[k, row],
                    lambda k=k, source=source, which=which: cut(work.at[k, source], which),
                    lambda k=k, row=row: a_in.at[k, row],
                    device,
                )
        if 1 <= turn <= extent:
            k = turn - 1
            for device, source, target, which, row in (
                routes_a[2],
                routes_a[3],
                routes_a[0],
                routes_a[1],
            ):
                wire.arrive(slots_a[k, row], lambda k=k, row=row: a_in.at[k, row], device)
                add_into(cut(work.at[k, target], which), a_in.at[k, row], half)
                if row >= 2:
                    to, origin, part, b_row = routes_b[row - 2]
                    slots_b[k, b_row] = wire.slot()
                    wire.start(
                        slots_b[k, b_row],
                        lambda k=k, origin=origin, part=part: cut(work.at[k, origin], part),
                        lambda k=k, b_row=b_row: b_in.at[k, b_row],
                        to,
                    )
        if turn >= 2:
            k = turn - 2
            for device, source, which, row in routes_b:
                wire.arrive(slots_b[k, row], lambda k=k, row=row: b_in.at[k, row], device)
                add_into(cut(work.at[k, 0], which), b_in.at[k, row], half)
            if k < extent - 1:
                line.step(k)
    line.last()
    return work.at[extent - 1, 0]


def plane_devices(d, t, extent):
    return line_devices(d, t, extent) + [(None, (flip(d, bits), t)) for bits in (1, 2, 4)]


def kernel_params(number):
    return pltpu.CompilerParams(
        collective_id=number, has_side_effects=True, vmem_limit_bytes=VMEM_LIMIT
    )


def dma_pair(count):
    return [pltpu.SemaphoreType.DMA((count,)), pltpu.SemaphoreType.DMA((count,))]


def fetch_kernel(
    extent,
    hid,
    qkv,
    o,
    gains,
    gate,
    up,
    down,
    hid_all,
    qkv_all,
    o_all,
    gains_all,
    *rest,
):
    pieces, (stage, send_sem, recv_sem, local_sem) = rest[:8], rest[8:]
    d, t = lax.axis_index("dp"), lax.axis_index("tensor")
    rows = hid.shape[0]
    depth, o_rows = qkv.shape[0], o.shape[0]
    width = o.shape[1]
    greet(line_devices(d, t, extent) + [(None, (flip(d, bits), t)) for bits in range(1, 8)])
    wire, local = Wire(send_sem, recv_sem), Local(local_sem)
    dx, dy, dxy, dc = flip(d, 2), flip(d, 4), flip(d, 6), flip(d, 1)
    to_x, to_y, to_c = (dx, t), (dy, t), (dc, t)

    def region(device, which):
        start = pl.multiple_of(device * width, width)
        if which is None:
            return [qkv_all.at[pl.ds(device * depth, depth)], o_all.at[:, pl.ds(start, width)]]
        return [
            qkv_all.at[pl.ds(device * depth + which * (depth // 2), depth // 2)],
            o_all.at[pl.ds(which * (o_rows // 2), o_rows // 2), pl.ds(start, width)],
        ]

    def own(which):
        if which is None:
            return [qkv, o]
        return [
            qkv.at[pl.ds(which * (depth // 2), depth // 2)],
            o.at[pl.ds(which * (o_rows // 2), o_rows // 2)],
        ]

    def send(device, sources, targets):
        slots = []
        for source, target in zip(sources, targets):
            slot = wire.slot()
            wire.start(slot, lambda source=source: source, lambda target=target: target, device)
            slots.append(slot)
        return slots

    def arrive(slots, regions, device):
        for slot, part in zip(slots, regions):
            wire.arrive(slot, lambda: part, device)

    def block(index):
        return hid_all.at[pl.ds(index * rows, rows)]

    x_slots, y_slots, c_slots = {}, {}, {}
    for which, other in ((0, 1), (1, 0)):
        x_slots[which] = send(to_x, own(which), region(d, which))
        y_slots[other] = send(to_y, own(other), region(d, other))
    c_slots[1] = send(to_c, own(None), region(d, None))
    passed = {}
    loads, copies = [], []
    for place, weight in enumerate((gate, up, down)):
        loads.append(local.start(weight, stage.at[place]))

    def store_pieces():
        for load in loads:
            load.wait()
        for bits in range(8):
            first = 2 * flip(d, bits)
            for place in range(3):
                copies.append(
                    local.start(stage.at[place, pl.ds(first, 2)], pieces[bits].at[place])
                )

    copies.append(local.start(hid, block(t)))
    for source, target in zip(own(None), region(d, None)):
        copies.append(local.start(source, target))
    line = LineGather(wire, d, t, extent, lambda: hid, block)
    store_pieces()
    arrive(x_slots[0], region(dx, 0), to_x)
    passed["y"] = send(to_y, region(dx, 0), region(dx, 0))
    arrive(y_slots[1], region(dy, 1), to_y)
    passed["x"] = send(to_x, region(dy, 1), region(dy, 1))
    line.step(1)
    arrive(x_slots[1], region(dx, 1), to_x)
    c_slots[3] = send(to_c, region(dx, None), region(dx, None))
    arrive(y_slots[0], region(dy, 0), to_y)
    c_slots[5] = send(to_c, region(dy, None), region(dy, None))
    for step in range(2, extent):
        line.step(step)
    gain_slots = {}
    for bits in range(1, 8):
        gain_slots[bits] = wire.slot()
        wire.start(
            gain_slots[bits],
            lambda: gains,
            lambda bits=bits: gains_all.at[bits],
            (flip(d, bits), t),
        )
    copies.append(local.start(gains, gains_all.at[0]))
    arrive(passed["y"], region(dxy, 0), to_y)
    arrive(passed["x"], region(dxy, 1), to_x)
    c_slots[7] = send(to_c, region(dxy, None), region(dxy, None))
    for bits in (1, 3, 5, 7):
        arrive(c_slots[bits], region(flip(d, bits), None), to_c)
    for bits in range(1, 8):
        wire.arrive(
            gain_slots[bits], lambda bits=bits: gains_all.at[bits], (flip(d, bits), t)
        )
    for copy in copies:
        copy.wait()
    wire.finish()


def fetch(extent, hid, qkv, o, gains, gate, up, down):
    rows, model_width = hid.shape
    piece = jax.ShapeDtypeStruct((3, 2) + gate.shape[1:], BF)
    return pl.pallas_call(
        functools.partial(fetch_kernel, extent),
        out_shape=[
            jax.ShapeDtypeStruct((rows * extent, model_width), BF),
            jax.ShapeDtypeStruct((8 * qkv.shape[0], qkv.shape[1]), BF),
            jax.ShapeDtypeStruct((o.shape[0], 8 * o.shape[1]), BF),
            jax.ShapeDtypeStruct((8,) + gains.shape, F32),
        ]
        + [piece] * 8,
        in_specs=[VM] * 4 + [ANY] * 3,
        out_specs=[ANY] * 12,
        scratch_shapes=[pltpu.VMEM((3,) + gate.shape, BF)]
        + dma_pair(64) + [pltpu.SemaphoreType.DMA((40,))],
        compiler_params=kernel_params(1),
        cost_estimate=pl.CostEstimate(flops=0, bytes_accessed=100_000_000, transcendentals=0),
    )(hid, qkv, o, gains, gate, up, down)


def line_total_kernel(extent, value, total, inbox, send_sem, recv_sem):
    d, t = lax.axis_index("dp"), lax.axis_index("tensor")
    peers = [(d, (t + k) % extent) for k in range(1, extent)]
    greet([(None, peer) for peer in peers])
    wire = Wire(send_sem, recv_sem)
    slots = []
    for k, peer in enumerate(peers):
        slot = wire.slot()
        slots.append(slot)
        wire.start(slot, lambda: value, lambda k=k: inbox.at[k], peer)
    result = value[...]
    for k, peer in enumerate(peers):
        wire.arrive(slots[k], lambda k=k: inbox.at[k], peer)
        result = result + inbox[k]
    total[...] = result
    wire.finish()


def line_total(extent, number, value):
    return pl.pallas_call(
        functools.partial(line_total_kernel, extent),
        out_shape=jax.ShapeDtypeStruct(value.shape, F32),
        in_specs=[VM],
        out_specs=VM,
        scratch_shapes=[pltpu.VMEM((extent - 1,) + value.shape, F32)] + dma_pair(extent - 1),
        compiler_params=kernel_params(number),
        cost_estimate=pl.CostEstimate(flops=0, bytes_accessed=10_000_000, transcendentals=0),
    )(value)


class Pieces:
    def __init__(self, d, in_weight, out_weight, sem, pieces):
        self.copies = {}
        slab = out_weight.shape[0] // 2
        for bits, piece in enumerate(pieces):
            start = pl.multiple_of(flip(d, bits) * slab, slab)
            pairs = []
            for place in range(3):
                for e in range(2):
                    if place < 2:
                        column = (2 * place + e) * slab
                        whole = in_weight.at[pl.ds(start, slab), pl.ds(column, slab)]
                    else:
                        whole = out_weight.at[pl.ds(e * slab, slab), pl.ds(start, slab)]
                    pairs.append((piece.at[place, e], whole, sem.at[bits * 6 + place * 2 + e]))
            self.copies[bits] = pairs

    def load(self, bits):
        for piece, whole, sem in self.copies[bits]:
            pltpu.make_async_copy(piece, whole, sem).start()

    def loaded(self, bits):
        for piece, whole, sem in self.copies[bits]:
            pltpu.make_async_copy(piece, whole, sem).wait()

    def store(self, bits):
        for piece, whole, sem in self.copies[bits]:
            pltpu.make_async_copy(whole, piece, sem).start()

    def stored(self, bits):
        for piece, whole, sem in self.copies[bits]:
            pltpu.make_async_copy(whole, piece, sem).wait()


def coefficients(columns, d, slab):
    values = columns.astype(F32)
    lane = lax.broadcasted_iota(jnp.int32, values.shape, 1)
    parts = []
    for e in range(2):
        wanted = jnp.logical_or(lane == 2 * d + e, lane == 16 + 2 * d + e)
        one = jnp.sum(jnp.where(wanted, values, 0.0), axis=-1, keepdims=True)
        parts.append(jnp.broadcast_to(one, (values.shape[0], slab)))
    return jnp.concatenate(parts, axis=1)


def enter_kernel(extent, partial, hid, gain, router, chosen, *rest):
    near, corner = rest[:6], rest[6:8]
    middle, gates, ffn_own, tokens, hidden, out = rest[8:14]
    landed = rest[14:16]
    (
        gathered,
        work,
        up_in,
        down_in,
        in_weight,
        out_weight,
        hidden_stage,
        out_stage,
        send_sem,
        recv_sem,
        local_sem,
        weight_sem,
        stage_sem,
        token_sem,
    ) = rest[16:]
    d, t = lax.axis_index("dp"), lax.axis_index("tensor")
    rows, width = hid.shape
    greet(line_devices(d, t, extent) + [(None, (flip(d, bits), t)) for bits in (1, 2, 4, 6, 7)])
    wire, local = Wire(send_sem, recv_sem), Local(local_sem)
    corner_slots = []
    for n in range(2):
        slot = wire.slot()
        corner_slots.append(slot)
        wire.start(slot, lambda n=n: corner[n], lambda n=n: landed[n], (flip(d, 6 + n), t))
    work_load = local.start(partial, work)
    weights = Pieces(d, in_weight, out_weight, weight_sem, list(near) + list(landed))
    for bits in range(6):
        weights.load(bits)
    work_load.wait()
    line = LineSum(
        wire, d, t, extent, lambda index: work.at[index], up_in, down_in, rows, 2
    )
    for step in range(extent - 1):
        line.step(step)
    line.last()
    mine = work.at[t]
    everything = pl.ds(0, width)
    packet = gathered.at[t, 0, pl.ds(0, rows)]

    def body(start):
        part = pl.ds(start, 16)
        value = hid[part].astype(F32) + own_sum(
            mine, up_in.at[extent - 2], down_in.at[extent - 2], part, everything
        )
        middle[part] = value
        unit = value * lax.rsqrt(jnp.mean(value * value, axis=-1, keepdims=True) + EPSILON)
        ffn_own[part] = (unit * gain[...]).astype(BF)

    rows_loop(rows, 16, body)
    logits = jnp.dot(ffn_own[...], router[...], preferred_element_type=F32)
    lane = lax.broadcasted_iota(jnp.int32, logits.shape, 1)
    top = jnp.max(jnp.where(lane < 16, logits, -1e30), axis=-1, keepdims=True)
    powers = jnp.where(lane < 32, jnp.exp(logits - top), 0.0)
    probs = powers / jnp.sum(jnp.where(lane < 16, powers, 0.0), axis=-1, keepdims=True)
    gates[...] = probs
    coeff = probs * chosen[...]
    high = coeff.astype(BF).astype(F32)
    packet[:, 0:width] = ffn_own[...]
    packet[:, width : width + 128] = jnp.where(lane < 16, high, coeff - high).astype(BF)

    def place(j, c, i):
        return gathered.at[j, c, pl.ds(i * rows, rows)]

    gather = PlaneGather(wire, d, t, extent, lambda: packet, place, rows // 2)
    gather.stage(0)
    for n in range(2):
        wire.arrive(corner_slots[n], lambda: landed[n], (flip(d, 6 + n), t))
        weights.load(6 + n)
    for bits in range(8):
        weights.loaded(bits)
    units = out_weight.shape[0]
    tile = 256

    def stage_copies(slot, j, c):
        return (
            pltpu.make_async_copy(hidden_stage.at[slot], hidden.at[j, c], stage_sem.at[0, slot]),
            pltpu.make_async_copy(out_stage.at[slot], out.at[j, c], stage_sem.at[1, slot]),
        )

    actions = gather.actions()

    def group(g, carry):
        for number, steps in enumerate(actions):

            @pl.when(g == number)
            def _():
                for action, argument in steps:
                    action(argument)

        j, c, slot = arrival(t, g // 2), g % 2, g % 2

        @pl.when(g >= 2)
        def _():
            for copy in stage_copies(slot, j, c):
                copy.wait()

        pltpu.make_async_copy(gathered.at[j, c], tokens.at[j, c], token_sem.at[g]).start()

        def some(start):
            part = pl.ds(start, tile)
            values = jnp.dot(
                gathered[j, c, part, 0:width], in_weight[...], preferred_element_type=F32
            )
            hidden_stage[slot, part] = values.astype(BF)
            gate_value, up_value = values[:, :units], values[:, units:]
            coeff = coefficients(gathered[j, c, part, width : width + 128], d, units // 2)
            active = (coeff * (gate_value * jax.nn.sigmoid(gate_value)) * up_value).astype(BF)
            out_stage[slot, part] = jnp.dot(
                active, out_weight[...], preferred_element_type=F32
            ).astype(BF)

        rows_loop(4 * rows, tile, some)
        for copy in stage_copies(slot, j, c):
            copy.start()
        return carry

    lax.fori_loop(0, 2 * extent, group, 0)
    for slot in range(2):
        for copy in stage_copies(slot, 0, slot):
            copy.wait()
    for g in range(2 * extent):
        pltpu.make_async_copy(
            gathered.at[arrival(t, g // 2), g % 2],
            tokens.at[arrival(t, g // 2), g % 2],
            token_sem.at[g],
        ).wait()
    wire.finish()


def enter(extent, partial, hid, gain, router, chosen, near, corner):
    rows, width = hid.shape
    slab = near[0].shape[2]
    piece = jax.ShapeDtypeStruct(near[0].shape, BF)
    return pl.pallas_call(
        functools.partial(enter_kernel, extent),
        out_shape=[
            jax.ShapeDtypeStruct((rows, width), F32),
            jax.ShapeDtypeStruct((rows, 128), F32),
            jax.ShapeDtypeStruct((rows, width), BF),
            jax.ShapeDtypeStruct((extent, 2, 4 * rows, width + 128), BF),
            jax.ShapeDtypeStruct((extent, 2, 4 * rows, 4 * slab), BF),
            jax.ShapeDtypeStruct((extent, 2, 4 * rows, width), BF),
            piece,
            piece,
        ],
        in_specs=[ANY, VM, VM, VM, VM] + [ANY] * 8,
        out_specs=[VM, VM, VM] + [ANY] * 5,
        scratch_shapes=[
            pltpu.VMEM((extent, 2, 4 * rows, width + 128), BF),
            pltpu.VMEM((extent, rows, width), BF),
            pltpu.VMEM((extent - 1, rows, width), BF),
            pltpu.VMEM((extent - 1, rows, width), BF),
            pltpu.VMEM((width, 4 * slab), BF),
            pltpu.VMEM((2 * slab, width), BF),
            pltpu.VMEM((2, 4 * rows, 4 * slab), BF),
            pltpu.VMEM((2, 4 * rows, width), BF),
        ]
        + dma_pair(80)
        + [
            pltpu.SemaphoreType.DMA((2,)),
            pltpu.SemaphoreType.DMA((48,)),
            pltpu.SemaphoreType.DMA((2, 2)),
            pltpu.SemaphoreType.DMA((2 * extent,)),
        ],
        compiler_params=kernel_params(3),
        cost_estimate=pl.CostEstimate(flops=0, bytes_accessed=300_000_000, transcendentals=0),
    )(partial, hid, gain, router, chosen, *near, *corner)


def sum_scratch(extent, rows, width):
    return [
        pltpu.VMEM((extent, 4, rows, width), BF),
        pltpu.VMEM((extent, 4, rows, width), BF),
        pltpu.VMEM((extent, 4, rows // 2, width), BF),
        pltpu.VMEM((extent, 2, rows // 2, width), BF),
        pltpu.VMEM((extent - 1, rows, width), BF),
        pltpu.VMEM((extent - 1, rows, width), BF),
    ]


def transposed_dot(left, right):
    return lax.dot_general(left, right, (((0,), (0,)), ((), ())), preferred_element_type=F32)


def dot_transposed(left, right):
    return lax.dot_general(left, right, (((1,), (1,)), ((), ())), preferred_element_type=F32)


def turn_kernel(extent, partial, middle, teacher, weight, tokens, hidden, *rest):
    pieces = rest[:8]
    grad_output, row_loss, out = rest[8:11]
    results, grads = rest[11:19], rest[19]
    (
        work,
        core_in,
        a_in,
        b_in,
        up_in,
        down_in,
        packet,
        in_weight,
        out_weight,
        in_total,
        out_total,
        token_tile,
        hidden_tile,
        grad_tile,
        out_stage,
        active_tile,
        inner_tile,
        send_sem,
        recv_sem,
        local_sem,
        weight_sem,
        tile_sem,
    ) = rest[20:]
    d, t = lax.axis_index("dp"), lax.axis_index("tensor")
    rows, width = middle.shape
    greet(plane_devices(d, t, extent))
    wire, local = Wire(send_sem, recv_sem), Local(local_sem)
    weights = Pieces(d, in_weight, out_weight, weight_sem, pieces)
    mine = sum_plane(
        wire, local, d, t, extent, partial, work, core_in, a_in, b_in, up_in, down_in, rows // 2
    )
    for bits in range(8):
        weights.load(bits)
    everything = pl.ds(0, width)

    def body(start):
        part = pl.ds(start, 16)
        output = middle[part] + own_sum(
            mine, up_in.at[extent - 2], down_in.at[extent - 2], part, everything
        )
        mismatch = output - teacher[part].astype(F32)
        scaled = mismatch * weight[part, 0:1]
        grad_output[part] = scaled
        packet[part] = scaled.astype(BF)
        row_loss[part] = jnp.broadcast_to(
            jnp.sum(scaled * mismatch, axis=-1, keepdims=True), (16, 128)
        )

    rows_loop(rows, 16, body)

    def place(j, c, i):
        return grads.at[j, c, pl.ds(i * rows, rows)]

    own_copy = local.start(packet, place(t, 0, 0))
    gather = PlaneGather(wire, d, t, extent, lambda: packet, place, rows // 2)
    gather.stage(0)
    in_total[...] = jnp.zeros(in_total.shape, F32)
    out_total[...] = jnp.zeros(out_total.shape, F32)
    for bits in range(8):
        weights.loaded(bits)
    own_copy.wait()
    units, slab = out_weight.shape[0], out_weight.shape[0] // 2
    tile = 256
    actions = gather.actions()

    def out_copy(j, c):
        return pltpu.make_async_copy(out_stage, out.at[j, c], tile_sem.at[3])

    def group(g, carry):
        j, c = arrival(t, g // 2), g % 2
        token_copy = pltpu.make_async_copy(tokens.at[j, c], token_tile, tile_sem.at[0])
        hidden_copy = pltpu.make_async_copy(hidden.at[j, c], hidden_tile, tile_sem.at[1])
        grad_copy = pltpu.make_async_copy(grads.at[j, c], grad_tile, tile_sem.at[2])
        token_copy.start()
        hidden_copy.start()
        for number, steps in enumerate(actions):

            @pl.when(g == number)
            def _():
                for action, argument in steps:
                    action(argument)

        grad_copy.start()

        @pl.when(g >= 1)
        def _():
            out_copy(j, c).wait()

        token_copy.wait()
        hidden_copy.wait()
        grad_copy.wait()

        def some(start):
            part = pl.ds(start, tile)
            grad_active = dot_transposed(grad_tile[part], out_weight[...])
            gate_value = hidden_tile[part, 0:units].astype(F32)
            up_value = hidden_tile[part, units : 2 * units].astype(F32)
            coeff = coefficients(token_tile[part, width : width + 128], d, slab)
            sigmoid_value = jax.nn.sigmoid(gate_value)
            silu_value = gate_value * sigmoid_value
            inner = grad_active * coeff
            direct = silu_value * up_value
            active_tile[part] = (coeff * direct).astype(BF)
            product = grad_active * direct
            lane = lax.broadcasted_iota(jnp.int32, (tile, 128), 1)
            sums = jnp.zeros((tile, 128), F32)
            for e in range(2):
                one = jnp.sum(product[:, e * slab : (e + 1) * slab], axis=-1, keepdims=True)
                sums = sums + jnp.where(lane == 2 * d + e, one, 0.0)
            out_stage[part, width : width + 128] = sums.astype(BF)
            grad_gate = (
                inner * up_value * sigmoid_value * (1.0 + gate_value * (1.0 - sigmoid_value))
            )
            inner_tile[part, 0:units] = grad_gate.astype(BF)
            inner_tile[part, units : 2 * units] = (inner * silu_value).astype(BF)
            out_stage[part, 0:width] = dot_transposed(inner_tile[part], in_weight[...]).astype(BF)

        rows_loop(4 * rows, tile, some)
        out_copy(j, c).start()

        def into_in(start):
            part = pl.ds(start, 256)
            in_total[part] += transposed_dot(token_tile[:, part], inner_tile[...])

        rows_loop(width, 256, into_in)

        def into_out(start):
            part = pl.ds(start, 512)
            out_total[:, part] += transposed_dot(active_tile[...], grad_tile[:, part])

        rows_loop(width, 512, into_out)
        return carry

    lax.fori_loop(0, 2 * extent, group, 0)
    in_weight[...] = in_total[...].astype(BF)
    out_weight[...] = out_total[...].astype(BF)
    stores = Pieces(d, in_weight, out_weight, weight_sem, results)
    for bits in range(8):
        stores.store(bits)
    for bits in range(8):
        stores.stored(bits)
    out_copy(0, 0).wait()
    wire.finish()


def turn(extent, partial, middle, teacher, weight, tokens, hidden, pieces):
    rows, width = middle.shape
    slab = pieces[0].shape[2]
    return pl.pallas_call(
        functools.partial(turn_kernel, extent),
        out_shape=[
            jax.ShapeDtypeStruct((rows, width), F32),
            jax.ShapeDtypeStruct((rows, 128), F32),
            jax.ShapeDtypeStruct((extent, 2, 4 * rows, width + 128), BF),
        ]
        + [jax.ShapeDtypeStruct(pieces[0].shape, BF)] * 8
        + [jax.ShapeDtypeStruct((extent, 2, 4 * rows, width), BF)],
        in_specs=[ANY, VM, VM, VM] + [ANY] * 10,
        out_specs=[VM, VM] + [ANY] * 10,
        scratch_shapes=sum_scratch(extent, rows, width)
        + [
            pltpu.VMEM((rows, width), BF),
            pltpu.VMEM((width, 4 * slab), BF),
            pltpu.VMEM((2 * slab, width), BF),
            pltpu.VMEM((width, 4 * slab), F32),
            pltpu.VMEM((2 * slab, width), F32),
            pltpu.VMEM((4 * rows, width + 128), BF),
            pltpu.VMEM((4 * rows, 4 * slab), BF),
            pltpu.VMEM((4 * rows, width), BF),
            pltpu.VMEM((4 * rows, width + 128), BF),
            pltpu.VMEM((4 * rows, 2 * slab), BF),
            pltpu.VMEM((4 * rows, 4 * slab), BF),
        ]
        + dma_pair(120)
        + [
            pltpu.SemaphoreType.DMA((20,)),
            pltpu.SemaphoreType.DMA((48,)),
            pltpu.SemaphoreType.DMA((4,)),
        ],
        compiler_params=kernel_params(4),
        cost_estimate=pl.CostEstimate(flops=0, bytes_accessed=450_000_000, transcendentals=0),
    )(partial, middle, teacher, weight, tokens, hidden, *pieces)[:11]


def leave_kernel(extent, partial, middle, grad_output, gates, chosen, gain, router_t, *rest):
    sent = rest[:5]
    grad_middle, grad_logits, gain_part, grads = rest[5:9]
    came = rest[9:14]
    (
        work,
        core_in,
        a_in,
        b_in,
        up_in,
        down_in,
        packet,
        extra,
        send_sem,
        recv_sem,
        local_sem,
    ) = rest[14:]
    d, t = lax.axis_index("dp"), lax.axis_index("tensor")
    rows, width = middle.shape
    greet(line_devices(d, t, extent) + [(None, (flip(d, bits), t)) for bits in range(1, 6)])
    wire, local = Wire(send_sem, recv_sem), Local(local_sem)
    mine = sum_plane(
        wire, local, d, t, extent, partial, work, core_in, a_in, b_in, up_in, down_in, rows // 2
    )
    piece_slots = []
    for n in range(5):
        slot = wire.slot()
        piece_slots.append(slot)
        wire.start(slot, lambda n=n: sent[n], lambda n=n: came[n], (flip(d, 1 + n), t))
    up_last, down_last = up_in.at[extent - 2], down_in.at[extent - 2]
    coeff_grad = (
        own_sum(mine, up_last, down_last, pl.ds(0, rows), pl.ds(width, 128)) * chosen[...]
    )
    lane = lax.broadcasted_iota(jnp.int32, coeff_grad.shape, 1)
    probs = jnp.where(lane < 16, gates[...], 0.0)
    coeff_grad = jnp.where(lane < 16, coeff_grad, 0.0)
    logit_grad = probs * (coeff_grad - jnp.sum(coeff_grad * probs, axis=-1, keepdims=True))
    grad_logits[...] = logit_grad
    high = logit_grad.astype(BF)
    low_part = (logit_grad - high.astype(F32)).astype(BF)
    for begin in range(0, width, 512):
        columns = slice(begin, begin + 512)
        extra[:, columns] = jnp.dot(
            high, router_t[:, columns], preferred_element_type=F32
        ) + jnp.dot(low_part, router_t[:, columns], preferred_element_type=F32)
    gain_part[...] = jnp.zeros(gain_part.shape, F32)

    def body(start):
        part = pl.ds(start, 16)
        grad = own_sum(mine, up_last, down_last, part, pl.ds(0, width)) + extra[part]
        value = middle[part]
        inverse = lax.rsqrt(jnp.mean(value * value, axis=-1, keepdims=True) + EPSILON)
        unit = value * inverse
        product = grad * unit
        gain_part[...] += product[0:8] + product[8:16]
        scaled = grad * gain[...]
        result = grad_output[part] + inverse * (
            scaled - unit * jnp.mean(scaled * unit, axis=-1, keepdims=True)
        )
        grad_middle[part] = result
        packet[part] = result.astype(BF)

    rows_loop(rows, 16, body)

    def place(index):
        return grads.at[index]

    copy = local.start(packet, place(t))
    line = LineGather(wire, d, t, extent, lambda: packet, place)
    for step in range(1, extent):
        line.step(step)
    copy.wait()
    for n in range(5):
        wire.arrive(piece_slots[n], lambda: came[n], (flip(d, 1 + n), t))
    wire.finish()


def leave(extent, partial, middle, grad_output, gates, chosen, gain, router_t, sent):
    rows, width = middle.shape
    return pl.pallas_call(
        functools.partial(leave_kernel, extent),
        out_shape=[
            jax.ShapeDtypeStruct((rows, width), F32),
            jax.ShapeDtypeStruct((rows, 128), F32),
            jax.ShapeDtypeStruct((8, width), F32),
            jax.ShapeDtypeStruct((extent, rows, width), BF),
        ]
        + [jax.ShapeDtypeStruct(piece.shape, BF) for piece in sent],
        in_specs=[ANY, VM, VM, VM, VM, VM, VM] + [ANY] * 5,
        out_specs=[VM, VM, VM] + [ANY] * 6,
        scratch_shapes=sum_scratch(extent, rows, width + 128)
        + [pltpu.VMEM((rows, width), BF), pltpu.VMEM((rows, width), F32)]
        + dma_pair(80)
        + [pltpu.SemaphoreType.DMA((20,))],
        compiler_params=kernel_params(5),
        cost_estimate=pl.CostEstimate(flops=0, bytes_accessed=350_000_000, transcendentals=0),
    )(partial, middle, grad_output, gates, chosen, gain, router_t, *sent)


def close_kernel(
    extent,
    partial,
    grad_middle,
    grad_qkv,
    grad_o,
    small,
    gains,
    grad_in,
    qkv_out,
    o_out,
    small_out,
    work,
    up_in,
    down_in,
    q_work,
    q_core,
    q_a,
    q_b,
    o_work,
    o_core,
    o_a,
    o_b,
    small_in,
    small_sum,
    small_last,
    send_sem,
    recv_sem,
    local_sem,
):
    d, t = lax.axis_index("dp"), lax.axis_index("tensor")
    rows, width = grad_middle.shape
    depth, o_width = qkv_out.shape[0], o_out.shape[1]
    line_peers = [(d, (t + k) % extent) for k in range(1, extent)]
    greet(
        [(None, peer) for peer in line_peers]
        + [(None, (flip(d, bits), t)) for bits in range(1, 8)]
    )
    wire, local = Wire(send_sem, recv_sem), Local(local_sem)
    to_x, to_y, to_c = (flip(d, 2), t), (flip(d, 4), t), (flip(d, 1), t)

    def slices(device):
        start = pl.multiple_of(device * o_width, o_width)
        return [
            grad_qkv.at[pl.ds(device * depth, depth)],
            grad_o.at[:, pl.ds(start, o_width)],
        ]

    turns = (3, 1, 2, 0)
    c_slots, loads = {}, {}
    work_load = local.start(partial, work)
    small_slots = []
    for k, peer in enumerate(line_peers):
        slot = wire.slot()
        small_slots.append(slot)
        wire.start(
            slot,
            lambda k=k: small.at[(t + k + 1) % extent],
            lambda k=k: small_in.at[k],
            peer,
        )
    for i in turns:
        sources = slices(flip(d, 1 + 2 * i))
        c_slots[i] = [wire.slot(), wire.slot()]
        wire.start(c_slots[i][0], lambda s=sources: s[0], lambda i=i: q_core.at[i], to_c)
        wire.start(c_slots[i][1], lambda s=sources: s[1], lambda i=i: o_core.at[i], to_c)
        mine = slices(flip(d, 2 * i))
        loads[i] = [local.start(mine[0], q_work.at[i]), local.start(mine[1], o_work.at[i])]
    work_load.wait()
    line = LineSum(
        wire, d, t, extent, lambda index: work.at[index], up_in, down_in, rows, 2
    )
    line.step(0)

    def cut(ref, which):
        half = ref.shape[0] // 2
        return ref.at[pl.ds(which * half, half)]

    a_slots, b_slots = {}, {}
    routes_a = ((to_x, 3, 2, 0, 0), (to_y, 3, 1, 1, 1), (to_x, 1, 0, 0, 2), (to_y, 2, 0, 1, 3))
    routes_b = ((to_y, 2, 0, 0), (to_x, 1, 1, 1))

    def core_add(i):
        for load in loads[i]:
            load.wait()
        wire.arrive(c_slots[i][0], lambda: q_core.at[i], to_c)
        wire.arrive(c_slots[i][1], lambda: o_core.at[i], to_c)
        add_into(q_work.at[i], q_core.at[i], q_work.shape[1])
        add_into(o_work.at[i], o_core.at[i], o_work.shape[1])

    def a_send(route):
        device, source, target, which, row = route
        a_slots[row] = [wire.slot(), wire.slot()]
        wire.start(
            a_slots[row][0], lambda: cut(q_work.at[source], which), lambda: q_a.at[row], device
        )
        wire.start(
            a_slots[row][1], lambda: cut(o_work.at[source], which), lambda: o_a.at[row], device
        )

    def b_send(route):
        device, source, which, row = route
        b_slots[row] = [wire.slot(), wire.slot()]
        wire.start(
            b_slots[row][0], lambda: cut(q_work.at[source], which), lambda: q_b.at[row], device
        )
        wire.start(
            b_slots[row][1], lambda: cut(o_work.at[source], which), lambda: o_b.at[row], device
        )

    core_add(3)
    a_send(routes_a[0])
    a_send(routes_a[1])
    core_add(1)
    a_send(routes_a[2])
    core_add(2)
    a_send(routes_a[3])
    core_add(0)
    line.step(1)
    for device, source, target, which, row in routes_a:
        wire.arrive(a_slots[row][0], lambda: q_a.at[row], device)
        wire.arrive(a_slots[row][1], lambda: o_a.at[row], device)
        add_into(cut(q_work.at[target], which), q_a.at[row], q_a.shape[1])
        add_into(cut(o_work.at[target], which), o_a.at[row], o_a.shape[1])
        if row < 2:
            b_send(routes_b[row])
    for k, peer in enumerate(line_peers):
        wire.arrive(small_slots[k], lambda k=k: small_in.at[k], peer)
    total = small[t] + small_in[0]
    for k in range(1, extent - 1):
        total = total + small_in[k]
    small_sum[:, 0:16] = total
    small_sum[:, 16:24] = jnp.broadcast_to(gains[...][None], (8, 8, 128))
    last_slots = {}
    for bits in range(1, 8):
        last_slots[bits] = wire.slot()
        wire.start(
            last_slots[bits],
            lambda bits=bits: small_sum.at[flip(d, bits)],
            lambda bits=bits: small_last.at[bits],
            (flip(d, bits), t),
        )
    line.step(2)
    for device, source, which, row in routes_b:
        wire.arrive(b_slots[row][0], lambda: q_b.at[row], device)
        wire.arrive(b_slots[row][1], lambda: o_b.at[row], device)
        for kept, came, result in (
            (cut(q_work.at[0], which), q_b.at[row], cut(qkv_out, which)),
            (cut(o_work.at[0], which), o_b.at[row], cut(o_out, which)),
        ):

            def body(start, kept=kept, came=came, result=result):
                part = pl.ds(start, 16)
                result[part] = kept[part].astype(F32) + came[part].astype(F32)

            rows_loop(kept.shape[0], 16, body)
    line.last()
    mine = work.at[t]

    def body(start):
        part = pl.ds(start, 16)
        grad_in[part] = grad_middle[part] + own_sum(
            mine, up_in.at[extent - 2], down_in.at[extent - 2], part, pl.ds(0, width)
        )

    rows_loop(rows, 16, body)
    total = small_sum[d]
    for bits in range(1, 8):
        wire.arrive(
            last_slots[bits], lambda bits=bits: small_last.at[bits], (flip(d, bits), t)
        )
        total = total + small_last[bits]
    small_out[...] = total
    wire.finish()


def close(extent, partial, grad_middle, grad_qkv, grad_o, small, gains):
    rows, width = grad_middle.shape
    depth, q_width = grad_qkv.shape[0] // 8, grad_qkv.shape[1]
    o_rows, o_width = grad_o.shape[0], grad_o.shape[1] // 8
    scratch = [
        pltpu.VMEM((extent, rows, width), BF),
        pltpu.VMEM((extent - 1, rows, width), BF),
        pltpu.VMEM((extent - 1, rows, width), BF),
    ]
    for tall, wide in ((depth, q_width), (o_rows, o_width)):
        scratch += [
            pltpu.VMEM((4, tall, wide), BF),
            pltpu.VMEM((4, tall, wide), BF),
            pltpu.VMEM((4, tall // 2, wide), BF),
            pltpu.VMEM((2, tall // 2, wide), BF),
        ]
    scratch += [
        pltpu.VMEM((extent - 1, 8, 16, 128), F32),
        pltpu.VMEM((8, 24, 128), F32),
        pltpu.VMEM((8, 24, 128), F32),
    ]
    return pl.pallas_call(
        functools.partial(close_kernel, extent),
        out_shape=[
            jax.ShapeDtypeStruct((rows, width), F32),
            jax.ShapeDtypeStruct((depth, q_width), F32),
            jax.ShapeDtypeStruct((o_rows, o_width), F32),
            jax.ShapeDtypeStruct((24, 128), F32),
        ],
        in_specs=[ANY, VM, ANY, ANY, VM, VM],
        out_specs=[VM] * 4,
        scratch_shapes=scratch + dma_pair(64) + [pltpu.SemaphoreType.DMA((16,))],
        compiler_params=kernel_params(7),
        cost_estimate=pl.CostEstimate(flops=0, bytes_accessed=150_000_000, transcendentals=0),
    )(partial, grad_middle, grad_qkv, grad_o, small, gains)


def spread_kernel(*refs):
    pieces, outs = refs[:8], refs[8:]
    d = lax.axis_index("dp")
    for bits in range(8):
        first = 2 * flip(d, bits)
        for place in range(3):
            for e in range(2):
                outs[place][first + e] = pieces[bits][place, e].astype(F32)


def spread(pieces):
    shape = (16,) + pieces[0].shape[2:]
    return pl.pallas_call(
        spread_kernel,
        out_shape=[jax.ShapeDtypeStruct(shape, F32)] * 3,
        in_specs=[VM] * 8,
        out_specs=[VM] * 3,
        compiler_params=pltpu.CompilerParams(vmem_limit_bytes=VMEM_LIMIT),
        cost_estimate=pl.CostEstimate(flops=0, bytes_accessed=20_000_000, transcendentals=0),
    )(*pieces)


def exchange(value, bits):
    if bits == 0:
        return value
    return lax.ppermute(value, "dp", [(i, i ^ bits) for i in range(8)])


def per_device_block(
    hidden_in,
    teacher,
    lengths,
    routes,
    attn_norm_gain,
    ffn_norm_gain,
    q_weight,
    k_weight,
    v_weight,
    q_gain,
    k_gain,
    o_weight,
    router_weight,
    gate_weight,
    up_weight,
    down_weight,
):
    dp_count = lax.axis_size("dp")
    extent = lax.axis_size("tensor")
    d = lax.axis_index("dp")
    t = lax.axis_index("tensor")
    rows, width = hidden_in.shape
    seq_len = rows * extent
    all_tokens = seq_len * dp_count
    length = lengths[d]
    total_count = jnp.sum(lengths).astype(F32)
    attn_gain = attn_norm_gain.astype(F32)
    ffn_gain = ffn_norm_gain.astype(F32)[None, :]
    root_size = math.sqrt(HD)
    expert_count = router_weight.shape[1]
    head_width = q_gain.shape[1]
    local_heads = q_gain.shape[0]
    columns = local_heads * HD

    qkv_own = jnp.concatenate([q_weight, k_weight, v_weight], axis=1)
    gains_own = lax.dynamic_update_slice(
        jnp.zeros((2 * local_heads, HD), F32),
        jnp.concatenate([q_gain, k_gain], axis=0).astype(F32),
        (0, d * head_width),
    )
    hidden_bf, qkv_full, o_full, gains_all, *sent = fetch(
        extent, hidden_in, qkv_own, o_weight, gains_own, gate_weight, up_weight, down_weight
    )
    pieces = [exchange(piece, bits) for bits, piece in enumerate(sent[:6])]
    gains_full = jnp.sum(gains_all, axis=0)
    query_gain = gains_full[:local_heads].reshape(-1)
    key_gain = gains_full[local_heads:].reshape(-1)

    hidden_all = hidden_bf.astype(F32)
    inverse_one = inverse_rms(hidden_all)
    unit_one = hidden_all * inverse_one
    normed = (unit_one * attn_gain).astype(BF)
    qkv = jnp.dot(normed, qkv_full, preferred_element_type=F32)
    query_raw, key_raw = qkv[:, :columns], qkv[:, columns : 2 * columns]
    value_low = qkv[:, 2 * columns :].astype(BF)
    squares = jnp.stack(
        [jnp.sum(query_raw * query_raw, axis=1), jnp.sum(key_raw * key_raw, axis=1)]
    )
    squares = line_total(extent, 2, squares.reshape(-1, 128)).reshape(2, seq_len)
    query_inv = lax.rsqrt(squares[0] / width + EPSILON)[:, None]
    key_inv = lax.rsqrt(squares[1] / width + EPSILON)[:, None]
    query_unit = query_raw * query_inv
    key_unit = key_raw * key_inv
    positions = jnp.arange(seq_len)
    frequency = THETA ** (-jnp.arange(HD // 2).astype(F32) / (HD // 2))
    angles = positions.astype(F32)[:, None] * frequency[None, :]
    cosine = jnp.cos(angles)[:, None, :]
    sinus_table = jnp.sin(angles)[:, None, :]
    queries = rotate(
        (query_unit * query_gain).reshape(seq_len, local_heads, HD), cosine, sinus_table, 1.0
    ).astype(BF)
    key_rows = rotate(
        (key_unit * key_gain).reshape(seq_len, local_heads, HD), cosine, sinus_table, 1.0
    ).astype(BF)
    value_rows = value_low.reshape(seq_len, local_heads, HD)
    scores = (
        jnp.einsum("qhd,khd->hqk", queries, key_rows, preferred_element_type=F32) / root_size
    )
    allowed = (positions[None, :] <= positions[:, None]) & (positions[None, :] < length)
    scores = jnp.where(allowed[None], scores, -1e30)
    row_top = jnp.max(scores, axis=-1, keepdims=True)
    exponent = jnp.exp(scores - row_top)
    probs_float = exponent / jnp.sum(exponent, axis=-1, keepdims=True)
    probs_low = probs_float.astype(BF)
    mixed = (
        jnp.einsum("hqk,khd->qhd", probs_low, value_rows, preferred_element_type=F32)
        .astype(BF)
        .reshape(seq_len, columns)
    )
    attn_partial = jnp.dot(mixed, o_full, preferred_element_type=F32).astype(BF)

    lane = jnp.arange(128)
    lane_expert = jnp.where(lane < 2 * expert_count, lane % expert_count, -1)
    routes_own = lax.dynamic_slice_in_dim(routes, t * rows, rows, 0)
    chosen = jnp.any(routes_own[:, :, None] == lane_expert[None, None, :], axis=1).astype(F32)
    blank = jnp.zeros((width, 128 - 2 * expert_count), BF)
    router_wide = jnp.concatenate([router_weight, router_weight, blank], axis=1)
    router_t = jnp.concatenate(
        [router_weight.T, jnp.zeros((128 - expert_count, width), BF)], axis=0
    )
    middle, gates, ffn_own, tokens, hidden, expert_partial, *last_pieces = enter(
        extent,
        attn_partial.reshape(extent, rows, width),
        hidden_in,
        ffn_gain,
        router_wide,
        chosen,
        pieces,
        sent[6:],
    )
    pieces = pieces + last_pieces
    own_positions = t * rows + jnp.arange(rows)
    row_scale = jnp.where(own_positions < length, all_tokens / total_count, 0.0)
    grad_output, row_loss, ffn_grad_partial, *expert_grads = turn(
        extent,
        expert_partial,
        middle,
        teacher,
        jnp.broadcast_to(row_scale[:, None], (rows, 128)),
        tokens,
        hidden,
        pieces,
    )
    loss_own = jnp.sum(row_loss[:, 0]) / (2.0 * width * all_tokens)
    grad_middle, grad_logits, ffn_gain_part, attn_grad_rows, *came = leave(
        extent,
        ffn_grad_partial,
        middle,
        grad_output,
        gates,
        chosen,
        ffn_gain,
        router_t,
        expert_grads[1:6],
    )
    corner_grads = lax.optimization_barrier((*expert_grads[6:], attn_grad_rows))
    attn_grad_rows = corner_grads[2]
    expert_grads = (
        expert_grads[:1] + came + [exchange(corner_grads[n], 6 + n) for n in range(2)]
    )
    attn_grad_rows = attn_grad_rows.reshape(seq_len, width)
    router_part = jnp.einsum(
        "sd,se->de",
        ffn_own,
        grad_logits[:, :expert_count],
        precision=HIGHEST,
        preferred_element_type=F32,
    )
    grad_o = jnp.einsum("sa,sb->ab", mixed, attn_grad_rows, preferred_element_type=F32)
    grad_mixed = (
        jnp.einsum("sb,ab->sa", attn_grad_rows, o_full, preferred_element_type=F32)
        .astype(BF)
        .reshape(seq_len, local_heads, HD)
    )
    value_grad = jnp.einsum("hqk,qhd->khd", probs_low, grad_mixed, preferred_element_type=F32)
    grad_weights = jnp.einsum(
        "qhd,khd->hqk", grad_mixed, value_rows, preferred_element_type=F32
    )
    grad_scores = (
        probs_float
        * (grad_weights - jnp.sum(grad_weights * probs_float, axis=-1, keepdims=True))
    ).astype(BF)
    query_grad_rot = (
        jnp.einsum("hqk,khd->qhd", grad_scores, key_rows, preferred_element_type=F32) / root_size
    )
    key_grad_rot = (
        jnp.einsum("hqk,qhd->khd", grad_scores, queries, preferred_element_type=F32) / root_size
    )
    query_grad = rotate(query_grad_rot, cosine, sinus_table, -1.0).reshape(seq_len, columns)
    key_grad = rotate(key_grad_rot, cosine, sinus_table, -1.0).reshape(seq_len, columns)
    query_scaled = query_grad * query_gain
    key_scaled = key_grad * key_gain
    qgain_part = jnp.sum(query_grad * query_unit, axis=0)
    kgain_part = jnp.sum(key_grad * key_unit, axis=0)
    dots = jnp.concatenate(
        [
            jnp.sum(query_scaled * query_unit, axis=1),
            jnp.sum(key_scaled * key_unit, axis=1),
            jnp.full((1024,), loss_own, F32),
        ]
    )
    dots = line_total(extent, 6, dots.reshape(-1, 128)).reshape(-1)
    query_dot, key_dot, loss_group = (
        dots[:seq_len],
        dots[seq_len : 2 * seq_len],
        dots[2 * seq_len : 2 * seq_len + 1],
    )
    query_raw_grad = query_inv * (query_scaled - query_unit * (query_dot / width)[:, None])
    key_raw_grad = key_inv * (key_scaled - key_unit * (key_dot / width)[:, None])
    raw_grad = jnp.concatenate(
        [
            query_raw_grad.astype(BF),
            key_raw_grad.astype(BF),
            value_grad.reshape(seq_len, columns).astype(BF),
        ],
        axis=1,
    )
    grad_qkv = jnp.einsum("sd,sa->da", normed, raw_grad, preferred_element_type=F32)
    normed_grad = jnp.einsum("sa,da->sd", raw_grad, qkv_full, preferred_element_type=F32)
    attn_gain_part = jnp.sum(normed_grad * unit_one, axis=0)
    input_part = norm_backward(normed_grad, unit_one, inverse_one, attn_gain).astype(BF)

    split = width // (dp_count * extent)
    small = jnp.concatenate(
        [
            jnp.concatenate(
                [
                    attn_gain_part.reshape(dp_count, extent, 1, split),
                    jnp.sum(ffn_gain_part, axis=0).reshape(dp_count, extent, 1, split),
                ],
                axis=3,
            ),
            router_part.reshape(dp_count, extent, split * expert_count // 128, 128),
            jnp.zeros((dp_count, extent, 15 - split * expert_count // 128, 128), F32),
        ],
        axis=2,
    ).transpose(1, 0, 2, 3)
    gains_part = jnp.concatenate([qgain_part, kgain_part]).reshape(2 * local_heads, HD)
    grad_in, qkv_out, o_out, small_out = close(
        extent,
        input_part.reshape(extent, rows, width),
        grad_middle,
        grad_qkv.astype(BF),
        grad_o.astype(BF),
        small,
        gains_part,
    )
    grad_gate, grad_up, grad_down = spread(expert_grads)
    router_out = small_out[1 : 1 + split * expert_count // 128].reshape(split, expert_count)
    gain_out = lax.dynamic_slice(small_out, (16, d * head_width), (2 * local_heads, head_width))
    return (
        loss_group,
        grad_in,
        small_out[0, :split],
        small_out[0, split : 2 * split],
        qkv_out[:, :columns],
        qkv_out[:, columns : 2 * columns],
        qkv_out[:, 2 * columns :],
        gain_out[:local_heads],
        gain_out[local_heads:],
        o_out,
        router_out,
        grad_gate,
        grad_up,
        grad_down,
    )


def solution(mesh):
    placed = (
        P(("dp", "tensor"), None),
        P(("dp", "tensor"), None),
        P(),
        P("dp", None),
        P(),
        P(),
        P("dp", "tensor"),
        P("dp", "tensor"),
        P("dp", "tensor"),
        P("tensor", "dp"),
        P("tensor", "dp"),
        P("tensor", "dp"),
        P(),
        P(None, "dp", "tensor"),
        P(None, "dp", "tensor"),
        P(None, "tensor", "dp"),
    )
    block = mesh.shape["dp"] == 8 and mesh.shape["tensor"] == 4
    return jax.shard_map(
        per_device_block if block else per_device,
        mesh=mesh,
        in_specs=placed,
        out_specs=(
            P("dp"),
            P(("dp", "tensor"), None),
            P(("dp", "tensor")),
            P(("dp", "tensor")),
            P("dp", "tensor"),
            P("dp", "tensor"),
            P("dp", "tensor"),
            P("tensor", "dp"),
            P("tensor", "dp"),
            P("tensor", "dp"),
            P(("dp", "tensor"), None),
            P(None, "dp", "tensor"),
            P(None, "dp", "tensor"),
            P(None, "tensor", "dp"),
        ),
        check_vma=False,
    )
```

```python
import functools
import math

import jax
import jax.numpy as jnp
from jax import lax
from jax.experimental import pallas as pl
from jax.experimental.pallas import tpu as pltpu
from jax.sharding import PartitionSpec as P

HD = 128
TOK_DEV = 128
CAP = 68


EPSILON = 1e-05
THETA = 10000.0
HIGHEST = lax.Precision.HIGHEST


def inverse_rms(value):
    return lax.rsqrt(jnp.mean(value * value, axis=-1, keepdims=True) + EPSILON)


def rotate(value, cosine, sinus_table, direction):
    middle_index = value.shape[-1] // 2
    leading = value[..., :middle_index]
    trailing = value[..., middle_index:]
    return jnp.concatenate(
        [
            leading * cosine - direction * trailing * sinus_table,
            trailing * cosine + direction * leading * sinus_table,
        ],
        axis=-1,
    )


def norm_backward(grad_norm, unit_rows, inverse_rows, gain_row):
    scaled = grad_norm * gain_row
    return inverse_rows * (
        scaled - unit_rows * jnp.mean(scaled * unit_rows, axis=-1, keepdims=True)
    )


def fetch_attention(q_weight, k_weight, v_weight, o_weight, q_gain, k_gain):
    return (
        lax.all_gather(q_weight, "dp", axis=0, tiled=True),
        lax.all_gather(k_weight, "dp", axis=0, tiled=True),
        lax.all_gather(v_weight, "dp", axis=0, tiled=True),
        lax.all_gather(o_weight, "dp", axis=1, tiled=True),
        lax.all_gather(q_gain, "dp", axis=1, tiled=True),
        lax.all_gather(k_gain, "dp", axis=1, tiled=True),
    )


def fetch_experts(gate_weight, up_weight, down_weight):
    return (
        lax.all_gather(gate_weight, "dp", axis=1, tiled=True),
        lax.all_gather(up_weight, "dp", axis=1, tiled=True),
        lax.all_gather(down_weight, "dp", axis=2, tiled=True),
    )


def per_device(
    hidden_in,
    teacher,
    lengths,
    routes,
    attn_norm_gain,
    ffn_norm_gain,
    q_weight,
    k_weight,
    v_weight,
    q_gain,
    k_gain,
    o_weight,
    router_weight,
    gate_weight,
    up_weight,
    down_weight,
):
    dp_count = lax.axis_size("dp")
    tp_count = lax.axis_size("tensor")
    group_index = lax.axis_index("dp")
    member = lax.axis_index("tensor")
    row_count, model_width = hidden_in.shape
    seq_len = row_count * tp_count
    all_tokens = seq_len * dp_count
    length = lengths[group_index]
    total_count = jnp.sum(lengths).astype(jnp.float32)
    attn_gain = attn_norm_gain.astype(jnp.float32)
    ffn_gain = ffn_norm_gain.astype(jnp.float32)
    root_size = math.sqrt(HD)
    q_full, k_full, v_full, o_full, qgain_full, kgain_full = fetch_attention(
        q_weight, k_weight, v_weight, o_weight, q_gain, k_gain
    )
    local_heads = q_full.shape[1] // HD
    hidden_all = lax.all_gather(hidden_in, "tensor", axis=0, tiled=True).astype(jnp.float32)
    inverse_one = inverse_rms(hidden_all)
    unit_one = hidden_all * inverse_one
    normed = (unit_one * attn_gain).astype(jnp.bfloat16)
    query_raw = jnp.dot(normed, q_full, preferred_element_type=jnp.float32)
    key_raw = jnp.dot(normed, k_full, preferred_element_type=jnp.float32)
    value_low = jnp.dot(normed, v_full, preferred_element_type=jnp.float32).astype(jnp.bfloat16)
    query_sq, key_sq = lax.psum(
        (jnp.sum(query_raw * query_raw, axis=1), jnp.sum(key_raw * key_raw, axis=1)), "tensor"
    )
    query_inv = lax.rsqrt(query_sq / model_width + EPSILON)[:, None]
    key_inv = lax.rsqrt(key_sq / model_width + EPSILON)[:, None]
    query_unit = query_raw * query_inv
    key_unit = key_raw * key_inv
    query_gain = qgain_full.astype(jnp.float32).reshape(-1)
    key_gain = kgain_full.astype(jnp.float32).reshape(-1)
    positions = jnp.arange(seq_len)
    frequency = THETA ** (-jnp.arange(HD // 2).astype(jnp.float32) / (HD // 2))
    angles = positions.astype(jnp.float32)[:, None] * frequency[None, :]
    cosine = jnp.cos(angles)[:, None, :]
    sinus_table = jnp.sin(angles)[:, None, :]
    queries = rotate(
        (query_unit * query_gain).reshape(seq_len, local_heads, HD), cosine, sinus_table, 1.0
    ).astype(jnp.bfloat16)
    key_rows = rotate(
        (key_unit * key_gain).reshape(seq_len, local_heads, HD), cosine, sinus_table, 1.0
    ).astype(jnp.bfloat16)
    value_rows = value_low.reshape(seq_len, local_heads, HD)
    block_rows = min(512, seq_len)
    starts = jnp.arange(seq_len // block_rows) * block_rows

    def block_scores(start):
        query_block = lax.dynamic_slice_in_dim(queries, start, block_rows, 0)
        scores = (
            jnp.einsum("qhd,khd->hqk", query_block, key_rows, preferred_element_type=jnp.float32)
            / root_size
        )
        query_pos = start + jnp.arange(block_rows)
        allowed = (positions[None, :] <= query_pos[:, None]) & (positions[None, :] < length)
        return (query_block, jnp.where(allowed[None], scores, -1e30))

    def attend(start):
        unused_block, scores = block_scores(start)
        row_top = jnp.max(scores, axis=-1, keepdims=True)
        exponent = jnp.exp(scores - row_top)
        row_total = jnp.sum(exponent, axis=-1, keepdims=True)
        weights = (exponent / row_total).astype(jnp.bfloat16)
        mixed_block = jnp.einsum(
            "hqk,khd->qhd", weights, value_rows, preferred_element_type=jnp.float32
        )
        return (mixed_block.astype(jnp.bfloat16), (row_top + jnp.log(row_total))[..., 0])

    mixed_blocks, log_totals = lax.map(attend, starts)
    mixed = mixed_blocks.reshape(seq_len, local_heads * HD)
    attn_own = lax.psum_scatter(
        jnp.dot(mixed, o_full, preferred_element_type=jnp.float32).astype(jnp.bfloat16),
        "tensor",
        scatter_dimension=0,
        tiled=True,
    ).astype(jnp.float32)
    middle = hidden_in.astype(jnp.float32) + attn_own
    inverse_two = inverse_rms(middle)
    unit_two = middle * inverse_two
    ffn_own = (unit_two * ffn_gain).astype(jnp.bfloat16)
    gate_full, up_full, down_full = fetch_experts(gate_weight, up_weight, down_weight)
    ffn_all = lax.all_gather(ffn_own, "tensor", axis=0, tiled=True)
    expert_count = router_weight.shape[1]
    route_width = routes.shape[1]
    gate_probs = jax.nn.softmax(
        jnp.dot(ffn_all, router_weight, preferred_element_type=jnp.float32), axis=-1
    )
    picked = routes[:, :, None] == jnp.arange(expert_count)[None, None, :]
    route_gates = jnp.sum(jnp.where(picked, gate_probs[:, None, :], 0.0), axis=-1)
    block_count = seq_len // TOK_DEV
    per_expert = block_count * CAP
    picked_ints = picked.reshape(block_count, TOK_DEV * route_width, expert_count).astype(jnp.int32)
    slot_ranks = jnp.sum((jnp.cumsum(picked_ints, axis=1) - 1) * picked_ints, axis=-1).reshape(
        seq_len, route_width
    )
    block_ids = (positions // TOK_DEV)[:, None]
    slot_ids = (routes * per_expert + block_ids * CAP + slot_ranks).reshape(-1)
    slot_total = expert_count * per_expert
    token_ids = jnp.repeat(positions, route_width)
    group_width = 4
    turn_count = expert_count // group_width
    sources = (
        jnp.full((slot_total,), seq_len, jnp.int32)
        .at[slot_ids]
        .set(token_ids)
        .reshape(turn_count, group_width, per_expert)
    )
    slot_gates = (
        jnp.zeros((slot_total,), jnp.float32)
        .at[slot_ids]
        .set(route_gates.reshape(-1))
        .reshape(turn_count, group_width, per_expert, 1)
    )
    ffn_padded = jnp.concatenate([ffn_all, jnp.zeros((1, model_width), jnp.bfloat16)], axis=0)
    expert_running = jnp.zeros((seq_len + 1, model_width), jnp.float32)
    kept_values = []
    for turn_index in range(turn_count):
        lower = turn_index * group_width
        upper = lower + group_width
        expert_inputs = ffn_padded[sources[turn_index]]
        gate_value = jnp.einsum(
            "gpd,gdf->gpf",
            expert_inputs,
            gate_full[lower:upper],
            preferred_element_type=jnp.float32,
        )
        up_value = jnp.einsum(
            "gpd,gdf->gpf", expert_inputs, up_full[lower:upper], preferred_element_type=jnp.float32
        )
        active = (slot_gates[turn_index] * jax.nn.silu(gate_value) * up_value).astype(jnp.bfloat16)
        expert_outputs = jnp.einsum(
            "gpf,gfd->gpd", active, down_full[lower:upper], preferred_element_type=jnp.float32
        )
        expert_running = expert_running.at[sources[turn_index].reshape(-1)].add(
            expert_outputs.reshape(-1, model_width)
        )
        kept_values.append((gate_value, up_value, active))
    expert_own = lax.psum_scatter(
        expert_running[:seq_len].astype(jnp.bfloat16), "tensor", scatter_dimension=0, tiled=True
    ).astype(jnp.float32)
    output = middle + expert_own
    own_positions = member * row_count + jnp.arange(row_count)
    valid_rows = (own_positions < length)[:, None]
    mismatch = output - teacher.astype(jnp.float32)
    loss_own = jnp.sum(jnp.where(valid_rows, mismatch * mismatch, 0.0)) / (
        2.0 * model_width * total_count
    )
    grad_output = jnp.where(valid_rows, mismatch * (all_tokens / total_count), 0.0)
    grad_rows = lax.all_gather(grad_output.astype(jnp.bfloat16), "tensor", axis=0, tiled=True)
    gate_full, up_full, down_full = fetch_experts(gate_weight, up_weight, down_weight)
    grad_padded = jnp.concatenate([grad_rows, jnp.zeros((1, model_width), jnp.bfloat16)], axis=0)
    ffn_grad_running = jnp.zeros((seq_len + 1, model_width), jnp.float32)
    gate_grads = []
    up_grads = []
    down_grads = []
    slot_grads = []
    for turn_index in range(turn_count):
        gate_value, up_value, active = kept_values[turn_index]
        lower = turn_index * group_width
        upper = lower + group_width
        source_rows = sources[turn_index]
        expert_inputs = ffn_padded[source_rows]
        incoming = grad_padded[source_rows]
        grad_active = jnp.einsum(
            "gpd,gfd->gpf", incoming, down_full[lower:upper], preferred_element_type=jnp.float32
        )
        down_turn = jnp.einsum("gpf,gpd->gfd", active, incoming, preferred_element_type=jnp.float32)
        sigmoid_value = jax.nn.sigmoid(gate_value)
        silu_value = gate_value * sigmoid_value
        slot_grads.append(jnp.sum(grad_active * silu_value * up_value, axis=-1))
        grad_inner = grad_active * slot_gates[turn_index]
        grad_gate_value = (
            grad_inner * up_value * sigmoid_value * (1.0 + gate_value * (1.0 - sigmoid_value))
        ).astype(jnp.bfloat16)
        grad_up_value = (grad_inner * silu_value).astype(jnp.bfloat16)
        gate_turn = jnp.einsum(
            "gpd,gpf->gdf", expert_inputs, grad_gate_value, preferred_element_type=jnp.float32
        )
        up_turn = jnp.einsum(
            "gpd,gpf->gdf", expert_inputs, grad_up_value, preferred_element_type=jnp.float32
        )
        gate_grads.append(gate_turn)
        up_grads.append(up_turn)
        down_grads.append(down_turn)
        grad_inputs = jnp.einsum(
            "gpf,gdf->gpd",
            grad_gate_value,
            gate_full[lower:upper],
            preferred_element_type=jnp.float32,
        )
        grad_inputs = grad_inputs + jnp.einsum(
            "gpf,gdf->gpd", grad_up_value, up_full[lower:upper], preferred_element_type=jnp.float32
        )
        ffn_grad_running = ffn_grad_running.at[source_rows.reshape(-1)].add(
            grad_inputs.reshape(-1, model_width)
        )
    slot_grad_all = jnp.concatenate([entry.reshape(-1) for entry in slot_grads])
    route_grads = slot_grad_all[slot_ids].reshape(seq_len, route_width)
    grad_probs = jnp.sum(jnp.where(picked, route_grads[:, :, None], 0.0), axis=1)
    grad_logits = gate_probs * (
        grad_probs - jnp.sum(grad_probs * gate_probs, axis=-1, keepdims=True)
    )
    router_float = router_weight.astype(jnp.float32)
    ffn_grad_part = ffn_grad_running[:seq_len] + jnp.einsum(
        "se,de->sd", grad_logits, router_float, precision=HIGHEST
    )
    router_part = jnp.einsum(
        "sd,se->de", ffn_all, grad_logits, precision=HIGHEST, preferred_element_type=jnp.float32
    )
    ffn_grad_own = lax.psum_scatter(
        ffn_grad_part.astype(jnp.bfloat16), "tensor", scatter_dimension=0, tiled=True
    ).astype(jnp.float32)
    ffn_gain_part = jnp.sum(ffn_grad_own * unit_two, axis=0)
    grad_middle = grad_output + norm_backward(ffn_grad_own, unit_two, inverse_two, ffn_gain)
    attn_grad_rows = lax.all_gather(grad_middle.astype(jnp.bfloat16), "tensor", axis=0, tiled=True)
    q_full, k_full, v_full, o_full, qgain_full, kgain_full = fetch_attention(
        q_weight, k_weight, v_weight, o_weight, q_gain, k_gain
    )
    grad_o = jnp.einsum("sa,sb->ab", mixed, attn_grad_rows, preferred_element_type=jnp.float32)
    grad_mixed = (
        jnp.einsum("sb,ab->sa", attn_grad_rows, o_full, preferred_element_type=jnp.float32)
        .astype(jnp.bfloat16)
        .reshape(seq_len, local_heads, HD)
    )

    def attend_back(carry, inputs):
        key_running, value_running = carry
        start, log_total = inputs
        query_block, scores = block_scores(start)
        probs_float = jnp.exp(scores - log_total[..., None])
        probs_low = probs_float.astype(jnp.bfloat16)
        grad_block = lax.dynamic_slice_in_dim(grad_mixed, start, block_rows, 0)
        value_running = value_running + jnp.einsum(
            "hqk,qhd->khd", probs_low, grad_block, preferred_element_type=jnp.float32
        )
        grad_weights = jnp.einsum(
            "qhd,khd->hqk", grad_block, value_rows, preferred_element_type=jnp.float32
        )
        grad_scores = (
            probs_float
            * (grad_weights - jnp.sum(grad_weights * probs_float, axis=-1, keepdims=True))
        ).astype(jnp.bfloat16)
        query_grad_block = (
            jnp.einsum("hqk,khd->qhd", grad_scores, key_rows, preferred_element_type=jnp.float32)
            / root_size
        )
        key_running = (
            key_running
            + jnp.einsum(
                "hqk,qhd->khd", grad_scores, query_block, preferred_element_type=jnp.float32
            )
            / root_size
        )
        return ((key_running, value_running), query_grad_block)

    zero_heads = jnp.zeros((seq_len, local_heads, HD), jnp.float32)
    (key_grad_rot, value_grad), query_grad_blocks = lax.scan(
        attend_back, (zero_heads, zero_heads), (starts, log_totals)
    )
    query_grad = rotate(
        query_grad_blocks.reshape(seq_len, local_heads, HD), cosine, sinus_table, -1.0
    ).reshape(seq_len, local_heads * HD)
    key_grad = rotate(key_grad_rot, cosine, sinus_table, -1.0).reshape(seq_len, local_heads * HD)
    query_scaled = query_grad * query_gain
    key_scaled = key_grad * key_gain
    qgain_part = jnp.sum(query_grad * query_unit, axis=0)
    kgain_part = jnp.sum(key_grad * key_unit, axis=0)
    query_dot, key_dot, loss_group = lax.psum(
        (
            jnp.sum(query_scaled * query_unit, axis=1),
            jnp.sum(key_scaled * key_unit, axis=1),
            loss_own,
        ),
        "tensor",
    )
    query_raw_grad = (
        query_inv * (query_scaled - query_unit * (query_dot / model_width)[:, None])
    ).astype(jnp.bfloat16)
    key_raw_grad = (key_inv * (key_scaled - key_unit * (key_dot / model_width)[:, None])).astype(
        jnp.bfloat16
    )
    value_raw_grad = value_grad.reshape(seq_len, local_heads * HD).astype(jnp.bfloat16)
    grad_q = jnp.einsum("sd,sa->da", normed, query_raw_grad, preferred_element_type=jnp.float32)
    grad_k = jnp.einsum("sd,sa->da", normed, key_raw_grad, preferred_element_type=jnp.float32)
    grad_v = jnp.einsum("sd,sa->da", normed, value_raw_grad, preferred_element_type=jnp.float32)
    normed_grad = jnp.einsum(
        "sa,da->sd", query_raw_grad, q_full, preferred_element_type=jnp.float32
    )
    normed_grad = normed_grad + jnp.einsum(
        "sa,da->sd", key_raw_grad, k_full, preferred_element_type=jnp.float32
    )
    normed_grad = normed_grad + jnp.einsum(
        "sa,da->sd", value_raw_grad, v_full, preferred_element_type=jnp.float32
    )
    attn_gain_part = jnp.sum(normed_grad * unit_one, axis=0)
    input_part = norm_backward(normed_grad, unit_one, inverse_one, attn_gain)
    split_width = model_width // (dp_count * tp_count)
    input_own, attn_gain_share, ffn_gain_share, router_share = (
        lax.psum_scatter(
            input_part.astype(jnp.bfloat16), "tensor", scatter_dimension=0, tiled=True
        ).astype(jnp.float32),
        lax.psum_scatter(
            attn_gain_part.reshape(dp_count, tp_count, split_width).astype(jnp.bfloat16),
            "tensor",
            scatter_dimension=1,
            tiled=True,
        ).astype(jnp.float32),
        lax.psum_scatter(
            ffn_gain_part.reshape(dp_count, tp_count, split_width).astype(jnp.bfloat16),
            "tensor",
            scatter_dimension=1,
            tiled=True,
        ).astype(jnp.float32),
        lax.psum_scatter(
            router_part.reshape(dp_count, tp_count, split_width, expert_count).astype(jnp.bfloat16),
            "tensor",
            scatter_dimension=1,
            tiled=True,
        ).astype(jnp.float32),
    )
    grad_in = grad_middle + input_own
    (
        grad_q,
        grad_k,
        grad_v,
        grad_o,
        grad_qgain,
        grad_kgain,
        attn_gain_sum,
        ffn_gain_sum,
        router_sum,
    ) = (
        lax.psum_scatter(grad_q.astype(jnp.bfloat16), "dp", scatter_dimension=0, tiled=True).astype(
            jnp.float32
        ),
        lax.psum_scatter(grad_k.astype(jnp.bfloat16), "dp", scatter_dimension=0, tiled=True).astype(
            jnp.float32
        ),
        lax.psum_scatter(grad_v.astype(jnp.bfloat16), "dp", scatter_dimension=0, tiled=True).astype(
            jnp.float32
        ),
        lax.psum_scatter(grad_o.astype(jnp.bfloat16), "dp", scatter_dimension=1, tiled=True).astype(
            jnp.float32
        ),
        lax.psum_scatter(
            qgain_part.reshape(local_heads, HD).astype(jnp.bfloat16),
            "dp",
            scatter_dimension=1,
            tiled=True,
        ).astype(jnp.float32),
        lax.psum_scatter(
            kgain_part.reshape(local_heads, HD).astype(jnp.bfloat16),
            "dp",
            scatter_dimension=1,
            tiled=True,
        ).astype(jnp.float32),
        lax.psum_scatter(
            attn_gain_share.astype(jnp.bfloat16), "dp", scatter_dimension=0, tiled=True
        ).astype(jnp.float32),
        lax.psum_scatter(
            ffn_gain_share.astype(jnp.bfloat16), "dp", scatter_dimension=0, tiled=True
        ).astype(jnp.float32),
        lax.psum_scatter(
            router_share.astype(jnp.bfloat16), "dp", scatter_dimension=0, tiled=True
        ).astype(jnp.float32),
    )
    grad_gate, grad_up, grad_down = (
        lax.psum_scatter(
            jnp.concatenate(gate_grads, axis=0).astype(jnp.bfloat16),
            "dp",
            scatter_dimension=1,
            tiled=True,
        ).astype(jnp.float32),
        lax.psum_scatter(
            jnp.concatenate(up_grads, axis=0).astype(jnp.bfloat16),
            "dp",
            scatter_dimension=1,
            tiled=True,
        ).astype(jnp.float32),
        lax.psum_scatter(
            jnp.concatenate(down_grads, axis=0).astype(jnp.bfloat16),
            "dp",
            scatter_dimension=2,
            tiled=True,
        ).astype(jnp.float32),
    )
    return (
        loss_group.reshape(1),
        grad_in,
        attn_gain_sum.reshape(-1),
        ffn_gain_sum.reshape(-1),
        grad_q,
        grad_k,
        grad_v,
        grad_qgain,
        grad_kgain,
        grad_o,
        router_sum.reshape(-1, expert_count),
        grad_gate,
        grad_up,
        grad_down,
    )


MESH = pl.DeviceIdType.MESH
BF = jnp.bfloat16
F32 = jnp.float32
VMEM_LIMIT = 62 * 1024 * 1024
ANY = pl.BlockSpec(memory_space=pl.ANY)
VM = pl.BlockSpec(memory_space=pltpu.VMEM)


def flip(index, bits):
    for bit in (1, 2, 4):
        if bits & bit:
            index = index + bit * (1 - 2 * ((index // bit) % 2))
    return index


def both(first, second):
    return jnp.logical_and(first, second)


def under(condition, action):
    if condition is None:
        action()
    else:
        pl.when(condition)(action)


class Wire:
    def __init__(self, send_sem, recv_sem):
        self.send_sem, self.recv_sem, self.count, self.sent = send_sem, recv_sem, 0, []

    def slot(self):
        self.count += 1
        return self.count - 1

    def start(self, slot, source, target, device, condition=None):
        def make():
            return pltpu.make_async_remote_copy(
                src_ref=source(),
                dst_ref=target(),
                send_sem=self.send_sem.at[slot],
                recv_sem=self.recv_sem.at[slot],
                device_id=device,
                device_id_type=MESH,
            )

        under(condition, lambda: make().start())
        self.sent.append((condition, make))

    def arrive(self, slot, region, device, condition=None):
        copy = pltpu.make_async_remote_copy(
            src_ref=region(),
            dst_ref=region(),
            send_sem=self.send_sem.at[slot],
            recv_sem=self.recv_sem.at[slot],
            device_id=device,
            device_id_type=MESH,
        )
        under(condition, lambda: copy.wait_recv())

    def finish(self):
        for condition, make in self.sent:
            under(condition, lambda make=make: make().wait_send())
        self.sent = []


class Local:
    def __init__(self, sem):
        self.sem, self.count = sem, 0

    def start(self, source, target):
        copy = pltpu.make_async_copy(source, target, self.sem.at[self.count])
        self.count += 1
        copy.start()
        return copy


def greet(devices):
    barrier = pltpu.get_barrier_semaphore()
    for condition, device in devices:
        under(
            condition,
            lambda device=device: pl.semaphore_signal(
                barrier, inc=1, device_id=device, device_id_type=MESH
            ),
        )
    amount = sum(1 for condition, device in devices if condition is None)
    for condition, device in devices:
        if condition is not None:
            amount = amount + jnp.where(condition, 1, 0)
    pl.semaphore_wait(barrier, amount)


def line_devices(d, t, extent):
    return [(t < extent - 1, (d, t + 1)), (t > 0, (d, t - 1))]


def rows_loop(rows, step, body):
    def run(index, carry):
        body(pl.multiple_of(index * step, step))
        return carry

    lax.fori_loop(0, rows // step, run, 0)


def add_into(target, source, rows):
    def body(start):
        part = pl.ds(start, 16)
        target[part] = target[part] + source[part]

    rows_loop(rows, 16, body)


class LineGather:
    def __init__(self, wire, d, t, extent, own, place):
        self.wire, self.extent = wire, extent
        up = [wire.slot() for unused in range(extent - 1)]
        down = [wire.slot() for unused in range(extent - 1)]
        last = extent - 1
        above, below = (d, t + 1), (d, t - 1)
        wire.start(up[0], own, lambda: place(t), above, t < last)
        wire.start(down[0], own, lambda: place(t), below, t > 0)
        self.steps = {}
        for step in range(1, extent):
            from_below, from_above = t >= step, t <= last - step
            lower, upper = t - step, t + step
            self.steps[step] = (
                (
                    up,
                    lambda index=lower: place(index),
                    from_below,
                    both(from_below, t < last),
                    above,
                    below,
                ),
                (
                    down,
                    lambda index=upper: place(index),
                    from_above,
                    both(from_above, t > 0),
                    below,
                    above,
                ),
            )

    def step(self, step):
        for slots, region, valid, onward, to, source in self.steps[step]:
            self.wire.arrive(slots[step - 1], region, source, valid)
            if step < self.extent - 1:
                self.wire.start(slots[step], region, region, to, onward)


def arrival(t, turn):
    near = t - 1 + 2 * (1 - (t + 3) // 4)
    far = 3 * (1 - t // 2)
    choices = (t, near, 6 - t - near - far, far)
    if isinstance(turn, int):
        return choices[turn]
    result = choices[0]
    for number in range(1, 4):
        result = jnp.where(turn == number, choices[number], result)
    return result


LATE = 32


class PlaneGather:
    def __init__(self, wire, d, t, extent, own, place, bundle, rows):
        self.wire, self.place, self.bundle, self.own = wire, place, bundle, own
        self.early, self.half = rows - LATE, (rows - LATE) // 2
        self.to_x, self.to_y, self.to_c = (flip(d, 2), t), (flip(d, 4), t), (flip(d, 1), t)
        self.index = [arrival(t, turn) for turn in range(extent)]
        self.slots = {}
        self.where = (wire, d, t, extent)
        late = lambda n: (self.early + n * (LATE // 2), LATE // 2)
        self.parts = {0: (0, self.half), 1: (self.half, self.half), 2: late(0), 3: late(1)}
        self.parts["early"], self.parts["late"] = (0, self.early), (self.early, LATE)
        self.send("gx", 0, self.source(0, "late"), self.spot(0, 0, 1, "late"), self.to_x)
        self.send("gy", 0, self.source(0, "late"), self.spot(0, 0, 2, "late"), self.to_y)
        self.line = LineGather(
            wire, d, t, extent, lambda: self.cut(own(), "early"), lambda j: self.cut(place(j, 0, 0), "early")
        )
        self.stage_first(0)
        for name, i, which, onward, to, source in (
            ("gx", 1, 2, "gfy", self.to_y, self.to_x),
            ("gy", 2, 3, "gfx", self.to_x, self.to_y),
        ):
            self.wait(name, 0, self.spot(0, 0, i, "late"), source)
            self.send(onward, 0, self.spot(0, 0, i, which), self.spot(0, 0, 3, which), to)
        self.stage_second(0)

    def cut(self, ref, which):
        start, size = self.parts[which]
        return ref.at[pl.ds(start, size)]

    def send(self, name, turn, source, target, device):
        slot = self.wire.slot()
        self.slots[name, turn] = slot
        self.wire.start(slot, source, target, device)

    def wait(self, name, turn, region, device):
        self.wire.arrive(self.slots[name, turn], region, device)

    def spot(self, turn, c, i, which):
        return lambda: self.cut(self.place(self.index[turn], c, i), which)

    def source(self, turn, which):
        if turn == 0:
            return lambda: self.cut(self.own(), which)
        return self.spot(turn, 0, 0, which)

    def stage_first(self, turn):
        source, spot = self.source, self.spot
        self.send("x0", turn, source(turn, 0), spot(turn, 0, 1, 0), self.to_x)
        self.send("y1", turn, source(turn, 1), spot(turn, 0, 2, 1), self.to_y)

    def stage_second(self, turn):
        source, spot = self.source, self.spot
        self.send("x1", turn, source(turn, 1), spot(turn, 0, 1, 1), self.to_x)
        self.send("y0", turn, source(turn, 0), spot(turn, 0, 2, 0), self.to_y)
        self.send("c0", turn, source(turn, "early"), spot(turn, 1, 0, "early"), self.to_c)

    def stage(self, turn):
        self.stage_first(turn)
        self.stage_second(turn)

    def relay(self, turn):
        spot = self.spot
        self.wait("x0", turn, spot(turn, 0, 1, 0), self.to_x)
        self.send("fy", turn, spot(turn, 0, 1, 0), spot(turn, 0, 3, 0), self.to_y)
        self.wait("y1", turn, spot(turn, 0, 2, 1), self.to_y)
        self.send("fx", turn, spot(turn, 0, 2, 1), spot(turn, 0, 3, 1), self.to_x)
        self.wait("x1", turn, spot(turn, 0, 1, 1), self.to_x)
        self.send("c1", turn, spot(turn, 0, 1, "early"), spot(turn, 1, 1, "early"), self.to_c)
        self.wait("y0", turn, spot(turn, 0, 2, 0), self.to_y)
        self.send("c2", turn, spot(turn, 0, 2, "early"), spot(turn, 1, 2, "early"), self.to_c)

    def corner(self, turn):
        spot = self.spot
        self.wait("fy", turn, spot(turn, 0, 3, 0), self.to_y)
        self.wait("fx", turn, spot(turn, 0, 3, 1), self.to_x)
        self.send("c3", turn, spot(turn, 0, 3, "early"), spot(turn, 1, 3, "early"), self.to_c)

    def pass_bundle(self, turn):
        region = lambda c: (lambda: self.bundle(self.index[turn], c))
        self.send("cb", turn, region(0), region(1), self.to_c)

    def bundle_start(self):
        spot = self.spot
        self.wait("gfy", 0, spot(0, 0, 3, 2), self.to_y)
        self.wait("gfx", 0, spot(0, 0, 3, 3), self.to_x)
        here = self.index[0]
        wire, d, t, extent = self.where
        self.late_line = LineGather(
            wire, d, t, extent, lambda: self.bundle(here, 0), lambda j: self.bundle(j, 0)
        )
        self.pass_bundle(0)

    def bundle_step(self, step):
        self.late_line.step(step)
        self.pass_bundle(step)

    def other(self, turn):
        for i in range(4):
            self.wait("c%d" % i, turn, self.spot(turn, 1, i, "early"), self.to_c)
        self.wait("cb", turn, lambda: self.bundle(self.index[turn], 1), self.to_c)

    def actions(self):
        line, stage, relay, corner, other, late = (
            self.line.step,
            self.stage,
            self.relay,
            self.corner,
            self.other,
            self.bundle_step,
        )
        return (
            (
                (line, 1),
                (stage, 1),
                (relay, 0),
                (line, 2),
                (stage, 2),
                (corner, 0),
                (late, 1),
            ),
            ((relay, 1), (line, 3), (stage, 3), (other, 0)),
            ((relay, 2), (corner, 1), (late, 2)),
            ((other, 1),),
            ((relay, 3), (corner, 2), (late, 3)),
            ((other, 2),),
            ((corner, 3),),
            ((other, 3),),
        )


class LineSum:
    def __init__(self, wire, d, t, extent, block, up_in, down_in, rows, parts):
        self.wire, self.d, self.t, self.extent = wire, d, t, extent
        self.block, self.up_in, self.down_in = block, up_in, down_in
        self.rows, self.parts = rows // parts, parts
        self.up = [[wire.slot() for p in range(parts)] for s in range(extent - 1)]
        self.down = [[wire.slot() for p in range(parts)] for s in range(extent - 1)]

    def cut(self, ref, part):
        return ref.at[pl.ds(part * self.rows, self.rows)]

    def add(self, target, source):
        add_into(target, source, self.rows)

    def flow(self, step, part, near, index, slots, buffers, to_device, from_device):
        wire, extent = self.wire, self.extent
        block = lambda: self.cut(self.block(index), part)
        if step >= 1:
            source = lambda: self.cut(buffers.at[step - 1], part)
            active = both(both(near <= step, near < extent - 1), near >= 1)
            wire.arrive(slots[step - 1][part], source, from_device, active)
            under(active, lambda: self.add(block(), source()))
        wire.start(
            slots[step][part],
            block,
            lambda: self.cut(buffers.at[step], part),
            to_device,
            both(near <= step, near < extent - 1),
        )

    def step(self, step):
        d, t, extent = self.d, self.t, self.extent
        up, down = extent - 1 - step + t, step + t - (extent - 1)
        above, below = (d, t + 1), (d, t - 1)
        for part in range(self.parts):
            self.flow(step, part, t, up, self.up, self.up_in, above, below)
            self.flow(step, part, extent - 1 - t, down, self.down, self.down_in, below, above)

    def last(self):
        d, t, extent = self.d, self.t, self.extent
        for ready, missing, slots, buffers, device in (
            (t > 0, t == 0, self.up, self.up_in, (d, t - 1)),
            (t < extent - 1, t == extent - 1, self.down, self.down_in, (d, t + 1)),
        ):
            buffer = buffers.at[extent - 2]
            for part in range(self.parts):
                self.wire.arrive(
                    slots[extent - 2][part],
                    lambda part=part, buffer=buffer: self.cut(buffer, part),
                    device,
                    ready,
                )

            def clear(buffer=buffer):
                buffer[...] = jnp.zeros(buffer.shape, BF)

            under(missing, clear)


class BundleSum(LineSum):
    def cut(self, ref, part):
        return ref

    def add(self, target, source):
        for i in range(4):
            add_into(target.at[i], source.at[i], LATE)


def own_sum(block, up_in, down_in, part, columns):
    return (
        block[part, columns].astype(F32)
        + up_in[part, columns].astype(F32)
        + down_in[part, columns].astype(F32)
    )


def plane_order(t):
    top = t // 2
    inner = ((t + 1) // 2) % 2
    return (
        3 - 3 * top,
        2 - top,
        (1 - inner) * (1 - top) + (2 + inner) * top,
        inner * (1 - top) + (3 - inner) * top,
    )


def sum_plane(wire, local, d, t, extent, partial, buffers, rows, between=lambda turn: None):
    (
        work,
        own_in,
        a_in,
        b_in,
        up_in,
        down_in,
        late_up,
        late_down,
        late_a,
        late_b,
    ) = buffers
    order = plane_order(t)
    early, half = rows - LATE, (rows - LATE) // 2
    to_x, to_y, to_c = (flip(d, 2), t), (flip(d, 4), t), (flip(d, 1), t)
    turns = (3, 1, 2, 0)
    slots_c, slots_a, slots_b, loads = {}, {}, {}, {}

    def cut(ref, which):
        return ref.at[pl.ds(which * half, half)]

    def late_cut(ref, which):
        return ref.at[pl.ds(early + which * (LATE // 2), LATE // 2)]

    def begin(k):
        for i in turns:
            slots_c[k, i] = wire.slot()
            wire.start(
                slots_c[k, i],
                lambda i=i: partial.at[order[k], 1, i],
                lambda i=i: work.at[k, i],
                to_c,
            )
            loads[k, i] = local.start(partial.at[order[k], 0, i], own_in.at[k % 2, i])

    begin(0)

    def inverse(index):
        where = jnp.int32(0)
        for k in range(1, extent):
            where = where + k * jnp.where(order[k] == index, 1, 0)
        return where

    line = LineSum(
        wire,
        d,
        t,
        extent,
        lambda index: work.at[inverse(index), 0, pl.ds(0, early)],
        up_in,
        down_in,
        early,
        1,
    )
    late_line = BundleSum(
        wire,
        d,
        t,
        extent,
        lambda index: work.at[inverse(index), pl.ds(0, 4), pl.ds(early, LATE)],
        late_up,
        late_down,
        LATE,
        1,
    )
    routes_a = (
        (to_x, 3, 2, 0, 0),
        (to_y, 3, 1, 1, 1),
        (to_x, 1, 0, 0, 2),
        (to_y, 2, 0, 1, 3),
    )
    routes_b = ((to_y, 2, 0, 0), (to_x, 1, 1, 1))
    last = extent - 1

    def send_a(k, source, cutter, inbox):
        for device, origin, unused, which, row in routes_a:
            if origin == source:
                slots_a[inbox is a_in, k, row] = wire.slot()
                wire.start(
                    slots_a[inbox is a_in, k, row],
                    lambda origin=origin, which=which: cutter(work.at[k, origin], which),
                    lambda row=row: inbox.at[k, row] if inbox is a_in else inbox.at[row],
                    device,
                )

    def receive_a(k, cutter, inbox, second, size):
        for device, unused, target, which, row in routes_a:
            region = inbox.at[k, row] if inbox is a_in else inbox.at[row]
            wire.arrive(slots_a[inbox is a_in, k, row], lambda: region, device)
            add_into(cutter(work.at[k, target], which), region, size)
            if row < 2:
                to, origin, part, b_row = routes_b[row]
                slots_b[inbox is a_in, k, b_row] = wire.slot()
                wire.start(
                    slots_b[inbox is a_in, k, b_row],
                    lambda origin=origin, part=part: cutter(work.at[k, origin], part),
                    lambda b_row=b_row: second.at[k, b_row]
                    if inbox is a_in
                    else second.at[b_row],
                    to,
                )

    def receive_b(k, cutter, inbox, second, size):
        for device, unused, which, row in routes_b:
            region = second.at[k, row] if inbox is a_in else second.at[row]
            wire.arrive(slots_b[inbox is a_in, k, row], lambda: region, device)
            add_into(cutter(work.at[k, 0], which), region, size)

    for turn in range(extent + 2):
        if turn + 1 < extent:
            begin(turn + 1)
        if turn < extent:
            k = turn
            for i in turns:
                loads[k, i].wait()
                wire.arrive(slots_c[k, i], lambda k=k, i=i: work.at[k, i], to_c)
                add_into(work.at[k, i], own_in.at[k % 2, i], rows)
                send_a(k, i, cut, a_in)
            if k < last:
                late_line.step(k)
        if turn == extent:
            late_line.last()
            for i in turns:
                for inbox in (late_up, late_down):
                    add_into(
                        work.at[last, i, pl.ds(early, LATE)], inbox.at[last - 1, i], LATE
                    )
                send_a(last, i, late_cut, late_a)
        between(turn)
        if 1 <= turn <= extent:
            receive_a(turn - 1, cut, a_in, b_in, half)
        if turn == extent + 1:
            receive_a(last, late_cut, late_a, late_b, LATE // 2)
        if turn >= 2:
            k = turn - 2
            receive_b(k, cut, a_in, b_in, half)
            if k < last:
                line.step(k)
    receive_b(last, late_cut, late_a, late_b, LATE // 2)
    line.last()


def own_rows(buffers, rows, columns, body):
    work, up_in, down_in = buffers[0], buffers[4], buffers[5]
    mine = work.at[work.shape[0] - 1, 0]
    up_last, down_last = up_in.at[up_in.shape[0] - 1], down_in.at[down_in.shape[0] - 1]
    early = rows - LATE

    def first(start):
        part = pl.ds(start, 16)
        body(part, own_sum(mine, up_last, down_last, part, columns))

    def second(start):
        part = pl.ds(pl.multiple_of(early + start, 16), 16)
        body(part, mine[part, columns].astype(F32))

    rows_loop(early, 16, first)
    rows_loop(LATE, 16, second)


def sum_scratch(extent, rows, width):
    early = rows - LATE
    return [
        pltpu.VMEM((extent, 4, rows, width), BF),
        pltpu.VMEM((2, 4, rows, width), BF),
        pltpu.VMEM((extent, 4, early // 2, width), BF),
        pltpu.VMEM((extent, 2, early // 2, width), BF),
        pltpu.VMEM((extent - 1, early, width), BF),
        pltpu.VMEM((extent - 1, early, width), BF),
        pltpu.VMEM((extent - 1, 4, LATE, width), BF),
        pltpu.VMEM((extent - 1, 4, LATE, width), BF),
        pltpu.VMEM((4, LATE // 2, width), BF),
        pltpu.VMEM((2, LATE // 2, width), BF),
    ]


def plane_devices(d, t, extent):
    return line_devices(d, t, extent) + [(None, (flip(d, bits), t)) for bits in (1, 2, 4)]


def kernel_params(number):
    return pltpu.CompilerParams(
        collective_id=number, has_side_effects=True, vmem_limit_bytes=VMEM_LIMIT
    )


def dma_pair(count):
    return [pltpu.SemaphoreType.DMA((count,)), pltpu.SemaphoreType.DMA((count,))]


def fetch_kernel(
    extent,
    hid,
    qkv,
    o,
    gains,
    gate,
    up,
    down,
    hid_all,
    qkv_all,
    o_all,
    gains_all,
    *rest,
):
    pieces, (stage, send_sem, recv_sem, local_sem) = rest[:8], rest[8:]
    d, t = lax.axis_index("dp"), lax.axis_index("tensor")
    rows = hid.shape[0]
    depth, o_rows = qkv.shape[0], o.shape[0]
    width = o.shape[1]
    greet(line_devices(d, t, extent) + [(None, (flip(d, bits), t)) for bits in range(1, 8)])
    wire, local = Wire(send_sem, recv_sem), Local(local_sem)
    dx, dy, dxy, dc = flip(d, 2), flip(d, 4), flip(d, 6), flip(d, 1)
    to_x, to_y, to_c = (dx, t), (dy, t), (dc, t)

    def region(device, which):
        start = pl.multiple_of(device * width, width)
        if which is None:
            return [qkv_all.at[pl.ds(device * depth, depth)], o_all.at[:, pl.ds(start, width)]]
        return [
            qkv_all.at[pl.ds(device * depth + which * (depth // 2), depth // 2)],
            o_all.at[pl.ds(which * (o_rows // 2), o_rows // 2), pl.ds(start, width)],
        ]

    def own(which):
        if which is None:
            return [qkv, o]
        return [
            qkv.at[pl.ds(which * (depth // 2), depth // 2)],
            o.at[pl.ds(which * (o_rows // 2), o_rows // 2)],
        ]

    def send(device, sources, targets):
        slots = []
        for source, target in zip(sources, targets):
            slot = wire.slot()
            wire.start(slot, lambda source=source: source, lambda target=target: target, device)
            slots.append(slot)
        return slots

    def arrive(slots, regions, device):
        for slot, part in zip(slots, regions):
            wire.arrive(slot, lambda: part, device)

    def block(index):
        return hid_all.at[pl.ds(index * rows, rows)]

    x_slots, y_slots, c_slots = {}, {}, {}
    for which, other in ((0, 1), (1, 0)):
        x_slots[which] = send(to_x, own(which), region(d, which))
        y_slots[other] = send(to_y, own(other), region(d, other))
    c_slots[1] = send(to_c, own(None), region(d, None))
    passed = {}
    loads, copies = [], []
    for place, weight in enumerate((gate, up, down)):
        loads.append(local.start(weight, stage.at[place]))

    def store_pieces():
        for load in loads:
            load.wait()
        for bits in range(8):
            first = 2 * flip(d, bits)
            for place in range(3):
                copies.append(
                    local.start(stage.at[place, pl.ds(first, 2)], pieces[bits].at[place])
                )

    copies.append(local.start(hid, block(t)))
    for source, target in zip(own(None), region(d, None)):
        copies.append(local.start(source, target))
    line = LineGather(wire, d, t, extent, lambda: hid, block)
    store_pieces()
    arrive(x_slots[0], region(dx, 0), to_x)
    passed["y"] = send(to_y, region(dx, 0), region(dx, 0))
    arrive(y_slots[1], region(dy, 1), to_y)
    passed["x"] = send(to_x, region(dy, 1), region(dy, 1))
    line.step(1)
    arrive(x_slots[1], region(dx, 1), to_x)
    c_slots[3] = send(to_c, region(dx, None), region(dx, None))
    arrive(y_slots[0], region(dy, 0), to_y)
    c_slots[5] = send(to_c, region(dy, None), region(dy, None))
    for step in range(2, extent):
        line.step(step)
    gain_slots = {}
    for bits in range(1, 8):
        gain_slots[bits] = wire.slot()
        wire.start(
            gain_slots[bits],
            lambda: gains,
            lambda bits=bits: gains_all.at[bits],
            (flip(d, bits), t),
        )
    copies.append(local.start(gains, gains_all.at[0]))
    arrive(passed["y"], region(dxy, 0), to_y)
    arrive(passed["x"], region(dxy, 1), to_x)
    c_slots[7] = send(to_c, region(dxy, None), region(dxy, None))
    for bits in (1, 3, 5, 7):
        arrive(c_slots[bits], region(flip(d, bits), None), to_c)
    for bits in range(1, 8):
        wire.arrive(
            gain_slots[bits], lambda bits=bits: gains_all.at[bits], (flip(d, bits), t)
        )
    for copy in copies:
        copy.wait()
    wire.finish()


def fetch(extent, hid, qkv, o, gains, gate, up, down):
    rows, model_width = hid.shape
    piece = jax.ShapeDtypeStruct((3, 2) + gate.shape[1:], BF)
    return pl.pallas_call(
        functools.partial(fetch_kernel, extent),
        out_shape=[
            jax.ShapeDtypeStruct((rows * extent, model_width), BF),
            jax.ShapeDtypeStruct((8 * qkv.shape[0], qkv.shape[1]), BF),
            jax.ShapeDtypeStruct((o.shape[0], 8 * o.shape[1]), BF),
            jax.ShapeDtypeStruct((8,) + gains.shape, F32),
        ]
        + [piece] * 8,
        in_specs=[VM] * 4 + [ANY] * 3,
        out_specs=[ANY] * 12,
        scratch_shapes=[pltpu.VMEM((3,) + gate.shape, BF)]
        + dma_pair(64) + [pltpu.SemaphoreType.DMA((40,))],
        compiler_params=kernel_params(1),
        cost_estimate=pl.CostEstimate(flops=0, bytes_accessed=100_000_000, transcendentals=0),
    )(hid, qkv, o, gains, gate, up, down)


class Pieces:
    def __init__(self, d, in_weight, out_weight, sem, pieces):
        self.copies = {}
        slab = out_weight.shape[0] // 2
        for bits, piece in enumerate(pieces):
            start = pl.multiple_of(flip(d, bits) * slab, slab)
            pairs = []
            for place in range(3):
                for e in range(2):
                    if place < 2:
                        column = (2 * place + e) * slab
                        whole = in_weight.at[pl.ds(start, slab), pl.ds(column, slab)]
                    else:
                        whole = out_weight.at[pl.ds(e * slab, slab), pl.ds(start, slab)]
                    pairs.append((piece.at[place, e], whole, sem.at[bits * 6 + place * 2 + e]))
            self.copies[bits] = pairs

    def load(self, bits):
        for piece, whole, sem in self.copies[bits]:
            pltpu.make_async_copy(piece, whole, sem).start()

    def loaded(self, bits):
        for piece, whole, sem in self.copies[bits]:
            pltpu.make_async_copy(piece, whole, sem).wait()

    def store(self, bits):
        for piece, whole, sem in self.copies[bits]:
            pltpu.make_async_copy(whole, piece, sem).start()

    def stored(self, bits):
        for piece, whole, sem in self.copies[bits]:
            pltpu.make_async_copy(whole, piece, sem).wait()


def coefficients(columns, d, slab):
    values = columns.astype(F32)
    lane = lax.broadcasted_iota(jnp.int32, values.shape, 1)
    parts = []
    for e in range(2):
        wanted = jnp.logical_or(lane == 2 * d + e, lane == 16 + 2 * d + e)
        one = jnp.sum(jnp.where(wanted, values, 0.0), axis=-1, keepdims=True)
        parts.append(jnp.broadcast_to(one, (values.shape[0], slab)))
    return jnp.concatenate(parts, axis=1)


def enter_kernel(extent, partial, hid, gain, router, chosen, *rest):
    near, corner = rest[:6], rest[6:8]
    middle, gates, ffn_own, tokens, hidden, out = rest[8:14]
    landed = rest[14:16]
    (
        gathered,
        work,
        up_in,
        down_in,
        in_weight,
        out_weight,
        hidden_stage,
        out_stage,
        send_sem,
        recv_sem,
        local_sem,
        weight_sem,
        stage_sem,
        token_sem,
    ) = rest[16:]
    d, t = lax.axis_index("dp"), lax.axis_index("tensor")
    rows, width = hid.shape
    greet(line_devices(d, t, extent) + [(None, (flip(d, bits), t)) for bits in (1, 2, 4, 6, 7)])
    wire, local = Wire(send_sem, recv_sem), Local(local_sem)
    corner_slots = []
    for n in range(2):
        slot = wire.slot()
        corner_slots.append(slot)
        wire.start(slot, lambda n=n: corner[n], lambda n=n: landed[n], (flip(d, 6 + n), t))
    work_load = local.start(partial, work)
    weights = Pieces(d, in_weight, out_weight, weight_sem, list(near) + list(landed))
    for bits in range(6):
        weights.load(bits)
    work_load.wait()
    line = LineSum(
        wire, d, t, extent, lambda index: work.at[index], up_in, down_in, rows, 2
    )
    for step in range(extent - 1):
        line.step(step)
    line.last()
    mine = work.at[t]
    everything = pl.ds(0, width)
    packet = gathered.at[t, 0, 0]

    def body(start):
        part = pl.ds(start, 16)
        value = hid[part].astype(F32) + own_sum(
            mine, up_in.at[extent - 2], down_in.at[extent - 2], part, everything
        )
        middle[part] = value
        unit = value * lax.rsqrt(jnp.mean(value * value, axis=-1, keepdims=True) + EPSILON)
        ffn_own[part] = (unit * gain[...]).astype(BF)

    rows_loop(rows, 16, body)
    logits = jnp.dot(ffn_own[...], router[...], preferred_element_type=F32)
    lane = lax.broadcasted_iota(jnp.int32, logits.shape, 1)
    top = jnp.max(jnp.where(lane < 16, logits, -1e30), axis=-1, keepdims=True)
    powers = jnp.where(lane < 32, jnp.exp(logits - top), 0.0)
    probs = powers / jnp.sum(jnp.where(lane < 16, powers, 0.0), axis=-1, keepdims=True)
    gates[...] = probs
    coeff = probs * chosen[...]
    high = coeff.astype(BF).astype(F32)
    packet[:, 0:width] = ffn_own[...]
    packet[:, width : width + 128] = jnp.where(lane < 16, high, coeff - high).astype(BF)

    def place(j, c, i):
        return gathered.at[j, c, i]

    def bundle(j, c):
        return gathered.at[j, c, pl.ds(0, 4), pl.ds(rows - LATE, LATE)]

    gather = PlaneGather(wire, d, t, extent, lambda: packet, place, bundle, rows)
    for n in range(2):
        wire.arrive(corner_slots[n], lambda: landed[n], (flip(d, 6 + n), t))
        weights.load(6 + n)
    for bits in range(8):
        weights.loaded(bits)
    gather.bundle_start()
    units = out_weight.shape[0]

    def stage_copies(slot, j, c):
        return (
            pltpu.make_async_copy(hidden_stage.at[slot], hidden.at[j, c], stage_sem.at[0, slot]),
            pltpu.make_async_copy(out_stage.at[slot], out.at[j, c], stage_sem.at[1, slot]),
        )

    actions = gather.actions()

    def group(g, carry):
        for number, steps in enumerate(actions):

            @pl.when(g == number)
            def _():
                for action, argument in steps:
                    action(argument)

        j, c, slot = arrival(t, g // 2), g % 2, g % 2

        @pl.when(g >= 2)
        def _():
            for copy in stage_copies(slot, j, c):
                copy.wait()

        pltpu.make_async_copy(gathered.at[j, c], tokens.at[j, c], token_sem.at[g]).start()

        def some(first, carry):
            blocks, part = pl.ds(2 * first, 2), pl.ds(first * 2 * rows, 2 * rows)
            values = jnp.dot(
                gathered[j, c, blocks, :, 0:width].reshape(2 * rows, width),
                in_weight[...],
                preferred_element_type=F32,
            )
            hidden_stage[slot, part] = values.astype(BF)
            gate_value, up_value = values[:, :units], values[:, units:]
            coeff = coefficients(
                gathered[j, c, blocks, :, width : width + 128].reshape(2 * rows, 128),
                d,
                units // 2,
            )
            active = (coeff * (gate_value * jax.nn.sigmoid(gate_value)) * up_value).astype(BF)
            result = jnp.dot(active, out_weight[...], preferred_element_type=F32)
            out_stage[slot, blocks] = result.astype(BF).reshape(2, rows, width)
            return carry

        lax.fori_loop(0, 2, some, 0)
        for copy in stage_copies(slot, j, c):
            copy.start()
        return carry

    lax.fori_loop(0, 2 * extent, group, 0)
    for slot in range(2):
        for copy in stage_copies(slot, 0, slot):
            copy.wait()
    for g in range(2 * extent):
        pltpu.make_async_copy(
            gathered.at[arrival(t, g // 2), g % 2],
            tokens.at[arrival(t, g // 2), g % 2],
            token_sem.at[g],
        ).wait()
    wire.finish()


def enter(extent, partial, hid, gain, router, chosen, near, corner):
    rows, width = hid.shape
    slab = near[0].shape[2]
    piece = jax.ShapeDtypeStruct(near[0].shape, BF)
    return pl.pallas_call(
        functools.partial(enter_kernel, extent),
        out_shape=[
            jax.ShapeDtypeStruct((rows, width), F32),
            jax.ShapeDtypeStruct((rows, 128), F32),
            jax.ShapeDtypeStruct((rows, width), BF),
            jax.ShapeDtypeStruct((extent, 2, 4, rows, width + 128), BF),
            jax.ShapeDtypeStruct((extent, 2, 4 * rows, 4 * slab), BF),
            jax.ShapeDtypeStruct((extent, 2, 4, rows, width), BF),
            piece,
            piece,
        ],
        in_specs=[ANY, VM, VM, VM, VM] + [ANY] * 8,
        out_specs=[VM, VM, VM] + [ANY] * 5,
        scratch_shapes=[
            pltpu.VMEM((extent, 2, 4, rows, width + 128), BF),
            pltpu.VMEM((extent, rows, width), BF),
            pltpu.VMEM((extent - 1, rows, width), BF),
            pltpu.VMEM((extent - 1, rows, width), BF),
            pltpu.VMEM((width, 4 * slab), BF),
            pltpu.VMEM((2 * slab, width), BF),
            pltpu.VMEM((2, 4 * rows, 4 * slab), BF),
            pltpu.VMEM((2, 4, rows, width), BF),
        ]
        + dma_pair(100)
        + [
            pltpu.SemaphoreType.DMA((2,)),
            pltpu.SemaphoreType.DMA((48,)),
            pltpu.SemaphoreType.DMA((2, 2)),
            pltpu.SemaphoreType.DMA((2 * extent,)),
        ],
        compiler_params=kernel_params(3),
        cost_estimate=pl.CostEstimate(flops=0, bytes_accessed=300_000_000, transcendentals=0),
    )(partial, hid, gain, router, chosen, *near, *corner)


def transposed_dot(left, right):
    return lax.dot_general(left, right, (((0,), (0,)), ((), ())), preferred_element_type=F32)


def dot_transposed(left, right):
    return lax.dot_general(left, right, (((1,), (1,)), ((), ())), preferred_element_type=F32)


def turn_kernel(extent, partial, middle, teacher, weight, tokens, hidden, *rest):
    pieces = rest[:8]
    grad_output, row_loss, out, inner_out, active_out, grads = rest[8:14]
    buffers = rest[14:24]
    (
        packet,
        in_weight,
        out_weight,
        coeff_tile,
        hidden_tile,
        grad_tile,
        out_stage,
        active_tile,
        inner_tile,
        send_sem,
        recv_sem,
        local_sem,
        weight_sem,
        tile_sem,
    ) = rest[24:]
    d, t = lax.axis_index("dp"), lax.axis_index("tensor")
    rows, width = middle.shape
    greet(plane_devices(d, t, extent))
    wire, local = Wire(send_sem, recv_sem), Local(local_sem)
    weights = Pieces(d, in_weight, out_weight, weight_sem, pieces)

    def between(turn_number):
        if turn_number == 1:
            for bits in range(8):
                weights.load(bits)

    sum_plane(wire, local, d, t, extent, partial, buffers, rows, between)

    def body(part, value):
        output = middle[part] + value
        mismatch = output - teacher[part].astype(F32)
        scaled = mismatch * weight[part, 0:1]
        grad_output[part] = scaled
        packet[part] = scaled.astype(BF)
        row_loss[part] = jnp.broadcast_to(
            jnp.sum(scaled * mismatch, axis=-1, keepdims=True), (16, 128)
        )

    own_rows(buffers, rows, pl.ds(0, width), body)

    def place(j, c, i):
        return grads.at[j, c, i]

    def bundle(j, c):
        return grads.at[j, c, pl.ds(0, 4), pl.ds(rows - LATE, LATE)]

    own_copy = local.start(packet, place(t, 0, 0))
    gather = PlaneGather(wire, d, t, extent, lambda: packet, place, bundle, rows)
    own_copy.wait()
    gather.bundle_start()
    for bits in range(8):
        weights.loaded(bits)
    units, slab = out_weight.shape[0], out_weight.shape[0] // 2
    actions = gather.actions()

    def out_copies(j, c):
        return (
            pltpu.make_async_copy(out_stage, out.at[j, c], tile_sem.at[3]),
            pltpu.make_async_copy(inner_tile, inner_out.at[j, c], tile_sem.at[4]),
            pltpu.make_async_copy(active_tile, active_out.at[j, c], tile_sem.at[5]),
        )

    def group(g, carry):
        j, c = arrival(t, g // 2), g % 2
        coeff_copy = pltpu.make_async_copy(
            tokens.at[j, c, pl.ds(0, 4), pl.ds(0, rows), pl.ds(width, 128)],
            coeff_tile,
            tile_sem.at[0],
        )
        hidden_copy = pltpu.make_async_copy(hidden.at[j, c], hidden_tile, tile_sem.at[1])
        grad_copy = pltpu.make_async_copy(grads.at[j, c], grad_tile, tile_sem.at[2])
        coeff_copy.start()
        hidden_copy.start()
        for number, steps in enumerate(actions):

            @pl.when(g == number)
            def _():
                for action, argument in steps:
                    action(argument)

        grad_copy.start()

        @pl.when(g >= 1)
        def _():
            for copy in out_copies(j, c):
                copy.wait()

        coeff_copy.wait()
        hidden_copy.wait()
        grad_copy.wait()

        def some(first, carry):
            size = 2 * rows
            blocks, part = pl.ds(2 * first, 2), pl.ds(first * size, size)
            grad_active = dot_transposed(
                grad_tile[blocks].reshape(size, width), out_weight[...]
            )
            gate_value = hidden_tile[part, 0:units].astype(F32)
            up_value = hidden_tile[part, units : 2 * units].astype(F32)
            coeff = coefficients(coeff_tile[blocks].reshape(size, 128), d, slab)
            sigmoid_value = jax.nn.sigmoid(gate_value)
            silu_value = gate_value * sigmoid_value
            inner = grad_active * coeff
            direct = silu_value * up_value
            active_tile[part] = (coeff * direct).astype(BF)
            product = grad_active * direct
            lane = lax.broadcasted_iota(jnp.int32, (size, 128), 1)
            sums = jnp.zeros((size, 128), F32)
            for e in range(2):
                one = jnp.sum(product[:, e * slab : (e + 1) * slab], axis=-1, keepdims=True)
                sums = sums + jnp.where(lane == 2 * d + e, one, 0.0)
            out_stage[blocks, :, width : width + 128] = sums.astype(BF).reshape(2, rows, 128)
            grad_gate = (
                inner * up_value * sigmoid_value * (1.0 + gate_value * (1.0 - sigmoid_value))
            )
            inner_tile[part, 0:units] = grad_gate.astype(BF)
            inner_tile[part, units : 2 * units] = (inner * silu_value).astype(BF)
            result = dot_transposed(inner_tile[part], in_weight[...]).astype(BF)
            out_stage[blocks, :, 0:width] = result.reshape(2, rows, width)
            return carry

        lax.fori_loop(0, 2, some, 0)
        for copy in out_copies(j, c):
            copy.start()
        return carry

    lax.fori_loop(0, 2 * extent, group, 0)
    for copy in out_copies(0, 0):
        copy.wait()
    wire.finish()


def turn(extent, partial, middle, teacher, weight, tokens, hidden, pieces):
    rows, width = middle.shape
    slab = pieces[0].shape[2]
    return pl.pallas_call(
        functools.partial(turn_kernel, extent),
        out_shape=[
            jax.ShapeDtypeStruct((rows, width), F32),
            jax.ShapeDtypeStruct((rows, 128), F32),
            jax.ShapeDtypeStruct((extent, 2, 4, rows, width + 128), BF),
            jax.ShapeDtypeStruct((extent, 2, 4 * rows, 4 * slab), BF),
            jax.ShapeDtypeStruct((extent, 2, 4 * rows, 2 * slab), BF),
            jax.ShapeDtypeStruct((extent, 2, 4, rows, width), BF),
        ],
        in_specs=[ANY, VM, VM, VM] + [ANY] * 10,
        out_specs=[VM, VM] + [ANY] * 4,
        scratch_shapes=sum_scratch(extent, rows, width)
        + [
            pltpu.VMEM((rows, width), BF),
            pltpu.VMEM((width, 4 * slab), BF),
            pltpu.VMEM((2 * slab, width), BF),
            pltpu.VMEM((4, rows, 128), BF),
            pltpu.VMEM((4 * rows, 4 * slab), BF),
            pltpu.VMEM((4, rows, width), BF),
            pltpu.VMEM((4, rows, width + 128), BF),
            pltpu.VMEM((4 * rows, 2 * slab), BF),
            pltpu.VMEM((4 * rows, 4 * slab), BF),
        ]
        + dma_pair(150)
        + [
            pltpu.SemaphoreType.DMA((20,)),
            pltpu.SemaphoreType.DMA((48,)),
            pltpu.SemaphoreType.DMA((6,)),
        ],
        compiler_params=kernel_params(4),
        cost_estimate=pl.CostEstimate(flops=0, bytes_accessed=450_000_000, transcendentals=0),
    )(partial, middle, teacher, weight, tokens, hidden, *pieces)


class WeightGrads:
    def __init__(self, sources, tiles, totals, sem):
        self.sources, self.tiles, self.sem = sources, tiles, sem
        self.in_total, self.out_total = totals

    def copies(self, g):
        j, c, slot = g // 2, g % 2, g % 2
        return [
            pltpu.make_async_copy(source.at[j, c], tile.at[slot], self.sem.at[n, slot])
            for n, (source, tile) in enumerate(zip(self.sources, self.tiles))
        ]

    def start(self, g):
        for copy in self.copies(g):
            copy.start()

    def clear(self):
        self.in_total[...] = jnp.zeros(self.in_total.shape, F32)
        self.out_total[...] = jnp.zeros(self.out_total.shape, F32)

    def work(self, g, count):
        if g + 1 < count:
            self.start(g + 1)
        for copy in self.copies(g):
            copy.wait()
        slot = g % 2
        token_tile, grad_tile, inner_tile, active_tile = (tile.at[slot] for tile in self.tiles)
        size, width = inner_tile.shape[0], grad_tile.shape[2]

        def into_in(start):
            part = pl.ds(start, 256)
            left = token_tile[:, :, part].reshape(size, 256)
            self.in_total[part] += transposed_dot(left, inner_tile[...])

        rows_loop(width, 256, into_in)

        def into_out(start):
            part = pl.ds(start, 512)
            right = grad_tile[:, :, part].reshape(size, 512)
            self.out_total[:, part] += transposed_dot(active_tile[...], right)

        rows_loop(width, 512, into_out)

    def pieces(self, d, stage):
        slab = stage.shape[3]
        for bits in range(8):
            part = pl.ds(pl.multiple_of(flip(d, bits) * slab, slab), slab)
            for place in range(3):
                for e in range(2):
                    if place < 2:
                        column = (2 * place + e) * slab
                        value = self.in_total[part, column : column + slab]
                    else:
                        value = self.out_total[e * slab : (e + 1) * slab, part]
                    stage[bits, place, e] = value.astype(BF)


def leave_kernel(extent, partial, middle, grad_output, gates, chosen, gain, router_t, *rest):
    sources = rest[:4]
    grad_middle, grad_logits, gain_part, grads = rest[4:8]
    came = rest[8:16]
    buffers = rest[16:26]
    tiles, totals = rest[26:30], rest[30:32]
    stage, packet, send_sem, recv_sem, local_sem, tile_sem = rest[32:]
    d, t = lax.axis_index("dp"), lax.axis_index("tensor")
    rows, width = middle.shape
    greet(line_devices(d, t, extent) + [(None, (flip(d, bits), t)) for bits in range(1, 6)])
    wire, local = Wire(send_sem, recv_sem), Local(local_sem)
    weight_grads = WeightGrads(sources, tiles, totals, tile_sem)
    count = 2 * extent
    weight_grads.start(0)

    def between(turn_number):
        if turn_number == 0:
            weight_grads.clear()
        if turn_number < extent:
            weight_grads.work(2 * turn_number, count)
            weight_grads.work(2 * turn_number + 1, count)

    sum_plane(wire, local, d, t, extent, partial, buffers, rows, between)
    weight_grads.pieces(d, stage)
    piece_slots = []
    for bits in range(1, 6):
        slot = wire.slot()
        piece_slots.append(slot)
        wire.start(
            slot, lambda bits=bits: stage.at[bits], lambda bits=bits: came[bits], (flip(d, bits), t)
        )
    copies = [local.start(stage.at[bits], came[bits]) for bits in (0, 6, 7)]
    coeff_grads = []

    def collect(part, value):
        grad_logits[part] = value

    own_rows(buffers, rows, pl.ds(width, 128), collect)
    coeff_grad = grad_logits[...] * chosen[...]
    lane = lax.broadcasted_iota(jnp.int32, coeff_grad.shape, 1)
    probs = jnp.where(lane < 16, gates[...], 0.0)
    coeff_grad = jnp.where(lane < 16, coeff_grad, 0.0)
    logit_grad = probs * (coeff_grad - jnp.sum(coeff_grad * probs, axis=-1, keepdims=True))
    grad_logits[...] = logit_grad
    high = logit_grad.astype(BF)
    low_part = (logit_grad - high.astype(F32)).astype(BF)
    for begin in range(0, width, 512):
        columns = slice(begin, begin + 512)
        grad_middle[:, columns] = jnp.dot(
            high, router_t[:, columns], preferred_element_type=F32
        ) + jnp.dot(low_part, router_t[:, columns], preferred_element_type=F32)
    gain_part[...] = jnp.zeros(gain_part.shape, F32)

    def body(part, value):
        grad = value + grad_middle[part]
        value = middle[part]
        inverse = lax.rsqrt(jnp.mean(value * value, axis=-1, keepdims=True) + EPSILON)
        unit = value * inverse
        product = grad * unit
        gain_part[...] += product[0:8] + product[8:16]
        scaled = grad * gain[...]
        result = grad_output[part] + inverse * (
            scaled - unit * jnp.mean(scaled * unit, axis=-1, keepdims=True)
        )
        grad_middle[part] = result
        packet[part] = result.astype(BF)

    own_rows(buffers, rows, pl.ds(0, width), body)

    def place(index):
        return grads.at[index]

    copies.append(local.start(packet, place(t)))
    line = LineGather(wire, d, t, extent, lambda: packet, place)
    for step in range(1, extent):
        line.step(step)
    for copy in copies:
        copy.wait()
    for n, slot in enumerate(piece_slots):
        wire.arrive(slot, lambda: came[1 + n], (flip(d, 1 + n), t))
    wire.finish()


def leave(extent, partial, middle, grad_output, gates, chosen, gain, router_t, sources):
    rows, width = middle.shape
    tokens, grads, inner, active = sources
    units = active.shape[3]
    piece = jax.ShapeDtypeStruct((3, 2, units // 2, units // 2), BF)
    return pl.pallas_call(
        functools.partial(leave_kernel, extent),
        out_shape=[
            jax.ShapeDtypeStruct((rows, width), F32),
            jax.ShapeDtypeStruct((rows, 128), F32),
            jax.ShapeDtypeStruct((8, width), F32),
            jax.ShapeDtypeStruct((extent, rows, width), BF),
        ]
        + [piece] * 8,
        in_specs=[ANY, VM, VM, VM, VM, VM, VM] + [ANY] * 4,
        out_specs=[VM, VM, VM] + [ANY] * 9,
        scratch_shapes=sum_scratch(extent, rows, width + 128)
        + [pltpu.VMEM((2,) + source.shape[2:], BF) for source in sources]
        + [
            pltpu.VMEM((width, 2 * units), F32),
            pltpu.VMEM((units, width), F32),
            pltpu.VMEM((8,) + piece.shape, BF),
            pltpu.VMEM((rows, width), BF),
        ]
        + dma_pair(120)
        + [pltpu.SemaphoreType.DMA((24,)), pltpu.SemaphoreType.DMA((4, 2))],
        compiler_params=kernel_params(5),
        cost_estimate=pl.CostEstimate(flops=0, bytes_accessed=350_000_000, transcendentals=0),
    )(partial, middle, grad_output, gates, chosen, gain, router_t, *sources)


def line_exchange(wire, t, d, extent, outbox, inbox):
    peers = [(d, (t + k) % extent) for k in range(1, extent)]
    slots = []
    for k, peer in enumerate(peers):
        slot = wire.slot()
        slots.append(slot)
        wire.start(slot, lambda: outbox, lambda k=k: inbox.at[k], peer)
    result = outbox[...]
    for k, peer in enumerate(peers):
        wire.arrive(slots[k], lambda k=k: inbox.at[k], peer)
        result = result + inbox[k]
    return result


def columns_to_rows(ref):
    return ref[...].T[0:8]


def rows_to_columns(value):
    return jnp.concatenate([value, jnp.zeros((120, value.shape[1]), F32)], axis=0).T


def turned(value, cosine, sine, direction):
    return value * cosine + direction * pltpu.roll(value, HD // 2, 1) * sine


def line_peers(d, t, extent):
    return [(None, (d, (t + k) % extent)) for k in range(1, extent)]


def attend_kernel(
    extent,
    length,
    hid,
    gain,
    qkv_weight,
    o_weight,
    head_gain,
    cosine,
    sine,
    normed,
    units,
    low,
    probs,
    mixed,
    out,
    inverses,
    raw,
    sums,
    outbox,
    inbox,
    send_sem,
    recv_sem,
):
    d, t = lax.axis_index("dp"), lax.axis_index("tensor")
    seq_len, width = hid.shape
    heads = head_gain.shape[0] // 2
    columns = heads * HD
    greet(line_peers(d, t, extent))
    wire = Wire(send_sem, recv_sem)
    tile = 256

    def project(start):
        part = pl.ds(start, tile)
        value = hid[part].astype(F32)
        unit = value * lax.rsqrt(jnp.mean(value * value, axis=-1, keepdims=True) + EPSILON)
        normed[part] = (unit * gain[...]).astype(BF)
        result = jnp.dot(normed[part], qkv_weight[...], preferred_element_type=F32)
        raw[part] = result
        lane = lax.broadcasted_iota(jnp.int32, (tile, 128), 1)
        squares = [
            jnp.sum(jnp.square(result[:, n * columns : (n + 1) * columns]), axis=-1, keepdims=True)
            for n in range(2)
        ]
        sums[part] = jnp.where(lane == 0, squares[0], jnp.where(lane == 1, squares[1], 0.0))

    rows_loop(seq_len, tile, project)
    outbox[...] = columns_to_rows(sums)
    total = line_exchange(wire, t, d, extent, outbox, inbox)
    inverses[...] = rows_to_columns(lax.rsqrt(total / width + EPSILON))
    low[:, 2 * columns :] = raw[:, 2 * columns :].astype(BF)

    def head(h, carry):
        for n in range(2):
            section = pl.ds(pl.multiple_of(n * columns + h * HD, HD), HD)
            unit = raw[:, section] * inverses[:, n : n + 1]
            units[:, section] = unit
            scaled = unit * head_gain[pl.ds(n * heads + h, 1)]
            low[:, section] = turned(scaled, cosine[...], sine[...], 1.0).astype(BF)
        section = pl.ds(pl.multiple_of(h * HD, HD), HD)
        key_section = pl.ds(pl.multiple_of(columns + h * HD, HD), HD)
        value_section = pl.ds(pl.multiple_of(2 * columns + h * HD, HD), HD)

        def some(start):
            part = pl.ds(start, tile)
            scores = dot_transposed(low[part, section], low[:, key_section]) / math.sqrt(HD)
            row = start + lax.broadcasted_iota(jnp.int32, scores.shape, 0)
            column = lax.broadcasted_iota(jnp.int32, scores.shape, 1)
            allowed = both(column <= row, column < length[0])
            scores = jnp.where(allowed, scores, -1e30)
            powers = jnp.exp(scores - jnp.max(scores, axis=-1, keepdims=True))
            result = powers / jnp.sum(powers, axis=-1, keepdims=True)
            probs[h, part] = result
            mixed[part, section] = jnp.dot(
                result.astype(BF), low[:, value_section], preferred_element_type=F32
            ).astype(BF)

        rows_loop(seq_len, tile, some)
        return carry

    lax.fori_loop(0, heads, head, 0)

    def finish(start):
        part = pl.ds(start, tile)
        out[part] = jnp.dot(mixed[part], o_weight[...], preferred_element_type=F32).astype(BF)

    rows_loop(seq_len, tile, finish)
    wire.finish()


SMEM = pl.BlockSpec(memory_space=pltpu.SMEM)


def attend(extent, length, hid, gain, qkv_weight, o_weight, head_gain, cosine, sine):
    seq_len, width = hid.shape
    heads = head_gain.shape[0] // 2
    columns = heads * HD
    return pl.pallas_call(
        functools.partial(attend_kernel, extent),
        out_shape=[
            jax.ShapeDtypeStruct((seq_len, width), BF),
            jax.ShapeDtypeStruct((seq_len, 2 * columns), F32),
            jax.ShapeDtypeStruct((seq_len, 3 * columns), BF),
            jax.ShapeDtypeStruct((heads, seq_len, seq_len), F32),
            jax.ShapeDtypeStruct((seq_len, columns), BF),
            jax.ShapeDtypeStruct((seq_len, width), BF),
            jax.ShapeDtypeStruct((seq_len, 128), F32),
        ],
        in_specs=[SMEM] + [VM] * 7,
        out_specs=[VM] * 7,
        scratch_shapes=[
            pltpu.VMEM((seq_len, 3 * columns), F32),
            pltpu.VMEM((seq_len, 128), F32),
            pltpu.VMEM((8, seq_len), F32),
            pltpu.VMEM((extent - 1, 8, seq_len), F32),
        ]
        + dma_pair(extent - 1),
        compiler_params=kernel_params(2),
        cost_estimate=pl.CostEstimate(flops=0, bytes_accessed=60_000_000, transcendentals=0),
    )(length, hid, gain, qkv_weight, o_weight, head_gain, cosine, sine)


def attend_back_kernel(
    extent,
    grads,
    row_loss,
    hid,
    gain,
    qkv_weight,
    o_weight,
    head_gain,
    cosine,
    sine,
    normed,
    units,
    low,
    probs,
    mixed,
    inverses,
    out,
    grad_qkv,
    grad_o,
    attn_gain_part,
    head_gain_part,
    loss,
    grad_mixed,
    scaled,
    raw_grad,
    sums,
    dots,
    outbox,
    inbox,
    send_sem,
    recv_sem,
):
    d, t = lax.axis_index("dp"), lax.axis_index("tensor")
    seq_len, width = hid.shape
    heads = head_gain.shape[0] // 2
    columns = heads * HD
    greet(line_peers(d, t, extent))
    wire = Wire(send_sem, recv_sem)
    tile = 256
    root = math.sqrt(HD)

    def mix(start):
        part = pl.ds(start, tile)
        grad_mixed[part] = dot_transposed(grads[part], o_weight[...]).astype(BF)

    rows_loop(seq_len, tile, mix)

    def into_o(start):
        part = pl.ds(start, 512)
        grad_o[:, part] = transposed_dot(mixed[...], grads[:, part]).astype(BF)

    rows_loop(width, 512, into_o)
    sums[...] = jnp.zeros(sums.shape, F32)

    def head(h, carry):
        section = pl.ds(pl.multiple_of(h * HD, HD), HD)
        key_section = pl.ds(pl.multiple_of(columns + h * HD, HD), HD)
        value_section = pl.ds(pl.multiple_of(2 * columns + h * HD, HD), HD)
        chance = probs[h]
        incoming = grad_mixed[:, section]
        raw_grad[:, value_section] = transposed_dot(chance.astype(BF), incoming).astype(BF)
        grad_probs = dot_transposed(incoming, low[:, value_section])
        grad_scores = (
            chance * (grad_probs - jnp.sum(grad_probs * chance, axis=-1, keepdims=True))
        ).astype(BF)
        pair = (
            jnp.dot(grad_scores, low[:, key_section], preferred_element_type=F32) / root,
            transposed_dot(grad_scores, low[:, section]) / root,
        )
        lane = lax.broadcasted_iota(jnp.int32, (seq_len, 128), 1)
        for n, where in enumerate((section, key_section)):
            value = turned(pair[n], cosine[...], sine[...], -1.0)
            unit = units[:, where]
            head_gain_part[pl.ds(n * heads + h, 1)] = jnp.sum(value * unit, axis=0, keepdims=True)
            value = value * head_gain[pl.ds(n * heads + h, 1)]
            scaled[:, where] = value
            sums[...] += jnp.where(lane == n, jnp.sum(value * unit, axis=-1, keepdims=True), 0.0)
        return carry

    lax.fori_loop(0, heads, head, 0)
    outbox[...] = columns_to_rows(sums)
    outbox[2:3] = jnp.broadcast_to(jnp.sum(row_loss[:, 0:1], axis=0, keepdims=True), (1, seq_len))
    total = line_exchange(wire, t, d, extent, outbox, inbox)
    loss[...] = total[:, 0:128]
    dots[...] = rows_to_columns(total / width)

    def head_again(h, carry):
        for n in range(2):
            section = pl.ds(pl.multiple_of(n * columns + h * HD, HD), HD)
            raw_grad[:, section] = (
                inverses[:, n : n + 1]
                * (scaled[:, section] - units[:, section] * dots[:, n : n + 1])
            ).astype(BF)
        return carry

    lax.fori_loop(0, heads, head_again, 0)
    attn_gain_part[...] = jnp.zeros(attn_gain_part.shape, F32)

    def finish(start):
        part = pl.ds(start, tile)
        grad = dot_transposed(raw_grad[part], qkv_weight[...])
        value = hid[part].astype(F32)
        inverse = lax.rsqrt(jnp.mean(value * value, axis=-1, keepdims=True) + EPSILON)
        unit = value * inverse
        attn_gain_part[...] += jnp.sum((grad * unit).reshape(tile // 8, 8, width), axis=0)
        change = grad * gain[...]
        out[part] = (
            inverse * (change - unit * jnp.mean(change * unit, axis=-1, keepdims=True))
        ).astype(BF)

    rows_loop(seq_len, tile, finish)

    def into_qkv(start):
        part = pl.ds(start, 256)
        grad_qkv[part] = transposed_dot(normed[:, part], raw_grad[...]).astype(BF)

    rows_loop(width, 256, into_qkv)
    wire.finish()


def attend_back(extent, *operands):
    seq_len, width = operands[0].shape
    head_gain = operands[6]
    heads = head_gain.shape[0] // 2
    columns = heads * HD
    return pl.pallas_call(
        functools.partial(attend_back_kernel, extent),
        out_shape=[
            jax.ShapeDtypeStruct((seq_len, width), BF),
            jax.ShapeDtypeStruct((width, 3 * columns), BF),
            jax.ShapeDtypeStruct((columns, width), BF),
            jax.ShapeDtypeStruct((8, width), F32),
            jax.ShapeDtypeStruct((2 * heads, HD), F32),
            jax.ShapeDtypeStruct((8, 128), F32),
        ],
        in_specs=[VM] * len(operands),
        out_specs=[VM] * 6,
        scratch_shapes=[
            pltpu.VMEM((seq_len, columns), BF),
            pltpu.VMEM((seq_len, 2 * columns), F32),
            pltpu.VMEM((seq_len, 3 * columns), BF),
            pltpu.VMEM((seq_len, 128), F32),
            pltpu.VMEM((seq_len, 128), F32),
            pltpu.VMEM((8, seq_len), F32),
            pltpu.VMEM((extent - 1, 8, seq_len), F32),
        ]
        + dma_pair(extent - 1),
        compiler_params=kernel_params(6),
        cost_estimate=pl.CostEstimate(flops=0, bytes_accessed=1_000_000, transcendentals=0),
    )(*operands)


def close_kernel(
    extent,
    partial,
    grad_middle,
    grad_qkv,
    grad_o,
    small,
    gains,
    grad_in,
    qkv_out,
    o_out,
    small_out,
    work,
    up_in,
    down_in,
    q_work,
    q_core,
    q_a,
    q_b,
    o_work,
    o_core,
    o_a,
    o_b,
    small_in,
    small_sum,
    small_last,
    send_sem,
    recv_sem,
    local_sem,
):
    d, t = lax.axis_index("dp"), lax.axis_index("tensor")
    rows, width = grad_middle.shape
    depth, o_width = qkv_out.shape[0], o_out.shape[1]
    line_peers = [(d, (t + k) % extent) for k in range(1, extent)]
    greet(
        [(None, peer) for peer in line_peers]
        + [(None, (flip(d, bits), t)) for bits in range(1, 8)]
    )
    wire, local = Wire(send_sem, recv_sem), Local(local_sem)
    to_x, to_y, to_c = (flip(d, 2), t), (flip(d, 4), t), (flip(d, 1), t)

    def slices(device):
        start = pl.multiple_of(device * o_width, o_width)
        return [
            grad_qkv.at[pl.ds(device * depth, depth)],
            grad_o.at[:, pl.ds(start, o_width)],
        ]

    turns = (3, 1, 2, 0)
    c_slots, loads = {}, {}
    work_load = local.start(partial, work)
    small_slots = []
    for k, peer in enumerate(line_peers):
        slot = wire.slot()
        small_slots.append(slot)
        wire.start(
            slot,
            lambda k=k: small.at[(t + k + 1) % extent],
            lambda k=k: small_in.at[k],
            peer,
        )
    for i in turns:
        sources = slices(flip(d, 1 + 2 * i))
        c_slots[i] = [wire.slot(), wire.slot()]
        wire.start(c_slots[i][0], lambda s=sources: s[0], lambda i=i: q_core.at[i], to_c)
        wire.start(c_slots[i][1], lambda s=sources: s[1], lambda i=i: o_core.at[i], to_c)
        mine = slices(flip(d, 2 * i))
        loads[i] = [local.start(mine[0], q_work.at[i]), local.start(mine[1], o_work.at[i])]
    work_load.wait()
    line = LineSum(
        wire, d, t, extent, lambda index: work.at[index], up_in, down_in, rows, 2
    )
    line.step(0)

    def cut(ref, which):
        half = ref.shape[0] // 2
        return ref.at[pl.ds(which * half, half)]

    a_slots, b_slots = {}, {}
    routes_a = ((to_x, 3, 2, 0, 0), (to_y, 3, 1, 1, 1), (to_x, 1, 0, 0, 2), (to_y, 2, 0, 1, 3))
    routes_b = ((to_y, 2, 0, 0), (to_x, 1, 1, 1))

    def core_add(i):
        for load in loads[i]:
            load.wait()
        wire.arrive(c_slots[i][0], lambda: q_core.at[i], to_c)
        wire.arrive(c_slots[i][1], lambda: o_core.at[i], to_c)
        add_into(q_work.at[i], q_core.at[i], q_work.shape[1])
        add_into(o_work.at[i], o_core.at[i], o_work.shape[1])

    def a_send(route):
        device, source, target, which, row = route
        a_slots[row] = [wire.slot(), wire.slot()]
        wire.start(
            a_slots[row][0], lambda: cut(q_work.at[source], which), lambda: q_a.at[row], device
        )
        wire.start(
            a_slots[row][1], lambda: cut(o_work.at[source], which), lambda: o_a.at[row], device
        )

    def b_send(route):
        device, source, which, row = route
        b_slots[row] = [wire.slot(), wire.slot()]
        wire.start(
            b_slots[row][0], lambda: cut(q_work.at[source], which), lambda: q_b.at[row], device
        )
        wire.start(
            b_slots[row][1], lambda: cut(o_work.at[source], which), lambda: o_b.at[row], device
        )

    core_add(3)
    a_send(routes_a[0])
    a_send(routes_a[1])
    core_add(1)
    a_send(routes_a[2])
    core_add(2)
    a_send(routes_a[3])
    core_add(0)
    line.step(1)
    for device, source, target, which, row in routes_a:
        wire.arrive(a_slots[row][0], lambda: q_a.at[row], device)
        wire.arrive(a_slots[row][1], lambda: o_a.at[row], device)
        add_into(cut(q_work.at[target], which), q_a.at[row], q_a.shape[1])
        add_into(cut(o_work.at[target], which), o_a.at[row], o_a.shape[1])
        if row < 2:
            b_send(routes_b[row])
    for k, peer in enumerate(line_peers):
        wire.arrive(small_slots[k], lambda k=k: small_in.at[k], peer)
    total = small[t] + small_in[0]
    for k in range(1, extent - 1):
        total = total + small_in[k]
    small_sum[:, 0:16] = total
    small_sum[:, 16:24] = jnp.broadcast_to(gains[...][None], (8, 8, 128))
    last_slots = {}
    for bits in range(1, 8):
        last_slots[bits] = wire.slot()
        wire.start(
            last_slots[bits],
            lambda bits=bits: small_sum.at[flip(d, bits)],
            lambda bits=bits: small_last.at[bits],
            (flip(d, bits), t),
        )
    line.step(2)
    for device, source, which, row in routes_b:
        wire.arrive(b_slots[row][0], lambda: q_b.at[row], device)
        wire.arrive(b_slots[row][1], lambda: o_b.at[row], device)
        for kept, came, result in (
            (cut(q_work.at[0], which), q_b.at[row], cut(qkv_out, which)),
            (cut(o_work.at[0], which), o_b.at[row], cut(o_out, which)),
        ):

            def body(start, kept=kept, came=came, result=result):
                part = pl.ds(start, 16)
                result[part] = kept[part].astype(F32) + came[part].astype(F32)

            rows_loop(kept.shape[0], 16, body)
    line.last()
    mine = work.at[t]

    def body(start):
        part = pl.ds(start, 16)
        grad_in[part] = grad_middle[part] + own_sum(
            mine, up_in.at[extent - 2], down_in.at[extent - 2], part, pl.ds(0, width)
        )

    rows_loop(rows, 16, body)
    total = small_sum[d]
    for bits in range(1, 8):
        wire.arrive(
            last_slots[bits], lambda bits=bits: small_last.at[bits], (flip(d, bits), t)
        )
        total = total + small_last[bits]
    small_out[...] = total
    wire.finish()


def close(extent, partial, grad_middle, grad_qkv, grad_o, small, gains):
    rows, width = grad_middle.shape
    depth, q_width = grad_qkv.shape[0] // 8, grad_qkv.shape[1]
    o_rows, o_width = grad_o.shape[0], grad_o.shape[1] // 8
    scratch = [
        pltpu.VMEM((extent, rows, width), BF),
        pltpu.VMEM((extent - 1, rows, width), BF),
        pltpu.VMEM((extent - 1, rows, width), BF),
    ]
    for tall, wide in ((depth, q_width), (o_rows, o_width)):
        scratch += [
            pltpu.VMEM((4, tall, wide), BF),
            pltpu.VMEM((4, tall, wide), BF),
            pltpu.VMEM((4, tall // 2, wide), BF),
            pltpu.VMEM((2, tall // 2, wide), BF),
        ]
    scratch += [
        pltpu.VMEM((extent - 1, 8, 16, 128), F32),
        pltpu.VMEM((8, 24, 128), F32),
        pltpu.VMEM((8, 24, 128), F32),
    ]
    return pl.pallas_call(
        functools.partial(close_kernel, extent),
        out_shape=[
            jax.ShapeDtypeStruct((rows, width), F32),
            jax.ShapeDtypeStruct((depth, q_width), F32),
            jax.ShapeDtypeStruct((o_rows, o_width), F32),
            jax.ShapeDtypeStruct((24, 128), F32),
        ],
        in_specs=[ANY, VM, ANY, ANY, VM, VM],
        out_specs=[VM] * 4,
        scratch_shapes=scratch + dma_pair(64) + [pltpu.SemaphoreType.DMA((16,))],
        compiler_params=kernel_params(7),
        cost_estimate=pl.CostEstimate(flops=0, bytes_accessed=150_000_000, transcendentals=0),
    )(partial, grad_middle, grad_qkv, grad_o, small, gains)


def spread_kernel(*refs):
    pieces, outs = refs[:8], refs[8:]
    d = lax.axis_index("dp")
    for bits in range(8):
        first = 2 * flip(d, bits)
        for place in range(3):
            for e in range(2):
                outs[place][first + e] = pieces[bits][place, e].astype(F32)


def spread(pieces):
    shape = (16,) + pieces[0].shape[2:]
    return pl.pallas_call(
        spread_kernel,
        out_shape=[jax.ShapeDtypeStruct(shape, F32)] * 3,
        in_specs=[VM] * 8,
        out_specs=[VM] * 3,
        compiler_params=pltpu.CompilerParams(vmem_limit_bytes=VMEM_LIMIT),
        cost_estimate=pl.CostEstimate(flops=0, bytes_accessed=20_000_000, transcendentals=0),
    )(*pieces)


def exchange(value, bits):
    if bits == 0:
        return value
    return lax.ppermute(value, "dp", [(i, i ^ bits) for i in range(8)])


def per_device_block(
    hidden_in,
    teacher,
    lengths,
    routes,
    attn_norm_gain,
    ffn_norm_gain,
    q_weight,
    k_weight,
    v_weight,
    q_gain,
    k_gain,
    o_weight,
    router_weight,
    gate_weight,
    up_weight,
    down_weight,
):
    dp_count = lax.axis_size("dp")
    extent = lax.axis_size("tensor")
    d = lax.axis_index("dp")
    t = lax.axis_index("tensor")
    rows, width = hidden_in.shape
    seq_len = rows * extent
    all_tokens = seq_len * dp_count
    length = lengths[d]
    total_count = jnp.sum(lengths).astype(F32)
    attn_gain = attn_norm_gain.astype(F32)
    ffn_gain = ffn_norm_gain.astype(F32)[None, :]
    expert_count = router_weight.shape[1]
    head_width = q_gain.shape[1]
    local_heads = q_gain.shape[0]
    columns = local_heads * HD

    qkv_own = jnp.concatenate([q_weight, k_weight, v_weight], axis=1)
    gains_own = lax.dynamic_update_slice(
        jnp.zeros((2 * local_heads, HD), F32),
        jnp.concatenate([q_gain, k_gain], axis=0).astype(F32),
        (0, d * head_width),
    )
    hidden_bf, qkv_full, o_full, gains_all, *sent = fetch(
        extent, hidden_in, qkv_own, o_weight, gains_own, gate_weight, up_weight, down_weight
    )
    pieces = [exchange(piece, bits) for bits, piece in enumerate(sent[:6])]
    head_gain = jnp.sum(gains_all, axis=0)
    positions = jnp.arange(seq_len)
    frequency = THETA ** (-jnp.arange(HD // 2).astype(F32) / (HD // 2))
    angles = positions.astype(F32)[:, None] * frequency[None, :]
    cosine = jnp.concatenate([jnp.cos(angles)] * 2, axis=1)
    sine = jnp.concatenate([-jnp.sin(angles), jnp.sin(angles)], axis=1)
    attn_operands = (hidden_bf, attn_gain[None, :], qkv_full, o_full, head_gain, cosine, sine)
    normed, units, low, probs, mixed, attn_partial, inverses = attend(
        extent, length[None], *attn_operands
    )

    lane = jnp.arange(128)
    lane_expert = jnp.where(lane < 2 * expert_count, lane % expert_count, -1)
    routes_own = lax.dynamic_slice_in_dim(routes, t * rows, rows, 0)
    chosen = jnp.any(routes_own[:, :, None] == lane_expert[None, None, :], axis=1).astype(F32)
    blank = jnp.zeros((width, 128 - 2 * expert_count), BF)
    router_wide = jnp.concatenate([router_weight, router_weight, blank], axis=1)
    router_t = jnp.concatenate(
        [router_weight.T, jnp.zeros((128 - expert_count, width), BF)], axis=0
    )
    middle, gates, ffn_own, tokens, hidden, expert_partial, *last_pieces = enter(
        extent,
        attn_partial.reshape(extent, rows, width),
        hidden_in,
        ffn_gain,
        router_wide,
        chosen,
        pieces,
        sent[6:],
    )
    pieces = pieces + last_pieces
    own_positions = t * rows + jnp.arange(rows)
    row_scale = jnp.where(own_positions < length, all_tokens / total_count, 0.0)
    grad_output, row_loss, ffn_grad_partial, inner, active, grads = turn(
        extent,
        expert_partial,
        middle,
        teacher,
        jnp.broadcast_to(row_scale[:, None], (rows, 128)),
        tokens,
        hidden,
        pieces,
    )
    grad_middle, grad_logits, ffn_gain_part, attn_grad_rows, *came = leave(
        extent,
        ffn_grad_partial,
        middle,
        grad_output,
        gates,
        chosen,
        ffn_gain,
        router_t,
        (tokens, grads, inner, active),
    )
    expert_grads = came[:6] + [exchange(came[bits], bits) for bits in (6, 7)]
    attn_grad_rows = attn_grad_rows.reshape(seq_len, width)
    router_part = jnp.einsum(
        "sd,se->de",
        ffn_own,
        grad_logits[:, :expert_count],
        precision=HIGHEST,
        preferred_element_type=F32,
    )
    input_part, grad_qkv, grad_o, attn_gain_part, gains_part, loss_rows = attend_back(
        extent,
        attn_grad_rows,
        row_loss,
        *attn_operands,
        normed,
        units,
        low,
        probs,
        mixed,
        inverses,
    )
    loss_group = loss_rows[2, :1] / (2.0 * width * all_tokens)
    attn_gain_part = jnp.sum(attn_gain_part, axis=0)

    split = width // (dp_count * extent)
    small = jnp.concatenate(
        [
            jnp.concatenate(
                [
                    attn_gain_part.reshape(dp_count, extent, 1, split),
                    jnp.sum(ffn_gain_part, axis=0).reshape(dp_count, extent, 1, split),
                ],
                axis=3,
            ),
            router_part.reshape(dp_count, extent, split * expert_count // 128, 128),
            jnp.zeros((dp_count, extent, 15 - split * expert_count // 128, 128), F32),
        ],
        axis=2,
    ).transpose(1, 0, 2, 3)
    grad_in, qkv_out, o_out, small_out = close(
        extent,
        input_part.reshape(extent, rows, width),
        grad_middle,
        grad_qkv,
        grad_o,
        small,
        gains_part,
    )
    grad_gate, grad_up, grad_down = spread(expert_grads)
    router_out = small_out[1 : 1 + split * expert_count // 128].reshape(split, expert_count)
    gain_out = lax.dynamic_slice(small_out, (16, d * head_width), (2 * local_heads, head_width))
    return (
        loss_group,
        grad_in,
        small_out[0, :split],
        small_out[0, split : 2 * split],
        qkv_out[:, :columns],
        qkv_out[:, columns : 2 * columns],
        qkv_out[:, 2 * columns :],
        gain_out[:local_heads],
        gain_out[local_heads:],
        o_out,
        router_out,
        grad_gate,
        grad_up,
        grad_down,
    )


def solution(mesh):
    placed = (
        P(("dp", "tensor"), None),
        P(("dp", "tensor"), None),
        P(),
        P("dp", None),
        P(),
        P(),
        P("dp", "tensor"),
        P("dp", "tensor"),
        P("dp", "tensor"),
        P("tensor", "dp"),
        P("tensor", "dp"),
        P("tensor", "dp"),
        P(),
        P(None, "dp", "tensor"),
        P(None, "dp", "tensor"),
        P(None, "tensor", "dp"),
    )
    block = mesh.shape["dp"] == 8 and mesh.shape["tensor"] == 4
    return jax.shard_map(
        per_device_block if block else per_device,
        mesh=mesh,
        in_specs=placed,
        out_specs=(
            P("dp"),
            P(("dp", "tensor"), None),
            P(("dp", "tensor")),
            P(("dp", "tensor")),
            P("dp", "tensor"),
            P("dp", "tensor"),
            P("dp", "tensor"),
            P("tensor", "dp"),
            P("tensor", "dp"),
            P("tensor", "dp"),
            P(("dp", "tensor"), None),
            P(None, "dp", "tensor"),
            P(None, "dp", "tensor"),
            P(None, "tensor", "dp"),
        ),
        check_vma=False,
    )
```

```python
import functools
import math

import jax
import jax.numpy as jnp
import numpy as np
from jax import lax
from jax.experimental import pallas as pl
from jax.experimental.pallas import tpu as pltpu
from jax.sharding import PartitionSpec as P

HD = 128
TOK_DEV = 128
CAP = 68


EPSILON = 1e-05
THETA = 10000.0
HIGHEST = lax.Precision.HIGHEST


def inverse_rms(value):
    return lax.rsqrt(jnp.mean(value * value, axis=-1, keepdims=True) + EPSILON)


def rotate(value, cosine, sinus_table, direction):
    middle_index = value.shape[-1] // 2
    leading = value[..., :middle_index]
    trailing = value[..., middle_index:]
    return jnp.concatenate(
        [
            leading * cosine - direction * trailing * sinus_table,
            trailing * cosine + direction * leading * sinus_table,
        ],
        axis=-1,
    )


def norm_backward(grad_norm, unit_rows, inverse_rows, gain_row):
    scaled = grad_norm * gain_row
    return inverse_rows * (
        scaled - unit_rows * jnp.mean(scaled * unit_rows, axis=-1, keepdims=True)
    )


def fetch_attention(q_weight, k_weight, v_weight, o_weight, q_gain, k_gain):
    return (
        lax.all_gather(q_weight, "dp", axis=0, tiled=True),
        lax.all_gather(k_weight, "dp", axis=0, tiled=True),
        lax.all_gather(v_weight, "dp", axis=0, tiled=True),
        lax.all_gather(o_weight, "dp", axis=1, tiled=True),
        lax.all_gather(q_gain, "dp", axis=1, tiled=True),
        lax.all_gather(k_gain, "dp", axis=1, tiled=True),
    )


def fetch_experts(gate_weight, up_weight, down_weight):
    return (
        lax.all_gather(gate_weight, "dp", axis=1, tiled=True),
        lax.all_gather(up_weight, "dp", axis=1, tiled=True),
        lax.all_gather(down_weight, "dp", axis=2, tiled=True),
    )


def per_device(
    hidden_in,
    teacher,
    lengths,
    routes,
    attn_norm_gain,
    ffn_norm_gain,
    q_weight,
    k_weight,
    v_weight,
    q_gain,
    k_gain,
    o_weight,
    router_weight,
    gate_weight,
    up_weight,
    down_weight,
):
    dp_count = lax.axis_size("dp")
    tp_count = lax.axis_size("tensor")
    group_index = lax.axis_index("dp")
    member = lax.axis_index("tensor")
    row_count, model_width = hidden_in.shape
    seq_len = row_count * tp_count
    all_tokens = seq_len * dp_count
    length = lengths[group_index]
    total_count = jnp.sum(lengths).astype(jnp.float32)
    attn_gain = attn_norm_gain.astype(jnp.float32)
    ffn_gain = ffn_norm_gain.astype(jnp.float32)
    root_size = math.sqrt(HD)
    q_full, k_full, v_full, o_full, qgain_full, kgain_full = fetch_attention(
        q_weight, k_weight, v_weight, o_weight, q_gain, k_gain
    )
    local_heads = q_full.shape[1] // HD
    hidden_all = lax.all_gather(hidden_in, "tensor", axis=0, tiled=True).astype(jnp.float32)
    inverse_one = inverse_rms(hidden_all)
    unit_one = hidden_all * inverse_one
    normed = (unit_one * attn_gain).astype(jnp.bfloat16)
    query_raw = jnp.dot(normed, q_full, preferred_element_type=jnp.float32)
    key_raw = jnp.dot(normed, k_full, preferred_element_type=jnp.float32)
    value_low = jnp.dot(normed, v_full, preferred_element_type=jnp.float32).astype(jnp.bfloat16)
    query_sq, key_sq = lax.psum(
        (jnp.sum(query_raw * query_raw, axis=1), jnp.sum(key_raw * key_raw, axis=1)), "tensor"
    )
    query_inv = lax.rsqrt(query_sq / model_width + EPSILON)[:, None]
    key_inv = lax.rsqrt(key_sq / model_width + EPSILON)[:, None]
    query_unit = query_raw * query_inv
    key_unit = key_raw * key_inv
    query_gain = qgain_full.astype(jnp.float32).reshape(-1)
    key_gain = kgain_full.astype(jnp.float32).reshape(-1)
    positions = jnp.arange(seq_len)
    frequency = THETA ** (-jnp.arange(HD // 2).astype(jnp.float32) / (HD // 2))
    angles = positions.astype(jnp.float32)[:, None] * frequency[None, :]
    cosine = jnp.cos(angles)[:, None, :]
    sinus_table = jnp.sin(angles)[:, None, :]
    queries = rotate(
        (query_unit * query_gain).reshape(seq_len, local_heads, HD), cosine, sinus_table, 1.0
    ).astype(jnp.bfloat16)
    key_rows = rotate(
        (key_unit * key_gain).reshape(seq_len, local_heads, HD), cosine, sinus_table, 1.0
    ).astype(jnp.bfloat16)
    value_rows = value_low.reshape(seq_len, local_heads, HD)
    block_rows = min(512, seq_len)
    starts = jnp.arange(seq_len // block_rows) * block_rows

    def block_scores(start):
        query_block = lax.dynamic_slice_in_dim(queries, start, block_rows, 0)
        scores = (
            jnp.einsum("qhd,khd->hqk", query_block, key_rows, preferred_element_type=jnp.float32)
            / root_size
        )
        query_pos = start + jnp.arange(block_rows)
        allowed = (positions[None, :] <= query_pos[:, None]) & (positions[None, :] < length)
        return (query_block, jnp.where(allowed[None], scores, -1e30))

    def attend(start):
        unused_block, scores = block_scores(start)
        row_top = jnp.max(scores, axis=-1, keepdims=True)
        exponent = jnp.exp(scores - row_top)
        row_total = jnp.sum(exponent, axis=-1, keepdims=True)
        weights = (exponent / row_total).astype(jnp.bfloat16)
        mixed_block = jnp.einsum(
            "hqk,khd->qhd", weights, value_rows, preferred_element_type=jnp.float32
        )
        return (mixed_block.astype(jnp.bfloat16), (row_top + jnp.log(row_total))[..., 0])

    mixed_blocks, log_totals = lax.map(attend, starts)
    mixed = mixed_blocks.reshape(seq_len, local_heads * HD)
    attn_own = lax.psum_scatter(
        jnp.dot(mixed, o_full, preferred_element_type=jnp.float32).astype(jnp.bfloat16),
        "tensor",
        scatter_dimension=0,
        tiled=True,
    ).astype(jnp.float32)
    middle = hidden_in.astype(jnp.float32) + attn_own
    inverse_two = inverse_rms(middle)
    unit_two = middle * inverse_two
    ffn_own = (unit_two * ffn_gain).astype(jnp.bfloat16)
    gate_full, up_full, down_full = fetch_experts(gate_weight, up_weight, down_weight)
    ffn_all = lax.all_gather(ffn_own, "tensor", axis=0, tiled=True)
    expert_count = router_weight.shape[1]
    route_width = routes.shape[1]
    gate_probs = jax.nn.softmax(
        jnp.dot(ffn_all, router_weight, preferred_element_type=jnp.float32), axis=-1
    )
    picked = routes[:, :, None] == jnp.arange(expert_count)[None, None, :]
    route_gates = jnp.sum(jnp.where(picked, gate_probs[:, None, :], 0.0), axis=-1)
    block_count = seq_len // TOK_DEV
    per_expert = block_count * CAP
    picked_ints = picked.reshape(block_count, TOK_DEV * route_width, expert_count).astype(jnp.int32)
    slot_ranks = jnp.sum((jnp.cumsum(picked_ints, axis=1) - 1) * picked_ints, axis=-1).reshape(
        seq_len, route_width
    )
    block_ids = (positions // TOK_DEV)[:, None]
    slot_ids = (routes * per_expert + block_ids * CAP + slot_ranks).reshape(-1)
    slot_total = expert_count * per_expert
    token_ids = jnp.repeat(positions, route_width)
    group_width = 4
    turn_count = expert_count // group_width
    sources = (
        jnp.full((slot_total,), seq_len, jnp.int32)
        .at[slot_ids]
        .set(token_ids)
        .reshape(turn_count, group_width, per_expert)
    )
    slot_gates = (
        jnp.zeros((slot_total,), jnp.float32)
        .at[slot_ids]
        .set(route_gates.reshape(-1))
        .reshape(turn_count, group_width, per_expert, 1)
    )
    ffn_padded = jnp.concatenate([ffn_all, jnp.zeros((1, model_width), jnp.bfloat16)], axis=0)
    expert_running = jnp.zeros((seq_len + 1, model_width), jnp.float32)
    kept_values = []
    for turn_index in range(turn_count):
        lower = turn_index * group_width
        upper = lower + group_width
        expert_inputs = ffn_padded[sources[turn_index]]
        gate_value = jnp.einsum(
            "gpd,gdf->gpf",
            expert_inputs,
            gate_full[lower:upper],
            preferred_element_type=jnp.float32,
        )
        up_value = jnp.einsum(
            "gpd,gdf->gpf", expert_inputs, up_full[lower:upper], preferred_element_type=jnp.float32
        )
        active = (slot_gates[turn_index] * jax.nn.silu(gate_value) * up_value).astype(jnp.bfloat16)
        expert_outputs = jnp.einsum(
            "gpf,gfd->gpd", active, down_full[lower:upper], preferred_element_type=jnp.float32
        )
        expert_running = expert_running.at[sources[turn_index].reshape(-1)].add(
            expert_outputs.reshape(-1, model_width)
        )
        kept_values.append((gate_value, up_value, active))
    expert_own = lax.psum_scatter(
        expert_running[:seq_len].astype(jnp.bfloat16), "tensor", scatter_dimension=0, tiled=True
    ).astype(jnp.float32)
    output = middle + expert_own
    own_positions = member * row_count + jnp.arange(row_count)
    valid_rows = (own_positions < length)[:, None]
    mismatch = output - teacher.astype(jnp.float32)
    loss_own = jnp.sum(jnp.where(valid_rows, mismatch * mismatch, 0.0)) / (
        2.0 * model_width * total_count
    )
    grad_output = jnp.where(valid_rows, mismatch * (all_tokens / total_count), 0.0)
    grad_rows = lax.all_gather(grad_output.astype(jnp.bfloat16), "tensor", axis=0, tiled=True)
    gate_full, up_full, down_full = fetch_experts(gate_weight, up_weight, down_weight)
    grad_padded = jnp.concatenate([grad_rows, jnp.zeros((1, model_width), jnp.bfloat16)], axis=0)
    ffn_grad_running = jnp.zeros((seq_len + 1, model_width), jnp.float32)
    gate_grads = []
    up_grads = []
    down_grads = []
    slot_grads = []
    for turn_index in range(turn_count):
        gate_value, up_value, active = kept_values[turn_index]
        lower = turn_index * group_width
        upper = lower + group_width
        source_rows = sources[turn_index]
        expert_inputs = ffn_padded[source_rows]
        incoming = grad_padded[source_rows]
        grad_active = jnp.einsum(
            "gpd,gfd->gpf", incoming, down_full[lower:upper], preferred_element_type=jnp.float32
        )
        down_turn = jnp.einsum("gpf,gpd->gfd", active, incoming, preferred_element_type=jnp.float32)
        sigmoid_value = jax.nn.sigmoid(gate_value)
        silu_value = gate_value * sigmoid_value
        slot_grads.append(jnp.sum(grad_active * silu_value * up_value, axis=-1))
        grad_inner = grad_active * slot_gates[turn_index]
        grad_gate_value = (
            grad_inner * up_value * sigmoid_value * (1.0 + gate_value * (1.0 - sigmoid_value))
        ).astype(jnp.bfloat16)
        grad_up_value = (grad_inner * silu_value).astype(jnp.bfloat16)
        gate_turn = jnp.einsum(
            "gpd,gpf->gdf", expert_inputs, grad_gate_value, preferred_element_type=jnp.float32
        )
        up_turn = jnp.einsum(
            "gpd,gpf->gdf", expert_inputs, grad_up_value, preferred_element_type=jnp.float32
        )
        gate_grads.append(gate_turn)
        up_grads.append(up_turn)
        down_grads.append(down_turn)
        grad_inputs = jnp.einsum(
            "gpf,gdf->gpd",
            grad_gate_value,
            gate_full[lower:upper],
            preferred_element_type=jnp.float32,
        )
        grad_inputs = grad_inputs + jnp.einsum(
            "gpf,gdf->gpd", grad_up_value, up_full[lower:upper], preferred_element_type=jnp.float32
        )
        ffn_grad_running = ffn_grad_running.at[source_rows.reshape(-1)].add(
            grad_inputs.reshape(-1, model_width)
        )
    slot_grad_all = jnp.concatenate([entry.reshape(-1) for entry in slot_grads])
    route_grads = slot_grad_all[slot_ids].reshape(seq_len, route_width)
    grad_probs = jnp.sum(jnp.where(picked, route_grads[:, :, None], 0.0), axis=1)
    grad_logits = gate_probs * (
        grad_probs - jnp.sum(grad_probs * gate_probs, axis=-1, keepdims=True)
    )
    router_float = router_weight.astype(jnp.float32)
    ffn_grad_part = ffn_grad_running[:seq_len] + jnp.einsum(
        "se,de->sd", grad_logits, router_float, precision=HIGHEST
    )
    router_part = jnp.einsum(
        "sd,se->de", ffn_all, grad_logits, precision=HIGHEST, preferred_element_type=jnp.float32
    )
    ffn_grad_own = lax.psum_scatter(
        ffn_grad_part.astype(jnp.bfloat16), "tensor", scatter_dimension=0, tiled=True
    ).astype(jnp.float32)
    ffn_gain_part = jnp.sum(ffn_grad_own * unit_two, axis=0)
    grad_middle = grad_output + norm_backward(ffn_grad_own, unit_two, inverse_two, ffn_gain)
    attn_grad_rows = lax.all_gather(grad_middle.astype(jnp.bfloat16), "tensor", axis=0, tiled=True)
    q_full, k_full, v_full, o_full, qgain_full, kgain_full = fetch_attention(
        q_weight, k_weight, v_weight, o_weight, q_gain, k_gain
    )
    grad_o = jnp.einsum("sa,sb->ab", mixed, attn_grad_rows, preferred_element_type=jnp.float32)
    grad_mixed = (
        jnp.einsum("sb,ab->sa", attn_grad_rows, o_full, preferred_element_type=jnp.float32)
        .astype(jnp.bfloat16)
        .reshape(seq_len, local_heads, HD)
    )

    def attend_back(carry, inputs):
        key_running, value_running = carry
        start, log_total = inputs
        query_block, scores = block_scores(start)
        probs_float = jnp.exp(scores - log_total[..., None])
        probs_low = probs_float.astype(jnp.bfloat16)
        grad_block = lax.dynamic_slice_in_dim(grad_mixed, start, block_rows, 0)
        value_running = value_running + jnp.einsum(
            "hqk,qhd->khd", probs_low, grad_block, preferred_element_type=jnp.float32
        )
        grad_weights = jnp.einsum(
            "qhd,khd->hqk", grad_block, value_rows, preferred_element_type=jnp.float32
        )
        grad_scores = (
            probs_float
            * (grad_weights - jnp.sum(grad_weights * probs_float, axis=-1, keepdims=True))
        ).astype(jnp.bfloat16)
        query_grad_block = (
            jnp.einsum("hqk,khd->qhd", grad_scores, key_rows, preferred_element_type=jnp.float32)
            / root_size
        )
        key_running = (
            key_running
            + jnp.einsum(
                "hqk,qhd->khd", grad_scores, query_block, preferred_element_type=jnp.float32
            )
            / root_size
        )
        return ((key_running, value_running), query_grad_block)

    zero_heads = jnp.zeros((seq_len, local_heads, HD), jnp.float32)
    (key_grad_rot, value_grad), query_grad_blocks = lax.scan(
        attend_back, (zero_heads, zero_heads), (starts, log_totals)
    )
    query_grad = rotate(
        query_grad_blocks.reshape(seq_len, local_heads, HD), cosine, sinus_table, -1.0
    ).reshape(seq_len, local_heads * HD)
    key_grad = rotate(key_grad_rot, cosine, sinus_table, -1.0).reshape(seq_len, local_heads * HD)
    query_scaled = query_grad * query_gain
    key_scaled = key_grad * key_gain
    qgain_part = jnp.sum(query_grad * query_unit, axis=0)
    kgain_part = jnp.sum(key_grad * key_unit, axis=0)
    query_dot, key_dot, loss_group = lax.psum(
        (
            jnp.sum(query_scaled * query_unit, axis=1),
            jnp.sum(key_scaled * key_unit, axis=1),
            loss_own,
        ),
        "tensor",
    )
    query_raw_grad = (
        query_inv * (query_scaled - query_unit * (query_dot / model_width)[:, None])
    ).astype(jnp.bfloat16)
    key_raw_grad = (key_inv * (key_scaled - key_unit * (key_dot / model_width)[:, None])).astype(
        jnp.bfloat16
    )
    value_raw_grad = value_grad.reshape(seq_len, local_heads * HD).astype(jnp.bfloat16)
    grad_q = jnp.einsum("sd,sa->da", normed, query_raw_grad, preferred_element_type=jnp.float32)
    grad_k = jnp.einsum("sd,sa->da", normed, key_raw_grad, preferred_element_type=jnp.float32)
    grad_v = jnp.einsum("sd,sa->da", normed, value_raw_grad, preferred_element_type=jnp.float32)
    normed_grad = jnp.einsum(
        "sa,da->sd", query_raw_grad, q_full, preferred_element_type=jnp.float32
    )
    normed_grad = normed_grad + jnp.einsum(
        "sa,da->sd", key_raw_grad, k_full, preferred_element_type=jnp.float32
    )
    normed_grad = normed_grad + jnp.einsum(
        "sa,da->sd", value_raw_grad, v_full, preferred_element_type=jnp.float32
    )
    attn_gain_part = jnp.sum(normed_grad * unit_one, axis=0)
    input_part = norm_backward(normed_grad, unit_one, inverse_one, attn_gain)
    split_width = model_width // (dp_count * tp_count)
    input_own, attn_gain_share, ffn_gain_share, router_share = (
        lax.psum_scatter(
            input_part.astype(jnp.bfloat16), "tensor", scatter_dimension=0, tiled=True
        ).astype(jnp.float32),
        lax.psum_scatter(
            attn_gain_part.reshape(dp_count, tp_count, split_width).astype(jnp.bfloat16),
            "tensor",
            scatter_dimension=1,
            tiled=True,
        ).astype(jnp.float32),
        lax.psum_scatter(
            ffn_gain_part.reshape(dp_count, tp_count, split_width).astype(jnp.bfloat16),
            "tensor",
            scatter_dimension=1,
            tiled=True,
        ).astype(jnp.float32),
        lax.psum_scatter(
            router_part.reshape(dp_count, tp_count, split_width, expert_count).astype(jnp.bfloat16),
            "tensor",
            scatter_dimension=1,
            tiled=True,
        ).astype(jnp.float32),
    )
    grad_in = grad_middle + input_own
    (
        grad_q,
        grad_k,
        grad_v,
        grad_o,
        grad_qgain,
        grad_kgain,
        attn_gain_sum,
        ffn_gain_sum,
        router_sum,
    ) = (
        lax.psum_scatter(grad_q.astype(jnp.bfloat16), "dp", scatter_dimension=0, tiled=True).astype(
            jnp.float32
        ),
        lax.psum_scatter(grad_k.astype(jnp.bfloat16), "dp", scatter_dimension=0, tiled=True).astype(
            jnp.float32
        ),
        lax.psum_scatter(grad_v.astype(jnp.bfloat16), "dp", scatter_dimension=0, tiled=True).astype(
            jnp.float32
        ),
        lax.psum_scatter(grad_o.astype(jnp.bfloat16), "dp", scatter_dimension=1, tiled=True).astype(
            jnp.float32
        ),
        lax.psum_scatter(
            qgain_part.reshape(local_heads, HD).astype(jnp.bfloat16),
            "dp",
            scatter_dimension=1,
            tiled=True,
        ).astype(jnp.float32),
        lax.psum_scatter(
            kgain_part.reshape(local_heads, HD).astype(jnp.bfloat16),
            "dp",
            scatter_dimension=1,
            tiled=True,
        ).astype(jnp.float32),
        lax.psum_scatter(
            attn_gain_share.astype(jnp.bfloat16), "dp", scatter_dimension=0, tiled=True
        ).astype(jnp.float32),
        lax.psum_scatter(
            ffn_gain_share.astype(jnp.bfloat16), "dp", scatter_dimension=0, tiled=True
        ).astype(jnp.float32),
        lax.psum_scatter(
            router_share.astype(jnp.bfloat16), "dp", scatter_dimension=0, tiled=True
        ).astype(jnp.float32),
    )
    grad_gate, grad_up, grad_down = (
        lax.psum_scatter(
            jnp.concatenate(gate_grads, axis=0).astype(jnp.bfloat16),
            "dp",
            scatter_dimension=1,
            tiled=True,
        ).astype(jnp.float32),
        lax.psum_scatter(
            jnp.concatenate(up_grads, axis=0).astype(jnp.bfloat16),
            "dp",
            scatter_dimension=1,
            tiled=True,
        ).astype(jnp.float32),
        lax.psum_scatter(
            jnp.concatenate(down_grads, axis=0).astype(jnp.bfloat16),
            "dp",
            scatter_dimension=2,
            tiled=True,
        ).astype(jnp.float32),
    )
    return (
        loss_group.reshape(1),
        grad_in,
        attn_gain_sum.reshape(-1),
        ffn_gain_sum.reshape(-1),
        grad_q,
        grad_k,
        grad_v,
        grad_qgain,
        grad_kgain,
        grad_o,
        router_sum.reshape(-1, expert_count),
        grad_gate,
        grad_up,
        grad_down,
    )


MESH = pl.DeviceIdType.MESH
BF = jnp.bfloat16
F32 = jnp.float32
VMEM_LIMIT = 62 * 1024 * 1024
ANY = pl.BlockSpec(memory_space=pl.ANY)
VM = pl.BlockSpec(memory_space=pltpu.VMEM)


def flip(index, bits):
    for bit in (1, 2, 4):
        if bits & bit:
            index = index + bit * (1 - 2 * ((index // bit) % 2))
    return index


def both(first, second):
    return jnp.logical_and(first, second)


def under(condition, action):
    if condition is None:
        action()
    else:
        pl.when(condition)(action)


class Wire:
    def __init__(self, send_sem, recv_sem):
        self.send_sem, self.recv_sem, self.count, self.sent = send_sem, recv_sem, 0, []

    def slot(self):
        self.count += 1
        return self.count - 1

    def start(self, slot, source, target, device, condition=None):
        def make():
            return pltpu.make_async_remote_copy(
                src_ref=source(),
                dst_ref=target(),
                send_sem=self.send_sem.at[slot],
                recv_sem=self.recv_sem.at[slot],
                device_id=device,
                device_id_type=MESH,
            )

        under(condition, lambda: make().start())
        self.sent.append((condition, make))

    def arrive(self, slot, region, device, condition=None):
        copy = pltpu.make_async_remote_copy(
            src_ref=region(),
            dst_ref=region(),
            send_sem=self.send_sem.at[slot],
            recv_sem=self.recv_sem.at[slot],
            device_id=device,
            device_id_type=MESH,
        )
        under(condition, lambda: copy.wait_recv())

    def finish(self):
        for condition, make in self.sent:
            under(condition, lambda make=make: make().wait_send())
        self.sent = []


class Local:
    def __init__(self, sem):
        self.sem, self.count = sem, 0

    def start(self, source, target):
        copy = pltpu.make_async_copy(source, target, self.sem.at[self.count])
        self.count += 1
        copy.start()
        return copy


def greet(devices):
    barrier = pltpu.get_barrier_semaphore()
    for condition, device in devices:
        under(
            condition,
            lambda device=device: pl.semaphore_signal(
                barrier, inc=1, device_id=device, device_id_type=MESH
            ),
        )
    amount = sum(1 for condition, device in devices if condition is None)
    for condition, device in devices:
        if condition is not None:
            amount = amount + jnp.where(condition, 1, 0)
    pl.semaphore_wait(barrier, amount)


def line_devices(d, t, extent):
    return [(t < extent - 1, (d, t + 1)), (t > 0, (d, t - 1))]


def rows_loop(rows, step, body):
    def run(index, carry):
        body(pl.multiple_of(index * step, step))
        return carry

    lax.fori_loop(0, rows // step, run, 0)


def add_into(target, source, rows):
    def body(start):
        part = pl.ds(start, 16)
        target[part] = target[part] + source[part]

    rows_loop(rows, 16, body)


class LineGather:
    def __init__(self, wire, d, t, extent, own, place):
        self.wire, self.extent = wire, extent
        up = [wire.slot() for unused in range(extent - 1)]
        down = [wire.slot() for unused in range(extent - 1)]
        last = extent - 1
        above, below = (d, t + 1), (d, t - 1)
        self.first = (
            (up[0], own, lambda: place(t), above, t < last),
            (down[0], own, lambda: place(t), below, t > 0),
        )
        self.steps = {}
        for step in range(1, extent):
            from_below, from_above = t >= step, t <= last - step
            lower, upper = t - step, t + step
            self.steps[step] = (
                (
                    up,
                    lambda index=lower: place(index),
                    from_below,
                    both(from_below, t < last),
                    above,
                    below,
                ),
                (
                    down,
                    lambda index=upper: place(index),
                    from_above,
                    both(from_above, t > 0),
                    below,
                    above,
                ),
            )

    def begin(self):
        for slot, own, target, device, condition in self.first:
            self.wire.start(slot, own, target, device, condition)

    def step(self, step):
        for slots, region, valid, onward, to, source in self.steps[step]:
            self.wire.arrive(slots[step - 1], region, source, valid)
            if step < self.extent - 1:
                self.wire.start(slots[step], region, region, to, onward)


def arrival(t, turn):
    near = t - 1 + 2 * (1 - (t + 3) // 4)
    far = 3 * (1 - t // 2)
    choices = (t, near, 6 - t - near - far, far)
    if isinstance(turn, int):
        return choices[turn]
    result = choices[0]
    for number in range(1, 4):
        result = jnp.where(turn == number, choices[number], result)
    return result


LATE = 32


class PlaneGather:
    def __init__(self, wire, d, t, extent, own, place, bundle, rows):
        self.wire, self.place, self.bundle, self.own = wire, place, bundle, own
        self.early, self.half = rows - LATE, (rows - LATE) // 2
        self.to_x, self.to_y, self.to_c = (flip(d, 2), t), (flip(d, 4), t), (flip(d, 1), t)
        self.index = [arrival(t, turn) for turn in range(extent)]
        self.slots = {}
        late = lambda n: (self.early + n * (LATE // 2), LATE // 2)
        self.parts = {0: (0, self.half), 1: (self.half, self.half), 2: late(0), 3: late(1)}
        self.parts["early"], self.parts["late"] = (0, self.early), (self.early, LATE)
        self.send("gx", 0, self.source(0, "late"), self.spot(0, 0, 1, "late"), self.to_x)
        self.send("gy", 0, self.source(0, "late"), self.spot(0, 0, 2, "late"), self.to_y)
        here = self.index[0]
        self.line = LineGather(
            wire,
            d,
            t,
            extent,
            lambda: self.cut(own(), "early"),
            lambda j: self.cut(place(j, 0, 0), "early"),
        )
        self.late_line = LineGather(
            wire, d, t, extent, lambda: bundle(here, 0), lambda j: bundle(j, 0)
        )
        self.line.begin()
        self.stage_first(0)
        for name, i, which, onward, to, source in (
            ("gx", 1, 2, "gfy", self.to_y, self.to_x),
            ("gy", 2, 3, "gfx", self.to_x, self.to_y),
        ):
            self.wait(name, 0, self.spot(0, 0, i, "late"), source)
            self.send(onward, 0, self.spot(0, 0, i, which), self.spot(0, 0, 3, which), to)
        self.stage_second(0)

    def cut(self, ref, which):
        start, size = self.parts[which]
        return ref.at[pl.ds(start, size)]

    def send(self, name, turn, source, target, device):
        slot = self.wire.slot()
        self.slots[name, turn] = slot
        self.wire.start(slot, source, target, device)

    def wait(self, name, turn, region, device):
        self.wire.arrive(self.slots[name, turn], region, device)

    def spot(self, turn, c, i, which):
        return lambda: self.cut(self.place(self.index[turn], c, i), which)

    def source(self, turn, which):
        if turn == 0:
            return lambda: self.cut(self.own(), which)
        return self.spot(turn, 0, 0, which)

    def stage_first(self, turn):
        source, spot = self.source, self.spot
        self.send("x0", turn, source(turn, 0), spot(turn, 0, 1, 0), self.to_x)
        self.send("y1", turn, source(turn, 1), spot(turn, 0, 2, 1), self.to_y)

    def stage_second(self, turn):
        source, spot = self.source, self.spot
        self.send("x1", turn, source(turn, 1), spot(turn, 0, 1, 1), self.to_x)
        self.send("y0", turn, source(turn, 0), spot(turn, 0, 2, 0), self.to_y)
        self.send("c0", turn, source(turn, "early"), spot(turn, 1, 0, "early"), self.to_c)

    def stage(self, turn):
        self.stage_first(turn)
        self.stage_second(turn)

    def relay(self, turn):
        spot = self.spot
        self.wait("x0", turn, spot(turn, 0, 1, 0), self.to_x)
        self.send("fy", turn, spot(turn, 0, 1, 0), spot(turn, 0, 3, 0), self.to_y)
        self.wait("y1", turn, spot(turn, 0, 2, 1), self.to_y)
        self.send("fx", turn, spot(turn, 0, 2, 1), spot(turn, 0, 3, 1), self.to_x)
        self.wait("x1", turn, spot(turn, 0, 1, 1), self.to_x)
        self.send("c1", turn, spot(turn, 0, 1, "early"), spot(turn, 1, 1, "early"), self.to_c)
        self.wait("y0", turn, spot(turn, 0, 2, 0), self.to_y)
        self.send("c2", turn, spot(turn, 0, 2, "early"), spot(turn, 1, 2, "early"), self.to_c)

    def corner(self, turn):
        spot = self.spot
        self.wait("fy", turn, spot(turn, 0, 3, 0), self.to_y)
        self.wait("fx", turn, spot(turn, 0, 3, 1), self.to_x)
        self.send("c3", turn, spot(turn, 0, 3, "early"), spot(turn, 1, 3, "early"), self.to_c)

    def pass_bundle(self, turn):
        region = lambda c: (lambda: self.bundle(self.index[turn], c))
        self.send("cb", turn, region(0), region(1), self.to_c)

    def bundle_start(self, unused):
        spot = self.spot
        self.wait("gfy", 0, spot(0, 0, 3, 2), self.to_y)
        self.wait("gfx", 0, spot(0, 0, 3, 3), self.to_x)
        self.late_line.begin()
        self.pass_bundle(0)

    def bundle_step(self, step):
        self.late_line.step(step)
        self.pass_bundle(step)

    def other(self, turn):
        for i in range(4):
            self.wait("c%d" % i, turn, self.spot(turn, 1, i, "early"), self.to_c)
        self.wait("cb", turn, lambda: self.bundle(self.index[turn], 1), self.to_c)

    def actions(self):
        line, stage, relay, corner, other, late = (
            self.line.step,
            self.stage,
            self.relay,
            self.corner,
            self.other,
            self.bundle_step,
        )
        return (
            (
                (line, 1),
                (stage, 1),
                (self.bundle_start, 0),
                (relay, 0),
                (line, 2),
                (stage, 2),
                (corner, 0),
            ),
            ((relay, 1), (late, 1), (other, 0)),
            ((relay, 2), (line, 3), (stage, 3), (corner, 1)),
            ((other, 1),),
            ((late, 2), (corner, 2), (relay, 3)),
            ((other, 2),),
            ((late, 3), (corner, 3)),
            ((other, 3),),
        )


class LineSum:
    def __init__(self, wire, d, t, extent, block, up_in, down_in, rows, parts):
        self.wire, self.d, self.t, self.extent = wire, d, t, extent
        self.block, self.up_in, self.down_in = block, up_in, down_in
        self.rows, self.parts = rows // parts, parts
        self.up = [[wire.slot() for p in range(parts)] for s in range(extent - 1)]
        self.down = [[wire.slot() for p in range(parts)] for s in range(extent - 1)]

    def cut(self, ref, part):
        return ref.at[pl.ds(part * self.rows, self.rows)]

    def add(self, target, source):
        add_into(target, source, self.rows)

    def flow(self, step, part, near, index, slots, buffers, to_device, from_device):
        wire, extent = self.wire, self.extent
        block = lambda: self.cut(self.block(index), part)
        if step >= 1:
            source = lambda: self.cut(buffers.at[step - 1], part)
            active = both(both(near <= step, near < extent - 1), near >= 1)
            wire.arrive(slots[step - 1][part], source, from_device, active)
            under(active, lambda: self.add(block(), source()))
        wire.start(
            slots[step][part],
            block,
            lambda: self.cut(buffers.at[step], part),
            to_device,
            both(near <= step, near < extent - 1),
        )

    def step(self, step):
        d, t, extent = self.d, self.t, self.extent
        up, down = extent - 1 - step + t, step + t - (extent - 1)
        above, below = (d, t + 1), (d, t - 1)
        for part in range(self.parts):
            self.flow(step, part, t, up, self.up, self.up_in, above, below)
            self.flow(step, part, extent - 1 - t, down, self.down, self.down_in, below, above)

    def last(self):
        d, t, extent = self.d, self.t, self.extent
        for ready, missing, slots, buffers, device in (
            (t > 0, t == 0, self.up, self.up_in, (d, t - 1)),
            (t < extent - 1, t == extent - 1, self.down, self.down_in, (d, t + 1)),
        ):
            buffer = buffers.at[extent - 2]
            for part in range(self.parts):
                self.wire.arrive(
                    slots[extent - 2][part],
                    lambda part=part, buffer=buffer: self.cut(buffer, part),
                    device,
                    ready,
                )

            def clear(buffer=buffer):
                buffer[...] = jnp.zeros(buffer.shape, BF)

            under(missing, clear)


class BundleSum(LineSum):
    def cut(self, ref, part):
        return ref

    def add(self, target, source):
        for i in range(4):
            add_into(target.at[i], source.at[i], LATE)


def own_sum(block, up_in, down_in, part, columns):
    return (
        block[part, columns].astype(F32)
        + up_in[part, columns].astype(F32)
        + down_in[part, columns].astype(F32)
    )


def plane_order(t):
    top = t // 2
    inner = ((t + 1) // 2) % 2
    return (
        3 - 3 * top,
        2 - top,
        (1 - inner) * (1 - top) + (2 + inner) * top,
        inner * (1 - top) + (3 - inner) * top,
    )


def sum_plane(wire, local, d, t, extent, partial, buffers, rows, between=lambda turn: None):
    (
        work,
        own_in,
        a_in,
        b_in,
        up_in,
        down_in,
        late_up,
        late_down,
        late_a,
        late_b,
    ) = buffers
    order = plane_order(t)
    early, half = rows - LATE, (rows - LATE) // 2
    to_x, to_y, to_c = (flip(d, 2), t), (flip(d, 4), t), (flip(d, 1), t)
    turns = (3, 1, 2, 0)
    slots_c, slots_a, slots_b, loads = {}, {}, {}, {}

    def cut(ref, which):
        return ref.at[pl.ds(which * half, half)]

    def late_cut(ref, which):
        return ref.at[pl.ds(early + which * (LATE // 2), LATE // 2)]

    def begin(k):
        for i in turns:
            slots_c[k, i] = wire.slot()
            wire.start(
                slots_c[k, i],
                lambda i=i: partial.at[order[k], 1, i],
                lambda i=i: work.at[k, i],
                to_c,
            )
            loads[k, i] = local.start(partial.at[order[k], 0, i], own_in.at[k % 2, i])

    begin(0)

    def inverse(index):
        where = jnp.int32(0)
        for k in range(1, extent):
            where = where + k * jnp.where(order[k] == index, 1, 0)
        return where

    line = LineSum(
        wire,
        d,
        t,
        extent,
        lambda index: work.at[inverse(index), 0, pl.ds(0, early)],
        up_in,
        down_in,
        early,
        1,
    )
    late_line = BundleSum(
        wire,
        d,
        t,
        extent,
        lambda index: work.at[inverse(index), pl.ds(0, 4), pl.ds(early, LATE)],
        late_up,
        late_down,
        LATE,
        1,
    )
    routes_a = (
        (to_x, 3, 2, 0, 0),
        (to_y, 3, 1, 1, 1),
        (to_x, 1, 0, 0, 2),
        (to_y, 2, 0, 1, 3),
    )
    routes_b = ((to_y, 2, 0, 0), (to_x, 1, 1, 1))
    last = extent - 1

    def send_a(k, source, cutter, inbox):
        for device, origin, unused, which, row in routes_a:
            if origin == source:
                slots_a[inbox is a_in, k, row] = wire.slot()
                wire.start(
                    slots_a[inbox is a_in, k, row],
                    lambda origin=origin, which=which: cutter(work.at[k, origin], which),
                    lambda row=row: inbox.at[k, row] if inbox is a_in else inbox.at[row],
                    device,
                )

    def receive_a(k, cutter, inbox, second, size):
        for device, unused, target, which, row in routes_a:
            region = inbox.at[k, row] if inbox is a_in else inbox.at[row]
            wire.arrive(slots_a[inbox is a_in, k, row], lambda: region, device)
            add_into(cutter(work.at[k, target], which), region, size)
            if row < 2:
                to, origin, part, b_row = routes_b[row]
                slots_b[inbox is a_in, k, b_row] = wire.slot()
                wire.start(
                    slots_b[inbox is a_in, k, b_row],
                    lambda origin=origin, part=part: cutter(work.at[k, origin], part),
                    lambda b_row=b_row: second.at[k, b_row]
                    if inbox is a_in
                    else second.at[b_row],
                    to,
                )

    def receive_b(k, cutter, inbox, second, size):
        for device, unused, which, row in routes_b:
            region = second.at[k, row] if inbox is a_in else second.at[row]
            wire.arrive(slots_b[inbox is a_in, k, row], lambda: region, device)
            add_into(cutter(work.at[k, 0], which), region, size)

    for turn in range(extent + 2):
        if turn + 1 < extent:
            begin(turn + 1)
        if turn < extent:
            k = turn
            for i in turns:
                loads[k, i].wait()
                wire.arrive(slots_c[k, i], lambda k=k, i=i: work.at[k, i], to_c)
                add_into(work.at[k, i], own_in.at[k % 2, i], rows)
                send_a(k, i, cut, a_in)
            if k < last:
                late_line.step(k)
        if turn == extent:
            late_line.last()
            for i in turns:
                for inbox in (late_up, late_down):
                    add_into(
                        work.at[last, i, pl.ds(early, LATE)], inbox.at[last - 1, i], LATE
                    )
                send_a(last, i, late_cut, late_a)
        between(turn)
        if 1 <= turn <= extent:
            receive_a(turn - 1, cut, a_in, b_in, half)
        if turn == extent + 1:
            receive_a(last, late_cut, late_a, late_b, LATE // 2)
        if turn >= 2:
            k = turn - 2
            receive_b(k, cut, a_in, b_in, half)
            if k < last:
                line.step(k)
    between(extent + 2)
    receive_b(last, late_cut, late_a, late_b, LATE // 2)
    line.last()


def own_rows(buffers, rows, columns, body):
    work, up_in, down_in = buffers[0], buffers[4], buffers[5]
    mine = work.at[work.shape[0] - 1, 0]
    up_last, down_last = up_in.at[up_in.shape[0] - 1], down_in.at[down_in.shape[0] - 1]
    early = rows - LATE

    def first(start):
        part = pl.ds(start, 16)
        body(part, own_sum(mine, up_last, down_last, part, columns))

    def second(start):
        part = pl.ds(pl.multiple_of(early + start, 16), 16)
        body(part, mine[part, columns].astype(F32))

    rows_loop(early, 16, first)
    rows_loop(LATE, 16, second)


def sum_scratch(extent, rows, width):
    early = rows - LATE
    return [
        pltpu.VMEM((extent, 4, rows, width), BF),
        pltpu.VMEM((2, 4, rows, width), BF),
        pltpu.VMEM((extent, 4, early // 2, width), BF),
        pltpu.VMEM((extent, 2, early // 2, width), BF),
        pltpu.VMEM((extent - 1, early, width), BF),
        pltpu.VMEM((extent - 1, early, width), BF),
        pltpu.VMEM((extent - 1, 4, LATE, width), BF),
        pltpu.VMEM((extent - 1, 4, LATE, width), BF),
        pltpu.VMEM((4, LATE // 2, width), BF),
        pltpu.VMEM((2, LATE // 2, width), BF),
    ]


def plane_devices(d, t, extent):
    return line_devices(d, t, extent) + [(None, (flip(d, bits), t)) for bits in (1, 2, 4)]


def kernel_params(number):
    return pltpu.CompilerParams(
        collective_id=number, has_side_effects=True, vmem_limit_bytes=VMEM_LIMIT
    )


def dma_pair(count):
    return [pltpu.SemaphoreType.DMA((count,)), pltpu.SemaphoreType.DMA((count,))]


class Pieces:
    def __init__(self, d, in_weight, out_weight, sem, pieces, tables=None):
        self.copies = {}
        slab = out_weight.shape[0] // 2
        for bits, piece in enumerate(pieces):
            start = pl.multiple_of(flip(d, bits) * slab, slab)
            pairs = []
            for place in range(3):
                for e in range(2):
                    if place < 2:
                        column = (2 * place + e) * slab
                        whole = in_weight.at[pl.ds(start, slab), pl.ds(column, slab)]
                    else:
                        whole = out_weight.at[pl.ds(e * slab, slab), pl.ds(start, slab)]
                    if tables is not None and bits == 0:
                        part = tables[place].at[2 * d + e]
                    else:
                        part = piece.at[place, e]
                    pairs.append((part, whole, sem.at[bits * 6 + place * 2 + e]))
            self.copies[bits] = pairs

    def load(self, bits):
        for piece, whole, sem in self.copies[bits]:
            pltpu.make_async_copy(piece, whole, sem).start()

    def loaded(self, bits):
        for piece, whole, sem in self.copies[bits]:
            pltpu.make_async_copy(piece, whole, sem).wait()

    def store(self, bits):
        for piece, whole, sem in self.copies[bits]:
            pltpu.make_async_copy(whole, piece, sem).start()

    def stored(self, bits):
        for piece, whole, sem in self.copies[bits]:
            pltpu.make_async_copy(whole, piece, sem).wait()


def coefficients(columns, d, slab):
    values = columns.astype(F32)
    lane = lax.broadcasted_iota(jnp.int32, values.shape, 1)
    parts = []
    for e in range(2):
        wanted = jnp.logical_or(lane == 2 * d + e, lane == 16 + 2 * d + e)
        one = jnp.sum(jnp.where(wanted, values, 0.0), axis=-1, keepdims=True)
        parts.append(jnp.broadcast_to(one, (values.shape[0], slab)))
    return jnp.concatenate(parts, axis=1)


def line_exchange(wire, t, d, extent, outbox, inbox):
    peers = [(d, (t + k) % extent) for k in range(1, extent)]
    slots = []
    for k, peer in enumerate(peers):
        slot = wire.slot()
        slots.append(slot)
        wire.start(slot, lambda: outbox, lambda k=k: inbox.at[k], peer)
    result = outbox[...]
    for k, peer in enumerate(peers):
        wire.arrive(slots[k], lambda k=k: inbox.at[k], peer)
        result = result + inbox[k]
    return result


def columns_to_rows(ref):
    return ref[...].T[0:8]


def rows_to_columns(value):
    return jnp.concatenate([value, jnp.zeros((120, value.shape[1]), F32)], axis=0).T


def turned(value, cosine, sine, direction):
    return value * cosine + direction * pltpu.roll(value, HD // 2, 1) * sine


def line_peers(d, t, extent):
    return [(None, (d, (t + k) % extent)) for k in range(1, extent)]


def transposed_dot(left, right):
    return lax.dot_general(left, right, (((0,), (0,)), ((), ())), preferred_element_type=F32)


def dot_transposed(left, right):
    return lax.dot_general(left, right, (((1,), (1,)), ((), ())), preferred_element_type=F32)


def front_kernel(
    extent,
    length,
    hid,
    q_weight,
    k_weight,
    v_weight,
    o_weight,
    gains,
    gate,
    up,
    down,
    attn_gain,
    cosine,
    sine,
    ffn_gain,
    router,
    chosen,
    middle,
    gates,
    ffn_own,
    head_gain,
    inverses,
    hid_out,
    qkv_out,
    o_out,
    normed_out,
    raw_out,
    low_out,
    probs_out,
    mixed_out,
    tokens,
    hidden,
    out,
    landed,
    hid_all,
    qkv_all,
    o_all,
    gains_all,
    normed,
    raw,
    low,
    probs,
    mixed,
    sums,
    outbox,
    inbox,
    gathered,
    work,
    up_in,
    down_in,
    in_weight,
    out_weight,
    hidden_stage,
    out_stage,
    send_sem,
    recv_sem,
    local_sem,
    weight_sem,
    stage_sem,
    token_sem,
    probs_sem,
):
    d, t = lax.axis_index("dp"), lax.axis_index("tensor")
    seq_len, width = hid_all.shape
    rows = seq_len // extent
    heads = gains.shape[0] // 2
    columns = heads * HD
    depth, o_rows, o_width = q_weight.shape[0], o_weight.shape[0], o_weight.shape[1]
    wire, local = Wire(send_sem, recv_sem), Local(local_sem)
    dx, dy, dxy = flip(d, 2), flip(d, 4), flip(d, 6)
    to_x, to_y, to_c = (dx, t), (dy, t), (flip(d, 1), t)

    def block(index):
        return hid_all.at[pl.ds(index * rows, rows)]

    def region(device, which):
        start = pl.multiple_of(device * o_width, o_width)
        if which is None:
            return [qkv_all.at[pl.ds(device * depth, depth)], o_all.at[:, pl.ds(start, o_width)]]
        return [
            qkv_all.at[pl.ds(device * depth + which * (depth // 2), depth // 2)],
            o_all.at[pl.ds(which * (o_rows // 2), o_rows // 2), pl.ds(start, o_width)],
        ]

    copies = [local.start(hid, block(t))]
    for n, weight in enumerate((q_weight, k_weight, v_weight)):
        target = qkv_all.at[pl.ds(d * depth, depth), pl.ds(n * columns, columns)]
        copies.append(local.start(weight, target))
    copies.append(local.start(o_weight, region(d, None)[1]))
    gains_all[0] = gains[...]
    greet(line_peers(d, t, extent) + [(None, (flip(d, bits), t)) for bits in range(1, 8)])
    for copy in copies:
        copy.wait()

    def send(device, sources, targets):
        slots = []
        for source, target in zip(sources, targets):
            slot = wire.slot()
            wire.start(slot, lambda source=source: source, lambda target=target: target, device)
            slots.append(slot)
        return slots

    def arrive(slots, regions, device):
        for slot, part in zip(slots, regions):
            wire.arrive(slot, lambda: part, device)

    line = LineGather(wire, d, t, extent, lambda: block(t), block)
    line.begin()
    x_slots, y_slots, c_slots = {}, {}, {}
    for which, other in ((0, 1), (1, 0)):
        x_slots[which] = send(to_x, region(d, which), region(d, which))
        y_slots[other] = send(to_y, region(d, other), region(d, other))
    c_slots[1] = send(to_c, region(d, None), region(d, None))
    gain_slots = {}
    for bits in range(1, 8):
        gain_slots[bits] = wire.slot()
        wire.start(
            gain_slots[bits],
            lambda: gains,
            lambda bits=bits: gains_all.at[bits],
            (flip(d, bits), t),
        )
    weights = Pieces(
        d, in_weight, out_weight, weight_sem, [landed.at[bits] for bits in range(8)]
    )
    own_experts = Pieces(d, in_weight, out_weight, weight_sem, [None], (gate, up, down))
    own_experts.load(0)
    arrive(x_slots[0], region(dx, 0), to_x)
    over_y = send(to_y, region(dx, 0), region(dx, 0))
    arrive(y_slots[1], region(dy, 1), to_y)
    over_x = send(to_x, region(dy, 1), region(dy, 1))
    piece_slots = {}
    for bits in (2, 4, 1, 3, 5, 6, 7):
        first = 2 * flip(d, bits)
        piece_slots[bits] = send(
            (flip(d, bits), t),
            [weight.at[pl.ds(first, 2)] for weight in (gate, up, down)],
            [landed.at[bits, place] for place in range(3)],
        )
    line.step(1)
    arrive(x_slots[1], region(dx, 1), to_x)
    c_slots[3] = send(to_c, region(dx, None), region(dx, None))
    arrive(y_slots[0], region(dy, 0), to_y)
    c_slots[5] = send(to_c, region(dy, None), region(dy, None))
    for step in range(2, extent):
        line.step(step)
    arrive(over_y, region(dxy, 0), to_y)
    arrive(over_x, region(dxy, 1), to_x)
    c_slots[7] = send(to_c, region(dxy, None), region(dxy, None))
    for bits in range(1, 8):
        wire.arrive(
            gain_slots[bits], lambda bits=bits: gains_all.at[bits], (flip(d, bits), t)
        )
    total_gain = gains_all[0]
    for bits in range(1, 8):
        total_gain = total_gain + gains_all[bits]
    head_gain[...] = total_gain
    tile = 256

    def normalize(start):
        part = pl.ds(start, 64)
        value = hid_all[part].astype(F32)
        unit = value * lax.rsqrt(jnp.mean(value * value, axis=-1, keepdims=True) + EPSILON)
        normed[part] = (unit * attn_gain[...]).astype(BF)

    rows_loop(seq_len, 64, normalize)
    for bits in (1, 3, 5, 7):
        arrive(c_slots[bits], region(flip(d, bits), None), to_c)
    kept = [
        local.start(hid_all, hid_out),
        local.start(qkv_all, qkv_out),
        local.start(o_all, o_out),
        local.start(normed, normed_out),
    ]

    def project(start):
        part = pl.ds(start, tile)
        result = jnp.dot(normed[part], qkv_all[...], preferred_element_type=F32)
        raw[part] = result
        lane = lax.broadcasted_iota(jnp.int32, (tile, 128), 1)
        squares = [
            jnp.sum(jnp.square(result[:, n * columns : (n + 1) * columns]), axis=-1, keepdims=True)
            for n in range(2)
        ]
        sums[part] = jnp.where(lane == 0, squares[0], jnp.where(lane == 1, squares[1], 0.0))

    rows_loop(seq_len, tile, project)
    outbox[...] = columns_to_rows(sums)
    total = line_exchange(wire, t, d, extent, outbox, inbox)
    inverses[...] = rows_to_columns(lax.rsqrt(total / width + EPSILON))
    low[:, 2 * columns :] = raw[:, 2 * columns :].astype(BF)

    def probs_copy(h):
        return pltpu.make_async_copy(probs.at[h % 2], probs_out.at[h], probs_sem.at[h % 2])

    def head(h, carry):
        for n in range(2):
            section = pl.ds(pl.multiple_of(n * columns + h * HD, HD), HD)
            unit = raw[:, section] * inverses[:, n : n + 1]
            raw[:, section] = unit
            scaled = unit * head_gain[pl.ds(n * heads + h, 1)]
            low[:, section] = turned(scaled, cosine[...], sine[...], 1.0).astype(BF)
        section = pl.ds(pl.multiple_of(h * HD, HD), HD)
        key_section = pl.ds(pl.multiple_of(columns + h * HD, HD), HD)
        value_section = pl.ds(pl.multiple_of(2 * columns + h * HD, HD), HD)

        @pl.when(h >= 2)
        def _():
            probs_copy(h).wait()

        def some(start):
            part = pl.ds(start, tile)
            scores = dot_transposed(low[part, section], low[:, key_section]) / math.sqrt(HD)
            row = start + lax.broadcasted_iota(jnp.int32, scores.shape, 0)
            column = lax.broadcasted_iota(jnp.int32, scores.shape, 1)
            allowed = both(column <= row, column < length[0])
            scores = jnp.where(allowed, scores, -1e30)
            powers = jnp.exp(scores - jnp.max(scores, axis=-1, keepdims=True))
            result = powers / jnp.sum(powers, axis=-1, keepdims=True)
            probs[h % 2, part] = result
            mixed[part, section] = jnp.dot(
                result.astype(BF), low[:, value_section], preferred_element_type=F32
            ).astype(BF)

        rows_loop(seq_len, tile, some)
        probs_copy(h).start()
        return carry

    lax.fori_loop(0, heads, head, 0)
    kept += [local.start(raw, raw_out), local.start(low, low_out), local.start(mixed, mixed_out)]

    def join(first, carry):
        result = jnp.dot(
            mixed[pl.ds(first * 2 * rows, 2 * rows)], o_all[...], preferred_element_type=F32
        )
        work[pl.ds(2 * first, 2)] = result.astype(BF).reshape(2, rows, width)
        return carry

    lax.fori_loop(0, extent // 2, join, 0)
    total_line = LineSum(
        wire, d, t, extent, lambda index: work.at[index], up_in, down_in, rows, 2
    )
    for step in range(extent - 1):
        total_line.step(step)
    total_line.last()
    mine = work.at[t]
    everything = pl.ds(0, width)
    packet = gathered.at[t, 0, 0]

    def body(start):
        part = pl.ds(start, 16)
        value = hid[part].astype(F32) + own_sum(
            mine, up_in.at[extent - 2], down_in.at[extent - 2], part, everything
        )
        middle[part] = value
        unit = value * lax.rsqrt(jnp.mean(value * value, axis=-1, keepdims=True) + EPSILON)
        ffn_own[part] = (unit * ffn_gain[...]).astype(BF)

    rows_loop(rows, 16, body)
    logits = jnp.dot(ffn_own[...], router[...], preferred_element_type=F32)
    lane = lax.broadcasted_iota(jnp.int32, logits.shape, 1)
    top = jnp.max(jnp.where(lane < 16, logits, -1e30), axis=-1, keepdims=True)
    powers = jnp.where(lane < 32, jnp.exp(logits - top), 0.0)
    chance = powers / jnp.sum(jnp.where(lane < 16, powers, 0.0), axis=-1, keepdims=True)
    gates[...] = chance
    coeff = chance * chosen[...]
    high = coeff.astype(BF).astype(F32)
    packet[:, 0:width] = ffn_own[...]
    packet[:, width : width + 128] = jnp.where(lane < 16, high, coeff - high).astype(BF)

    def place(j, c, i):
        return gathered.at[j, c, i]

    def bundle(j, c):
        return gathered.at[j, c, pl.ds(0, 4), pl.ds(rows - LATE, LATE)]

    gather = PlaneGather(wire, d, t, extent, lambda: packet, place, bundle, rows)
    for bits in range(1, 8):
        arrive(
            piece_slots[bits], [landed.at[bits, place] for place in range(3)], (flip(d, bits), t)
        )
        weights.load(bits)
    own_experts.loaded(0)
    for bits in range(1, 8):
        weights.loaded(bits)
    units = out_weight.shape[0]

    def stage_copies(slot, j, c):
        return (
            pltpu.make_async_copy(hidden_stage.at[slot], hidden.at[j, c], stage_sem.at[0, slot]),
            pltpu.make_async_copy(out_stage.at[slot], out.at[j, c], stage_sem.at[1, slot]),
        )

    actions = gather.actions()

    def group(g, carry):
        for number, steps in enumerate(actions):

            @pl.when(g == number)
            def _():
                for action, argument in steps:
                    action(argument)

        j, c, slot = arrival(t, g // 2), g % 2, g % 2

        @pl.when(g >= 2)
        def _():
            for copy in stage_copies(slot, j, c):
                copy.wait()

        pltpu.make_async_copy(gathered.at[j, c], tokens.at[j, c], token_sem.at[g]).start()

        def some(first, carry):
            blocks, part = pl.ds(2 * first, 2), pl.ds(first * 2 * rows, 2 * rows)
            values = jnp.dot(
                gathered[j, c, blocks, :, 0:width].reshape(2 * rows, width),
                in_weight[...],
                preferred_element_type=F32,
            )
            hidden_stage[slot, part] = values.astype(BF)
            gate_value, up_value = values[:, :units], values[:, units:]
            coeff = coefficients(
                gathered[j, c, blocks, :, width : width + 128].reshape(2 * rows, 128),
                d,
                units // 2,
            )
            active = (coeff * (gate_value * jax.nn.sigmoid(gate_value)) * up_value).astype(BF)
            result = jnp.dot(active, out_weight[...], preferred_element_type=F32)
            out_stage[slot, blocks] = result.astype(BF).reshape(2, rows, width)
            return carry

        lax.fori_loop(0, 2, some, 0)
        for copy in stage_copies(slot, j, c):
            copy.start()
        return carry

    lax.fori_loop(0, 2 * extent, group, 0)
    for slot in range(2):
        for copy in stage_copies(slot, 0, slot):
            copy.wait()
    for g in range(2 * extent):
        pltpu.make_async_copy(
            gathered.at[arrival(t, g // 2), g % 2],
            tokens.at[arrival(t, g // 2), g % 2],
            token_sem.at[g],
        ).wait()
    for h in range(heads - 2, heads):
        probs_copy(h).wait()
    for copy in kept:
        copy.wait()
    wire.finish()


SMEM = pl.BlockSpec(memory_space=pltpu.SMEM)


def front(extent, length, hid, q_weight, k_weight, v_weight, o_weight, gains, gate, up, down, *rest):
    rows, width = hid.shape
    seq_len = rows * extent
    slab = gate.shape[1]
    heads = gains.shape[0] // 2
    columns = heads * HD
    shape = jax.ShapeDtypeStruct
    kept = [
        shape((seq_len, width), BF),
        shape((width, 3 * columns), BF),
        shape((columns, width), BF),
        shape((seq_len, width), BF),
        shape((seq_len, 3 * columns), F32),
        shape((seq_len, 3 * columns), BF),
        shape((heads, seq_len, seq_len), F32),
        shape((seq_len, columns), BF),
    ]
    return pl.pallas_call(
        functools.partial(front_kernel, extent),
        out_shape=[
            shape((rows, width), F32),
            shape((rows, 128), F32),
            shape((rows, width), BF),
            shape((2 * heads, HD), F32),
            shape((seq_len, 128), F32),
        ]
        + kept
        + [
            shape((extent, 2, 4, rows, width + 128), BF),
            shape((extent, 2, 4 * rows, 4 * slab), BF),
            shape((extent, 2, 4, rows, width), BF),
            shape((8, 3, 2, slab, slab), BF),
        ],
        in_specs=[SMEM, VM] + [ANY] * 4 + [VM] + [ANY] * 3 + [VM] * 6,
        out_specs=[VM] * 5 + [ANY] * 12,
        scratch_shapes=[
            pltpu.VMEM((seq_len, width), BF),
            pltpu.VMEM((width, 3 * columns), BF),
            pltpu.VMEM((columns, width), BF),
            pltpu.VMEM((8,) + gains.shape, F32),
            pltpu.VMEM((seq_len, width), BF),
            pltpu.VMEM((seq_len, 3 * columns), F32),
            pltpu.VMEM((seq_len, 3 * columns), BF),
            pltpu.VMEM((2, seq_len, seq_len), F32),
            pltpu.VMEM((seq_len, columns), BF),
            pltpu.VMEM((seq_len, 128), F32),
            pltpu.VMEM((8, seq_len), F32),
            pltpu.VMEM((extent - 1, 8, seq_len), F32),
            pltpu.VMEM((extent, 2, 4, rows, width + 128), BF),
            pltpu.VMEM((extent, rows, width), BF),
            pltpu.VMEM((extent - 1, rows, width), BF),
            pltpu.VMEM((extent - 1, rows, width), BF),
            pltpu.VMEM((width, 4 * slab), BF),
            pltpu.VMEM((2 * slab, width), BF),
            pltpu.VMEM((2, 4 * rows, 4 * slab), BF),
            pltpu.VMEM((2, 4, rows, width), BF),
        ]
        + dma_pair(180)
        + [
            pltpu.SemaphoreType.DMA((16,)),
            pltpu.SemaphoreType.DMA((48,)),
            pltpu.SemaphoreType.DMA((2, 2)),
            pltpu.SemaphoreType.DMA((2 * extent,)),
            pltpu.SemaphoreType.DMA((2,)),
        ],
        compiler_params=kernel_params(1),
        cost_estimate=pl.CostEstimate(flops=0, bytes_accessed=300_000_000, transcendentals=0),
    )(length, hid, q_weight, k_weight, v_weight, o_weight, gains, gate, up, down, *rest)


def turn_kernel(extent, partial, middle, teacher, weight, tokens, hidden, *rest):
    landed, tables = rest[0], rest[1:4]
    grad_output, row_loss, out, inner_out, active_out, grads = rest[4:10]
    buffers = rest[10:20]
    (
        packet,
        in_weight,
        out_weight,
        coeff_tile,
        hidden_tile,
        factors,
        grad_tile,
        out_stage,
        active_tile,
        inner_tile,
        send_sem,
        recv_sem,
        local_sem,
        weight_sem,
        tile_sem,
        load_sem,
    ) = rest[20:]
    d, t = lax.axis_index("dp"), lax.axis_index("tensor")
    rows, width = middle.shape
    greet(plane_devices(d, t, extent))
    wire, local = Wire(send_sem, recv_sem), Local(local_sem)
    pieces = [landed.at[bits] for bits in range(8)]
    weights = Pieces(d, in_weight, out_weight, weight_sem, pieces, tables)
    units, slab = out_weight.shape[0], out_weight.shape[0] // 2
    count = 2 * extent

    def factor_loads(g):
        j, c, slot = g // 2, g % 2, g % 2
        part = (pl.ds(0, 4), pl.ds(0, rows), pl.ds(width, 128))
        return (
            pltpu.make_async_copy(
                tokens.at[(j, c) + part], coeff_tile.at[slot], load_sem.at[0, slot]
            ),
            pltpu.make_async_copy(hidden.at[j, c], hidden_tile.at[slot], load_sem.at[1, slot]),
        )

    def active_store(g):
        return pltpu.make_async_copy(
            active_tile.at[g % 2], active_out.at[g // 2, g % 2], load_sem.at[2, g % 2]
        )

    def prepare(g):
        if g + 1 < count:
            for copy in factor_loads(g + 1):
                copy.start()
        for copy in factor_loads(g):
            copy.wait()
        if g >= 2:
            active_store(g - 2).wait()
        slot = g % 2

        def some(first, carry):
            size = 2 * rows
            blocks, part = pl.ds(2 * first, 2), pl.ds(first * size, size)
            gate_value = hidden_tile[slot, part, 0:units].astype(F32)
            up_value = hidden_tile[slot, part, units : 2 * units].astype(F32)
            coeff = coefficients(coeff_tile[slot, blocks].reshape(size, 128), d, slab)
            sigmoid_value = jax.nn.sigmoid(gate_value)
            silu_value = gate_value * sigmoid_value
            slope = sigmoid_value * (1.0 + gate_value * (1.0 - sigmoid_value))
            direct = silu_value * up_value
            factors[g, part, 0:units] = (coeff * up_value * slope).astype(BF)
            factors[g, part, units : 2 * units] = (coeff * silu_value).astype(BF)
            factors[g, part, 2 * units : 3 * units] = direct.astype(BF)
            active_tile[slot, part] = (coeff * direct).astype(BF)
            return carry

        lax.fori_loop(0, 2, some, 0)
        active_store(g).start()

    for copy in factor_loads(0):
        copy.start()

    def between(turn_number):
        if turn_number == 1:
            for bits in range(8):
                weights.load(bits)
        if turn_number < extent:
            prepare(2 * turn_number)
            prepare(2 * turn_number + 1)

    sum_plane(wire, local, d, t, extent, partial, buffers, rows, between)
    for g in (count - 2, count - 1):
        active_store(g).wait()

    def body(part, value):
        output = middle[part] + value
        mismatch = output - teacher[part].astype(F32)
        scaled = mismatch * weight[part, 0:1]
        grad_output[part] = scaled
        packet[part] = scaled.astype(BF)
        row_loss[part] = jnp.broadcast_to(
            jnp.sum(scaled * mismatch, axis=-1, keepdims=True), (16, 128)
        )

    own_rows(buffers, rows, pl.ds(0, width), body)

    def place(j, c, i):
        return grads.at[j, c, i]

    def bundle(j, c):
        return grads.at[j, c, pl.ds(0, 4), pl.ds(rows - LATE, LATE)]

    own_copy = local.start(packet, place(t, 0, 0))
    gather = PlaneGather(wire, d, t, extent, lambda: packet, place, bundle, rows)
    own_copy.wait()
    for bits in range(8):
        weights.loaded(bits)
    actions = gather.actions()

    def out_copies(j, c):
        return (
            pltpu.make_async_copy(out_stage, out.at[j, c], tile_sem.at[1]),
            pltpu.make_async_copy(inner_tile, inner_out.at[j, c], tile_sem.at[2]),
        )

    def group(g, carry):
        j, c = arrival(t, g // 2), g % 2
        grad_copy = pltpu.make_async_copy(grads.at[j, c], grad_tile, tile_sem.at[0])
        for number, steps in enumerate(actions):

            @pl.when(g == number)
            def _():
                for action, argument in steps:
                    action(argument)

        grad_copy.start()

        @pl.when(g >= 1)
        def _():
            for copy in out_copies(j, c):
                copy.wait()

        grad_copy.wait()
        index = 2 * j + c

        def some(first, carry):
            size = 2 * rows
            blocks, part = pl.ds(2 * first, 2), pl.ds(first * size, size)
            grad_active = dot_transposed(
                grad_tile[blocks].reshape(size, width), out_weight[...]
            )
            product = grad_active * factors[index, part, 2 * units : 3 * units].astype(F32)
            lane = lax.broadcasted_iota(jnp.int32, (size, 128), 1)
            sums = jnp.zeros((size, 128), F32)
            for e in range(2):
                one = jnp.sum(product[:, e * slab : (e + 1) * slab], axis=-1, keepdims=True)
                sums = sums + jnp.where(lane == 2 * d + e, one, 0.0)
            out_stage[blocks, :, width : width + 128] = sums.astype(BF).reshape(2, rows, 128)
            for n in range(2):
                columns = pl.ds(n * units, units)
                inner_tile[part, columns] = (
                    grad_active * factors[index, part, columns].astype(F32)
                ).astype(BF)
            result = dot_transposed(inner_tile[part], in_weight[...]).astype(BF)
            out_stage[blocks, :, 0:width] = result.reshape(2, rows, width)
            return carry

        lax.fori_loop(0, 2, some, 0)
        for copy in out_copies(j, c):
            copy.start()
        return carry

    lax.fori_loop(0, 2 * extent, group, 0)
    for copy in out_copies(0, 0):
        copy.wait()
    wire.finish()


def turn(extent, partial, middle, teacher, weight, tokens, hidden, landed, *tables):
    rows, width = middle.shape
    slab = landed.shape[3]
    return pl.pallas_call(
        functools.partial(turn_kernel, extent),
        out_shape=[
            jax.ShapeDtypeStruct((rows, width), F32),
            jax.ShapeDtypeStruct((rows, 128), F32),
            jax.ShapeDtypeStruct((extent, 2, 4, rows, width + 128), BF),
            jax.ShapeDtypeStruct((extent, 2, 4 * rows, 4 * slab), BF),
            jax.ShapeDtypeStruct((extent, 2, 4 * rows, 2 * slab), BF),
            jax.ShapeDtypeStruct((extent, 2, 4, rows, width), BF),
        ],
        in_specs=[ANY, VM, VM, VM] + [ANY] * 6,
        out_specs=[VM, VM] + [ANY] * 4,
        scratch_shapes=sum_scratch(extent, rows, width)
        + [
            pltpu.VMEM((rows, width), BF),
            pltpu.VMEM((width, 4 * slab), BF),
            pltpu.VMEM((2 * slab, width), BF),
            pltpu.VMEM((2, 4, rows, 128), BF),
            pltpu.VMEM((2, 4 * rows, 4 * slab), BF),
            pltpu.VMEM((2 * extent, 4 * rows, 6 * slab), BF),
            pltpu.VMEM((4, rows, width), BF),
            pltpu.VMEM((4, rows, width + 128), BF),
            pltpu.VMEM((2, 4 * rows, 2 * slab), BF),
            pltpu.VMEM((4 * rows, 4 * slab), BF),
        ]
        + dma_pair(150)
        + [
            pltpu.SemaphoreType.DMA((20,)),
            pltpu.SemaphoreType.DMA((48,)),
            pltpu.SemaphoreType.DMA((3,)),
            pltpu.SemaphoreType.DMA((3, 2)),
        ],
        compiler_params=kernel_params(4),
        cost_estimate=pl.CostEstimate(flops=0, bytes_accessed=450_000_000, transcendentals=0),
    )(partial, middle, teacher, weight, tokens, hidden, landed, *tables)


class WeightGrads:
    def __init__(self, sources, tiles, totals, sem):
        self.sources, self.tiles, self.sem = sources, tiles, sem
        self.in_total, self.out_total = totals

    def copies(self, g):
        j, c, slot = g // 2, g % 2, g % 2
        return [
            pltpu.make_async_copy(source.at[j, c], tile.at[slot], self.sem.at[n, slot])
            for n, (source, tile) in enumerate(zip(self.sources, self.tiles))
        ]

    def start(self, g):
        for copy in self.copies(g):
            copy.start()

    def clear(self):
        self.in_total[...] = jnp.zeros(self.in_total.shape, F32)
        self.out_total[...] = jnp.zeros(self.out_total.shape, F32)

    def work(self, g, count):
        if g + 1 < count:
            self.start(g + 1)
        for copy in self.copies(g):
            copy.wait()
        slot = g % 2
        token_tile, grad_tile, inner_tile, active_tile = (tile.at[slot] for tile in self.tiles)
        size, width = inner_tile.shape[0], grad_tile.shape[2]

        def into_in(start):
            part = pl.ds(start, 256)
            left = token_tile[:, :, part].reshape(size, 256)
            self.in_total[part] += transposed_dot(left, inner_tile[...])

        rows_loop(width, 256, into_in)

        def into_out(start):
            part = pl.ds(start, 512)
            right = grad_tile[:, :, part].reshape(size, 512)
            self.out_total[:, part] += transposed_dot(active_tile[...], right)

        rows_loop(width, 512, into_out)

    def pieces(self, d, stage):
        slab = stage.shape[3]
        for bits in range(8):
            part = pl.ds(pl.multiple_of(flip(d, bits) * slab, slab), slab)
            for place in range(3):
                for e in range(2):
                    if place < 2:
                        column = (2 * place + e) * slab
                        value = self.in_total[part, column : column + slab]
                    else:
                        value = self.out_total[e * slab : (e + 1) * slab, part]
                    stage[bits, place, e] = value.astype(BF)


def leave_kernel(extent, partial, middle, grad_output, gates, chosen, gain, router_t, *rest):
    sources = rest[:4]
    grad_middle, grad_logits, gain_part, grads = rest[4:8]
    came = rest[8:16]
    buffers = rest[16:26]
    tiles, totals = rest[26:30], rest[30:32]
    stage, packet, send_sem, recv_sem, local_sem, tile_sem = rest[32:]
    d, t = lax.axis_index("dp"), lax.axis_index("tensor")
    rows, width = middle.shape
    greet(line_devices(d, t, extent) + [(None, (flip(d, bits), t)) for bits in range(1, 6)])
    wire, local = Wire(send_sem, recv_sem), Local(local_sem)
    weight_grads = WeightGrads(sources, tiles, totals, tile_sem)
    count = 2 * extent
    piece_slots, copies = [], []
    weight_grads.start(0)

    def between(turn_number):
        if turn_number == 0:
            weight_grads.clear()
        if turn_number < extent:
            weight_grads.work(2 * turn_number, count)
            weight_grads.work(2 * turn_number + 1, count)
        if turn_number == extent + 2:
            weight_grads.pieces(d, stage)
            for bits in range(1, 6):
                slot = wire.slot()
                piece_slots.append(slot)
                wire.start(
                    slot,
                    lambda bits=bits: stage.at[bits],
                    lambda bits=bits: came[bits],
                    (flip(d, bits), t),
                )
            for bits in (0, 6, 7):
                copies.append(local.start(stage.at[bits], came[bits]))

    sum_plane(wire, local, d, t, extent, partial, buffers, rows, between)

    def collect(part, value):
        grad_logits[part] = value

    own_rows(buffers, rows, pl.ds(width, 128), collect)
    coeff_grad = grad_logits[...] * chosen[...]
    lane = lax.broadcasted_iota(jnp.int32, coeff_grad.shape, 1)
    probs = jnp.where(lane < 16, gates[...], 0.0)
    coeff_grad = jnp.where(lane < 16, coeff_grad, 0.0)
    logit_grad = probs * (coeff_grad - jnp.sum(coeff_grad * probs, axis=-1, keepdims=True))
    grad_logits[...] = logit_grad
    high = logit_grad.astype(BF)
    low_part = (logit_grad - high.astype(F32)).astype(BF)
    for begin in range(0, width, 512):
        columns = slice(begin, begin + 512)
        grad_middle[:, columns] = jnp.dot(
            high, router_t[:, columns], preferred_element_type=F32
        ) + jnp.dot(low_part, router_t[:, columns], preferred_element_type=F32)
    gain_part[...] = jnp.zeros(gain_part.shape, F32)

    def body(part, value):
        grad = value + grad_middle[part]
        value = middle[part]
        inverse = lax.rsqrt(jnp.mean(value * value, axis=-1, keepdims=True) + EPSILON)
        unit = value * inverse
        product = grad * unit
        gain_part[...] += product[0:8] + product[8:16]
        scaled = grad * gain[...]
        result = grad_output[part] + inverse * (
            scaled - unit * jnp.mean(scaled * unit, axis=-1, keepdims=True)
        )
        grad_middle[part] = result
        packet[part] = result.astype(BF)

    own_rows(buffers, rows, pl.ds(0, width), body)

    def place(index):
        return grads.at[index]

    copies.append(local.start(packet, place(t)))
    line = LineGather(wire, d, t, extent, lambda: packet, place)
    line.begin()
    for step in range(1, extent):
        line.step(step)
    for copy in copies:
        copy.wait()
    for n, slot in enumerate(piece_slots):
        wire.arrive(slot, lambda: came[1 + n], (flip(d, 1 + n), t))
    wire.finish()


def leave(extent, partial, middle, grad_output, gates, chosen, gain, router_t, sources):
    rows, width = middle.shape
    tokens, grads, inner, active = sources
    units = active.shape[3]
    piece = jax.ShapeDtypeStruct((3, 2, units // 2, units // 2), BF)
    return pl.pallas_call(
        functools.partial(leave_kernel, extent),
        out_shape=[
            jax.ShapeDtypeStruct((rows, width), F32),
            jax.ShapeDtypeStruct((rows, 128), F32),
            jax.ShapeDtypeStruct((8, width), F32),
            jax.ShapeDtypeStruct((extent, rows, width), BF),
        ]
        + [piece] * 8,
        in_specs=[ANY, VM, VM, VM, VM, VM, VM] + [ANY] * 4,
        out_specs=[VM, VM, VM] + [ANY] * 9,
        scratch_shapes=sum_scratch(extent, rows, width + 128)
        + [pltpu.VMEM((2,) + source.shape[2:], BF) for source in sources]
        + [
            pltpu.VMEM((width, 2 * units), F32),
            pltpu.VMEM((units, width), F32),
            pltpu.VMEM((8,) + piece.shape, BF),
            pltpu.VMEM((rows, width), BF),
        ]
        + dma_pair(120)
        + [pltpu.SemaphoreType.DMA((24,)), pltpu.SemaphoreType.DMA((4, 2))],
        compiler_params=kernel_params(5),
        cost_estimate=pl.CostEstimate(flops=0, bytes_accessed=350_000_000, transcendentals=0),
    )(partial, middle, grad_output, gates, chosen, gain, router_t, *sources)


def attend_back_kernel(
    extent,
    grads,
    row_loss,
    hid,
    gain,
    qkv_weight,
    o_weight,
    head_gain,
    cosine,
    sine,
    normed,
    units,
    low,
    probs,
    mixed,
    inverses,
    out,
    grad_qkv,
    grad_o,
    attn_gain_part,
    head_gain_part,
    loss,
    grad_mixed,
    scaled,
    raw_grad,
    sums,
    dots,
    outbox,
    inbox,
    send_sem,
    recv_sem,
):
    d, t = lax.axis_index("dp"), lax.axis_index("tensor")
    seq_len, width = hid.shape
    heads = head_gain.shape[0] // 2
    columns = heads * HD
    greet(line_peers(d, t, extent))
    wire = Wire(send_sem, recv_sem)
    tile = 256
    root = math.sqrt(HD)

    def mix(start):
        part = pl.ds(start, tile)
        grad_mixed[part] = dot_transposed(grads[part], o_weight[...]).astype(BF)

    rows_loop(seq_len, tile, mix)

    def into_o(start):
        part = pl.ds(start, 512)
        grad_o[:, part] = transposed_dot(mixed[...], grads[:, part]).astype(BF)

    rows_loop(width, 512, into_o)
    sums[...] = jnp.zeros(sums.shape, F32)

    def head(h, carry):
        section = pl.ds(pl.multiple_of(h * HD, HD), HD)
        key_section = pl.ds(pl.multiple_of(columns + h * HD, HD), HD)
        value_section = pl.ds(pl.multiple_of(2 * columns + h * HD, HD), HD)
        chance = probs[h]
        incoming = grad_mixed[:, section]
        raw_grad[:, value_section] = transposed_dot(chance.astype(BF), incoming).astype(BF)
        grad_probs = dot_transposed(incoming, low[:, value_section])
        grad_scores = (
            chance * (grad_probs - jnp.sum(grad_probs * chance, axis=-1, keepdims=True))
        ).astype(BF)
        pair = (
            jnp.dot(grad_scores, low[:, key_section], preferred_element_type=F32) / root,
            transposed_dot(grad_scores, low[:, section]) / root,
        )
        lane = lax.broadcasted_iota(jnp.int32, (seq_len, 128), 1)
        for n, where in enumerate((section, key_section)):
            value = turned(pair[n], cosine[...], sine[...], -1.0)
            unit = units[:, where]
            head_gain_part[pl.ds(n * heads + h, 1)] = jnp.sum(value * unit, axis=0, keepdims=True)
            value = value * head_gain[pl.ds(n * heads + h, 1)]
            scaled[:, where] = value
            sums[...] += jnp.where(lane == n, jnp.sum(value * unit, axis=-1, keepdims=True), 0.0)
        return carry

    lax.fori_loop(0, heads, head, 0)
    outbox[...] = columns_to_rows(sums)
    outbox[2:3] = jnp.broadcast_to(jnp.sum(row_loss[:, 0:1], axis=0, keepdims=True), (1, seq_len))
    total = line_exchange(wire, t, d, extent, outbox, inbox)
    loss[...] = total[:, 0:128]
    dots[...] = rows_to_columns(total / width)

    def head_again(h, carry):
        for n in range(2):
            section = pl.ds(pl.multiple_of(n * columns + h * HD, HD), HD)
            raw_grad[:, section] = (
                inverses[:, n : n + 1]
                * (scaled[:, section] - units[:, section] * dots[:, n : n + 1])
            ).astype(BF)
        return carry

    lax.fori_loop(0, heads, head_again, 0)
    attn_gain_part[...] = jnp.zeros(attn_gain_part.shape, F32)

    def finish(start):
        part = pl.ds(start, tile)
        grad = dot_transposed(raw_grad[part], qkv_weight[...])
        value = hid[part].astype(F32)
        inverse = lax.rsqrt(jnp.mean(value * value, axis=-1, keepdims=True) + EPSILON)
        unit = value * inverse
        attn_gain_part[...] += jnp.sum((grad * unit).reshape(tile // 8, 8, width), axis=0)
        change = grad * gain[...]
        out[part] = (
            inverse * (change - unit * jnp.mean(change * unit, axis=-1, keepdims=True))
        ).astype(BF)

    rows_loop(seq_len, tile, finish)

    def into_qkv(start):
        part = pl.ds(start, 256)
        grad_qkv[part] = transposed_dot(normed[:, part], raw_grad[...]).astype(BF)

    rows_loop(width, 256, into_qkv)
    wire.finish()


def attend_back(extent, *operands):
    seq_len, width = operands[0].shape
    head_gain = operands[6]
    heads = head_gain.shape[0] // 2
    columns = heads * HD
    return pl.pallas_call(
        functools.partial(attend_back_kernel, extent),
        out_shape=[
            jax.ShapeDtypeStruct((seq_len, width), BF),
            jax.ShapeDtypeStruct((width, 3 * columns), BF),
            jax.ShapeDtypeStruct((columns, width), BF),
            jax.ShapeDtypeStruct((8, width), F32),
            jax.ShapeDtypeStruct((2 * heads, HD), F32),
            jax.ShapeDtypeStruct((8, 128), F32),
        ],
        in_specs=[VM] * len(operands),
        out_specs=[VM] * 6,
        scratch_shapes=[
            pltpu.VMEM((seq_len, columns), BF),
            pltpu.VMEM((seq_len, 2 * columns), F32),
            pltpu.VMEM((seq_len, 3 * columns), BF),
            pltpu.VMEM((seq_len, 128), F32),
            pltpu.VMEM((seq_len, 128), F32),
            pltpu.VMEM((8, seq_len), F32),
            pltpu.VMEM((extent - 1, 8, seq_len), F32),
        ]
        + dma_pair(extent - 1),
        compiler_params=kernel_params(6),
        cost_estimate=pl.CostEstimate(flops=0, bytes_accessed=1_000_000, transcendentals=0),
    )(*operands)


def close_kernel(
    extent,
    partial,
    grad_middle,
    grad_qkv,
    grad_o,
    small,
    gains,
    grad_in,
    qkv_out,
    o_out,
    small_out,
    work,
    up_in,
    down_in,
    q_work,
    q_core,
    q_a,
    q_b,
    o_work,
    o_core,
    o_a,
    o_b,
    small_in,
    small_sum,
    small_last,
    send_sem,
    recv_sem,
    local_sem,
):
    d, t = lax.axis_index("dp"), lax.axis_index("tensor")
    rows, width = grad_middle.shape
    depth, o_width = qkv_out.shape[0], o_out.shape[1]
    line_peers = [(d, (t + k) % extent) for k in range(1, extent)]
    greet(
        [(None, peer) for peer in line_peers]
        + [(None, (flip(d, bits), t)) for bits in range(1, 8)]
    )
    wire, local = Wire(send_sem, recv_sem), Local(local_sem)
    to_x, to_y, to_c = (flip(d, 2), t), (flip(d, 4), t), (flip(d, 1), t)

    def slices(device):
        start = pl.multiple_of(device * o_width, o_width)
        return [
            grad_qkv.at[pl.ds(device * depth, depth)],
            grad_o.at[:, pl.ds(start, o_width)],
        ]

    turns = (3, 1, 2, 0)
    c_slots, loads = {}, {}
    work_load = local.start(partial, work)
    small_slots = []
    for k, peer in enumerate(line_peers):
        slot = wire.slot()
        small_slots.append(slot)
        wire.start(
            slot,
            lambda k=k: small.at[(t + k + 1) % extent],
            lambda k=k: small_in.at[k],
            peer,
        )
    for i in turns:
        sources = slices(flip(d, 1 + 2 * i))
        c_slots[i] = [wire.slot(), wire.slot()]
        wire.start(c_slots[i][0], lambda s=sources: s[0], lambda i=i: q_core.at[i], to_c)
        wire.start(c_slots[i][1], lambda s=sources: s[1], lambda i=i: o_core.at[i], to_c)
        mine = slices(flip(d, 2 * i))
        loads[i] = [local.start(mine[0], q_work.at[i]), local.start(mine[1], o_work.at[i])]
    work_load.wait()
    line = LineSum(
        wire, d, t, extent, lambda index: work.at[index], up_in, down_in, rows, 2
    )
    line.step(0)

    def cut(ref, which):
        half = ref.shape[0] // 2
        return ref.at[pl.ds(which * half, half)]

    a_slots, b_slots = {}, {}
    routes_a = ((to_x, 3, 2, 0, 0), (to_y, 3, 1, 1, 1), (to_x, 1, 0, 0, 2), (to_y, 2, 0, 1, 3))
    routes_b = ((to_y, 2, 0, 0), (to_x, 1, 1, 1))

    def core_add(i):
        for load in loads[i]:
            load.wait()
        wire.arrive(c_slots[i][0], lambda: q_core.at[i], to_c)
        wire.arrive(c_slots[i][1], lambda: o_core.at[i], to_c)
        add_into(q_work.at[i], q_core.at[i], q_work.shape[1])
        add_into(o_work.at[i], o_core.at[i], o_work.shape[1])

    def a_send(route):
        device, source, target, which, row = route
        a_slots[row] = [wire.slot(), wire.slot()]
        wire.start(
            a_slots[row][0], lambda: cut(q_work.at[source], which), lambda: q_a.at[row], device
        )
        wire.start(
            a_slots[row][1], lambda: cut(o_work.at[source], which), lambda: o_a.at[row], device
        )

    def b_send(route):
        device, source, which, row = route
        b_slots[row] = [wire.slot(), wire.slot()]
        wire.start(
            b_slots[row][0], lambda: cut(q_work.at[source], which), lambda: q_b.at[row], device
        )
        wire.start(
            b_slots[row][1], lambda: cut(o_work.at[source], which), lambda: o_b.at[row], device
        )

    core_add(3)
    a_send(routes_a[0])
    a_send(routes_a[1])
    core_add(1)
    a_send(routes_a[2])
    core_add(2)
    a_send(routes_a[3])
    core_add(0)
    line.step(1)
    for device, source, target, which, row in routes_a:
        wire.arrive(a_slots[row][0], lambda: q_a.at[row], device)
        wire.arrive(a_slots[row][1], lambda: o_a.at[row], device)
        add_into(cut(q_work.at[target], which), q_a.at[row], q_a.shape[1])
        add_into(cut(o_work.at[target], which), o_a.at[row], o_a.shape[1])
        if row < 2:
            b_send(routes_b[row])
    for k, peer in enumerate(line_peers):
        wire.arrive(small_slots[k], lambda k=k: small_in.at[k], peer)
    total = small[t] + small_in[0]
    for k in range(1, extent - 1):
        total = total + small_in[k]
    small_sum[:, 0:16] = total
    small_sum[:, 16:24] = jnp.broadcast_to(gains[...][None], (8, 8, 128))
    last_slots = {}
    for bits in range(1, 8):
        last_slots[bits] = wire.slot()
        wire.start(
            last_slots[bits],
            lambda bits=bits: small_sum.at[flip(d, bits)],
            lambda bits=bits: small_last.at[bits],
            (flip(d, bits), t),
        )
    line.step(2)
    for device, source, which, row in routes_b:
        wire.arrive(b_slots[row][0], lambda: q_b.at[row], device)
        wire.arrive(b_slots[row][1], lambda: o_b.at[row], device)
        for kept, came, result in (
            (cut(q_work.at[0], which), q_b.at[row], cut(qkv_out, which)),
            (cut(o_work.at[0], which), o_b.at[row], cut(o_out, which)),
        ):

            def body(start, kept=kept, came=came, result=result):
                part = pl.ds(start, 16)
                result[part] = kept[part].astype(F32) + came[part].astype(F32)

            rows_loop(kept.shape[0], 16, body)
    line.last()
    mine = work.at[t]

    def body(start):
        part = pl.ds(start, 16)
        grad_in[part] = grad_middle[part] + own_sum(
            mine, up_in.at[extent - 2], down_in.at[extent - 2], part, pl.ds(0, width)
        )

    rows_loop(rows, 16, body)
    total = small_sum[d]
    for bits in range(1, 8):
        wire.arrive(
            last_slots[bits], lambda bits=bits: small_last.at[bits], (flip(d, bits), t)
        )
        total = total + small_last[bits]
    small_out[...] = total
    wire.finish()


def close(extent, partial, grad_middle, grad_qkv, grad_o, small, gains):
    rows, width = grad_middle.shape
    depth, q_width = grad_qkv.shape[0] // 8, grad_qkv.shape[1]
    o_rows, o_width = grad_o.shape[0], grad_o.shape[1] // 8
    scratch = [
        pltpu.VMEM((extent, rows, width), BF),
        pltpu.VMEM((extent - 1, rows, width), BF),
        pltpu.VMEM((extent - 1, rows, width), BF),
    ]
    for tall, wide in ((depth, q_width), (o_rows, o_width)):
        scratch += [
            pltpu.VMEM((4, tall, wide), BF),
            pltpu.VMEM((4, tall, wide), BF),
            pltpu.VMEM((4, tall // 2, wide), BF),
            pltpu.VMEM((2, tall // 2, wide), BF),
        ]
    scratch += [
        pltpu.VMEM((extent - 1, 8, 16, 128), F32),
        pltpu.VMEM((8, 24, 128), F32),
        pltpu.VMEM((8, 24, 128), F32),
    ]
    return pl.pallas_call(
        functools.partial(close_kernel, extent),
        out_shape=[
            jax.ShapeDtypeStruct((rows, width), F32),
            jax.ShapeDtypeStruct((depth, q_width), F32),
            jax.ShapeDtypeStruct((o_rows, o_width), F32),
            jax.ShapeDtypeStruct((24, 128), F32),
        ],
        in_specs=[ANY, VM, ANY, ANY, VM, VM],
        out_specs=[VM] * 4,
        scratch_shapes=scratch + dma_pair(64) + [pltpu.SemaphoreType.DMA((16,))],
        compiler_params=kernel_params(7),
        cost_estimate=pl.CostEstimate(flops=0, bytes_accessed=150_000_000, transcendentals=0),
    )(partial, grad_middle, grad_qkv, grad_o, small, gains)


def spread_kernel(*refs):
    pieces, outs = refs[:8], refs[8:]
    d = lax.axis_index("dp")
    for bits in range(8):
        first = 2 * flip(d, bits)
        for place in range(3):
            for e in range(2):
                outs[place][first + e] = pieces[bits][place, e].astype(F32)


def spread(pieces):
    shape = (16,) + pieces[0].shape[2:]
    return pl.pallas_call(
        spread_kernel,
        out_shape=[jax.ShapeDtypeStruct(shape, F32)] * 3,
        in_specs=[VM] * 8,
        out_specs=[VM] * 3,
        compiler_params=pltpu.CompilerParams(vmem_limit_bytes=VMEM_LIMIT),
        cost_estimate=pl.CostEstimate(flops=0, bytes_accessed=20_000_000, transcendentals=0),
    )(*pieces)


def exchange(value, bits):
    if bits == 0:
        return value
    return lax.ppermute(value, "dp", [(i, i ^ bits) for i in range(8)])


def per_device_block(
    hidden_in,
    teacher,
    lengths,
    routes,
    attn_norm_gain,
    ffn_norm_gain,
    q_weight,
    k_weight,
    v_weight,
    q_gain,
    k_gain,
    o_weight,
    router_weight,
    gate_weight,
    up_weight,
    down_weight,
):
    dp_count = lax.axis_size("dp")
    extent = lax.axis_size("tensor")
    d = lax.axis_index("dp")
    t = lax.axis_index("tensor")
    rows, width = hidden_in.shape
    seq_len = rows * extent
    all_tokens = seq_len * dp_count
    length = lengths[d]
    total_count = jnp.sum(lengths).astype(F32)
    attn_gain = attn_norm_gain.astype(F32)
    ffn_gain = ffn_norm_gain.astype(F32)[None, :]
    expert_count = router_weight.shape[1]
    head_width = q_gain.shape[1]
    local_heads = q_gain.shape[0]
    columns = local_heads * HD

    gains_own = lax.dynamic_update_slice(
        jnp.zeros((2 * local_heads, HD), F32),
        jnp.concatenate([q_gain, k_gain], axis=0).astype(F32),
        (0, d * head_width),
    )
    lane = jnp.arange(128)
    lane_expert = jnp.where(lane < 2 * expert_count, lane % expert_count, -1)
    routes_own = lax.dynamic_slice_in_dim(routes, t * rows, rows, 0)
    chosen = jnp.any(routes_own[:, :, None] == lane_expert[None, None, :], axis=1).astype(F32)
    blank = jnp.zeros((width, 128 - 2 * expert_count), BF)
    router_wide = jnp.concatenate([router_weight, router_weight, blank], axis=1)
    router_t = jnp.concatenate(
        [router_weight.T, jnp.zeros((128 - expert_count, width), BF)], axis=0
    )
    angles = np.arange(seq_len)[:, None] * THETA ** (-np.arange(HD // 2) / (HD // 2))[None, :]
    cosine = jnp.asarray(np.concatenate([np.cos(angles)] * 2, axis=1), F32)
    sine = jnp.asarray(np.concatenate([-np.sin(angles), np.sin(angles)], axis=1), F32)
    (
        middle,
        gates,
        ffn_own,
        head_gain,
        inverses,
        hidden_bf,
        qkv_full,
        o_full,
        normed,
        units,
        low,
        probs,
        mixed,
        tokens,
        hidden,
        expert_partial,
        landed,
    ) = front(
        extent,
        length[None],
        hidden_in,
        q_weight,
        k_weight,
        v_weight,
        o_weight,
        gains_own,
        gate_weight,
        up_weight,
        down_weight,
        attn_gain[None, :],
        cosine,
        sine,
        ffn_gain,
        router_wide,
        chosen,
    )
    attn_operands = (hidden_bf, attn_gain[None, :], qkv_full, o_full, head_gain, cosine, sine)
    own_positions = t * rows + jnp.arange(rows)
    row_scale = jnp.where(own_positions < length, all_tokens / total_count, 0.0)
    grad_output, row_loss, ffn_grad_partial, inner, active, grads = turn(
        extent,
        expert_partial,
        middle,
        teacher,
        jnp.broadcast_to(row_scale[:, None], (rows, 128)),
        tokens,
        hidden,
        landed,
        gate_weight,
        up_weight,
        down_weight,
    )
    grad_middle, grad_logits, ffn_gain_part, attn_grad_rows, *came = leave(
        extent,
        ffn_grad_partial,
        middle,
        grad_output,
        gates,
        chosen,
        ffn_gain,
        router_t,
        (tokens, grads, inner, active),
    )
    expert_grads = came[:6] + [exchange(came[bits], bits) for bits in (6, 7)]
    attn_grad_rows = attn_grad_rows.reshape(seq_len, width)
    router_part = jnp.einsum(
        "sd,se->de",
        ffn_own,
        grad_logits[:, :expert_count],
        precision=HIGHEST,
        preferred_element_type=F32,
    )
    input_part, grad_qkv, grad_o, attn_gain_part, gains_part, loss_rows = attend_back(
        extent,
        attn_grad_rows,
        row_loss,
        *attn_operands,
        normed,
        units,
        low,
        probs,
        mixed,
        inverses,
    )
    loss_group = loss_rows[2, :1] / (2.0 * width * all_tokens)
    attn_gain_part = jnp.sum(attn_gain_part, axis=0)

    split = width // (dp_count * extent)
    small = jnp.concatenate(
        [
            jnp.concatenate(
                [
                    attn_gain_part.reshape(dp_count, extent, 1, split),
                    jnp.sum(ffn_gain_part, axis=0).reshape(dp_count, extent, 1, split),
                ],
                axis=3,
            ),
            router_part.reshape(dp_count, extent, split * expert_count // 128, 128),
            jnp.zeros((dp_count, extent, 15 - split * expert_count // 128, 128), F32),
        ],
        axis=2,
    ).transpose(1, 0, 2, 3)
    grad_in, qkv_out, o_out, small_out = close(
        extent,
        input_part.reshape(extent, rows, width),
        grad_middle,
        grad_qkv,
        grad_o,
        small,
        gains_part,
    )
    grad_gate, grad_up, grad_down = spread(expert_grads)
    router_out = small_out[1 : 1 + split * expert_count // 128].reshape(split, expert_count)
    gain_out = lax.dynamic_slice(small_out, (16, d * head_width), (2 * local_heads, head_width))
    return (
        loss_group,
        grad_in,
        small_out[0, :split],
        small_out[0, split : 2 * split],
        qkv_out[:, :columns],
        qkv_out[:, columns : 2 * columns],
        qkv_out[:, 2 * columns :],
        gain_out[:local_heads],
        gain_out[local_heads:],
        o_out,
        router_out,
        grad_gate,
        grad_up,
        grad_down,
    )


def solution(mesh):
    placed = (
        P(("dp", "tensor"), None),
        P(("dp", "tensor"), None),
        P(),
        P("dp", None),
        P(),
        P(),
        P("dp", "tensor"),
        P("dp", "tensor"),
        P("dp", "tensor"),
        P("tensor", "dp"),
        P("tensor", "dp"),
        P("tensor", "dp"),
        P(),
        P(None, "dp", "tensor"),
        P(None, "dp", "tensor"),
        P(None, "tensor", "dp"),
    )
    block = mesh.shape["dp"] == 8 and mesh.shape["tensor"] == 4
    return jax.shard_map(
        per_device_block if block else per_device,
        mesh=mesh,
        in_specs=placed,
        out_specs=(
            P("dp"),
            P(("dp", "tensor"), None),
            P(("dp", "tensor")),
            P(("dp", "tensor")),
            P("dp", "tensor"),
            P("dp", "tensor"),
            P("dp", "tensor"),
            P("tensor", "dp"),
            P("tensor", "dp"),
            P("tensor", "dp"),
            P(("dp", "tensor"), None),
            P(None, "dp", "tensor"),
            P(None, "dp", "tensor"),
            P(None, "tensor", "dp"),
        ),
        check_vma=False,
    )
```

```python
import functools
import math

import jax
import jax.numpy as jnp
import numpy as np
from jax import lax
from jax.experimental import pallas as pl
from jax.experimental.pallas import tpu as pltpu
from jax.sharding import PartitionSpec as P

HD = 128
TOK_DEV = 128
CAP = 68


EPSILON = 1e-05
THETA = 10000.0
HIGHEST = lax.Precision.HIGHEST


def inverse_rms(value):
    return lax.rsqrt(jnp.mean(value * value, axis=-1, keepdims=True) + EPSILON)


def rotate(value, cosine, sinus_table, direction):
    middle_index = value.shape[-1] // 2
    leading = value[..., :middle_index]
    trailing = value[..., middle_index:]
    return jnp.concatenate(
        [
            leading * cosine - direction * trailing * sinus_table,
            trailing * cosine + direction * leading * sinus_table,
        ],
        axis=-1,
    )


def norm_backward(grad_norm, unit_rows, inverse_rows, gain_row):
    scaled = grad_norm * gain_row
    return inverse_rows * (
        scaled - unit_rows * jnp.mean(scaled * unit_rows, axis=-1, keepdims=True)
    )


def fetch_attention(q_weight, k_weight, v_weight, o_weight, q_gain, k_gain):
    return (
        lax.all_gather(q_weight, "dp", axis=0, tiled=True),
        lax.all_gather(k_weight, "dp", axis=0, tiled=True),
        lax.all_gather(v_weight, "dp", axis=0, tiled=True),
        lax.all_gather(o_weight, "dp", axis=1, tiled=True),
        lax.all_gather(q_gain, "dp", axis=1, tiled=True),
        lax.all_gather(k_gain, "dp", axis=1, tiled=True),
    )


def fetch_experts(gate_weight, up_weight, down_weight):
    return (
        lax.all_gather(gate_weight, "dp", axis=1, tiled=True),
        lax.all_gather(up_weight, "dp", axis=1, tiled=True),
        lax.all_gather(down_weight, "dp", axis=2, tiled=True),
    )


def per_device(
    hidden_in,
    teacher,
    lengths,
    routes,
    attn_norm_gain,
    ffn_norm_gain,
    q_weight,
    k_weight,
    v_weight,
    q_gain,
    k_gain,
    o_weight,
    router_weight,
    gate_weight,
    up_weight,
    down_weight,
):
    dp_count = lax.axis_size("dp")
    tp_count = lax.axis_size("tensor")
    group_index = lax.axis_index("dp")
    member = lax.axis_index("tensor")
    row_count, model_width = hidden_in.shape
    seq_len = row_count * tp_count
    all_tokens = seq_len * dp_count
    length = lengths[group_index]
    total_count = jnp.sum(lengths).astype(jnp.float32)
    attn_gain = attn_norm_gain.astype(jnp.float32)
    ffn_gain = ffn_norm_gain.astype(jnp.float32)
    root_size = math.sqrt(HD)
    q_full, k_full, v_full, o_full, qgain_full, kgain_full = fetch_attention(
        q_weight, k_weight, v_weight, o_weight, q_gain, k_gain
    )
    local_heads = q_full.shape[1] // HD
    hidden_all = lax.all_gather(hidden_in, "tensor", axis=0, tiled=True).astype(jnp.float32)
    inverse_one = inverse_rms(hidden_all)
    unit_one = hidden_all * inverse_one
    normed = (unit_one * attn_gain).astype(jnp.bfloat16)
    query_raw = jnp.dot(normed, q_full, preferred_element_type=jnp.float32)
    key_raw = jnp.dot(normed, k_full, preferred_element_type=jnp.float32)
    value_low = jnp.dot(normed, v_full, preferred_element_type=jnp.float32).astype(jnp.bfloat16)
    query_sq, key_sq = lax.psum(
        (jnp.sum(query_raw * query_raw, axis=1), jnp.sum(key_raw * key_raw, axis=1)), "tensor"
    )
    query_inv = lax.rsqrt(query_sq / model_width + EPSILON)[:, None]
    key_inv = lax.rsqrt(key_sq / model_width + EPSILON)[:, None]
    query_unit = query_raw * query_inv
    key_unit = key_raw * key_inv
    query_gain = qgain_full.astype(jnp.float32).reshape(-1)
    key_gain = kgain_full.astype(jnp.float32).reshape(-1)
    positions = jnp.arange(seq_len)
    frequency = THETA ** (-jnp.arange(HD // 2).astype(jnp.float32) / (HD // 2))
    angles = positions.astype(jnp.float32)[:, None] * frequency[None, :]
    cosine = jnp.cos(angles)[:, None, :]
    sinus_table = jnp.sin(angles)[:, None, :]
    queries = rotate(
        (query_unit * query_gain).reshape(seq_len, local_heads, HD), cosine, sinus_table, 1.0
    ).astype(jnp.bfloat16)
    key_rows = rotate(
        (key_unit * key_gain).reshape(seq_len, local_heads, HD), cosine, sinus_table, 1.0
    ).astype(jnp.bfloat16)
    value_rows = value_low.reshape(seq_len, local_heads, HD)
    block_rows = min(512, seq_len)
    starts = jnp.arange(seq_len // block_rows) * block_rows

    def block_scores(start):
        query_block = lax.dynamic_slice_in_dim(queries, start, block_rows, 0)
        scores = (
            jnp.einsum("qhd,khd->hqk", query_block, key_rows, preferred_element_type=jnp.float32)
            / root_size
        )
        query_pos = start + jnp.arange(block_rows)
        allowed = (positions[None, :] <= query_pos[:, None]) & (positions[None, :] < length)
        return (query_block, jnp.where(allowed[None], scores, -1e30))

    def attend(start):
        unused_block, scores = block_scores(start)
        row_top = jnp.max(scores, axis=-1, keepdims=True)
        exponent = jnp.exp(scores - row_top)
        row_total = jnp.sum(exponent, axis=-1, keepdims=True)
        weights = (exponent / row_total).astype(jnp.bfloat16)
        mixed_block = jnp.einsum(
            "hqk,khd->qhd", weights, value_rows, preferred_element_type=jnp.float32
        )
        return (mixed_block.astype(jnp.bfloat16), (row_top + jnp.log(row_total))[..., 0])

    mixed_blocks, log_totals = lax.map(attend, starts)
    mixed = mixed_blocks.reshape(seq_len, local_heads * HD)
    attn_own = lax.psum_scatter(
        jnp.dot(mixed, o_full, preferred_element_type=jnp.float32).astype(jnp.bfloat16),
        "tensor",
        scatter_dimension=0,
        tiled=True,
    ).astype(jnp.float32)
    middle = hidden_in.astype(jnp.float32) + attn_own
    inverse_two = inverse_rms(middle)
    unit_two = middle * inverse_two
    ffn_own = (unit_two * ffn_gain).astype(jnp.bfloat16)
    gate_full, up_full, down_full = fetch_experts(gate_weight, up_weight, down_weight)
    ffn_all = lax.all_gather(ffn_own, "tensor", axis=0, tiled=True)
    expert_count = router_weight.shape[1]
    route_width = routes.shape[1]
    gate_probs = jax.nn.softmax(
        jnp.dot(ffn_all, router_weight, preferred_element_type=jnp.float32), axis=-1
    )
    picked = routes[:, :, None] == jnp.arange(expert_count)[None, None, :]
    route_gates = jnp.sum(jnp.where(picked, gate_probs[:, None, :], 0.0), axis=-1)
    block_count = seq_len // TOK_DEV
    per_expert = block_count * CAP
    picked_ints = picked.reshape(block_count, TOK_DEV * route_width, expert_count).astype(jnp.int32)
    slot_ranks = jnp.sum((jnp.cumsum(picked_ints, axis=1) - 1) * picked_ints, axis=-1).reshape(
        seq_len, route_width
    )
    block_ids = (positions // TOK_DEV)[:, None]
    slot_ids = (routes * per_expert + block_ids * CAP + slot_ranks).reshape(-1)
    slot_total = expert_count * per_expert
    token_ids = jnp.repeat(positions, route_width)
    group_width = 4
    turn_count = expert_count // group_width
    sources = (
        jnp.full((slot_total,), seq_len, jnp.int32)
        .at[slot_ids]
        .set(token_ids)
        .reshape(turn_count, group_width, per_expert)
    )
    slot_gates = (
        jnp.zeros((slot_total,), jnp.float32)
        .at[slot_ids]
        .set(route_gates.reshape(-1))
        .reshape(turn_count, group_width, per_expert, 1)
    )
    ffn_padded = jnp.concatenate([ffn_all, jnp.zeros((1, model_width), jnp.bfloat16)], axis=0)
    expert_running = jnp.zeros((seq_len + 1, model_width), jnp.float32)
    kept_values = []
    for turn_index in range(turn_count):
        lower = turn_index * group_width
        upper = lower + group_width
        expert_inputs = ffn_padded[sources[turn_index]]
        gate_value = jnp.einsum(
            "gpd,gdf->gpf",
            expert_inputs,
            gate_full[lower:upper],
            preferred_element_type=jnp.float32,
        )
        up_value = jnp.einsum(
            "gpd,gdf->gpf", expert_inputs, up_full[lower:upper], preferred_element_type=jnp.float32
        )
        active = (slot_gates[turn_index] * jax.nn.silu(gate_value) * up_value).astype(jnp.bfloat16)
        expert_outputs = jnp.einsum(
            "gpf,gfd->gpd", active, down_full[lower:upper], preferred_element_type=jnp.float32
        )
        expert_running = expert_running.at[sources[turn_index].reshape(-1)].add(
            expert_outputs.reshape(-1, model_width)
        )
        kept_values.append((gate_value, up_value, active))
    expert_own = lax.psum_scatter(
        expert_running[:seq_len].astype(jnp.bfloat16), "tensor", scatter_dimension=0, tiled=True
    ).astype(jnp.float32)
    output = middle + expert_own
    own_positions = member * row_count + jnp.arange(row_count)
    valid_rows = (own_positions < length)[:, None]
    mismatch = output - teacher.astype(jnp.float32)
    loss_own = jnp.sum(jnp.where(valid_rows, mismatch * mismatch, 0.0)) / (
        2.0 * model_width * total_count
    )
    grad_output = jnp.where(valid_rows, mismatch * (all_tokens / total_count), 0.0)
    grad_rows = lax.all_gather(grad_output.astype(jnp.bfloat16), "tensor", axis=0, tiled=True)
    gate_full, up_full, down_full = fetch_experts(gate_weight, up_weight, down_weight)
    grad_padded = jnp.concatenate([grad_rows, jnp.zeros((1, model_width), jnp.bfloat16)], axis=0)
    ffn_grad_running = jnp.zeros((seq_len + 1, model_width), jnp.float32)
    gate_grads = []
    up_grads = []
    down_grads = []
    slot_grads = []
    for turn_index in range(turn_count):
        gate_value, up_value, active = kept_values[turn_index]
        lower = turn_index * group_width
        upper = lower + group_width
        source_rows = sources[turn_index]
        expert_inputs = ffn_padded[source_rows]
        incoming = grad_padded[source_rows]
        grad_active = jnp.einsum(
            "gpd,gfd->gpf", incoming, down_full[lower:upper], preferred_element_type=jnp.float32
        )
        down_turn = jnp.einsum("gpf,gpd->gfd", active, incoming, preferred_element_type=jnp.float32)
        sigmoid_value = jax.nn.sigmoid(gate_value)
        silu_value = gate_value * sigmoid_value
        slot_grads.append(jnp.sum(grad_active * silu_value * up_value, axis=-1))
        grad_inner = grad_active * slot_gates[turn_index]
        grad_gate_value = (
            grad_inner * up_value * sigmoid_value * (1.0 + gate_value * (1.0 - sigmoid_value))
        ).astype(jnp.bfloat16)
        grad_up_value = (grad_inner * silu_value).astype(jnp.bfloat16)
        gate_turn = jnp.einsum(
            "gpd,gpf->gdf", expert_inputs, grad_gate_value, preferred_element_type=jnp.float32
        )
        up_turn = jnp.einsum(
            "gpd,gpf->gdf", expert_inputs, grad_up_value, preferred_element_type=jnp.float32
        )
        gate_grads.append(gate_turn)
        up_grads.append(up_turn)
        down_grads.append(down_turn)
        grad_inputs = jnp.einsum(
            "gpf,gdf->gpd",
            grad_gate_value,
            gate_full[lower:upper],
            preferred_element_type=jnp.float32,
        )
        grad_inputs = grad_inputs + jnp.einsum(
            "gpf,gdf->gpd", grad_up_value, up_full[lower:upper], preferred_element_type=jnp.float32
        )
        ffn_grad_running = ffn_grad_running.at[source_rows.reshape(-1)].add(
            grad_inputs.reshape(-1, model_width)
        )
    slot_grad_all = jnp.concatenate([entry.reshape(-1) for entry in slot_grads])
    route_grads = slot_grad_all[slot_ids].reshape(seq_len, route_width)
    grad_probs = jnp.sum(jnp.where(picked, route_grads[:, :, None], 0.0), axis=1)
    grad_logits = gate_probs * (
        grad_probs - jnp.sum(grad_probs * gate_probs, axis=-1, keepdims=True)
    )
    router_float = router_weight.astype(jnp.float32)
    ffn_grad_part = ffn_grad_running[:seq_len] + jnp.einsum(
        "se,de->sd", grad_logits, router_float, precision=HIGHEST
    )
    router_part = jnp.einsum(
        "sd,se->de", ffn_all, grad_logits, precision=HIGHEST, preferred_element_type=jnp.float32
    )
    ffn_grad_own = lax.psum_scatter(
        ffn_grad_part.astype(jnp.bfloat16), "tensor", scatter_dimension=0, tiled=True
    ).astype(jnp.float32)
    ffn_gain_part = jnp.sum(ffn_grad_own * unit_two, axis=0)
    grad_middle = grad_output + norm_backward(ffn_grad_own, unit_two, inverse_two, ffn_gain)
    attn_grad_rows = lax.all_gather(grad_middle.astype(jnp.bfloat16), "tensor", axis=0, tiled=True)
    q_full, k_full, v_full, o_full, qgain_full, kgain_full = fetch_attention(
        q_weight, k_weight, v_weight, o_weight, q_gain, k_gain
    )
    grad_o = jnp.einsum("sa,sb->ab", mixed, attn_grad_rows, preferred_element_type=jnp.float32)
    grad_mixed = (
        jnp.einsum("sb,ab->sa", attn_grad_rows, o_full, preferred_element_type=jnp.float32)
        .astype(jnp.bfloat16)
        .reshape(seq_len, local_heads, HD)
    )

    def attend_back(carry, inputs):
        key_running, value_running = carry
        start, log_total = inputs
        query_block, scores = block_scores(start)
        probs_float = jnp.exp(scores - log_total[..., None])
        probs_low = probs_float.astype(jnp.bfloat16)
        grad_block = lax.dynamic_slice_in_dim(grad_mixed, start, block_rows, 0)
        value_running = value_running + jnp.einsum(
            "hqk,qhd->khd", probs_low, grad_block, preferred_element_type=jnp.float32
        )
        grad_weights = jnp.einsum(
            "qhd,khd->hqk", grad_block, value_rows, preferred_element_type=jnp.float32
        )
        grad_scores = (
            probs_float
            * (grad_weights - jnp.sum(grad_weights * probs_float, axis=-1, keepdims=True))
        ).astype(jnp.bfloat16)
        query_grad_block = (
            jnp.einsum("hqk,khd->qhd", grad_scores, key_rows, preferred_element_type=jnp.float32)
            / root_size
        )
        key_running = (
            key_running
            + jnp.einsum(
                "hqk,qhd->khd", grad_scores, query_block, preferred_element_type=jnp.float32
            )
            / root_size
        )
        return ((key_running, value_running), query_grad_block)

    zero_heads = jnp.zeros((seq_len, local_heads, HD), jnp.float32)
    (key_grad_rot, value_grad), query_grad_blocks = lax.scan(
        attend_back, (zero_heads, zero_heads), (starts, log_totals)
    )
    query_grad = rotate(
        query_grad_blocks.reshape(seq_len, local_heads, HD), cosine, sinus_table, -1.0
    ).reshape(seq_len, local_heads * HD)
    key_grad = rotate(key_grad_rot, cosine, sinus_table, -1.0).reshape(seq_len, local_heads * HD)
    query_scaled = query_grad * query_gain
    key_scaled = key_grad * key_gain
    qgain_part = jnp.sum(query_grad * query_unit, axis=0)
    kgain_part = jnp.sum(key_grad * key_unit, axis=0)
    query_dot, key_dot, loss_group = lax.psum(
        (
            jnp.sum(query_scaled * query_unit, axis=1),
            jnp.sum(key_scaled * key_unit, axis=1),
            loss_own,
        ),
        "tensor",
    )
    query_raw_grad = (
        query_inv * (query_scaled - query_unit * (query_dot / model_width)[:, None])
    ).astype(jnp.bfloat16)
    key_raw_grad = (key_inv * (key_scaled - key_unit * (key_dot / model_width)[:, None])).astype(
        jnp.bfloat16
    )
    value_raw_grad = value_grad.reshape(seq_len, local_heads * HD).astype(jnp.bfloat16)
    grad_q = jnp.einsum("sd,sa->da", normed, query_raw_grad, preferred_element_type=jnp.float32)
    grad_k = jnp.einsum("sd,sa->da", normed, key_raw_grad, preferred_element_type=jnp.float32)
    grad_v = jnp.einsum("sd,sa->da", normed, value_raw_grad, preferred_element_type=jnp.float32)
    normed_grad = jnp.einsum(
        "sa,da->sd", query_raw_grad, q_full, preferred_element_type=jnp.float32
    )
    normed_grad = normed_grad + jnp.einsum(
        "sa,da->sd", key_raw_grad, k_full, preferred_element_type=jnp.float32
    )
    normed_grad = normed_grad + jnp.einsum(
        "sa,da->sd", value_raw_grad, v_full, preferred_element_type=jnp.float32
    )
    attn_gain_part = jnp.sum(normed_grad * unit_one, axis=0)
    input_part = norm_backward(normed_grad, unit_one, inverse_one, attn_gain)
    split_width = model_width // (dp_count * tp_count)
    input_own, attn_gain_share, ffn_gain_share, router_share = (
        lax.psum_scatter(
            input_part.astype(jnp.bfloat16), "tensor", scatter_dimension=0, tiled=True
        ).astype(jnp.float32),
        lax.psum_scatter(
            attn_gain_part.reshape(dp_count, tp_count, split_width).astype(jnp.bfloat16),
            "tensor",
            scatter_dimension=1,
            tiled=True,
        ).astype(jnp.float32),
        lax.psum_scatter(
            ffn_gain_part.reshape(dp_count, tp_count, split_width).astype(jnp.bfloat16),
            "tensor",
            scatter_dimension=1,
            tiled=True,
        ).astype(jnp.float32),
        lax.psum_scatter(
            router_part.reshape(dp_count, tp_count, split_width, expert_count).astype(jnp.bfloat16),
            "tensor",
            scatter_dimension=1,
            tiled=True,
        ).astype(jnp.float32),
    )
    grad_in = grad_middle + input_own
    (
        grad_q,
        grad_k,
        grad_v,
        grad_o,
        grad_qgain,
        grad_kgain,
        attn_gain_sum,
        ffn_gain_sum,
        router_sum,
    ) = (
        lax.psum_scatter(grad_q.astype(jnp.bfloat16), "dp", scatter_dimension=0, tiled=True).astype(
            jnp.float32
        ),
        lax.psum_scatter(grad_k.astype(jnp.bfloat16), "dp", scatter_dimension=0, tiled=True).astype(
            jnp.float32
        ),
        lax.psum_scatter(grad_v.astype(jnp.bfloat16), "dp", scatter_dimension=0, tiled=True).astype(
            jnp.float32
        ),
        lax.psum_scatter(grad_o.astype(jnp.bfloat16), "dp", scatter_dimension=1, tiled=True).astype(
            jnp.float32
        ),
        lax.psum_scatter(
            qgain_part.reshape(local_heads, HD).astype(jnp.bfloat16),
            "dp",
            scatter_dimension=1,
            tiled=True,
        ).astype(jnp.float32),
        lax.psum_scatter(
            kgain_part.reshape(local_heads, HD).astype(jnp.bfloat16),
            "dp",
            scatter_dimension=1,
            tiled=True,
        ).astype(jnp.float32),
        lax.psum_scatter(
            attn_gain_share.astype(jnp.bfloat16), "dp", scatter_dimension=0, tiled=True
        ).astype(jnp.float32),
        lax.psum_scatter(
            ffn_gain_share.astype(jnp.bfloat16), "dp", scatter_dimension=0, tiled=True
        ).astype(jnp.float32),
        lax.psum_scatter(
            router_share.astype(jnp.bfloat16), "dp", scatter_dimension=0, tiled=True
        ).astype(jnp.float32),
    )
    grad_gate, grad_up, grad_down = (
        lax.psum_scatter(
            jnp.concatenate(gate_grads, axis=0).astype(jnp.bfloat16),
            "dp",
            scatter_dimension=1,
            tiled=True,
        ).astype(jnp.float32),
        lax.psum_scatter(
            jnp.concatenate(up_grads, axis=0).astype(jnp.bfloat16),
            "dp",
            scatter_dimension=1,
            tiled=True,
        ).astype(jnp.float32),
        lax.psum_scatter(
            jnp.concatenate(down_grads, axis=0).astype(jnp.bfloat16),
            "dp",
            scatter_dimension=2,
            tiled=True,
        ).astype(jnp.float32),
    )
    return (
        loss_group.reshape(1),
        grad_in,
        attn_gain_sum.reshape(-1),
        ffn_gain_sum.reshape(-1),
        grad_q,
        grad_k,
        grad_v,
        grad_qgain,
        grad_kgain,
        grad_o,
        router_sum.reshape(-1, expert_count),
        grad_gate,
        grad_up,
        grad_down,
    )


MESH = pl.DeviceIdType.MESH
BF = jnp.bfloat16
F32 = jnp.float32
VMEM_LIMIT = 62 * 1024 * 1024
ANY = pl.BlockSpec(memory_space=pl.ANY)
VM = pl.BlockSpec(memory_space=pltpu.VMEM)


def flip(index, bits):
    for bit in (1, 2, 4):
        if bits & bit:
            index = index + bit * (1 - 2 * ((index // bit) % 2))
    return index


def both(first, second):
    return jnp.logical_and(first, second)


def under(condition, action):
    if condition is None:
        action()
    else:
        pl.when(condition)(action)


class Wire:
    def __init__(self, send_sem, recv_sem):
        self.send_sem, self.recv_sem, self.count, self.sent = send_sem, recv_sem, 0, []

    def slot(self):
        self.count += 1
        return self.count - 1

    def start(self, slot, source, target, device, condition=None):
        def make():
            return pltpu.make_async_remote_copy(
                src_ref=source(),
                dst_ref=target(),
                send_sem=self.send_sem.at[slot],
                recv_sem=self.recv_sem.at[slot],
                device_id=device,
                device_id_type=MESH,
            )

        under(condition, lambda: make().start())
        self.sent.append((condition, make))

    def arrive(self, slot, region, device, condition=None):
        copy = pltpu.make_async_remote_copy(
            src_ref=region(),
            dst_ref=region(),
            send_sem=self.send_sem.at[slot],
            recv_sem=self.recv_sem.at[slot],
            device_id=device,
            device_id_type=MESH,
        )
        under(condition, lambda: copy.wait_recv())

    def finish(self):
        for condition, make in self.sent:
            under(condition, lambda make=make: make().wait_send())
        self.sent = []


class Local:
    def __init__(self, sem):
        self.sem, self.count = sem, 0

    def start(self, source, target):
        copy = pltpu.make_async_copy(source, target, self.sem.at[self.count])
        self.count += 1
        copy.start()
        return copy


def greet(devices):
    barrier = pltpu.get_barrier_semaphore()
    for condition, device in devices:
        under(
            condition,
            lambda device=device: pl.semaphore_signal(
                barrier, inc=1, device_id=device, device_id_type=MESH
            ),
        )
    amount = sum(1 for condition, device in devices if condition is None)
    for condition, device in devices:
        if condition is not None:
            amount = amount + jnp.where(condition, 1, 0)
    pl.semaphore_wait(barrier, amount)


def line_devices(d, t, extent):
    return [(t < extent - 1, (d, t + 1)), (t > 0, (d, t - 1))]


def rows_loop(rows, step, body):
    def run(index, carry):
        body(pl.multiple_of(index * step, step))
        return carry

    lax.fori_loop(0, rows // step, run, 0)


def add_into(target, source, rows):
    def body(start):
        part = pl.ds(start, 16)
        target[part] = target[part] + source[part]

    rows_loop(rows, 16, body)


class LineGather:
    def __init__(self, wire, d, t, extent, own, place):
        self.wire, self.extent = wire, extent
        up = [wire.slot() for unused in range(extent - 1)]
        down = [wire.slot() for unused in range(extent - 1)]
        last = extent - 1
        above, below = (d, t + 1), (d, t - 1)
        self.first = (
            (up[0], own, lambda: place(t), above, t < last),
            (down[0], own, lambda: place(t), below, t > 0),
        )
        self.steps = {}
        for step in range(1, extent):
            from_below, from_above = t >= step, t <= last - step
            lower, upper = t - step, t + step
            self.steps[step] = (
                (
                    up,
                    lambda index=lower: place(index),
                    from_below,
                    both(from_below, t < last),
                    above,
                    below,
                ),
                (
                    down,
                    lambda index=upper: place(index),
                    from_above,
                    both(from_above, t > 0),
                    below,
                    above,
                ),
            )

    def begin(self):
        for slot, own, target, device, condition in self.first:
            self.wire.start(slot, own, target, device, condition)

    def step(self, step):
        for slots, region, valid, onward, to, source in self.steps[step]:
            self.wire.arrive(slots[step - 1], region, source, valid)
            if step < self.extent - 1:
                self.wire.start(slots[step], region, region, to, onward)


def arrival(t, turn):
    near = t - 1 + 2 * (1 - (t + 3) // 4)
    far = 3 * (1 - t // 2)
    choices = (t, near, 6 - t - near - far, far)
    if isinstance(turn, int):
        return choices[turn]
    result = choices[0]
    for number in range(1, 4):
        result = jnp.where(turn == number, choices[number], result)
    return result


LATE = 32


class PlaneGather:
    def __init__(self, wire, d, t, extent, own, place, bundle, rows):
        self.wire, self.place, self.bundle, self.own = wire, place, bundle, own
        self.early, self.half = rows - LATE, (rows - LATE) // 2
        self.to_x, self.to_y, self.to_c = (flip(d, 2), t), (flip(d, 4), t), (flip(d, 1), t)
        self.index = [arrival(t, turn) for turn in range(extent)]
        self.slots = {}
        late = lambda n: (self.early + n * (LATE // 2), LATE // 2)
        self.parts = {0: (0, self.half), 1: (self.half, self.half), 2: late(0), 3: late(1)}
        self.parts["early"], self.parts["late"] = (0, self.early), (self.early, LATE)
        self.send("gx", 0, self.source(0, "late"), self.spot(0, 0, 1, "late"), self.to_x)
        self.send("gy", 0, self.source(0, "late"), self.spot(0, 0, 2, "late"), self.to_y)
        here = self.index[0]
        self.line = LineGather(
            wire,
            d,
            t,
            extent,
            lambda: self.cut(own(), "early"),
            lambda j: self.cut(place(j, 0, 0), "early"),
        )
        self.late_line = LineGather(
            wire, d, t, extent, lambda: bundle(here, 0), lambda j: bundle(j, 0)
        )
        self.line.begin()
        self.stage_first(0)
        for name, i, which, onward, to, source in (
            ("gx", 1, 2, "gfy", self.to_y, self.to_x),
            ("gy", 2, 3, "gfx", self.to_x, self.to_y),
        ):
            self.wait(name, 0, self.spot(0, 0, i, "late"), source)
            self.send(onward, 0, self.spot(0, 0, i, which), self.spot(0, 0, 3, which), to)
        self.stage_second(0)

    def cut(self, ref, which):
        start, size = self.parts[which]
        return ref.at[pl.ds(start, size)]

    def send(self, name, turn, source, target, device):
        slot = self.wire.slot()
        self.slots[name, turn] = slot
        self.wire.start(slot, source, target, device)

    def wait(self, name, turn, region, device):
        self.wire.arrive(self.slots[name, turn], region, device)

    def spot(self, turn, c, i, which):
        return lambda: self.cut(self.place(self.index[turn], c, i), which)

    def source(self, turn, which):
        if turn == 0:
            return lambda: self.cut(self.own(), which)
        return self.spot(turn, 0, 0, which)

    def stage_first(self, turn):
        source, spot = self.source, self.spot
        self.send("x0", turn, source(turn, 0), spot(turn, 0, 1, 0), self.to_x)
        self.send("y1", turn, source(turn, 1), spot(turn, 0, 2, 1), self.to_y)

    def stage_second(self, turn):
        source, spot = self.source, self.spot
        self.send("x1", turn, source(turn, 1), spot(turn, 0, 1, 1), self.to_x)
        self.send("y0", turn, source(turn, 0), spot(turn, 0, 2, 0), self.to_y)
        self.send("c0", turn, source(turn, "early"), spot(turn, 1, 0, "early"), self.to_c)

    def stage(self, turn):
        self.stage_first(turn)
        self.stage_second(turn)

    def relay(self, turn):
        spot = self.spot
        self.wait("x0", turn, spot(turn, 0, 1, 0), self.to_x)
        self.send("fy", turn, spot(turn, 0, 1, 0), spot(turn, 0, 3, 0), self.to_y)
        self.wait("y1", turn, spot(turn, 0, 2, 1), self.to_y)
        self.send("fx", turn, spot(turn, 0, 2, 1), spot(turn, 0, 3, 1), self.to_x)
        self.wait("x1", turn, spot(turn, 0, 1, 1), self.to_x)
        self.send("c1", turn, spot(turn, 0, 1, "early"), spot(turn, 1, 1, "early"), self.to_c)
        self.wait("y0", turn, spot(turn, 0, 2, 0), self.to_y)
        self.send("c2", turn, spot(turn, 0, 2, "early"), spot(turn, 1, 2, "early"), self.to_c)

    def corner(self, turn):
        spot = self.spot
        self.wait("fy", turn, spot(turn, 0, 3, 0), self.to_y)
        self.wait("fx", turn, spot(turn, 0, 3, 1), self.to_x)
        self.send("c3", turn, spot(turn, 0, 3, "early"), spot(turn, 1, 3, "early"), self.to_c)

    def pass_bundle(self, turn):
        region = lambda c: (lambda: self.bundle(self.index[turn], c))
        self.send("cb", turn, region(0), region(1), self.to_c)

    def bundle_start(self, unused):
        spot = self.spot
        self.wait("gfy", 0, spot(0, 0, 3, 2), self.to_y)
        self.wait("gfx", 0, spot(0, 0, 3, 3), self.to_x)
        self.late_line.begin()
        self.pass_bundle(0)

    def bundle_step(self, step):
        self.late_line.step(step)
        self.pass_bundle(step)

    def other(self, turn):
        for i in range(4):
            self.wait("c%d" % i, turn, self.spot(turn, 1, i, "early"), self.to_c)
        self.wait("cb", turn, lambda: self.bundle(self.index[turn], 1), self.to_c)

    def actions(self):
        line, stage, relay, corner, other, late = (
            self.line.step,
            self.stage,
            self.relay,
            self.corner,
            self.other,
            self.bundle_step,
        )
        return (
            (
                (line, 1),
                (stage, 1),
                (self.bundle_start, 0),
                (relay, 0),
                (line, 2),
                (stage, 2),
                (corner, 0),
            ),
            ((relay, 1), (late, 1), (other, 0)),
            ((relay, 2), (line, 3), (stage, 3), (corner, 1)),
            ((other, 1),),
            ((late, 2), (corner, 2), (relay, 3)),
            ((other, 2),),
            ((late, 3), (corner, 3)),
            ((other, 3),),
        )


class LineSum:
    def __init__(self, wire, d, t, extent, block, up_in, down_in, rows, parts):
        self.wire, self.d, self.t, self.extent = wire, d, t, extent
        self.block, self.up_in, self.down_in = block, up_in, down_in
        self.rows, self.parts = rows // parts, parts
        self.up = [[wire.slot() for p in range(parts)] for s in range(extent - 1)]
        self.down = [[wire.slot() for p in range(parts)] for s in range(extent - 1)]

    def cut(self, ref, part):
        return ref.at[pl.ds(part * self.rows, self.rows)]

    def add(self, target, source):
        add_into(target, source, self.rows)

    def flow(self, step, part, near, index, slots, buffers, to_device, from_device):
        wire, extent = self.wire, self.extent
        block = lambda: self.cut(self.block(index), part)
        if step >= 1:
            source = lambda: self.cut(buffers.at[step - 1], part)
            active = both(both(near <= step, near < extent - 1), near >= 1)
            wire.arrive(slots[step - 1][part], source, from_device, active)
            under(active, lambda: self.add(block(), source()))
        wire.start(
            slots[step][part],
            block,
            lambda: self.cut(buffers.at[step], part),
            to_device,
            both(near <= step, near < extent - 1),
        )

    def step(self, step):
        d, t, extent = self.d, self.t, self.extent
        up, down = extent - 1 - step + t, step + t - (extent - 1)
        above, below = (d, t + 1), (d, t - 1)
        for part in range(self.parts):
            self.flow(step, part, t, up, self.up, self.up_in, above, below)
            self.flow(step, part, extent - 1 - t, down, self.down, self.down_in, below, above)

    def last(self):
        d, t, extent = self.d, self.t, self.extent
        for ready, missing, slots, buffers, device in (
            (t > 0, t == 0, self.up, self.up_in, (d, t - 1)),
            (t < extent - 1, t == extent - 1, self.down, self.down_in, (d, t + 1)),
        ):
            buffer = buffers.at[extent - 2]
            for part in range(self.parts):
                self.wire.arrive(
                    slots[extent - 2][part],
                    lambda part=part, buffer=buffer: self.cut(buffer, part),
                    device,
                    ready,
                )

            def clear(buffer=buffer):
                buffer[...] = jnp.zeros(buffer.shape, BF)

            under(missing, clear)


class BundleSum(LineSum):
    def cut(self, ref, part):
        return ref

    def add(self, target, source):
        for i in range(4):
            add_into(target.at[i], source.at[i], LATE)


def own_sum(block, up_in, down_in, part, columns):
    return (
        block[part, columns].astype(F32)
        + up_in[part, columns].astype(F32)
        + down_in[part, columns].astype(F32)
    )


def plane_order(t):
    top = t // 2
    inner = ((t + 1) // 2) % 2
    return (
        3 - 3 * top,
        2 - top,
        (1 - inner) * (1 - top) + (2 + inner) * top,
        inner * (1 - top) + (3 - inner) * top,
    )


def sum_plane(wire, local, d, t, extent, partial, buffers, rows, between=lambda turn: None):
    (
        work,
        own_in,
        a_in,
        b_in,
        up_in,
        down_in,
        late_up,
        late_down,
        late_a,
        late_b,
    ) = buffers
    order = plane_order(t)
    early, half = rows - LATE, (rows - LATE) // 2
    to_x, to_y, to_c = (flip(d, 2), t), (flip(d, 4), t), (flip(d, 1), t)
    turns = (3, 1, 2, 0)
    slots_c, slots_a, slots_b, loads = {}, {}, {}, {}

    def cut(ref, which):
        return ref.at[pl.ds(which * half, half)]

    def late_cut(ref, which):
        return ref.at[pl.ds(early + which * (LATE // 2), LATE // 2)]

    def begin(k):
        for i in turns:
            slots_c[k, i] = wire.slot()
            wire.start(
                slots_c[k, i],
                lambda i=i: partial.at[order[k], 1, i],
                lambda i=i: work.at[k, i],
                to_c,
            )
            loads[k, i] = local.start(partial.at[order[k], 0, i], own_in.at[k % 2, i])

    begin(0)

    def inverse(index):
        where = jnp.int32(0)
        for k in range(1, extent):
            where = where + k * jnp.where(order[k] == index, 1, 0)
        return where

    line = LineSum(
        wire,
        d,
        t,
        extent,
        lambda index: work.at[inverse(index), 0, pl.ds(0, early)],
        up_in,
        down_in,
        early,
        1,
    )
    late_line = BundleSum(
        wire,
        d,
        t,
        extent,
        lambda index: work.at[inverse(index), pl.ds(0, 4), pl.ds(early, LATE)],
        late_up,
        late_down,
        LATE,
        1,
    )
    routes_a = (
        (to_x, 3, 2, 0, 0),
        (to_y, 3, 1, 1, 1),
        (to_x, 1, 0, 0, 2),
        (to_y, 2, 0, 1, 3),
    )
    routes_b = ((to_y, 2, 0, 0), (to_x, 1, 1, 1))
    last = extent - 1

    def send_a(k, source, cutter, inbox):
        for device, origin, unused, which, row in routes_a:
            if origin == source:
                slots_a[inbox is a_in, k, row] = wire.slot()
                wire.start(
                    slots_a[inbox is a_in, k, row],
                    lambda origin=origin, which=which: cutter(work.at[k, origin], which),
                    lambda row=row: inbox.at[k, row] if inbox is a_in else inbox.at[row],
                    device,
                )

    def receive_a(k, cutter, inbox, second, size):
        for device, unused, target, which, row in routes_a:
            region = inbox.at[k, row] if inbox is a_in else inbox.at[row]
            wire.arrive(slots_a[inbox is a_in, k, row], lambda: region, device)
            add_into(cutter(work.at[k, target], which), region, size)
            if row < 2:
                to, origin, part, b_row = routes_b[row]
                slots_b[inbox is a_in, k, b_row] = wire.slot()
                wire.start(
                    slots_b[inbox is a_in, k, b_row],
                    lambda origin=origin, part=part: cutter(work.at[k, origin], part),
                    lambda b_row=b_row: second.at[k, b_row]
                    if inbox is a_in
                    else second.at[b_row],
                    to,
                )

    def receive_b(k, cutter, inbox, second, size):
        for device, unused, which, row in routes_b:
            region = second.at[k, row] if inbox is a_in else second.at[row]
            wire.arrive(slots_b[inbox is a_in, k, row], lambda: region, device)
            add_into(cutter(work.at[k, 0], which), region, size)

    for turn in range(extent + 2):
        if turn + 1 < extent:
            begin(turn + 1)
        if turn < extent:
            k = turn
            for i in turns:
                loads[k, i].wait()
                wire.arrive(slots_c[k, i], lambda k=k, i=i: work.at[k, i], to_c)
                add_into(work.at[k, i], own_in.at[k % 2, i], rows)
                send_a(k, i, cut, a_in)
            if k < last:
                late_line.step(k)
        if turn == extent:
            late_line.last()
            for i in turns:
                for inbox in (late_up, late_down):
                    add_into(
                        work.at[last, i, pl.ds(early, LATE)], inbox.at[last - 1, i], LATE
                    )
                send_a(last, i, late_cut, late_a)
        between(turn)
        if 1 <= turn <= extent:
            receive_a(turn - 1, cut, a_in, b_in, half)
        if turn == extent + 1:
            receive_a(last, late_cut, late_a, late_b, LATE // 2)
        if turn >= 2:
            k = turn - 2
            receive_b(k, cut, a_in, b_in, half)
            if k < last:
                line.step(k)
    between(extent + 2)
    receive_b(last, late_cut, late_a, late_b, LATE // 2)
    line.last()


def own_rows(buffers, rows, columns, body):
    work, up_in, down_in = buffers[0], buffers[4], buffers[5]
    mine = work.at[work.shape[0] - 1, 0]
    up_last, down_last = up_in.at[up_in.shape[0] - 1], down_in.at[down_in.shape[0] - 1]
    early = rows - LATE

    def first(start):
        part = pl.ds(start, 16)
        body(part, own_sum(mine, up_last, down_last, part, columns))

    def second(start):
        part = pl.ds(pl.multiple_of(early + start, 16), 16)
        body(part, mine[part, columns].astype(F32))

    rows_loop(early, 16, first)
    rows_loop(LATE, 16, second)


def sum_scratch(extent, rows, width):
    early = rows - LATE
    return [
        pltpu.VMEM((extent, 4, rows, width), BF),
        pltpu.VMEM((2, 4, rows, width), BF),
        pltpu.VMEM((extent, 4, early // 2, width), BF),
        pltpu.VMEM((extent, 2, early // 2, width), BF),
        pltpu.VMEM((extent - 1, early, width), BF),
        pltpu.VMEM((extent - 1, early, width), BF),
        pltpu.VMEM((extent - 1, 4, LATE, width), BF),
        pltpu.VMEM((extent - 1, 4, LATE, width), BF),
        pltpu.VMEM((4, LATE // 2, width), BF),
        pltpu.VMEM((2, LATE // 2, width), BF),
    ]


def plane_devices(d, t, extent):
    return line_devices(d, t, extent) + [(None, (flip(d, bits), t)) for bits in (1, 2, 4)]


def kernel_params(number):
    return pltpu.CompilerParams(
        collective_id=number, has_side_effects=True, vmem_limit_bytes=VMEM_LIMIT
    )


def dma_pair(count):
    return [pltpu.SemaphoreType.DMA((count,)), pltpu.SemaphoreType.DMA((count,))]


class Pieces:
    def __init__(self, d, in_weight, out_weight, sem, pieces, tables=None):
        self.copies = {}
        slab = out_weight.shape[0] // 2
        for bits, piece in enumerate(pieces):
            start = pl.multiple_of(flip(d, bits) * slab, slab)
            pairs = []
            for place in range(3):
                for e in range(2):
                    if place < 2:
                        column = (2 * place + e) * slab
                        whole = in_weight.at[pl.ds(start, slab), pl.ds(column, slab)]
                    else:
                        whole = out_weight.at[pl.ds(e * slab, slab), pl.ds(start, slab)]
                    if tables is not None and bits == 0:
                        part = tables[place].at[2 * d + e]
                    else:
                        part = piece.at[place, e]
                    pairs.append((part, whole, sem.at[bits * 6 + place * 2 + e]))
            self.copies[bits] = pairs

    def load(self, bits):
        for piece, whole, sem in self.copies[bits]:
            pltpu.make_async_copy(piece, whole, sem).start()

    def loaded(self, bits):
        for piece, whole, sem in self.copies[bits]:
            pltpu.make_async_copy(piece, whole, sem).wait()

    def store(self, bits):
        for piece, whole, sem in self.copies[bits]:
            pltpu.make_async_copy(whole, piece, sem).start()

    def stored(self, bits):
        for piece, whole, sem in self.copies[bits]:
            pltpu.make_async_copy(whole, piece, sem).wait()


def coefficients(columns, d, slab):
    values = columns.astype(F32)
    lane = lax.broadcasted_iota(jnp.int32, values.shape, 1)
    parts = []
    for e in range(2):
        wanted = jnp.logical_or(lane == 2 * d + e, lane == 16 + 2 * d + e)
        one = jnp.sum(jnp.where(wanted, values, 0.0), axis=-1, keepdims=True)
        parts.append(jnp.broadcast_to(one, (values.shape[0], slab)))
    return jnp.concatenate(parts, axis=1)


def line_exchange(wire, t, d, extent, outbox, inbox):
    peers = [(d, (t + k) % extent) for k in range(1, extent)]
    slots = []
    for k, peer in enumerate(peers):
        slot = wire.slot()
        slots.append(slot)
        wire.start(slot, lambda: outbox, lambda k=k: inbox.at[k], peer)
    result = outbox[...]
    for k, peer in enumerate(peers):
        wire.arrive(slots[k], lambda k=k: inbox.at[k], peer)
        result = result + inbox[k]
    return result


def columns_to_rows(ref):
    return ref[...].T[0:8]


def rows_to_columns(value):
    return jnp.concatenate([value, jnp.zeros((120, value.shape[1]), F32)], axis=0).T


def turned(value, cosine, sine, direction):
    return value * cosine + direction * pltpu.roll(value, HD // 2, 1) * sine


def line_peers(d, t, extent):
    return [(None, (d, (t + k) % extent)) for k in range(1, extent)]


def transposed_dot(left, right):
    return lax.dot_general(left, right, (((0,), (0,)), ((), ())), preferred_element_type=F32)


def dot_transposed(left, right):
    return lax.dot_general(left, right, (((1,), (1,)), ((), ())), preferred_element_type=F32)


def front_kernel(
    extent,
    lengths,
    hid,
    q_weight,
    k_weight,
    v_weight,
    o_weight,
    q_gain,
    k_gain,
    gate,
    up,
    down,
    attn_gain,
    cosine,
    sine,
    ffn_gain,
    router,
    routes,
    chosen,
    middle,
    gates,
    head_gain,
    inverses,
    hid_out,
    qkv_out,
    o_out,
    normed_out,
    raw_out,
    low_out,
    probs_out,
    mixed_out,
    tokens,
    hidden,
    out,
    landed,
    hid_all,
    qkv_all,
    o_all,
    gains_all,
    router_rows,
    normed,
    raw,
    low,
    probs,
    mixed,
    sums,
    outbox,
    inbox,
    gathered,
    work,
    up_in,
    down_in,
    in_weight,
    out_weight,
    hidden_stage,
    out_stage,
    send_sem,
    recv_sem,
    local_sem,
    weight_sem,
    stage_sem,
    token_sem,
    probs_sem,
):
    d, t = lax.axis_index("dp"), lax.axis_index("tensor")
    seq_len, width = hid_all.shape
    rows = seq_len // extent
    heads, head_width = q_gain.shape
    columns = heads * HD
    length = lengths[d]
    depth, o_rows, o_width = q_weight.shape[0], o_weight.shape[0], o_weight.shape[1]
    wire, local = Wire(send_sem, recv_sem), Local(local_sem)
    dx, dy, dxy = flip(d, 2), flip(d, 4), flip(d, 6)
    to_x, to_y, to_c = (dx, t), (dy, t), (flip(d, 1), t)

    def block(index):
        return hid_all.at[pl.ds(index * rows, rows)]

    def region(device, which):
        start = pl.multiple_of(device * o_width, o_width)
        if which is None:
            return [qkv_all.at[pl.ds(device * depth, depth)], o_all.at[:, pl.ds(start, o_width)]]
        return [
            qkv_all.at[pl.ds(device * depth + which * (depth // 2), depth // 2)],
            o_all.at[pl.ds(which * (o_rows // 2), o_rows // 2), pl.ds(start, o_width)],
        ]

    copies = [local.start(hid, block(t))]
    for n, weight in enumerate((q_weight, k_weight, v_weight)):
        target = qkv_all.at[pl.ds(d * depth, depth), pl.ds(n * columns, columns)]
        copies.append(local.start(weight, target))
    copies.append(local.start(o_weight, region(d, None)[1]))
    lane = lax.broadcasted_iota(jnp.int32, (heads, HD), 1)
    for n, source in enumerate((q_gain, k_gain)):
        value = source[...].astype(F32)
        spread_out = jnp.zeros((heads, HD), F32)
        for i in range(head_width):
            spread_out += jnp.where(lane == d * head_width + i, value[:, i : i + 1], 0.0)
        gains_all[0, n * heads : (n + 1) * heads] = spread_out
    router_rows[...] = jnp.zeros(router_rows.shape, BF)
    router_rows[0:16] = router[...]
    router_rows[16:32] = router[...]
    lane = lax.broadcasted_iota(jnp.int32, (rows, 128), 1)
    own_routes = routes[pl.ds(pl.multiple_of(t * rows, rows), rows)]
    picked = jnp.zeros((rows, 128), F32)
    for k in range(own_routes.shape[1]):
        match = both(own_routes[:, k : k + 1] == lane % 16, lane < 32)
        picked = jnp.where(match, 1.0, picked)
    chosen[...] = picked
    greet(line_peers(d, t, extent) + [(None, (flip(d, bits), t)) for bits in range(1, 8)])
    for copy in copies:
        copy.wait()

    def send(device, sources, targets):
        slots = []
        for source, target in zip(sources, targets):
            slot = wire.slot()
            wire.start(slot, lambda source=source: source, lambda target=target: target, device)
            slots.append(slot)
        return slots

    def arrive(slots, regions, device):
        for slot, part in zip(slots, regions):
            wire.arrive(slot, lambda: part, device)

    line = LineGather(wire, d, t, extent, lambda: block(t), block)
    line.begin()
    x_slots, y_slots, c_slots = {}, {}, {}
    for which, other in ((0, 1), (1, 0)):
        x_slots[which] = send(to_x, region(d, which), region(d, which))
        y_slots[other] = send(to_y, region(d, other), region(d, other))
    c_slots[1] = send(to_c, region(d, None), region(d, None))
    gain_slots = {}
    for bits in range(1, 8):
        gain_slots[bits] = wire.slot()
        wire.start(
            gain_slots[bits],
            lambda: gains_all.at[0],
            lambda bits=bits: gains_all.at[bits],
            (flip(d, bits), t),
        )
    weights = Pieces(
        d, in_weight, out_weight, weight_sem, [landed.at[bits] for bits in range(8)]
    )
    own_experts = Pieces(d, in_weight, out_weight, weight_sem, [None], (gate, up, down))
    own_experts.load(0)
    arrive(x_slots[0], region(dx, 0), to_x)
    over_y = send(to_y, region(dx, 0), region(dx, 0))
    arrive(y_slots[1], region(dy, 1), to_y)
    over_x = send(to_x, region(dy, 1), region(dy, 1))
    piece_slots = {}
    for bits in (2, 4, 1, 3, 5, 6, 7):
        first = 2 * flip(d, bits)
        piece_slots[bits] = send(
            (flip(d, bits), t),
            [weight.at[pl.ds(first, 2)] for weight in (gate, up, down)],
            [landed.at[bits, place] for place in range(3)],
        )
    line.step(1)
    arrive(x_slots[1], region(dx, 1), to_x)
    c_slots[3] = send(to_c, region(dx, None), region(dx, None))
    arrive(y_slots[0], region(dy, 0), to_y)
    c_slots[5] = send(to_c, region(dy, None), region(dy, None))
    for step in range(2, extent):
        line.step(step)
    arrive(over_y, region(dxy, 0), to_y)
    arrive(over_x, region(dxy, 1), to_x)
    c_slots[7] = send(to_c, region(dxy, None), region(dxy, None))
    for bits in range(1, 8):
        wire.arrive(
            gain_slots[bits], lambda bits=bits: gains_all.at[bits], (flip(d, bits), t)
        )
    total_gain = gains_all[0]
    for bits in range(1, 8):
        total_gain = total_gain + gains_all[bits]
    head_gain[...] = total_gain
    tile = 256

    def normalize(start):
        part = pl.ds(start, 64)
        value = hid_all[part].astype(F32)
        unit = value * lax.rsqrt(jnp.mean(value * value, axis=-1, keepdims=True) + EPSILON)
        normed[part] = (unit * attn_gain[...].astype(F32)).astype(BF)

    rows_loop(seq_len, 64, normalize)
    for bits in (1, 3, 5, 7):
        arrive(c_slots[bits], region(flip(d, bits), None), to_c)
    kept = [
        local.start(hid_all, hid_out),
        local.start(qkv_all, qkv_out),
        local.start(o_all, o_out),
        local.start(normed, normed_out),
    ]

    def project(start):
        part = pl.ds(start, tile)
        result = jnp.dot(normed[part], qkv_all[...], preferred_element_type=F32)
        raw[part] = result
        lane = lax.broadcasted_iota(jnp.int32, (tile, 128), 1)
        squares = [
            jnp.sum(jnp.square(result[:, n * columns : (n + 1) * columns]), axis=-1, keepdims=True)
            for n in range(2)
        ]
        sums[part] = jnp.where(lane == 0, squares[0], jnp.where(lane == 1, squares[1], 0.0))

    rows_loop(seq_len, tile, project)
    outbox[...] = columns_to_rows(sums)
    total = line_exchange(wire, t, d, extent, outbox, inbox)
    inverses[...] = rows_to_columns(lax.rsqrt(total / width + EPSILON))
    low[:, 2 * columns :] = raw[:, 2 * columns :].astype(BF)

    def probs_copy(h):
        return pltpu.make_async_copy(probs.at[h % 2], probs_out.at[h], probs_sem.at[h % 2])

    def head(h, carry):
        for n in range(2):
            section = pl.ds(pl.multiple_of(n * columns + h * HD, HD), HD)
            unit = raw[:, section] * inverses[:, n : n + 1]
            raw[:, section] = unit
            scaled = unit * head_gain[pl.ds(n * heads + h, 1)]
            low[:, section] = turned(scaled, cosine[...], sine[...], 1.0).astype(BF)
        section = pl.ds(pl.multiple_of(h * HD, HD), HD)
        key_section = pl.ds(pl.multiple_of(columns + h * HD, HD), HD)
        value_section = pl.ds(pl.multiple_of(2 * columns + h * HD, HD), HD)

        @pl.when(h >= 2)
        def _():
            probs_copy(h).wait()

        def some(start):
            part = pl.ds(start, tile)
            scores = dot_transposed(low[part, section], low[:, key_section]) / math.sqrt(HD)
            row = start + lax.broadcasted_iota(jnp.int32, scores.shape, 0)
            column = lax.broadcasted_iota(jnp.int32, scores.shape, 1)
            allowed = both(column <= row, column < length)
            scores = jnp.where(allowed, scores, -1e30)
            powers = jnp.exp(scores - jnp.max(scores, axis=-1, keepdims=True))
            result = powers / jnp.sum(powers, axis=-1, keepdims=True)
            probs[h % 2, part] = result
            mixed[part, section] = jnp.dot(
                result.astype(BF), low[:, value_section], preferred_element_type=F32
            ).astype(BF)

        rows_loop(seq_len, tile, some)
        probs_copy(h).start()
        return carry

    lax.fori_loop(0, heads, head, 0)
    kept += [local.start(raw, raw_out), local.start(low, low_out), local.start(mixed, mixed_out)]

    def join(first, carry):
        result = jnp.dot(
            mixed[pl.ds(first * 2 * rows, 2 * rows)], o_all[...], preferred_element_type=F32
        )
        work[pl.ds(2 * first, 2)] = result.astype(BF).reshape(2, rows, width)
        return carry

    lax.fori_loop(0, extent // 2, join, 0)
    total_line = LineSum(
        wire, d, t, extent, lambda index: work.at[index], up_in, down_in, rows, 2
    )
    for step in range(extent - 1):
        total_line.step(step)
    total_line.last()
    mine = work.at[t]
    everything = pl.ds(0, width)
    packet = gathered.at[t, 0, 0]

    def body(start):
        part = pl.ds(start, 16)
        value = hid[part].astype(F32) + own_sum(
            mine, up_in.at[extent - 2], down_in.at[extent - 2], part, everything
        )
        middle[part] = value
        unit = value * lax.rsqrt(jnp.mean(value * value, axis=-1, keepdims=True) + EPSILON)
        packet[part, 0:width] = (unit * ffn_gain[...].astype(F32)).astype(BF)

    rows_loop(rows, 16, body)
    logits = dot_transposed(packet[:, 0:width], router_rows[...])
    lane = lax.broadcasted_iota(jnp.int32, logits.shape, 1)
    top = jnp.max(jnp.where(lane < 16, logits, -1e30), axis=-1, keepdims=True)
    powers = jnp.where(lane < 32, jnp.exp(logits - top), 0.0)
    chance = powers / jnp.sum(jnp.where(lane < 16, powers, 0.0), axis=-1, keepdims=True)
    gates[...] = chance
    coeff = chance * chosen[...]
    high = coeff.astype(BF).astype(F32)
    packet[:, width : width + 128] = jnp.where(lane < 16, high, coeff - high).astype(BF)

    def place(j, c, i):
        return gathered.at[j, c, i]

    def bundle(j, c):
        return gathered.at[j, c, pl.ds(0, 4), pl.ds(rows - LATE, LATE)]

    gather = PlaneGather(wire, d, t, extent, lambda: packet, place, bundle, rows)
    for bits in range(1, 8):
        arrive(
            piece_slots[bits], [landed.at[bits, place] for place in range(3)], (flip(d, bits), t)
        )
        weights.load(bits)
    own_experts.loaded(0)
    for bits in range(1, 8):
        weights.loaded(bits)
    units = out_weight.shape[0]

    def stage_copies(slot, j, c):
        return (
            pltpu.make_async_copy(hidden_stage.at[slot], hidden.at[j, c], stage_sem.at[0, slot]),
            pltpu.make_async_copy(out_stage.at[slot], out.at[j, c], stage_sem.at[1, slot]),
        )

    actions = gather.actions()

    def group(g, carry):
        for number, steps in enumerate(actions):

            @pl.when(g == number)
            def _():
                for action, argument in steps:
                    action(argument)

        j, c, slot = arrival(t, g // 2), g % 2, g % 2

        @pl.when(g >= 2)
        def _():
            for copy in stage_copies(slot, j, c):
                copy.wait()

        pltpu.make_async_copy(gathered.at[j, c], tokens.at[j, c], token_sem.at[g]).start()

        def some(first, carry):
            blocks, part = pl.ds(2 * first, 2), pl.ds(first * 2 * rows, 2 * rows)
            values = jnp.dot(
                gathered[j, c, blocks, :, 0:width].reshape(2 * rows, width),
                in_weight[...],
                preferred_element_type=F32,
            )
            hidden_stage[slot, part] = values.astype(BF)
            gate_value, up_value = values[:, :units], values[:, units:]
            coeff = coefficients(
                gathered[j, c, blocks, :, width : width + 128].reshape(2 * rows, 128),
                d,
                units // 2,
            )
            active = (coeff * (gate_value * jax.nn.sigmoid(gate_value)) * up_value).astype(BF)
            result = jnp.dot(active, out_weight[...], preferred_element_type=F32)
            out_stage[slot, blocks] = result.astype(BF).reshape(2, rows, width)
            return carry

        lax.fori_loop(0, 2, some, 0)
        for copy in stage_copies(slot, j, c):
            copy.start()
        return carry

    lax.fori_loop(0, 2 * extent, group, 0)
    for slot in range(2):
        for copy in stage_copies(slot, 0, slot):
            copy.wait()
    for g in range(2 * extent):
        pltpu.make_async_copy(
            gathered.at[arrival(t, g // 2), g % 2],
            tokens.at[arrival(t, g // 2), g % 2],
            token_sem.at[g],
        ).wait()
    for h in range(heads - 2, heads):
        probs_copy(h).wait()
    for copy in kept:
        copy.wait()
    wire.finish()


SMEM = pl.BlockSpec(memory_space=pltpu.SMEM)


def front(extent, lengths, hid, *rest):
    rows, width = hid.shape
    seq_len = rows * extent
    slab = rest[6].shape[1]
    heads = rest[4].shape[0]
    columns = heads * HD
    shape = jax.ShapeDtypeStruct
    kept = [
        shape((seq_len, width), BF),
        shape((width, 3 * columns), BF),
        shape((columns, width), BF),
        shape((seq_len, width), BF),
        shape((seq_len, 3 * columns), F32),
        shape((seq_len, 3 * columns), BF),
        shape((heads, seq_len, seq_len), F32),
        shape((seq_len, columns), BF),
    ]
    return pl.pallas_call(
        functools.partial(front_kernel, extent),
        out_shape=[
            shape((rows, 128), F32),
            shape((rows, width), F32),
            shape((rows, 128), F32),
            shape((2 * heads, HD), F32),
            shape((seq_len, 128), F32),
        ]
        + kept
        + [
            shape((extent, 2, 4, rows, width + 128), BF),
            shape((extent, 2, 4 * rows, 4 * slab), BF),
            shape((extent, 2, 4, rows, width), BF),
            shape((8, 3, 2, slab, slab), BF),
        ],
        in_specs=[SMEM, VM] + [ANY] * 4 + [VM] * 2 + [ANY] * 3 + [VM] * 6,
        out_specs=[VM] * 5 + [ANY] * 12,
        scratch_shapes=[
            pltpu.VMEM((seq_len, width), BF),
            pltpu.VMEM((width, 3 * columns), BF),
            pltpu.VMEM((columns, width), BF),
            pltpu.VMEM((8, 2 * heads, HD), F32),
            pltpu.VMEM((128, width), BF),
            pltpu.VMEM((seq_len, width), BF),
            pltpu.VMEM((seq_len, 3 * columns), F32),
            pltpu.VMEM((seq_len, 3 * columns), BF),
            pltpu.VMEM((2, seq_len, seq_len), F32),
            pltpu.VMEM((seq_len, columns), BF),
            pltpu.VMEM((seq_len, 128), F32),
            pltpu.VMEM((8, seq_len), F32),
            pltpu.VMEM((extent - 1, 8, seq_len), F32),
            pltpu.VMEM((extent, 2, 4, rows, width + 128), BF),
            pltpu.VMEM((extent, rows, width), BF),
            pltpu.VMEM((extent - 1, rows, width), BF),
            pltpu.VMEM((extent - 1, rows, width), BF),
            pltpu.VMEM((width, 4 * slab), BF),
            pltpu.VMEM((2 * slab, width), BF),
            pltpu.VMEM((2, 4 * rows, 4 * slab), BF),
            pltpu.VMEM((2, 4, rows, width), BF),
        ]
        + dma_pair(180)
        + [
            pltpu.SemaphoreType.DMA((16,)),
            pltpu.SemaphoreType.DMA((48,)),
            pltpu.SemaphoreType.DMA((2, 2)),
            pltpu.SemaphoreType.DMA((2 * extent,)),
            pltpu.SemaphoreType.DMA((2,)),
        ],
        compiler_params=kernel_params(1),
        cost_estimate=pl.CostEstimate(flops=0, bytes_accessed=300_000_000, transcendentals=0),
    )(lengths, hid, *rest)


def turn_kernel(extent, lengths, partial, middle, teacher, tokens, hidden, *rest):
    landed, tables = rest[0], rest[1:4]
    grad_output, row_loss, out, inner_out, active_out, grads = rest[4:10]
    buffers = rest[10:20]
    (
        packet,
        in_weight,
        out_weight,
        coeff_tile,
        hidden_tile,
        factors,
        grad_tile,
        out_stage,
        active_tile,
        inner_tile,
        send_sem,
        recv_sem,
        local_sem,
        weight_sem,
        tile_sem,
        load_sem,
    ) = rest[20:]
    d, t = lax.axis_index("dp"), lax.axis_index("tensor")
    rows, width = middle.shape
    greet(plane_devices(d, t, extent))
    wire, local = Wire(send_sem, recv_sem), Local(local_sem)
    pieces = [landed.at[bits] for bits in range(8)]
    weights = Pieces(d, in_weight, out_weight, weight_sem, pieces, tables)
    units, slab = out_weight.shape[0], out_weight.shape[0] // 2
    count = 2 * extent

    def factor_loads(g):
        j, c, slot = g // 2, g % 2, g % 2
        part = (pl.ds(0, 4), pl.ds(0, rows), pl.ds(width, 128))
        return (
            pltpu.make_async_copy(
                tokens.at[(j, c) + part], coeff_tile.at[slot], load_sem.at[0, slot]
            ),
            pltpu.make_async_copy(hidden.at[j, c], hidden_tile.at[slot], load_sem.at[1, slot]),
        )

    def active_store(g):
        return pltpu.make_async_copy(
            active_tile.at[g % 2], active_out.at[g // 2, g % 2], load_sem.at[2, g % 2]
        )

    def prepare(g):
        if g + 1 < count:
            for copy in factor_loads(g + 1):
                copy.start()
        for copy in factor_loads(g):
            copy.wait()
        if g >= 2:
            active_store(g - 2).wait()
        slot = g % 2

        def some(first, carry):
            size = 2 * rows
            blocks, part = pl.ds(2 * first, 2), pl.ds(first * size, size)
            gate_value = hidden_tile[slot, part, 0:units].astype(F32)
            up_value = hidden_tile[slot, part, units : 2 * units].astype(F32)
            coeff = coefficients(coeff_tile[slot, blocks].reshape(size, 128), d, slab)
            sigmoid_value = jax.nn.sigmoid(gate_value)
            silu_value = gate_value * sigmoid_value
            slope = sigmoid_value * (1.0 + gate_value * (1.0 - sigmoid_value))
            direct = silu_value * up_value
            factors[g, part, 0:units] = (coeff * up_value * slope).astype(BF)
            factors[g, part, units : 2 * units] = (coeff * silu_value).astype(BF)
            factors[g, part, 2 * units : 3 * units] = direct.astype(BF)
            active_tile[slot, part] = (coeff * direct).astype(BF)
            return carry

        lax.fori_loop(0, 2, some, 0)
        active_store(g).start()

    for copy in factor_loads(0):
        copy.start()

    def between(turn_number):
        if turn_number == 1:
            for bits in range(8):
                weights.load(bits)
        if turn_number < extent:
            prepare(2 * turn_number)
            prepare(2 * turn_number + 1)

    sum_plane(wire, local, d, t, extent, partial, buffers, rows, between)
    for g in (count - 2, count - 1):
        active_store(g).wait()

    total_count = lengths[0]
    for n in range(1, lengths.shape[0]):
        total_count = total_count + lengths[n]
    length = lengths[d]

    def body(part, value):
        row = t * rows + part.start + lax.broadcasted_iota(jnp.int32, (16, 1), 0)
        count = jnp.broadcast_to(total_count, (16, 1)).astype(F32)
        weight = jnp.where(row < length, 8 * extent * rows / count, 0.0)
        output = middle[part] + value
        mismatch = output - teacher[part].astype(F32)
        scaled = mismatch * weight
        grad_output[part] = scaled
        packet[part] = scaled.astype(BF)
        row_loss[part] = jnp.broadcast_to(
            jnp.sum(scaled * mismatch, axis=-1, keepdims=True), (16, 128)
        )

    own_rows(buffers, rows, pl.ds(0, width), body)

    def place(j, c, i):
        return grads.at[j, c, i]

    def bundle(j, c):
        return grads.at[j, c, pl.ds(0, 4), pl.ds(rows - LATE, LATE)]

    own_copy = local.start(packet, place(t, 0, 0))
    gather = PlaneGather(wire, d, t, extent, lambda: packet, place, bundle, rows)
    own_copy.wait()
    for bits in range(8):
        weights.loaded(bits)
    actions = gather.actions()

    def out_copies(j, c):
        return (
            pltpu.make_async_copy(out_stage, out.at[j, c], tile_sem.at[1]),
            pltpu.make_async_copy(inner_tile, inner_out.at[j, c], tile_sem.at[2]),
        )

    def group(g, carry):
        j, c = arrival(t, g // 2), g % 2
        grad_copy = pltpu.make_async_copy(grads.at[j, c], grad_tile, tile_sem.at[0])
        for number, steps in enumerate(actions):

            @pl.when(g == number)
            def _():
                for action, argument in steps:
                    action(argument)

        grad_copy.start()

        @pl.when(g >= 1)
        def _():
            for copy in out_copies(j, c):
                copy.wait()

        grad_copy.wait()
        index = 2 * j + c

        def some(first, carry):
            size = 2 * rows
            blocks, part = pl.ds(2 * first, 2), pl.ds(first * size, size)
            grad_active = dot_transposed(
                grad_tile[blocks].reshape(size, width), out_weight[...]
            )
            product = grad_active * factors[index, part, 2 * units : 3 * units].astype(F32)
            lane = lax.broadcasted_iota(jnp.int32, (size, 128), 1)
            sums = jnp.zeros((size, 128), F32)
            for e in range(2):
                one = jnp.sum(product[:, e * slab : (e + 1) * slab], axis=-1, keepdims=True)
                sums = sums + jnp.where(lane == 2 * d + e, one, 0.0)
            out_stage[blocks, :, width : width + 128] = sums.astype(BF).reshape(2, rows, 128)
            for n in range(2):
                columns = pl.ds(n * units, units)
                inner_tile[part, columns] = (
                    grad_active * factors[index, part, columns].astype(F32)
                ).astype(BF)
            result = dot_transposed(inner_tile[part], in_weight[...]).astype(BF)
            out_stage[blocks, :, 0:width] = result.reshape(2, rows, width)
            return carry

        lax.fori_loop(0, 2, some, 0)
        for copy in out_copies(j, c):
            copy.start()
        return carry

    lax.fori_loop(0, 2 * extent, group, 0)
    for copy in out_copies(0, 0):
        copy.wait()
    wire.finish()


def turn(extent, lengths, partial, middle, teacher, tokens, hidden, landed, *tables):
    rows, width = middle.shape
    slab = landed.shape[3]
    return pl.pallas_call(
        functools.partial(turn_kernel, extent),
        out_shape=[
            jax.ShapeDtypeStruct((rows, width), F32),
            jax.ShapeDtypeStruct((rows, 128), F32),
            jax.ShapeDtypeStruct((extent, 2, 4, rows, width + 128), BF),
            jax.ShapeDtypeStruct((extent, 2, 4 * rows, 4 * slab), BF),
            jax.ShapeDtypeStruct((extent, 2, 4 * rows, 2 * slab), BF),
            jax.ShapeDtypeStruct((extent, 2, 4, rows, width), BF),
        ],
        in_specs=[SMEM, ANY, VM, VM] + [ANY] * 6,
        out_specs=[VM, VM] + [ANY] * 4,
        scratch_shapes=sum_scratch(extent, rows, width)
        + [
            pltpu.VMEM((rows, width), BF),
            pltpu.VMEM((width, 4 * slab), BF),
            pltpu.VMEM((2 * slab, width), BF),
            pltpu.VMEM((2, 4, rows, 128), BF),
            pltpu.VMEM((2, 4 * rows, 4 * slab), BF),
            pltpu.VMEM((2 * extent, 4 * rows, 6 * slab), BF),
            pltpu.VMEM((4, rows, width), BF),
            pltpu.VMEM((4, rows, width + 128), BF),
            pltpu.VMEM((2, 4 * rows, 2 * slab), BF),
            pltpu.VMEM((4 * rows, 4 * slab), BF),
        ]
        + dma_pair(150)
        + [
            pltpu.SemaphoreType.DMA((20,)),
            pltpu.SemaphoreType.DMA((48,)),
            pltpu.SemaphoreType.DMA((3,)),
            pltpu.SemaphoreType.DMA((3, 2)),
        ],
        compiler_params=kernel_params(4),
        cost_estimate=pl.CostEstimate(flops=0, bytes_accessed=450_000_000, transcendentals=0),
    )(lengths, partial, middle, teacher, tokens, hidden, landed, *tables)


class WeightGrads:
    def __init__(self, sources, tiles, totals, sem):
        self.sources, self.tiles, self.sem = sources, tiles, sem
        self.in_total, self.out_total = totals

    def copies(self, g):
        j, c, slot = g // 2, g % 2, g % 2
        return [
            pltpu.make_async_copy(source.at[j, c], tile.at[slot], self.sem.at[n, slot])
            for n, (source, tile) in enumerate(zip(self.sources, self.tiles))
        ]

    def start(self, g):
        for copy in self.copies(g):
            copy.start()

    def clear(self):
        self.in_total[...] = jnp.zeros(self.in_total.shape, F32)
        self.out_total[...] = jnp.zeros(self.out_total.shape, F32)

    def work(self, g, count):
        if g + 1 < count:
            self.start(g + 1)
        for copy in self.copies(g):
            copy.wait()
        slot = g % 2
        token_tile, grad_tile, inner_tile, active_tile = (tile.at[slot] for tile in self.tiles)
        size, width = inner_tile.shape[0], grad_tile.shape[2]

        def into_in(start):
            part = pl.ds(start, 256)
            left = token_tile[:, :, part].reshape(size, 256)
            self.in_total[part] += transposed_dot(left, inner_tile[...])

        rows_loop(width, 256, into_in)

        def into_out(start):
            part = pl.ds(start, 512)
            right = grad_tile[:, :, part].reshape(size, 512)
            self.out_total[:, part] += transposed_dot(active_tile[...], right)

        rows_loop(width, 512, into_out)

    def pieces(self, d, stage):
        slab = stage.shape[3]
        for bits in range(8):
            part = pl.ds(pl.multiple_of(flip(d, bits) * slab, slab), slab)
            for place in range(3):
                for e in range(2):
                    if place < 2:
                        column = (2 * place + e) * slab
                        value = self.in_total[part, column : column + slab]
                    else:
                        value = self.out_total[e * slab : (e + 1) * slab, part]
                    stage[bits, place, e] = value.astype(BF)


def leave_kernel(extent, partial, middle, grad_output, gates, chosen, gain, router, *rest):
    sources = rest[:4]
    grad_middle, small, grads = rest[4:7]
    came = rest[7:15]
    buffers = rest[15:25]
    tiles, totals = rest[25:29], rest[29:31]
    stage, packet, grad_logits, gain_part, ffn_own, send_sem, recv_sem, local_sem, tile_sem = rest[31:]
    d, t = lax.axis_index("dp"), lax.axis_index("tensor")
    rows, width = middle.shape
    greet(line_devices(d, t, extent) + [(None, (flip(d, bits), t)) for bits in range(1, 6)])
    wire, local = Wire(send_sem, recv_sem), Local(local_sem)
    weight_grads = WeightGrads(sources, tiles, totals, tile_sem)
    count = 2 * extent
    piece_slots, copies = [], []
    weight_grads.start(0)

    def between(turn_number):
        if turn_number == 0:
            weight_grads.clear()
        if turn_number < extent:
            weight_grads.work(2 * turn_number, count)
            weight_grads.work(2 * turn_number + 1, count)
        if turn_number == extent + 2:
            weight_grads.pieces(d, stage)
            for bits in range(1, 6):
                slot = wire.slot()
                piece_slots.append(slot)
                wire.start(
                    slot,
                    lambda bits=bits: stage.at[bits],
                    lambda bits=bits: came[bits],
                    (flip(d, bits), t),
                )
            for bits in (0, 6, 7):
                copies.append(local.start(stage.at[bits], came[bits]))

    sum_plane(wire, local, d, t, extent, partial, buffers, rows, between)

    def collect(part, value):
        grad_logits[part] = value

    own_rows(buffers, rows, pl.ds(width, 128), collect)
    coeff_grad = grad_logits[...] * chosen[...]
    lane = lax.broadcasted_iota(jnp.int32, coeff_grad.shape, 1)
    probs = jnp.where(lane < 16, gates[...], 0.0)
    coeff_grad = jnp.where(lane < 16, coeff_grad, 0.0)
    logit_grad = probs * (coeff_grad - jnp.sum(coeff_grad * probs, axis=-1, keepdims=True))
    grad_logits[...] = logit_grad
    high = logit_grad.astype(BF)
    low_part = (logit_grad - high.astype(F32)).astype(BF)
    for begin in range(0, width, 512):
        columns = slice(begin, begin + 512)
        grad_middle[:, columns] = jnp.dot(
            high[:, 0:16], router[:, columns], preferred_element_type=F32
        ) + jnp.dot(low_part[:, 0:16], router[:, columns], preferred_element_type=F32)
    gain_part[...] = jnp.zeros(gain_part.shape, F32)

    def body(part, value):
        grad = value + grad_middle[part]
        value = middle[part]
        inverse = lax.rsqrt(jnp.mean(value * value, axis=-1, keepdims=True) + EPSILON)
        unit = value * inverse
        product = grad * unit
        gain_part[...] += product[0:8] + product[8:16]
        gain_row = gain[...].astype(F32)
        ffn_own[part] = (unit * gain_row).astype(BF)
        scaled = grad * gain_row
        result = grad_output[part] + inverse * (
            scaled - unit * jnp.mean(scaled * unit, axis=-1, keepdims=True)
        )
        grad_middle[part] = result
        packet[part] = result.astype(BF)

    own_rows(buffers, rows, pl.ds(0, width), body)

    def place(index):
        return grads.at[index]

    copies.append(local.start(packet, place(t)))
    line = LineGather(wire, d, t, extent, lambda: packet, place)
    line.begin()
    router_part = transposed_dot(high, ffn_own[...]) + transposed_dot(low_part, ffn_own[...])
    small[0:16] = router_part[0:16]
    row = lax.broadcasted_iota(jnp.int32, (8, width), 0)
    gain_sum = jnp.sum(gain_part[...], axis=0, keepdims=True)
    small[16:24] = jnp.where(row == 1, gain_sum, 0.0)
    for step in range(1, extent):
        line.step(step)
    for copy in copies:
        copy.wait()
    for n, slot in enumerate(piece_slots):
        wire.arrive(slot, lambda: came[1 + n], (flip(d, 1 + n), t))
    wire.finish()


def leave(extent, partial, middle, grad_output, gates, chosen, gain, router, sources):
    rows, width = middle.shape
    tokens, grads, inner, active = sources
    units = active.shape[3]
    piece = jax.ShapeDtypeStruct((3, 2, units // 2, units // 2), BF)
    return pl.pallas_call(
        functools.partial(leave_kernel, extent),
        out_shape=[
            jax.ShapeDtypeStruct((rows, width), F32),
            jax.ShapeDtypeStruct((24, width), F32),
            jax.ShapeDtypeStruct((extent, rows, width), BF),
        ]
        + [piece] * 8,
        in_specs=[ANY, VM, VM, VM, VM, VM, VM] + [ANY] * 4,
        out_specs=[VM, VM] + [ANY] * 9,
        scratch_shapes=sum_scratch(extent, rows, width + 128)
        + [pltpu.VMEM((2,) + source.shape[2:], BF) for source in sources]
        + [
            pltpu.VMEM((width, 2 * units), F32),
            pltpu.VMEM((units, width), F32),
            pltpu.VMEM((8,) + piece.shape, BF),
            pltpu.VMEM((rows, width), BF),
            pltpu.VMEM((rows, 128), F32),
            pltpu.VMEM((8, width), F32),
            pltpu.VMEM((rows, width), BF),
        ]
        + dma_pair(120)
        + [pltpu.SemaphoreType.DMA((24,)), pltpu.SemaphoreType.DMA((4, 2))],
        compiler_params=kernel_params(5),
        cost_estimate=pl.CostEstimate(flops=0, bytes_accessed=350_000_000, transcendentals=0),
    )(partial, middle, grad_output, gates, chosen, gain, router, *sources)


def back_kernel(
    extent,
    grads,
    row_loss,
    hid,
    gain,
    qkv_weight,
    o_weight,
    head_gain,
    cosine,
    sine,
    normed,
    units,
    low,
    probs,
    mixed,
    inverses,
    small,
    grad_middle,
    grad_in,
    q_out,
    k_out,
    v_out,
    o_out,
    router_out,
    vectors_out,
    q_gain_out,
    k_gain_out,
    loss,
    grad_mixed,
    scaled,
    raw_grad,
    sums,
    dots,
    outbox,
    inbox,
    gain_part,
    head_part,
    work,
    up_in,
    down_in,
    q_send,
    q_work,
    q_core,
    q_a,
    q_b,
    o_send,
    o_work,
    o_core,
    o_a,
    o_b,
    small_send,
    small_in,
    small_sum,
    small_last,
    send_sem,
    recv_sem,
):
    d, t = lax.axis_index("dp"), lax.axis_index("tensor")
    seq_len, width = hid.shape
    rows = seq_len // extent
    heads = head_gain.shape[0] // 2
    columns = heads * HD
    depth, o_width = q_out.shape[0], o_out.shape[1]
    peers = [(d, (t + k) % extent) for k in range(1, extent)]
    greet(line_peers(d, t, extent) + [(None, (flip(d, bits), t)) for bits in range(1, 8)])
    wire = Wire(send_sem, recv_sem)
    to_x, to_y, to_c = (flip(d, 2), t), (flip(d, 4), t), (flip(d, 1), t)
    tile = 256
    root = math.sqrt(HD)
    turns = (3, 1, 2, 0)

    def mix(start):
        part = pl.ds(start, tile)
        grad_mixed[part] = dot_transposed(grads[part], o_weight[...]).astype(BF)

    rows_loop(seq_len, tile, mix)

    def o_slice(bits, target):
        start = pl.multiple_of(flip(d, bits) * o_width, o_width)
        target[...] = transposed_dot(mixed[...], grads[:, pl.ds(start, o_width)]).astype(BF)

    core_slots = {}
    for i in turns:
        o_slice(1 + 2 * i, o_send.at[i])
        core_slots["o", i] = wire.slot()
        wire.start(core_slots["o", i], lambda i=i: o_send.at[i], lambda i=i: o_core.at[i], to_c)
    for i in turns:
        o_slice(2 * i, o_work.at[i])
    sums[...] = jnp.zeros(sums.shape, F32)

    def head(h, carry):
        section = pl.ds(pl.multiple_of(h * HD, HD), HD)
        key_section = pl.ds(pl.multiple_of(columns + h * HD, HD), HD)
        value_section = pl.ds(pl.multiple_of(2 * columns + h * HD, HD), HD)
        chance = probs[h]
        incoming = grad_mixed[:, section]
        raw_grad[:, value_section] = transposed_dot(chance.astype(BF), incoming).astype(BF)
        grad_probs = dot_transposed(incoming, low[:, value_section])
        grad_scores = (
            chance * (grad_probs - jnp.sum(grad_probs * chance, axis=-1, keepdims=True))
        ).astype(BF)
        pair = (
            jnp.dot(grad_scores, low[:, key_section], preferred_element_type=F32) / root,
            transposed_dot(grad_scores, low[:, section]) / root,
        )
        lane = lax.broadcasted_iota(jnp.int32, (seq_len, 128), 1)
        for n, where in enumerate((section, key_section)):
            value = turned(pair[n], cosine[...], sine[...], -1.0)
            unit = units[:, where]
            head_part[pl.ds(n * heads + h, 1)] = jnp.sum(value * unit, axis=0, keepdims=True)
            value = value * head_gain[pl.ds(n * heads + h, 1)]
            scaled[:, where] = value
            sums[...] += jnp.where(lane == n, jnp.sum(value * unit, axis=-1, keepdims=True), 0.0)
        return carry

    lax.fori_loop(0, heads, head, 0)
    outbox[...] = columns_to_rows(sums)
    outbox[2:3] = jnp.broadcast_to(jnp.sum(row_loss[:, 0:1], axis=0, keepdims=True), (1, seq_len))
    total = line_exchange(wire, t, d, extent, outbox, inbox)
    loss[...] = total[:, 0:128] / (2.0 * width * 8 * seq_len)
    dots[...] = rows_to_columns(total / width)

    def head_again(h, carry):
        for n in range(2):
            section = pl.ds(pl.multiple_of(n * columns + h * HD, HD), HD)
            raw_grad[:, section] = (
                inverses[:, n : n + 1]
                * (scaled[:, section] - units[:, section] * dots[:, n : n + 1])
            ).astype(BF)
        return carry

    lax.fori_loop(0, heads, head_again, 0)
    gain_part[...] = jnp.zeros(gain_part.shape, F32)
    order = plane_order(t)

    def input_block(k):
        part = pl.ds(pl.multiple_of(order[k] * rows, rows), rows)
        grad = dot_transposed(raw_grad[part], qkv_weight[...])
        value = hid[part].astype(F32)
        inverse = lax.rsqrt(jnp.mean(value * value, axis=-1, keepdims=True) + EPSILON)
        unit = value * inverse
        gain_part[...] += jnp.sum((grad * unit).reshape(rows // 8, 8, width), axis=0)
        change = grad * gain[...].astype(F32)
        work[order[k]] = (
            inverse * (change - unit * jnp.mean(change * unit, axis=-1, keepdims=True))
        ).astype(BF)

    def q_slice(bits, target):
        start = pl.multiple_of(flip(d, bits) * depth, depth)
        target[...] = transposed_dot(normed[:, pl.ds(start, depth)], raw_grad[...]).astype(BF)

    def q_core_send(i):
        q_slice(1 + 2 * i, q_send.at[i])
        core_slots["q", i] = wire.slot()
        wire.start(core_slots["q", i], lambda: q_send.at[i], lambda: q_core.at[i], to_c)

    line = LineSum(
        wire, d, t, extent, lambda index: work.at[index], up_in, down_in, rows, 2
    )

    def cut(ref, which):
        half = ref.shape[0] // 2
        return ref.at[pl.ds(which * half, half)]

    slots = {}
    routes_a = ((to_x, 3, 2, 0, 0), (to_y, 3, 1, 1, 1), (to_x, 1, 0, 0, 2), (to_y, 2, 0, 1, 3))
    routes_b = ((to_y, 2, 0, 0), (to_x, 1, 1, 1))
    tables = (("q", q_work, q_core, q_a, q_b), ("o", o_work, o_core, o_a, o_b))

    def core_add(i):
        for name, kept, core, unused, unused_too in tables:
            wire.arrive(core_slots[name, i], lambda: core.at[i], to_c)
            add_into(kept.at[i], core.at[i], kept.shape[1])

    def forward(stage, device, source, which, row):
        for name, kept, unused, first, second in tables:
            slots[name, stage, row] = wire.slot()
            inbox_ref = first if stage == "a" else second
            wire.start(
                slots[name, stage, row],
                lambda kept=kept: cut(kept.at[source], which),
                lambda inbox_ref=inbox_ref: inbox_ref.at[row],
                device,
            )

    q_core_send(3)
    q_core_send(1)
    input_block(0)
    line.step(0)
    q_core_send(2)
    q_core_send(0)
    for i in turns:
        q_slice(2 * i, q_work.at[i])
        core_add(i)
        for device, source, unused, which, row in routes_a:
            if source == i:
                forward("a", device, source, which, row)
    input_block(1)
    input_block(2)
    line.step(1)
    input_block(3)
    small_rows = small.shape[0]
    vector = jnp.sum(gain_part[...], axis=0, keepdims=True)
    row = lax.broadcasted_iota(jnp.int32, (small_rows, 128), 0)
    for number in range(width // 128):
        lanes = slice(number * 128, number * 128 + 128)
        small_send[number % 2, number // 2] = jnp.where(
            row == 16, vector[:, lanes], small[:, lanes]
        )
    small_slots = []
    for k, peer in enumerate(peers):
        slot = wire.slot()
        small_slots.append(slot)
        wire.start(
            slot,
            lambda k=k: small_send.at[((t + k + 1) % extent) // 2],
            lambda k=k: small_in.at[k],
            peer,
        )
    for device, source, target, which, row_number in routes_a:
        for name, kept, unused, first, second in tables:
            wire.arrive(slots[name, "a", row_number], lambda: first.at[row_number], device)
            add_into(cut(kept.at[target], which), first.at[row_number], first.shape[1])
        if row_number < 2:
            to, origin, part, b_row = routes_b[row_number]
            forward("b", to, origin, part, b_row)
    result = small_send[t // 2]
    for k, peer in enumerate(peers):
        wire.arrive(small_slots[k], lambda k=k: small_in.at[k], peer)
        result = result + small_in[k]
    small_sum[:, 0:small_rows] = result
    small_sum[:, small_rows : small_rows + 2 * heads] = jnp.broadcast_to(
        head_part[...][None], (8, 2 * heads, 128)
    )
    last_slots = {}
    for bits in range(1, 8):
        last_slots[bits] = wire.slot()
        wire.start(
            last_slots[bits],
            lambda bits=bits: small_sum.at[flip(d, bits)],
            lambda bits=bits: small_last.at[bits],
            (flip(d, bits), t),
        )
    line.step(2)
    for device, source, which, row_number in routes_b:
        for name, kept, unused, first, second in tables:
            came = second.at[row_number]
            wire.arrive(slots[name, "b", row_number], lambda: came, device)
            base = which * (kept.shape[1] // 2)

            def body(start, kept=kept, came=came, base=base, name=name):
                here = pl.ds(start, 16)
                there = pl.ds(pl.multiple_of(base + start, 16), 16)
                value = kept[0, there].astype(F32) + came[here].astype(F32)
                if name == "o":
                    o_out[there] = value
                else:
                    for n, target in enumerate((q_out, k_out, v_out)):
                        target[there] = value[:, n * columns : (n + 1) * columns]

            rows_loop(kept.shape[1] // 2, 16, body)
    line.last()
    mine = work.at[t]

    def finish(start):
        part = pl.ds(start, 16)
        grad_in[part] = grad_middle[part] + own_sum(
            mine, up_in.at[extent - 2], down_in.at[extent - 2], part, pl.ds(0, width)
        )

    rows_loop(rows, 16, finish)
    total = small_sum[d]
    for bits in range(1, 8):
        wire.arrive(
            last_slots[bits], lambda bits=bits: small_last.at[bits], (flip(d, bits), t)
        )
        total = total + small_last[bits]
    share = pltpu.roll(total, (128 - 64 * (t % 2)) % 128, 1)
    square = jnp.concatenate([share, jnp.zeros((128 - share.shape[0], 128), F32)], axis=0).T
    router_out[...] = square[0 : router_out.shape[0], 0:16]
    vectors_out[...] = share[16:24]
    head_width = q_gain_out.shape[1]
    gains = pltpu.roll(total, (128 - head_width * d) % 128, 1)
    q_gain_out[...] = gains[small_rows : small_rows + heads, 0:head_width]
    k_gain_out[...] = gains[small_rows + heads : small_rows + 2 * heads, 0:head_width]
    wire.finish()


def back(extent, *operands):
    seq_len, width = operands[0].shape
    rows = seq_len // extent
    head_gain, small = operands[6], operands[15]
    heads = head_gain.shape[0] // 2
    columns = heads * HD
    depth, o_width = width // 8, width // 8
    split = rows // 2
    shape = jax.ShapeDtypeStruct
    scratch = [
        pltpu.VMEM((seq_len, columns), BF),
        pltpu.VMEM((seq_len, 2 * columns), F32),
        pltpu.VMEM((seq_len, 3 * columns), BF),
        pltpu.VMEM((seq_len, 128), F32),
        pltpu.VMEM((seq_len, 128), F32),
        pltpu.VMEM((8, seq_len), F32),
        pltpu.VMEM((extent - 1, 8, seq_len), F32),
        pltpu.VMEM((8, width), F32),
        pltpu.VMEM((2 * heads, HD), F32),
        pltpu.VMEM((extent, rows, width), BF),
        pltpu.VMEM((extent - 1, rows, width), BF),
        pltpu.VMEM((extent - 1, rows, width), BF),
    ]
    for tall, wide in ((depth, 3 * columns), (columns, o_width)):
        scratch += [
            pltpu.VMEM((4, tall, wide), BF),
            pltpu.VMEM((4, tall, wide), BF),
            pltpu.VMEM((4, tall, wide), BF),
            pltpu.VMEM((4, tall // 2, wide), BF),
            pltpu.VMEM((2, tall // 2, wide), BF),
        ]
    packed = small.shape[0] + 2 * heads
    scratch += [
        pltpu.VMEM((2, 8, small.shape[0], 128), F32),
        pltpu.VMEM((extent - 1, 8, small.shape[0], 128), F32),
        pltpu.VMEM((8, packed, 128), F32),
        pltpu.VMEM((8, packed, 128), F32),
    ]
    return pl.pallas_call(
        functools.partial(back_kernel, extent),
        out_shape=[
            shape((rows, width), F32),
            shape((depth, columns), F32),
            shape((depth, columns), F32),
            shape((depth, columns), F32),
            shape((columns, o_width), F32),
            shape((width // (8 * extent), 16), F32),
            shape((8, 128), F32),
            shape((heads, HD // 8), F32),
            shape((heads, HD // 8), F32),
            shape((8, 128), F32),
        ],
        in_specs=[VM] * len(operands),
        out_specs=[VM] * 10,
        scratch_shapes=scratch + dma_pair(80),
        compiler_params=kernel_params(6),
        cost_estimate=pl.CostEstimate(flops=0, bytes_accessed=1_000_000, transcendentals=0),
    )(*operands)


def spread_kernel(*refs):
    pieces, outs = refs[:8], refs[8:]
    d = lax.axis_index("dp")
    for bits in range(8):
        first = 2 * flip(d, bits)
        for place in range(3):
            for e in range(2):
                outs[place][first + e] = pieces[bits][place, e].astype(F32)


def spread(pieces):
    shape = (16,) + pieces[0].shape[2:]
    return pl.pallas_call(
        spread_kernel,
        out_shape=[jax.ShapeDtypeStruct(shape, F32)] * 3,
        in_specs=[VM] * 8,
        out_specs=[VM] * 3,
        compiler_params=pltpu.CompilerParams(vmem_limit_bytes=VMEM_LIMIT),
        cost_estimate=pl.CostEstimate(flops=0, bytes_accessed=20_000_000, transcendentals=0),
    )(*pieces)


def exchange(value, bits):
    if bits == 0:
        return value
    return lax.ppermute(value, "dp", [(i, i ^ bits) for i in range(8)])


def per_device_block(
    hidden_in,
    teacher,
    lengths,
    routes,
    attn_norm_gain,
    ffn_norm_gain,
    q_weight,
    k_weight,
    v_weight,
    q_gain,
    k_gain,
    o_weight,
    router_weight,
    gate_weight,
    up_weight,
    down_weight,
):
    dp_count = lax.axis_size("dp")
    extent = lax.axis_size("tensor")
    d = lax.axis_index("dp")
    t = lax.axis_index("tensor")
    rows, width = hidden_in.shape
    seq_len = rows * extent
    all_tokens = seq_len * dp_count
    angles = np.arange(seq_len)[:, None] * THETA ** (-np.arange(HD // 2) / (HD // 2))[None, :]
    cosine = jnp.asarray(np.concatenate([np.cos(angles)] * 2, axis=1), F32)
    sine = jnp.asarray(np.concatenate([-np.sin(angles), np.sin(angles)], axis=1), F32)
    (
        chosen,
        middle,
        gates,
        head_gain,
        inverses,
        hidden_bf,
        qkv_full,
        o_full,
        normed,
        units,
        low,
        probs,
        mixed,
        tokens,
        hidden,
        expert_partial,
        landed,
    ) = front(
        extent,
        lengths,
        hidden_in,
        q_weight,
        k_weight,
        v_weight,
        o_weight,
        q_gain,
        k_gain,
        gate_weight,
        up_weight,
        down_weight,
        attn_norm_gain[None, :],
        cosine,
        sine,
        ffn_norm_gain[None, :],
        router_weight.T,
        routes,
    )
    grad_output, row_loss, ffn_grad_partial, inner, active, grads = turn(
        extent,
        lengths,
        expert_partial,
        middle,
        teacher,
        tokens,
        hidden,
        landed,
        gate_weight,
        up_weight,
        down_weight,
    )
    grad_middle, small, attn_grad_rows, *came = leave(
        extent,
        ffn_grad_partial,
        middle,
        grad_output,
        gates,
        chosen,
        ffn_norm_gain[None, :],
        router_weight.T,
        (tokens, grads, inner, active),
    )
    expert_grads = came[:6] + [exchange(came[bits], bits) for bits in (6, 7)]
    (
        grad_in,
        grad_q,
        grad_k,
        grad_v,
        grad_o,
        grad_router,
        vectors,
        grad_q_gain,
        grad_k_gain,
        loss,
    ) = back(
        extent,
        attn_grad_rows.reshape(seq_len, width),
        row_loss,
        hidden_bf,
        attn_norm_gain[None, :],
        qkv_full,
        o_full,
        head_gain,
        cosine,
        sine,
        normed,
        units,
        low,
        probs,
        mixed,
        inverses,
        small,
        grad_middle,
    )
    grad_gate, grad_up, grad_down = spread(expert_grads)
    split = grad_router.shape[0]
    return (
        loss[2, :1],
        grad_in,
        vectors[0, :split],
        vectors[1, :split],
        grad_q,
        grad_k,
        grad_v,
        grad_q_gain,
        grad_k_gain,
        grad_o,
        grad_router,
        grad_gate,
        grad_up,
        grad_down,
    )


def solution(mesh):
    placed = (
        P(("dp", "tensor"), None),
        P(("dp", "tensor"), None),
        P(),
        P("dp", None),
        P(),
        P(),
        P("dp", "tensor"),
        P("dp", "tensor"),
        P("dp", "tensor"),
        P("tensor", "dp"),
        P("tensor", "dp"),
        P("tensor", "dp"),
        P(),
        P(None, "dp", "tensor"),
        P(None, "dp", "tensor"),
        P(None, "tensor", "dp"),
    )
    block = mesh.shape["dp"] == 8 and mesh.shape["tensor"] == 4
    return jax.shard_map(
        per_device_block if block else per_device,
        mesh=mesh,
        in_specs=placed,
        out_specs=(
            P("dp"),
            P(("dp", "tensor"), None),
            P(("dp", "tensor")),
            P(("dp", "tensor")),
            P("dp", "tensor"),
            P("dp", "tensor"),
            P("dp", "tensor"),
            P("tensor", "dp"),
            P("tensor", "dp"),
            P("tensor", "dp"),
            P(("dp", "tensor"), None),
            P(None, "dp", "tensor"),
            P(None, "dp", "tensor"),
            P(None, "tensor", "dp"),
        ),
        check_vma=False,
    )
```

```python
import functools
import math

import jax
import jax.numpy as jnp
import numpy as np
from jax import lax
from jax.experimental import pallas as pl
from jax.experimental.pallas import tpu as pltpu
from jax.sharding import PartitionSpec as P

HD = 128
TOK_DEV = 128
CAP = 68


EPSILON = 1e-05
THETA = 10000.0
HIGHEST = lax.Precision.HIGHEST


def inverse_rms(value):
    return lax.rsqrt(jnp.mean(value * value, axis=-1, keepdims=True) + EPSILON)


def rotate(value, cosine, sinus_table, direction):
    middle_index = value.shape[-1] // 2
    leading = value[..., :middle_index]
    trailing = value[..., middle_index:]
    return jnp.concatenate(
        [
            leading * cosine - direction * trailing * sinus_table,
            trailing * cosine + direction * leading * sinus_table,
        ],
        axis=-1,
    )


def norm_backward(grad_norm, unit_rows, inverse_rows, gain_row):
    scaled = grad_norm * gain_row
    return inverse_rows * (
        scaled - unit_rows * jnp.mean(scaled * unit_rows, axis=-1, keepdims=True)
    )


def fetch_attention(q_weight, k_weight, v_weight, o_weight, q_gain, k_gain):
    return (
        lax.all_gather(q_weight, "dp", axis=0, tiled=True),
        lax.all_gather(k_weight, "dp", axis=0, tiled=True),
        lax.all_gather(v_weight, "dp", axis=0, tiled=True),
        lax.all_gather(o_weight, "dp", axis=1, tiled=True),
        lax.all_gather(q_gain, "dp", axis=1, tiled=True),
        lax.all_gather(k_gain, "dp", axis=1, tiled=True),
    )


def fetch_experts(gate_weight, up_weight, down_weight):
    return (
        lax.all_gather(gate_weight, "dp", axis=1, tiled=True),
        lax.all_gather(up_weight, "dp", axis=1, tiled=True),
        lax.all_gather(down_weight, "dp", axis=2, tiled=True),
    )


def per_device(
    hidden_in,
    teacher,
    lengths,
    routes,
    attn_norm_gain,
    ffn_norm_gain,
    q_weight,
    k_weight,
    v_weight,
    q_gain,
    k_gain,
    o_weight,
    router_weight,
    gate_weight,
    up_weight,
    down_weight,
):
    dp_count = lax.axis_size("dp")
    tp_count = lax.axis_size("tensor")
    group_index = lax.axis_index("dp")
    member = lax.axis_index("tensor")
    row_count, model_width = hidden_in.shape
    seq_len = row_count * tp_count
    all_tokens = seq_len * dp_count
    length = lengths[group_index]
    total_count = jnp.sum(lengths).astype(jnp.float32)
    attn_gain = attn_norm_gain.astype(jnp.float32)
    ffn_gain = ffn_norm_gain.astype(jnp.float32)
    root_size = math.sqrt(HD)
    q_full, k_full, v_full, o_full, qgain_full, kgain_full = fetch_attention(
        q_weight, k_weight, v_weight, o_weight, q_gain, k_gain
    )
    local_heads = q_full.shape[1] // HD
    hidden_all = lax.all_gather(hidden_in, "tensor", axis=0, tiled=True).astype(jnp.float32)
    inverse_one = inverse_rms(hidden_all)
    unit_one = hidden_all * inverse_one
    normed = (unit_one * attn_gain).astype(jnp.bfloat16)
    query_raw = jnp.dot(normed, q_full, preferred_element_type=jnp.float32)
    key_raw = jnp.dot(normed, k_full, preferred_element_type=jnp.float32)
    value_low = jnp.dot(normed, v_full, preferred_element_type=jnp.float32).astype(jnp.bfloat16)
    query_sq, key_sq = lax.psum(
        (jnp.sum(query_raw * query_raw, axis=1), jnp.sum(key_raw * key_raw, axis=1)), "tensor"
    )
    query_inv = lax.rsqrt(query_sq / model_width + EPSILON)[:, None]
    key_inv = lax.rsqrt(key_sq / model_width + EPSILON)[:, None]
    query_unit = query_raw * query_inv
    key_unit = key_raw * key_inv
    query_gain = qgain_full.astype(jnp.float32).reshape(-1)
    key_gain = kgain_full.astype(jnp.float32).reshape(-1)
    positions = jnp.arange(seq_len)
    frequency = THETA ** (-jnp.arange(HD // 2).astype(jnp.float32) / (HD // 2))
    angles = positions.astype(jnp.float32)[:, None] * frequency[None, :]
    cosine = jnp.cos(angles)[:, None, :]
    sinus_table = jnp.sin(angles)[:, None, :]
    queries = rotate(
        (query_unit * query_gain).reshape(seq_len, local_heads, HD), cosine, sinus_table, 1.0
    ).astype(jnp.bfloat16)
    key_rows = rotate(
        (key_unit * key_gain).reshape(seq_len, local_heads, HD), cosine, sinus_table, 1.0
    ).astype(jnp.bfloat16)
    value_rows = value_low.reshape(seq_len, local_heads, HD)
    block_rows = min(512, seq_len)
    starts = jnp.arange(seq_len // block_rows) * block_rows

    def block_scores(start):
        query_block = lax.dynamic_slice_in_dim(queries, start, block_rows, 0)
        scores = (
            jnp.einsum("qhd,khd->hqk", query_block, key_rows, preferred_element_type=jnp.float32)
            / root_size
        )
        query_pos = start + jnp.arange(block_rows)
        allowed = (positions[None, :] <= query_pos[:, None]) & (positions[None, :] < length)
        return (query_block, jnp.where(allowed[None], scores, -1e30))

    def attend(start):
        unused_block, scores = block_scores(start)
        row_top = jnp.max(scores, axis=-1, keepdims=True)
        exponent = jnp.exp(scores - row_top)
        row_total = jnp.sum(exponent, axis=-1, keepdims=True)
        weights = (exponent / row_total).astype(jnp.bfloat16)
        mixed_block = jnp.einsum(
            "hqk,khd->qhd", weights, value_rows, preferred_element_type=jnp.float32
        )
        return (mixed_block.astype(jnp.bfloat16), (row_top + jnp.log(row_total))[..., 0])

    mixed_blocks, log_totals = lax.map(attend, starts)
    mixed = mixed_blocks.reshape(seq_len, local_heads * HD)
    attn_own = lax.psum_scatter(
        jnp.dot(mixed, o_full, preferred_element_type=jnp.float32).astype(jnp.bfloat16),
        "tensor",
        scatter_dimension=0,
        tiled=True,
    ).astype(jnp.float32)
    middle = hidden_in.astype(jnp.float32) + attn_own
    inverse_two = inverse_rms(middle)
    unit_two = middle * inverse_two
    ffn_own = (unit_two * ffn_gain).astype(jnp.bfloat16)
    gate_full, up_full, down_full = fetch_experts(gate_weight, up_weight, down_weight)
    ffn_all = lax.all_gather(ffn_own, "tensor", axis=0, tiled=True)
    expert_count = router_weight.shape[1]
    route_width = routes.shape[1]
    gate_probs = jax.nn.softmax(
        jnp.dot(ffn_all, router_weight, preferred_element_type=jnp.float32), axis=-1
    )
    picked = routes[:, :, None] == jnp.arange(expert_count)[None, None, :]
    route_gates = jnp.sum(jnp.where(picked, gate_probs[:, None, :], 0.0), axis=-1)
    block_count = seq_len // TOK_DEV
    per_expert = block_count * CAP
    picked_ints = picked.reshape(block_count, TOK_DEV * route_width, expert_count).astype(jnp.int32)
    slot_ranks = jnp.sum((jnp.cumsum(picked_ints, axis=1) - 1) * picked_ints, axis=-1).reshape(
        seq_len, route_width
    )
    block_ids = (positions // TOK_DEV)[:, None]
    slot_ids = (routes * per_expert + block_ids * CAP + slot_ranks).reshape(-1)
    slot_total = expert_count * per_expert
    token_ids = jnp.repeat(positions, route_width)
    group_width = 4
    turn_count = expert_count // group_width
    sources = (
        jnp.full((slot_total,), seq_len, jnp.int32)
        .at[slot_ids]
        .set(token_ids)
        .reshape(turn_count, group_width, per_expert)
    )
    slot_gates = (
        jnp.zeros((slot_total,), jnp.float32)
        .at[slot_ids]
        .set(route_gates.reshape(-1))
        .reshape(turn_count, group_width, per_expert, 1)
    )
    ffn_padded = jnp.concatenate([ffn_all, jnp.zeros((1, model_width), jnp.bfloat16)], axis=0)
    expert_running = jnp.zeros((seq_len + 1, model_width), jnp.float32)
    kept_values = []
    for turn_index in range(turn_count):
        lower = turn_index * group_width
        upper = lower + group_width
        expert_inputs = ffn_padded[sources[turn_index]]
        gate_value = jnp.einsum(
            "gpd,gdf->gpf",
            expert_inputs,
            gate_full[lower:upper],
            preferred_element_type=jnp.float32,
        )
        up_value = jnp.einsum(
            "gpd,gdf->gpf", expert_inputs, up_full[lower:upper], preferred_element_type=jnp.float32
        )
        active = (slot_gates[turn_index] * jax.nn.silu(gate_value) * up_value).astype(jnp.bfloat16)
        expert_outputs = jnp.einsum(
            "gpf,gfd->gpd", active, down_full[lower:upper], preferred_element_type=jnp.float32
        )
        expert_running = expert_running.at[sources[turn_index].reshape(-1)].add(
            expert_outputs.reshape(-1, model_width)
        )
        kept_values.append((gate_value, up_value, active))
    expert_own = lax.psum_scatter(
        expert_running[:seq_len].astype(jnp.bfloat16), "tensor", scatter_dimension=0, tiled=True
    ).astype(jnp.float32)
    output = middle + expert_own
    own_positions = member * row_count + jnp.arange(row_count)
    valid_rows = (own_positions < length)[:, None]
    mismatch = output - teacher.astype(jnp.float32)
    loss_own = jnp.sum(jnp.where(valid_rows, mismatch * mismatch, 0.0)) / (
        2.0 * model_width * total_count
    )
    grad_output = jnp.where(valid_rows, mismatch * (all_tokens / total_count), 0.0)
    grad_rows = lax.all_gather(grad_output.astype(jnp.bfloat16), "tensor", axis=0, tiled=True)
    gate_full, up_full, down_full = fetch_experts(gate_weight, up_weight, down_weight)
    grad_padded = jnp.concatenate([grad_rows, jnp.zeros((1, model_width), jnp.bfloat16)], axis=0)
    ffn_grad_running = jnp.zeros((seq_len + 1, model_width), jnp.float32)
    gate_grads = []
    up_grads = []
    down_grads = []
    slot_grads = []
    for turn_index in range(turn_count):
        gate_value, up_value, active = kept_values[turn_index]
        lower = turn_index * group_width
        upper = lower + group_width
        source_rows = sources[turn_index]
        expert_inputs = ffn_padded[source_rows]
        incoming = grad_padded[source_rows]
        grad_active = jnp.einsum(
            "gpd,gfd->gpf", incoming, down_full[lower:upper], preferred_element_type=jnp.float32
        )
        down_turn = jnp.einsum("gpf,gpd->gfd", active, incoming, preferred_element_type=jnp.float32)
        sigmoid_value = jax.nn.sigmoid(gate_value)
        silu_value = gate_value * sigmoid_value
        slot_grads.append(jnp.sum(grad_active * silu_value * up_value, axis=-1))
        grad_inner = grad_active * slot_gates[turn_index]
        grad_gate_value = (
            grad_inner * up_value * sigmoid_value * (1.0 + gate_value * (1.0 - sigmoid_value))
        ).astype(jnp.bfloat16)
        grad_up_value = (grad_inner * silu_value).astype(jnp.bfloat16)
        gate_turn = jnp.einsum(
            "gpd,gpf->gdf", expert_inputs, grad_gate_value, preferred_element_type=jnp.float32
        )
        up_turn = jnp.einsum(
            "gpd,gpf->gdf", expert_inputs, grad_up_value, preferred_element_type=jnp.float32
        )
        gate_grads.append(gate_turn)
        up_grads.append(up_turn)
        down_grads.append(down_turn)
        grad_inputs = jnp.einsum(
            "gpf,gdf->gpd",
            grad_gate_value,
            gate_full[lower:upper],
            preferred_element_type=jnp.float32,
        )
        grad_inputs = grad_inputs + jnp.einsum(
            "gpf,gdf->gpd", grad_up_value, up_full[lower:upper], preferred_element_type=jnp.float32
        )
        ffn_grad_running = ffn_grad_running.at[source_rows.reshape(-1)].add(
            grad_inputs.reshape(-1, model_width)
        )
    slot_grad_all = jnp.concatenate([entry.reshape(-1) for entry in slot_grads])
    route_grads = slot_grad_all[slot_ids].reshape(seq_len, route_width)
    grad_probs = jnp.sum(jnp.where(picked, route_grads[:, :, None], 0.0), axis=1)
    grad_logits = gate_probs * (
        grad_probs - jnp.sum(grad_probs * gate_probs, axis=-1, keepdims=True)
    )
    router_float = router_weight.astype(jnp.float32)
    ffn_grad_part = ffn_grad_running[:seq_len] + jnp.einsum(
        "se,de->sd", grad_logits, router_float, precision=HIGHEST
    )
    router_part = jnp.einsum(
        "sd,se->de", ffn_all, grad_logits, precision=HIGHEST, preferred_element_type=jnp.float32
    )
    ffn_grad_own = lax.psum_scatter(
        ffn_grad_part.astype(jnp.bfloat16), "tensor", scatter_dimension=0, tiled=True
    ).astype(jnp.float32)
    ffn_gain_part = jnp.sum(ffn_grad_own * unit_two, axis=0)
    grad_middle = grad_output + norm_backward(ffn_grad_own, unit_two, inverse_two, ffn_gain)
    attn_grad_rows = lax.all_gather(grad_middle.astype(jnp.bfloat16), "tensor", axis=0, tiled=True)
    q_full, k_full, v_full, o_full, qgain_full, kgain_full = fetch_attention(
        q_weight, k_weight, v_weight, o_weight, q_gain, k_gain
    )
    grad_o = jnp.einsum("sa,sb->ab", mixed, attn_grad_rows, preferred_element_type=jnp.float32)
    grad_mixed = (
        jnp.einsum("sb,ab->sa", attn_grad_rows, o_full, preferred_element_type=jnp.float32)
        .astype(jnp.bfloat16)
        .reshape(seq_len, local_heads, HD)
    )

    def attend_back(carry, inputs):
        key_running, value_running = carry
        start, log_total = inputs
        query_block, scores = block_scores(start)
        probs_float = jnp.exp(scores - log_total[..., None])
        probs_low = probs_float.astype(jnp.bfloat16)
        grad_block = lax.dynamic_slice_in_dim(grad_mixed, start, block_rows, 0)
        value_running = value_running + jnp.einsum(
            "hqk,qhd->khd", probs_low, grad_block, preferred_element_type=jnp.float32
        )
        grad_weights = jnp.einsum(
            "qhd,khd->hqk", grad_block, value_rows, preferred_element_type=jnp.float32
        )
        grad_scores = (
            probs_float
            * (grad_weights - jnp.sum(grad_weights * probs_float, axis=-1, keepdims=True))
        ).astype(jnp.bfloat16)
        query_grad_block = (
            jnp.einsum("hqk,khd->qhd", grad_scores, key_rows, preferred_element_type=jnp.float32)
            / root_size
        )
        key_running = (
            key_running
            + jnp.einsum(
                "hqk,qhd->khd", grad_scores, query_block, preferred_element_type=jnp.float32
            )
            / root_size
        )
        return ((key_running, value_running), query_grad_block)

    zero_heads = jnp.zeros((seq_len, local_heads, HD), jnp.float32)
    (key_grad_rot, value_grad), query_grad_blocks = lax.scan(
        attend_back, (zero_heads, zero_heads), (starts, log_totals)
    )
    query_grad = rotate(
        query_grad_blocks.reshape(seq_len, local_heads, HD), cosine, sinus_table, -1.0
    ).reshape(seq_len, local_heads * HD)
    key_grad = rotate(key_grad_rot, cosine, sinus_table, -1.0).reshape(seq_len, local_heads * HD)
    query_scaled = query_grad * query_gain
    key_scaled = key_grad * key_gain
    qgain_part = jnp.sum(query_grad * query_unit, axis=0)
    kgain_part = jnp.sum(key_grad * key_unit, axis=0)
    query_dot, key_dot, loss_group = lax.psum(
        (
            jnp.sum(query_scaled * query_unit, axis=1),
            jnp.sum(key_scaled * key_unit, axis=1),
            loss_own,
        ),
        "tensor",
    )
    query_raw_grad = (
        query_inv * (query_scaled - query_unit * (query_dot / model_width)[:, None])
    ).astype(jnp.bfloat16)
    key_raw_grad = (key_inv * (key_scaled - key_unit * (key_dot / model_width)[:, None])).astype(
        jnp.bfloat16
    )
    value_raw_grad = value_grad.reshape(seq_len, local_heads * HD).astype(jnp.bfloat16)
    grad_q = jnp.einsum("sd,sa->da", normed, query_raw_grad, preferred_element_type=jnp.float32)
    grad_k = jnp.einsum("sd,sa->da", normed, key_raw_grad, preferred_element_type=jnp.float32)
    grad_v = jnp.einsum("sd,sa->da", normed, value_raw_grad, preferred_element_type=jnp.float32)
    normed_grad = jnp.einsum(
        "sa,da->sd", query_raw_grad, q_full, preferred_element_type=jnp.float32
    )
    normed_grad = normed_grad + jnp.einsum(
        "sa,da->sd", key_raw_grad, k_full, preferred_element_type=jnp.float32
    )
    normed_grad = normed_grad + jnp.einsum(
        "sa,da->sd", value_raw_grad, v_full, preferred_element_type=jnp.float32
    )
    attn_gain_part = jnp.sum(normed_grad * unit_one, axis=0)
    input_part = norm_backward(normed_grad, unit_one, inverse_one, attn_gain)
    split_width = model_width // (dp_count * tp_count)
    input_own, attn_gain_share, ffn_gain_share, router_share = (
        lax.psum_scatter(
            input_part.astype(jnp.bfloat16), "tensor", scatter_dimension=0, tiled=True
        ).astype(jnp.float32),
        lax.psum_scatter(
            attn_gain_part.reshape(dp_count, tp_count, split_width).astype(jnp.bfloat16),
            "tensor",
            scatter_dimension=1,
            tiled=True,
        ).astype(jnp.float32),
        lax.psum_scatter(
            ffn_gain_part.reshape(dp_count, tp_count, split_width).astype(jnp.bfloat16),
            "tensor",
            scatter_dimension=1,
            tiled=True,
        ).astype(jnp.float32),
        lax.psum_scatter(
            router_part.reshape(dp_count, tp_count, split_width, expert_count).astype(jnp.bfloat16),
            "tensor",
            scatter_dimension=1,
            tiled=True,
        ).astype(jnp.float32),
    )
    grad_in = grad_middle + input_own
    (
        grad_q,
        grad_k,
        grad_v,
        grad_o,
        grad_qgain,
        grad_kgain,
        attn_gain_sum,
        ffn_gain_sum,
        router_sum,
    ) = (
        lax.psum_scatter(grad_q.astype(jnp.bfloat16), "dp", scatter_dimension=0, tiled=True).astype(
            jnp.float32
        ),
        lax.psum_scatter(grad_k.astype(jnp.bfloat16), "dp", scatter_dimension=0, tiled=True).astype(
            jnp.float32
        ),
        lax.psum_scatter(grad_v.astype(jnp.bfloat16), "dp", scatter_dimension=0, tiled=True).astype(
            jnp.float32
        ),
        lax.psum_scatter(grad_o.astype(jnp.bfloat16), "dp", scatter_dimension=1, tiled=True).astype(
            jnp.float32
        ),
        lax.psum_scatter(
            qgain_part.reshape(local_heads, HD).astype(jnp.bfloat16),
            "dp",
            scatter_dimension=1,
            tiled=True,
        ).astype(jnp.float32),
        lax.psum_scatter(
            kgain_part.reshape(local_heads, HD).astype(jnp.bfloat16),
            "dp",
            scatter_dimension=1,
            tiled=True,
        ).astype(jnp.float32),
        lax.psum_scatter(
            attn_gain_share.astype(jnp.bfloat16), "dp", scatter_dimension=0, tiled=True
        ).astype(jnp.float32),
        lax.psum_scatter(
            ffn_gain_share.astype(jnp.bfloat16), "dp", scatter_dimension=0, tiled=True
        ).astype(jnp.float32),
        lax.psum_scatter(
            router_share.astype(jnp.bfloat16), "dp", scatter_dimension=0, tiled=True
        ).astype(jnp.float32),
    )
    grad_gate, grad_up, grad_down = (
        lax.psum_scatter(
            jnp.concatenate(gate_grads, axis=0).astype(jnp.bfloat16),
            "dp",
            scatter_dimension=1,
            tiled=True,
        ).astype(jnp.float32),
        lax.psum_scatter(
            jnp.concatenate(up_grads, axis=0).astype(jnp.bfloat16),
            "dp",
            scatter_dimension=1,
            tiled=True,
        ).astype(jnp.float32),
        lax.psum_scatter(
            jnp.concatenate(down_grads, axis=0).astype(jnp.bfloat16),
            "dp",
            scatter_dimension=2,
            tiled=True,
        ).astype(jnp.float32),
    )
    return (
        loss_group.reshape(1),
        grad_in,
        attn_gain_sum.reshape(-1),
        ffn_gain_sum.reshape(-1),
        grad_q,
        grad_k,
        grad_v,
        grad_qgain,
        grad_kgain,
        grad_o,
        router_sum.reshape(-1, expert_count),
        grad_gate,
        grad_up,
        grad_down,
    )


MESH = pl.DeviceIdType.MESH
BF = jnp.bfloat16
F32 = jnp.float32
VMEM_LIMIT = 62 * 1024 * 1024
ANY = pl.BlockSpec(memory_space=pl.ANY)
VM = pl.BlockSpec(memory_space=pltpu.VMEM)


def flip(index, bits):
    for bit in (1, 2, 4):
        if bits & bit:
            index = index + bit * (1 - 2 * ((index // bit) % 2))
    return index


def both(first, second):
    return jnp.logical_and(first, second)


def under(condition, action):
    if condition is None:
        action()
    else:
        pl.when(condition)(action)


class Wire:
    def __init__(self, send_sem, recv_sem):
        self.send_sem, self.recv_sem, self.count, self.sent = send_sem, recv_sem, 0, []

    def slot(self):
        self.count += 1
        return self.count - 1

    def start(self, slot, source, target, device, condition=None):
        def make():
            return pltpu.make_async_remote_copy(
                src_ref=source(),
                dst_ref=target(),
                send_sem=self.send_sem.at[slot],
                recv_sem=self.recv_sem.at[slot],
                device_id=device,
                device_id_type=MESH,
            )

        under(condition, lambda: make().start())
        self.sent.append((condition, make))

    def arrive(self, slot, region, device, condition=None):
        copy = pltpu.make_async_remote_copy(
            src_ref=region(),
            dst_ref=region(),
            send_sem=self.send_sem.at[slot],
            recv_sem=self.recv_sem.at[slot],
            device_id=device,
            device_id_type=MESH,
        )
        under(condition, lambda: copy.wait_recv())

    def finish(self):
        for condition, make in self.sent:
            under(condition, lambda make=make: make().wait_send())
        self.sent = []


class Local:
    def __init__(self, sem):
        self.sem, self.count = sem, 0

    def start(self, source, target):
        copy = pltpu.make_async_copy(source, target, self.sem.at[self.count])
        self.count += 1
        copy.start()
        return copy


def greet(devices):
    barrier = pltpu.get_barrier_semaphore()
    for condition, device in devices:
        under(
            condition,
            lambda device=device: pl.semaphore_signal(
                barrier, inc=1, device_id=device, device_id_type=MESH
            ),
        )
    amount = sum(1 for condition, device in devices if condition is None)
    for condition, device in devices:
        if condition is not None:
            amount = amount + jnp.where(condition, 1, 0)
    pl.semaphore_wait(barrier, amount)


def line_devices(d, t, extent):
    return [(t < extent - 1, (d, t + 1)), (t > 0, (d, t - 1))]


def rows_loop(rows, step, body):
    def run(index, carry):
        body(pl.multiple_of(index * step, step))
        return carry

    lax.fori_loop(0, rows // step, run, 0)


def add_into(target, source, rows):
    def body(start):
        part = pl.ds(start, 16)
        target[part] = target[part] + source[part]

    rows_loop(rows, 16, body)


class LineGather:
    def __init__(self, wire, d, t, extent, own, place):
        self.wire, self.extent = wire, extent
        up = [wire.slot() for unused in range(extent - 1)]
        down = [wire.slot() for unused in range(extent - 1)]
        last = extent - 1
        above, below = (d, t + 1), (d, t - 1)
        self.first = (
            (up[0], own, lambda: place(t), above, t < last),
            (down[0], own, lambda: place(t), below, t > 0),
        )
        self.steps = {}
        for step in range(1, extent):
            from_below, from_above = t >= step, t <= last - step
            lower, upper = t - step, t + step
            self.steps[step] = (
                (
                    up,
                    lambda index=lower: place(index),
                    from_below,
                    both(from_below, t < last),
                    above,
                    below,
                ),
                (
                    down,
                    lambda index=upper: place(index),
                    from_above,
                    both(from_above, t > 0),
                    below,
                    above,
                ),
            )

    def begin(self):
        for slot, own, target, device, condition in self.first:
            self.wire.start(slot, own, target, device, condition)

    def step(self, step):
        for slots, region, valid, onward, to, source in self.steps[step]:
            self.wire.arrive(slots[step - 1], region, source, valid)
            if step < self.extent - 1:
                self.wire.start(slots[step], region, region, to, onward)


def arrival(t, turn):
    near = t - 1 + 2 * (1 - (t + 3) // 4)
    far = 3 * (1 - t // 2)
    choices = (t, near, 6 - t - near - far, far)
    if isinstance(turn, int):
        return choices[turn]
    result = choices[0]
    for number in range(1, 4):
        result = jnp.where(turn == number, choices[number], result)
    return result


LATE = 32


class PlaneGather:
    def __init__(self, wire, d, t, extent, own, place, bundle, rows):
        self.wire, self.place, self.bundle, self.own = wire, place, bundle, own
        self.early, self.half = rows - LATE, (rows - LATE) // 2
        self.to_x, self.to_y, self.to_c = (flip(d, 2), t), (flip(d, 4), t), (flip(d, 1), t)
        self.index = [arrival(t, turn) for turn in range(extent)]
        self.slots = {}
        late = lambda n: (self.early + n * (LATE // 2), LATE // 2)
        self.parts = {0: (0, self.half), 1: (self.half, self.half), 2: late(0), 3: late(1)}
        self.parts["early"], self.parts["late"] = (0, self.early), (self.early, LATE)
        self.send("gx", 0, self.source(0, "late"), self.spot(0, 0, 1, "late"), self.to_x)
        self.send("gy", 0, self.source(0, "late"), self.spot(0, 0, 2, "late"), self.to_y)
        here = self.index[0]
        self.line = LineGather(
            wire,
            d,
            t,
            extent,
            lambda: self.cut(own(), "early"),
            lambda j: self.cut(place(j, 0, 0), "early"),
        )
        self.late_line = LineGather(
            wire, d, t, extent, lambda: bundle(here, 0), lambda j: bundle(j, 0)
        )
        self.line.begin()
        self.stage_first(0)
        for name, i, which, onward, to, source in (
            ("gx", 1, 2, "gfy", self.to_y, self.to_x),
            ("gy", 2, 3, "gfx", self.to_x, self.to_y),
        ):
            self.wait(name, 0, self.spot(0, 0, i, "late"), source)
            self.send(onward, 0, self.spot(0, 0, i, which), self.spot(0, 0, 3, which), to)
        self.stage_second(0)

    def cut(self, ref, which):
        start, size = self.parts[which]
        return ref.at[pl.ds(start, size)]

    def send(self, name, turn, source, target, device):
        slot = self.wire.slot()
        self.slots[name, turn] = slot
        self.wire.start(slot, source, target, device)

    def wait(self, name, turn, region, device):
        self.wire.arrive(self.slots[name, turn], region, device)

    def spot(self, turn, c, i, which):
        return lambda: self.cut(self.place(self.index[turn], c, i), which)

    def source(self, turn, which):
        if turn == 0:
            return lambda: self.cut(self.own(), which)
        return self.spot(turn, 0, 0, which)

    def stage_first(self, turn):
        source, spot = self.source, self.spot
        self.send("x0", turn, source(turn, 0), spot(turn, 0, 1, 0), self.to_x)
        self.send("y1", turn, source(turn, 1), spot(turn, 0, 2, 1), self.to_y)

    def stage_second(self, turn):
        source, spot = self.source, self.spot
        self.send("x1", turn, source(turn, 1), spot(turn, 0, 1, 1), self.to_x)
        self.send("y0", turn, source(turn, 0), spot(turn, 0, 2, 0), self.to_y)
        self.send("c0", turn, source(turn, "early"), spot(turn, 1, 0, "early"), self.to_c)

    def stage(self, turn):
        self.stage_first(turn)
        self.stage_second(turn)

    def relay(self, turn):
        spot = self.spot
        self.wait("x0", turn, spot(turn, 0, 1, 0), self.to_x)
        self.send("fy", turn, spot(turn, 0, 1, 0), spot(turn, 0, 3, 0), self.to_y)
        self.wait("y1", turn, spot(turn, 0, 2, 1), self.to_y)
        self.send("fx", turn, spot(turn, 0, 2, 1), spot(turn, 0, 3, 1), self.to_x)
        self.wait("x1", turn, spot(turn, 0, 1, 1), self.to_x)
        self.send("c1", turn, spot(turn, 0, 1, "early"), spot(turn, 1, 1, "early"), self.to_c)
        self.wait("y0", turn, spot(turn, 0, 2, 0), self.to_y)
        self.send("c2", turn, spot(turn, 0, 2, "early"), spot(turn, 1, 2, "early"), self.to_c)

    def corner(self, turn):
        spot = self.spot
        self.wait("fy", turn, spot(turn, 0, 3, 0), self.to_y)
        self.wait("fx", turn, spot(turn, 0, 3, 1), self.to_x)
        self.send("c3", turn, spot(turn, 0, 3, "early"), spot(turn, 1, 3, "early"), self.to_c)

    def pass_bundle(self, turn):
        region = lambda c: (lambda: self.bundle(self.index[turn], c))
        self.send("cb", turn, region(0), region(1), self.to_c)

    def bundle_start(self, unused):
        spot = self.spot
        self.wait("gfy", 0, spot(0, 0, 3, 2), self.to_y)
        self.wait("gfx", 0, spot(0, 0, 3, 3), self.to_x)
        self.late_line.begin()
        self.pass_bundle(0)

    def bundle_step(self, step):
        self.late_line.step(step)
        self.pass_bundle(step)

    def other(self, turn):
        for i in range(4):
            self.wait("c%d" % i, turn, self.spot(turn, 1, i, "early"), self.to_c)
        self.wait("cb", turn, lambda: self.bundle(self.index[turn], 1), self.to_c)

    def actions(self):
        line, stage, relay, corner, other, late = (
            self.line.step,
            self.stage,
            self.relay,
            self.corner,
            self.other,
            self.bundle_step,
        )
        return (
            (
                (line, 1),
                (stage, 1),
                (self.bundle_start, 0),
                (relay, 0),
                (line, 2),
                (stage, 2),
                (corner, 0),
            ),
            ((relay, 1), (late, 1), (other, 0)),
            ((relay, 2), (line, 3), (stage, 3), (corner, 1)),
            ((other, 1),),
            ((late, 2), (corner, 2), (relay, 3)),
            ((other, 2),),
            ((late, 3), (corner, 3)),
            ((other, 3),),
        )


class LineSum:
    def __init__(self, wire, d, t, extent, block, up_in, down_in, rows, parts):
        self.wire, self.d, self.t, self.extent = wire, d, t, extent
        self.block, self.up_in, self.down_in = block, up_in, down_in
        self.rows, self.parts = rows // parts, parts
        self.up = [[wire.slot() for p in range(parts)] for s in range(extent - 1)]
        self.down = [[wire.slot() for p in range(parts)] for s in range(extent - 1)]

    def cut(self, ref, part):
        return ref.at[pl.ds(part * self.rows, self.rows)]

    def add(self, target, source):
        add_into(target, source, self.rows)

    def flow(self, step, part, near, index, slots, buffers, to_device, from_device):
        wire, extent = self.wire, self.extent
        block = lambda: self.cut(self.block(index), part)
        if step >= 1:
            source = lambda: self.cut(buffers.at[step - 1], part)
            active = both(both(near <= step, near < extent - 1), near >= 1)
            wire.arrive(slots[step - 1][part], source, from_device, active)
            under(active, lambda: self.add(block(), source()))
        wire.start(
            slots[step][part],
            block,
            lambda: self.cut(buffers.at[step], part),
            to_device,
            both(near <= step, near < extent - 1),
        )

    def step(self, step):
        d, t, extent = self.d, self.t, self.extent
        up, down = extent - 1 - step + t, step + t - (extent - 1)
        above, below = (d, t + 1), (d, t - 1)
        for part in range(self.parts):
            self.flow(step, part, t, up, self.up, self.up_in, above, below)
            self.flow(step, part, extent - 1 - t, down, self.down, self.down_in, below, above)

    def last(self):
        d, t, extent = self.d, self.t, self.extent
        for ready, missing, slots, buffers, device in (
            (t > 0, t == 0, self.up, self.up_in, (d, t - 1)),
            (t < extent - 1, t == extent - 1, self.down, self.down_in, (d, t + 1)),
        ):
            buffer = buffers.at[extent - 2]
            for part in range(self.parts):
                self.wire.arrive(
                    slots[extent - 2][part],
                    lambda part=part, buffer=buffer: self.cut(buffer, part),
                    device,
                    ready,
                )

            def clear(buffer=buffer):
                buffer[...] = jnp.zeros(buffer.shape, BF)

            under(missing, clear)


class BundleSum(LineSum):
    def cut(self, ref, part):
        return ref

    def add(self, target, source):
        for i in range(4):
            add_into(target.at[i], source.at[i], LATE)


def own_sum(block, up_in, down_in, part, columns):
    return (
        block[part, columns].astype(F32)
        + up_in[part, columns].astype(F32)
        + down_in[part, columns].astype(F32)
    )


def plane_order(t):
    top = t // 2
    inner = ((t + 1) // 2) % 2
    return (
        3 - 3 * top,
        2 - top,
        (1 - inner) * (1 - top) + (2 + inner) * top,
        inner * (1 - top) + (3 - inner) * top,
    )


def sum_plane(wire, local, d, t, extent, partial, buffers, rows, between=lambda turn: None):
    (
        work,
        own_in,
        a_in,
        b_in,
        up_in,
        down_in,
        late_up,
        late_down,
        late_a,
        late_b,
    ) = buffers
    order = plane_order(t)
    early, half = rows - LATE, (rows - LATE) // 2
    to_x, to_y, to_c = (flip(d, 2), t), (flip(d, 4), t), (flip(d, 1), t)
    turns = (3, 1, 2, 0)
    slots_c, slots_a, slots_b, loads = {}, {}, {}, {}

    def cut(ref, which):
        return ref.at[pl.ds(which * half, half)]

    def late_cut(ref, which):
        return ref.at[pl.ds(early + which * (LATE // 2), LATE // 2)]

    def begin(k):
        for i in turns:
            slots_c[k, i] = wire.slot()
            wire.start(
                slots_c[k, i],
                lambda i=i: partial.at[order[k], 1, i],
                lambda i=i: work.at[k, i],
                to_c,
            )
            loads[k, i] = local.start(partial.at[order[k], 0, i], own_in.at[k % 2, i])

    begin(0)

    def inverse(index):
        where = jnp.int32(0)
        for k in range(1, extent):
            where = where + k * jnp.where(order[k] == index, 1, 0)
        return where

    line = LineSum(
        wire,
        d,
        t,
        extent,
        lambda index: work.at[inverse(index), 0, pl.ds(0, early)],
        up_in,
        down_in,
        early,
        1,
    )
    late_line = BundleSum(
        wire,
        d,
        t,
        extent,
        lambda index: work.at[inverse(index), pl.ds(0, 4), pl.ds(early, LATE)],
        late_up,
        late_down,
        LATE,
        1,
    )
    routes_a = (
        (to_x, 3, 2, 0, 0),
        (to_y, 3, 1, 1, 1),
        (to_x, 1, 0, 0, 2),
        (to_y, 2, 0, 1, 3),
    )
    routes_b = ((to_y, 2, 0, 0), (to_x, 1, 1, 1))
    last = extent - 1

    def send_a(k, source, cutter, inbox):
        for device, origin, unused, which, row in routes_a:
            if origin == source:
                slots_a[inbox is a_in, k, row] = wire.slot()
                wire.start(
                    slots_a[inbox is a_in, k, row],
                    lambda origin=origin, which=which: cutter(work.at[k, origin], which),
                    lambda row=row: inbox.at[k, row] if inbox is a_in else inbox.at[row],
                    device,
                )

    def receive_a(k, cutter, inbox, second, size):
        for device, unused, target, which, row in routes_a:
            region = inbox.at[k, row] if inbox is a_in else inbox.at[row]
            wire.arrive(slots_a[inbox is a_in, k, row], lambda: region, device)
            add_into(cutter(work.at[k, target], which), region, size)
            if row < 2:
                to, origin, part, b_row = routes_b[row]
                slots_b[inbox is a_in, k, b_row] = wire.slot()
                wire.start(
                    slots_b[inbox is a_in, k, b_row],
                    lambda origin=origin, part=part: cutter(work.at[k, origin], part),
                    lambda b_row=b_row: second.at[k, b_row]
                    if inbox is a_in
                    else second.at[b_row],
                    to,
                )

    def receive_b(k, cutter, inbox, second, size):
        for device, unused, which, row in routes_b:
            region = second.at[k, row] if inbox is a_in else second.at[row]
            wire.arrive(slots_b[inbox is a_in, k, row], lambda: region, device)
            add_into(cutter(work.at[k, 0], which), region, size)

    for turn in range(extent + 2):
        if turn + 1 < extent:
            begin(turn + 1)
        if turn < extent:
            k = turn
            for i in turns:
                loads[k, i].wait()
                wire.arrive(slots_c[k, i], lambda k=k, i=i: work.at[k, i], to_c)
                add_into(work.at[k, i], own_in.at[k % 2, i], rows)
                send_a(k, i, cut, a_in)
            if k < last:
                late_line.step(k)
        if turn == extent:
            late_line.last()
            for i in turns:
                for inbox in (late_up, late_down):
                    add_into(
                        work.at[last, i, pl.ds(early, LATE)], inbox.at[last - 1, i], LATE
                    )
                send_a(last, i, late_cut, late_a)
        between(turn)
        if 1 <= turn <= extent:
            receive_a(turn - 1, cut, a_in, b_in, half)
        if turn == extent + 1:
            receive_a(last, late_cut, late_a, late_b, LATE // 2)
        if turn >= 2:
            k = turn - 2
            receive_b(k, cut, a_in, b_in, half)
            if k < last:
                line.step(k)
    between(extent + 2)
    receive_b(last, late_cut, late_a, late_b, LATE // 2)
    line.last()


def own_rows(buffers, rows, columns, body):
    work, up_in, down_in = buffers[0], buffers[4], buffers[5]
    mine = work.at[work.shape[0] - 1, 0]
    up_last, down_last = up_in.at[up_in.shape[0] - 1], down_in.at[down_in.shape[0] - 1]
    early = rows - LATE

    def first(start):
        part = pl.ds(start, 16)
        body(part, own_sum(mine, up_last, down_last, part, columns))

    def second(start):
        part = pl.ds(pl.multiple_of(early + start, 16), 16)
        body(part, mine[part, columns].astype(F32))

    rows_loop(early, 16, first)
    rows_loop(LATE, 16, second)


def sum_scratch(extent, rows, width):
    early = rows - LATE
    return [
        pltpu.VMEM((extent, 4, rows, width), BF),
        pltpu.VMEM((2, 4, rows, width), BF),
        pltpu.VMEM((extent, 4, early // 2, width), BF),
        pltpu.VMEM((extent, 2, early // 2, width), BF),
        pltpu.VMEM((extent - 1, early, width), BF),
        pltpu.VMEM((extent - 1, early, width), BF),
        pltpu.VMEM((extent - 1, 4, LATE, width), BF),
        pltpu.VMEM((extent - 1, 4, LATE, width), BF),
        pltpu.VMEM((4, LATE // 2, width), BF),
        pltpu.VMEM((2, LATE // 2, width), BF),
    ]


def plane_devices(d, t, extent):
    return line_devices(d, t, extent) + [(None, (flip(d, bits), t)) for bits in (1, 2, 4)]


def kernel_params(number):
    return pltpu.CompilerParams(
        collective_id=number, has_side_effects=True, vmem_limit_bytes=VMEM_LIMIT
    )


def dma_pair(count):
    return [pltpu.SemaphoreType.DMA((count,)), pltpu.SemaphoreType.DMA((count,))]


class Pieces:
    def __init__(self, d, in_weight, out_weight, sem, pieces, tables=None):
        self.copies = {}
        slab = out_weight.shape[0] // 2
        for bits, piece in enumerate(pieces):
            start = pl.multiple_of(flip(d, bits) * slab, slab)
            pairs = []
            for place in range(3):
                for e in range(2):
                    if place < 2:
                        column = (2 * place + e) * slab
                        whole = in_weight.at[pl.ds(start, slab), pl.ds(column, slab)]
                    else:
                        whole = out_weight.at[pl.ds(e * slab, slab), pl.ds(start, slab)]
                    if tables is not None and bits == 0:
                        part = tables[place].at[2 * d + e]
                    else:
                        part = piece.at[place, e]
                    pairs.append((part, whole, sem.at[bits * 6 + place * 2 + e]))
            self.copies[bits] = pairs

    def load(self, bits):
        for piece, whole, sem in self.copies[bits]:
            pltpu.make_async_copy(piece, whole, sem).start()

    def loaded(self, bits):
        for piece, whole, sem in self.copies[bits]:
            pltpu.make_async_copy(piece, whole, sem).wait()

    def store(self, bits):
        for piece, whole, sem in self.copies[bits]:
            pltpu.make_async_copy(whole, piece, sem).start()

    def stored(self, bits):
        for piece, whole, sem in self.copies[bits]:
            pltpu.make_async_copy(whole, piece, sem).wait()


def coefficients(columns, d, slab):
    values = columns.astype(F32)
    lane = lax.broadcasted_iota(jnp.int32, values.shape, 1)
    parts = []
    for e in range(2):
        wanted = jnp.logical_or(lane == 2 * d + e, lane == 16 + 2 * d + e)
        one = jnp.sum(jnp.where(wanted, values, 0.0), axis=-1, keepdims=True)
        parts.append(jnp.broadcast_to(one, (values.shape[0], slab)))
    return jnp.concatenate(parts, axis=1)


def line_exchange(wire, t, d, extent, outbox, inbox):
    peers = [(d, (t + k) % extent) for k in range(1, extent)]
    slots = []
    for k, peer in enumerate(peers):
        slot = wire.slot()
        slots.append(slot)
        wire.start(slot, lambda: outbox, lambda k=k: inbox.at[k], peer)
    result = outbox[...]
    for k, peer in enumerate(peers):
        wire.arrive(slots[k], lambda k=k: inbox.at[k], peer)
        result = result + inbox[k]
    return result


def columns_to_rows(ref):
    return ref[...].T[0:8]


def rows_to_columns(value):
    return jnp.concatenate([value, jnp.zeros((120, value.shape[1]), F32)], axis=0).T


def turned(value, cosine, sine, direction):
    return value * cosine + direction * pltpu.roll(value, HD // 2, 1) * sine


def line_peers(d, t, extent):
    return [(None, (d, (t + k) % extent)) for k in range(1, extent)]


def transposed_dot(left, right):
    return lax.dot_general(left, right, (((0,), (0,)), ((), ())), preferred_element_type=F32)


def dot_transposed(left, right):
    return lax.dot_general(left, right, (((1,), (1,)), ((), ())), preferred_element_type=F32)


def front_kernel(
    extent,
    lengths,
    hid,
    q_weight,
    k_weight,
    v_weight,
    o_weight,
    q_gain,
    k_gain,
    gate,
    up,
    down,
    attn_gain,
    cosine,
    sine,
    ffn_gain,
    router,
    routes,
    chosen,
    middle,
    gates,
    head_gain,
    inverses,
    hid_out,
    qkv_out,
    o_out,
    normed_out,
    raw_out,
    low_out,
    probs_out,
    mixed_out,
    tokens,
    hidden,
    out,
    landed,
    hid_all,
    qkv_all,
    o_all,
    gains_all,
    router_rows,
    normed,
    raw,
    low,
    probs,
    mixed,
    sums,
    outbox,
    inbox,
    gathered,
    work,
    up_in,
    down_in,
    in_weight,
    out_weight,
    hidden_stage,
    out_stage,
    send_sem,
    recv_sem,
    local_sem,
    weight_sem,
    stage_sem,
    token_sem,
    probs_sem,
):
    d, t = lax.axis_index("dp"), lax.axis_index("tensor")
    seq_len, width = hid_all.shape
    rows = seq_len // extent
    heads, head_width = q_gain.shape
    columns = heads * HD
    length = lengths[d]
    depth, o_rows, o_width = q_weight.shape[0], o_weight.shape[0], o_weight.shape[1]
    wire, local = Wire(send_sem, recv_sem), Local(local_sem)
    dx, dy, dxy = flip(d, 2), flip(d, 4), flip(d, 6)
    to_x, to_y, to_c = (dx, t), (dy, t), (flip(d, 1), t)

    def block(index):
        return hid_all.at[pl.ds(index * rows, rows)]

    def region(device, which):
        start = pl.multiple_of(device * o_width, o_width)
        if which is None:
            return [qkv_all.at[pl.ds(device * depth, depth)], o_all.at[:, pl.ds(start, o_width)]]
        return [
            qkv_all.at[pl.ds(device * depth + which * (depth // 2), depth // 2)],
            o_all.at[pl.ds(which * (o_rows // 2), o_rows // 2), pl.ds(start, o_width)],
        ]

    copies = [local.start(hid, block(t))]
    for n, weight in enumerate((q_weight, k_weight, v_weight)):
        target = qkv_all.at[pl.ds(d * depth, depth), pl.ds(n * columns, columns)]
        copies.append(local.start(weight, target))
    copies.append(local.start(o_weight, region(d, None)[1]))
    lane = lax.broadcasted_iota(jnp.int32, (heads, HD), 1)
    for n, source in enumerate((q_gain, k_gain)):
        value = source[...].astype(F32)
        spread_out = jnp.zeros((heads, HD), F32)
        for i in range(head_width):
            spread_out += jnp.where(lane == d * head_width + i, value[:, i : i + 1], 0.0)
        gains_all[0, n * heads : (n + 1) * heads] = spread_out
    router_rows[...] = jnp.zeros(router_rows.shape, BF)
    router_rows[0:16] = router[...]
    router_rows[16:32] = router[...]
    own_routes = routes[:, pl.ds(pl.multiple_of(t * rows, rows), rows)]
    expert = lax.broadcasted_iota(jnp.int32, (128, rows), 0)
    picked = jnp.zeros((128, rows), F32)
    for k in range(own_routes.shape[0]):
        match = both(own_routes[k : k + 1] == expert % 16, expert < 32)
        picked = jnp.where(match, 1.0, picked)
    chosen[...] = picked.T
    greet(line_peers(d, t, extent) + [(None, (flip(d, bits), t)) for bits in range(1, 8)])
    for copy in copies:
        copy.wait()

    def send(device, sources, targets):
        slots = []
        for source, target in zip(sources, targets):
            slot = wire.slot()
            wire.start(slot, lambda source=source: source, lambda target=target: target, device)
            slots.append(slot)
        return slots

    def arrive(slots, regions, device):
        for slot, part in zip(slots, regions):
            wire.arrive(slot, lambda: part, device)

    line = LineGather(wire, d, t, extent, lambda: block(t), block)
    line.begin()
    x_slots, y_slots, c_slots = {}, {}, {}
    for which, other in ((0, 1), (1, 0)):
        x_slots[which] = send(to_x, region(d, which), region(d, which))
        y_slots[other] = send(to_y, region(d, other), region(d, other))
    c_slots[1] = send(to_c, region(d, None), region(d, None))
    gain_slots = {}
    for bits in range(1, 8):
        gain_slots[bits] = wire.slot()
        wire.start(
            gain_slots[bits],
            lambda: gains_all.at[0],
            lambda bits=bits: gains_all.at[bits],
            (flip(d, bits), t),
        )
    weights = Pieces(
        d, in_weight, out_weight, weight_sem, [landed.at[bits] for bits in range(8)]
    )
    own_experts = Pieces(d, in_weight, out_weight, weight_sem, [None], (gate, up, down))
    own_experts.load(0)
    arrive(x_slots[0], region(dx, 0), to_x)
    over_y = send(to_y, region(dx, 0), region(dx, 0))
    arrive(y_slots[1], region(dy, 1), to_y)
    over_x = send(to_x, region(dy, 1), region(dy, 1))
    piece_slots = {}
    for bits in (2, 4, 1, 3, 5, 6, 7):
        first = 2 * flip(d, bits)
        piece_slots[bits] = send(
            (flip(d, bits), t),
            [weight.at[pl.ds(first, 2)] for weight in (gate, up, down)],
            [landed.at[bits, place] for place in range(3)],
        )
    line.step(1)
    arrive(x_slots[1], region(dx, 1), to_x)
    c_slots[3] = send(to_c, region(dx, None), region(dx, None))
    arrive(y_slots[0], region(dy, 0), to_y)
    c_slots[5] = send(to_c, region(dy, None), region(dy, None))
    for step in range(2, extent):
        line.step(step)
    arrive(over_y, region(dxy, 0), to_y)
    arrive(over_x, region(dxy, 1), to_x)
    c_slots[7] = send(to_c, region(dxy, None), region(dxy, None))
    for bits in range(1, 8):
        wire.arrive(
            gain_slots[bits], lambda bits=bits: gains_all.at[bits], (flip(d, bits), t)
        )
    total_gain = gains_all[0]
    for bits in range(1, 8):
        total_gain = total_gain + gains_all[bits]
    head_gain[...] = total_gain
    tile = 256

    def normalize(start):
        part = pl.ds(start, 64)
        value = hid_all[part].astype(F32)
        unit = value * lax.rsqrt(jnp.mean(value * value, axis=-1, keepdims=True) + EPSILON)
        normed[part] = (unit * attn_gain[...].astype(F32)).astype(BF)

    rows_loop(seq_len, 64, normalize)
    for bits in (1, 3, 5, 7):
        arrive(c_slots[bits], region(flip(d, bits), None), to_c)
    kept = [
        local.start(hid_all, hid_out),
        local.start(qkv_all, qkv_out),
        local.start(o_all, o_out),
        local.start(normed, normed_out),
    ]

    def project(start):
        part = pl.ds(start, tile)
        result = jnp.dot(normed[part], qkv_all[...], preferred_element_type=F32)
        raw[part] = result
        lane = lax.broadcasted_iota(jnp.int32, (tile, 128), 1)
        squares = [
            jnp.sum(jnp.square(result[:, n * columns : (n + 1) * columns]), axis=-1, keepdims=True)
            for n in range(2)
        ]
        sums[part] = jnp.where(lane == 0, squares[0], jnp.where(lane == 1, squares[1], 0.0))

    rows_loop(seq_len, tile, project)
    outbox[...] = columns_to_rows(sums)
    total = line_exchange(wire, t, d, extent, outbox, inbox)
    inverses[...] = rows_to_columns(lax.rsqrt(total / width + EPSILON))
    low[:, 2 * columns :] = raw[:, 2 * columns :].astype(BF)

    def turn_head(h, carry):
        for n in range(2):
            section = pl.ds(pl.multiple_of(n * columns + h * HD, HD), HD)
            unit = raw[:, section] * inverses[:, n : n + 1]
            raw[:, section] = unit
            scaled = unit * head_gain[pl.ds(n * heads + h, 1)]
            low[:, section] = turned(scaled, cosine[...], sine[...], 1.0).astype(BF)
        return carry

    lax.fori_loop(0, heads, turn_head, 0)
    kept += [local.start(raw, raw_out), local.start(low, low_out)]
    total_line = LineSum(
        wire, d, t, extent, lambda index: work.at[index], up_in, down_in, rows, 2
    )
    order = plane_order(t)

    def probs_copy(k):
        part = pl.ds(pl.multiple_of(order[k] * rows, rows), rows)
        return pltpu.make_async_copy(
            probs.at[k % 2], probs_out.at[pl.ds(0, heads), part], probs_sem.at[k % 2]
        )

    for k in range(extent):
        begin = pl.multiple_of(order[k] * rows, rows)
        part = pl.ds(begin, rows)
        if k >= 2:
            probs_copy(k - 2).wait()

        def head(h, carry, begin=begin, part=part, k=k):
            section = pl.ds(pl.multiple_of(h * HD, HD), HD)
            key_section = pl.ds(pl.multiple_of(columns + h * HD, HD), HD)
            value_section = pl.ds(pl.multiple_of(2 * columns + h * HD, HD), HD)
            scores = dot_transposed(low[part, section], low[:, key_section]) / math.sqrt(HD)
            row = begin + lax.broadcasted_iota(jnp.int32, scores.shape, 0)
            column = lax.broadcasted_iota(jnp.int32, scores.shape, 1)
            allowed = both(column <= row, column < length)
            scores = jnp.where(allowed, scores, -1e30)
            powers = jnp.exp(scores - jnp.max(scores, axis=-1, keepdims=True))
            result = powers / jnp.sum(powers, axis=-1, keepdims=True)
            probs[k % 2, h] = result
            mixed[part, section] = jnp.dot(
                result.astype(BF), low[:, value_section], preferred_element_type=F32
            ).astype(BF)
            return carry

        lax.fori_loop(0, heads, head, 0)
        probs_copy(k).start()
        work[order[k]] = jnp.dot(
            mixed[part], o_all[...], preferred_element_type=F32
        ).astype(BF)
        if k != 1:
            total_line.step(max(k - 1, 0))
    kept.append(local.start(mixed, mixed_out))
    total_line.last()
    mine = work.at[t]
    everything = pl.ds(0, width)
    packet = gathered.at[t, 0, 0]

    def body(start):
        part = pl.ds(start, 16)
        value = hid[part].astype(F32) + own_sum(
            mine, up_in.at[extent - 2], down_in.at[extent - 2], part, everything
        )
        middle[part] = value
        unit = value * lax.rsqrt(jnp.mean(value * value, axis=-1, keepdims=True) + EPSILON)
        packet[part, 0:width] = (unit * ffn_gain[...].astype(F32)).astype(BF)

    rows_loop(rows, 16, body)
    logits = dot_transposed(packet[:, 0:width], router_rows[...])
    lane = lax.broadcasted_iota(jnp.int32, logits.shape, 1)
    top = jnp.max(jnp.where(lane < 16, logits, -1e30), axis=-1, keepdims=True)
    powers = jnp.where(lane < 32, jnp.exp(logits - top), 0.0)
    chance = powers / jnp.sum(jnp.where(lane < 16, powers, 0.0), axis=-1, keepdims=True)
    gates[...] = chance
    coeff = chance * chosen[...]
    high = coeff.astype(BF).astype(F32)
    packet[:, width : width + 128] = jnp.where(lane < 16, high, coeff - high).astype(BF)

    def place(j, c, i):
        return gathered.at[j, c, i]

    def bundle(j, c):
        return gathered.at[j, c, pl.ds(0, 4), pl.ds(rows - LATE, LATE)]

    gather = PlaneGather(wire, d, t, extent, lambda: packet, place, bundle, rows)
    for bits in range(1, 8):
        arrive(
            piece_slots[bits], [landed.at[bits, place] for place in range(3)], (flip(d, bits), t)
        )
        weights.load(bits)
    own_experts.loaded(0)
    for bits in range(1, 8):
        weights.loaded(bits)
    units = out_weight.shape[0]

    def stage_copies(slot, j, c):
        return (
            pltpu.make_async_copy(hidden_stage.at[slot], hidden.at[j, c], stage_sem.at[0, slot]),
            pltpu.make_async_copy(out_stage.at[slot], out.at[j, c], stage_sem.at[1, slot]),
        )

    actions = gather.actions()

    def group(g, carry):
        for number, steps in enumerate(actions):

            @pl.when(g == number)
            def _():
                for action, argument in steps:
                    action(argument)

        j, c, slot = arrival(t, g // 2), g % 2, g % 2

        @pl.when(g >= 2)
        def _():
            for copy in stage_copies(slot, j, c):
                copy.wait()

        pltpu.make_async_copy(gathered.at[j, c], tokens.at[j, c], token_sem.at[g]).start()

        def some(first, carry):
            blocks, part = pl.ds(2 * first, 2), pl.ds(first * 2 * rows, 2 * rows)
            values = jnp.dot(
                gathered[j, c, blocks, :, 0:width].reshape(2 * rows, width),
                in_weight[...],
                preferred_element_type=F32,
            )
            hidden_stage[slot, part] = values.astype(BF)
            gate_value, up_value = values[:, :units], values[:, units:]
            coeff = coefficients(
                gathered[j, c, blocks, :, width : width + 128].reshape(2 * rows, 128),
                d,
                units // 2,
            )
            active = (coeff * (gate_value * jax.nn.sigmoid(gate_value)) * up_value).astype(BF)
            result = jnp.dot(active, out_weight[...], preferred_element_type=F32)
            out_stage[slot, blocks] = result.astype(BF).reshape(2, rows, width)
            return carry

        lax.fori_loop(0, 2, some, 0)
        for copy in stage_copies(slot, j, c):
            copy.start()
        return carry

    lax.fori_loop(0, 2 * extent, group, 0)
    for slot in range(2):
        for copy in stage_copies(slot, 0, slot):
            copy.wait()
    for g in range(2 * extent):
        pltpu.make_async_copy(
            gathered.at[arrival(t, g // 2), g % 2],
            tokens.at[arrival(t, g // 2), g % 2],
            token_sem.at[g],
        ).wait()
    for k in range(extent - 2, extent):
        probs_copy(k).wait()
    for copy in kept:
        copy.wait()
    wire.finish()


SMEM = pl.BlockSpec(memory_space=pltpu.SMEM)


def front(extent, lengths, hid, *rest):
    rows, width = hid.shape
    seq_len = rows * extent
    slab = rest[6].shape[1]
    heads = rest[4].shape[0]
    columns = heads * HD
    shape = jax.ShapeDtypeStruct
    kept = [
        shape((seq_len, width), BF),
        shape((width, 3 * columns), BF),
        shape((columns, width), BF),
        shape((seq_len, width), BF),
        shape((seq_len, 3 * columns), F32),
        shape((seq_len, 3 * columns), BF),
        shape((heads, seq_len, seq_len), F32),
        shape((seq_len, columns), BF),
    ]
    return pl.pallas_call(
        functools.partial(front_kernel, extent),
        out_shape=[
            shape((rows, 128), F32),
            shape((rows, width), F32),
            shape((rows, 128), F32),
            shape((2 * heads, HD), F32),
            shape((seq_len, 128), F32),
        ]
        + kept
        + [
            shape((extent, 2, 4, rows, width + 128), BF),
            shape((extent, 2, 4 * rows, 4 * slab), BF),
            shape((extent, 2, 4, rows, width), BF),
            shape((8, 3, 2, slab, slab), BF),
        ],
        in_specs=[SMEM, VM] + [ANY] * 4 + [VM] * 2 + [ANY] * 3 + [VM] * 6,
        out_specs=[VM] * 5 + [ANY] * 12,
        scratch_shapes=[
            pltpu.VMEM((seq_len, width), BF),
            pltpu.VMEM((width, 3 * columns), BF),
            pltpu.VMEM((columns, width), BF),
            pltpu.VMEM((8, 2 * heads, HD), F32),
            pltpu.VMEM((128, width), BF),
            pltpu.VMEM((seq_len, width), BF),
            pltpu.VMEM((seq_len, 3 * columns), F32),
            pltpu.VMEM((seq_len, 3 * columns), BF),
            pltpu.VMEM((2, heads, rows, seq_len), F32),
            pltpu.VMEM((seq_len, columns), BF),
            pltpu.VMEM((seq_len, 128), F32),
            pltpu.VMEM((8, seq_len), F32),
            pltpu.VMEM((extent - 1, 8, seq_len), F32),
            pltpu.VMEM((extent, 2, 4, rows, width + 128), BF),
            pltpu.VMEM((extent, rows, width), BF),
            pltpu.VMEM((extent - 1, rows, width), BF),
            pltpu.VMEM((extent - 1, rows, width), BF),
            pltpu.VMEM((width, 4 * slab), BF),
            pltpu.VMEM((2 * slab, width), BF),
            pltpu.VMEM((2, 4 * rows, 4 * slab), BF),
            pltpu.VMEM((2, 4, rows, width), BF),
        ]
        + dma_pair(180)
        + [
            pltpu.SemaphoreType.DMA((16,)),
            pltpu.SemaphoreType.DMA((48,)),
            pltpu.SemaphoreType.DMA((2, 2)),
            pltpu.SemaphoreType.DMA((2 * extent,)),
            pltpu.SemaphoreType.DMA((2,)),
        ],
        compiler_params=kernel_params(1),
        cost_estimate=pl.CostEstimate(flops=0, bytes_accessed=300_000_000, transcendentals=0),
    )(lengths, hid, *rest)


def turn_kernel(extent, lengths, partial, middle, teacher, tokens, hidden, *rest):
    landed, tables = rest[0], rest[1:4]
    grad_output, row_loss, out, inner_out, active_out, grads = rest[4:10]
    buffers = rest[10:20]
    (
        packet,
        in_weight,
        out_weight,
        coeff_tile,
        hidden_tile,
        factors,
        grad_tile,
        out_stage,
        active_tile,
        inner_tile,
        send_sem,
        recv_sem,
        local_sem,
        weight_sem,
        tile_sem,
        load_sem,
    ) = rest[20:]
    d, t = lax.axis_index("dp"), lax.axis_index("tensor")
    rows, width = middle.shape
    greet(plane_devices(d, t, extent))
    wire, local = Wire(send_sem, recv_sem), Local(local_sem)
    pieces = [landed.at[bits] for bits in range(8)]
    weights = Pieces(d, in_weight, out_weight, weight_sem, pieces, tables)
    units, slab = out_weight.shape[0], out_weight.shape[0] // 2
    count = 2 * extent

    def factor_loads(g):
        j, c, slot = g // 2, g % 2, g % 2
        part = (pl.ds(0, 4), pl.ds(0, rows), pl.ds(width, 128))
        return (
            pltpu.make_async_copy(
                tokens.at[(j, c) + part], coeff_tile.at[slot], load_sem.at[0, slot]
            ),
            pltpu.make_async_copy(hidden.at[j, c], hidden_tile.at[slot], load_sem.at[1, slot]),
        )

    def active_store(g):
        return pltpu.make_async_copy(
            active_tile.at[g % 2], active_out.at[g // 2, g % 2], load_sem.at[2, g % 2]
        )

    def prepare(g):
        if g + 1 < count:
            for copy in factor_loads(g + 1):
                copy.start()
        for copy in factor_loads(g):
            copy.wait()
        if g >= 2:
            active_store(g - 2).wait()
        slot = g % 2

        def some(first, carry):
            size = 2 * rows
            blocks, part = pl.ds(2 * first, 2), pl.ds(first * size, size)
            gate_value = hidden_tile[slot, part, 0:units].astype(F32)
            up_value = hidden_tile[slot, part, units : 2 * units].astype(F32)
            coeff = coefficients(coeff_tile[slot, blocks].reshape(size, 128), d, slab)
            sigmoid_value = jax.nn.sigmoid(gate_value)
            silu_value = gate_value * sigmoid_value
            slope = sigmoid_value * (1.0 + gate_value * (1.0 - sigmoid_value))
            direct = silu_value * up_value
            factors[g, part, 0:units] = (coeff * up_value * slope).astype(BF)
            factors[g, part, units : 2 * units] = (coeff * silu_value).astype(BF)
            factors[g, part, 2 * units : 3 * units] = direct.astype(BF)
            active_tile[slot, part] = (coeff * direct).astype(BF)
            return carry

        lax.fori_loop(0, 2, some, 0)
        active_store(g).start()

    for copy in factor_loads(0):
        copy.start()

    def between(turn_number):
        if turn_number == 1:
            for bits in range(8):
                weights.load(bits)
        if turn_number < extent:
            prepare(2 * turn_number)
            prepare(2 * turn_number + 1)

    sum_plane(wire, local, d, t, extent, partial, buffers, rows, between)
    for g in (count - 2, count - 1):
        active_store(g).wait()

    total_count = lengths[0]
    for n in range(1, lengths.shape[0]):
        total_count = total_count + lengths[n]
    length = lengths[d]

    def body(part, value):
        row = t * rows + part.start + lax.broadcasted_iota(jnp.int32, (16, 1), 0)
        count = jnp.broadcast_to(total_count, (16, 1)).astype(F32)
        weight = jnp.where(row < length, 8 * extent * rows / count, 0.0)
        output = middle[part] + value
        mismatch = output - teacher[part].astype(F32)
        scaled = mismatch * weight
        grad_output[part] = scaled
        packet[part] = scaled.astype(BF)
        row_loss[part] = jnp.broadcast_to(
            jnp.sum(scaled * mismatch, axis=-1, keepdims=True), (16, 128)
        )

    own_rows(buffers, rows, pl.ds(0, width), body)

    def place(j, c, i):
        return grads.at[j, c, i]

    def bundle(j, c):
        return grads.at[j, c, pl.ds(0, 4), pl.ds(rows - LATE, LATE)]

    own_copy = local.start(packet, place(t, 0, 0))
    gather = PlaneGather(wire, d, t, extent, lambda: packet, place, bundle, rows)
    own_copy.wait()
    for bits in range(8):
        weights.loaded(bits)
    actions = gather.actions()

    def out_copies(j, c):
        return (
            pltpu.make_async_copy(out_stage, out.at[j, c], tile_sem.at[1]),
            pltpu.make_async_copy(inner_tile, inner_out.at[j, c], tile_sem.at[2]),
        )

    def group(g, carry):
        j, c = arrival(t, g // 2), g % 2
        grad_copy = pltpu.make_async_copy(grads.at[j, c], grad_tile, tile_sem.at[0])
        for number, steps in enumerate(actions):

            @pl.when(g == number)
            def _():
                for action, argument in steps:
                    action(argument)

        grad_copy.start()

        @pl.when(g >= 1)
        def _():
            for copy in out_copies(j, c):
                copy.wait()

        grad_copy.wait()
        index = 2 * j + c

        def some(first, carry):
            size = 2 * rows
            blocks, part = pl.ds(2 * first, 2), pl.ds(first * size, size)
            grad_active = dot_transposed(
                grad_tile[blocks].reshape(size, width), out_weight[...]
            )
            product = grad_active * factors[index, part, 2 * units : 3 * units].astype(F32)
            lane = lax.broadcasted_iota(jnp.int32, (size, 128), 1)
            sums = jnp.zeros((size, 128), F32)
            for e in range(2):
                one = jnp.sum(product[:, e * slab : (e + 1) * slab], axis=-1, keepdims=True)
                sums = sums + jnp.where(lane == 2 * d + e, one, 0.0)
            out_stage[blocks, :, width : width + 128] = sums.astype(BF).reshape(2, rows, 128)
            for n in range(2):
                columns = pl.ds(n * units, units)
                inner_tile[part, columns] = (
                    grad_active * factors[index, part, columns].astype(F32)
                ).astype(BF)
            result = dot_transposed(inner_tile[part], in_weight[...]).astype(BF)
            out_stage[blocks, :, 0:width] = result.reshape(2, rows, width)
            return carry

        lax.fori_loop(0, 2, some, 0)
        for copy in out_copies(j, c):
            copy.start()
        return carry

    lax.fori_loop(0, 2 * extent, group, 0)
    for copy in out_copies(0, 0):
        copy.wait()
    wire.finish()


def turn(extent, lengths, partial, middle, teacher, tokens, hidden, landed, *tables):
    rows, width = middle.shape
    slab = landed.shape[3]
    return pl.pallas_call(
        functools.partial(turn_kernel, extent),
        out_shape=[
            jax.ShapeDtypeStruct((rows, width), F32),
            jax.ShapeDtypeStruct((rows, 128), F32),
            jax.ShapeDtypeStruct((extent, 2, 4, rows, width + 128), BF),
            jax.ShapeDtypeStruct((extent, 2, 4 * rows, 4 * slab), BF),
            jax.ShapeDtypeStruct((extent, 2, 4 * rows, 2 * slab), BF),
            jax.ShapeDtypeStruct((extent, 2, 4, rows, width), BF),
        ],
        in_specs=[SMEM, ANY, VM, VM] + [ANY] * 6,
        out_specs=[VM, VM] + [ANY] * 4,
        scratch_shapes=sum_scratch(extent, rows, width)
        + [
            pltpu.VMEM((rows, width), BF),
            pltpu.VMEM((width, 4 * slab), BF),
            pltpu.VMEM((2 * slab, width), BF),
            pltpu.VMEM((2, 4, rows, 128), BF),
            pltpu.VMEM((2, 4 * rows, 4 * slab), BF),
            pltpu.VMEM((2 * extent, 4 * rows, 6 * slab), BF),
            pltpu.VMEM((4, rows, width), BF),
            pltpu.VMEM((4, rows, width + 128), BF),
            pltpu.VMEM((2, 4 * rows, 2 * slab), BF),
            pltpu.VMEM((4 * rows, 4 * slab), BF),
        ]
        + dma_pair(150)
        + [
            pltpu.SemaphoreType.DMA((20,)),
            pltpu.SemaphoreType.DMA((48,)),
            pltpu.SemaphoreType.DMA((3,)),
            pltpu.SemaphoreType.DMA((3, 2)),
        ],
        compiler_params=kernel_params(4),
        cost_estimate=pl.CostEstimate(flops=0, bytes_accessed=450_000_000, transcendentals=0),
    )(lengths, partial, middle, teacher, tokens, hidden, landed, *tables)


class WeightGrads:
    def __init__(self, sources, tiles, totals, sem):
        self.sources, self.tiles, self.sem = sources, tiles, sem
        self.in_total, self.out_total = totals

    def copies(self, g):
        j, c, slot = g // 2, g % 2, g % 2
        return [
            pltpu.make_async_copy(source.at[j, c], tile.at[slot], self.sem.at[n, slot])
            for n, (source, tile) in enumerate(zip(self.sources, self.tiles))
        ]

    def start(self, g):
        for copy in self.copies(g):
            copy.start()

    def clear(self):
        self.in_total[...] = jnp.zeros(self.in_total.shape, F32)
        self.out_total[...] = jnp.zeros(self.out_total.shape, F32)

    def work(self, g, count):
        if g + 1 < count:
            self.start(g + 1)
        for copy in self.copies(g):
            copy.wait()
        slot = g % 2
        token_tile, grad_tile, inner_tile, active_tile = (tile.at[slot] for tile in self.tiles)
        size, width = inner_tile.shape[0], grad_tile.shape[2]

        def into_in(start):
            part = pl.ds(start, 256)
            left = token_tile[:, :, part].reshape(size, 256)
            self.in_total[part] += transposed_dot(left, inner_tile[...])

        rows_loop(width, 256, into_in)

        def into_out(start):
            part = pl.ds(start, 512)
            right = grad_tile[:, :, part].reshape(size, 512)
            self.out_total[:, part] += transposed_dot(active_tile[...], right)

        rows_loop(width, 512, into_out)

    def pieces(self, d, stage):
        slab = stage.shape[3]
        for bits in range(8):
            part = pl.ds(pl.multiple_of(flip(d, bits) * slab, slab), slab)
            for place in range(3):
                for e in range(2):
                    if place < 2:
                        column = (2 * place + e) * slab
                        value = self.in_total[part, column : column + slab]
                    else:
                        value = self.out_total[e * slab : (e + 1) * slab, part]
                    stage[bits, place, e] = value.astype(BF)


def leave_kernel(extent, partial, middle, grad_output, gates, chosen, gain, router, *rest):
    sources = rest[:4]
    grad_middle, small, grads = rest[4:7]
    came = rest[7:15]
    buffers = rest[15:25]
    tiles, totals = rest[25:29], rest[29:31]
    stage, packet, grad_logits, gain_part, ffn_own, send_sem, recv_sem, local_sem, tile_sem = rest[31:]
    d, t = lax.axis_index("dp"), lax.axis_index("tensor")
    rows, width = middle.shape
    greet(line_devices(d, t, extent) + [(None, (flip(d, bits), t)) for bits in range(1, 6)])
    wire, local = Wire(send_sem, recv_sem), Local(local_sem)
    weight_grads = WeightGrads(sources, tiles, totals, tile_sem)
    count = 2 * extent
    piece_slots, copies = [], []
    weight_grads.start(0)

    def between(turn_number):
        if turn_number == 0:
            weight_grads.clear()
        if turn_number < extent:
            weight_grads.work(2 * turn_number, count)
            weight_grads.work(2 * turn_number + 1, count)
        if turn_number == extent + 2:
            weight_grads.pieces(d, stage)
            for bits in range(1, 6):
                slot = wire.slot()
                piece_slots.append(slot)
                wire.start(
                    slot,
                    lambda bits=bits: stage.at[bits],
                    lambda bits=bits: came[bits],
                    (flip(d, bits), t),
                )
            for bits in (0, 6, 7):
                copies.append(local.start(stage.at[bits], came[bits]))

    sum_plane(wire, local, d, t, extent, partial, buffers, rows, between)

    def collect(part, value):
        grad_logits[part] = value

    own_rows(buffers, rows, pl.ds(width, 128), collect)
    coeff_grad = grad_logits[...] * chosen[...]
    lane = lax.broadcasted_iota(jnp.int32, coeff_grad.shape, 1)
    probs = jnp.where(lane < 16, gates[...], 0.0)
    coeff_grad = jnp.where(lane < 16, coeff_grad, 0.0)
    logit_grad = probs * (coeff_grad - jnp.sum(coeff_grad * probs, axis=-1, keepdims=True))
    grad_logits[...] = logit_grad
    high = logit_grad.astype(BF)
    low_part = (logit_grad - high.astype(F32)).astype(BF)
    for begin in range(0, width, 512):
        columns = slice(begin, begin + 512)
        grad_middle[:, columns] = jnp.dot(
            high[:, 0:16], router[:, columns], preferred_element_type=F32
        ) + jnp.dot(low_part[:, 0:16], router[:, columns], preferred_element_type=F32)
    gain_part[...] = jnp.zeros(gain_part.shape, F32)

    def body(part, value):
        grad = value + grad_middle[part]
        value = middle[part]
        inverse = lax.rsqrt(jnp.mean(value * value, axis=-1, keepdims=True) + EPSILON)
        unit = value * inverse
        product = grad * unit
        gain_part[...] += product[0:8] + product[8:16]
        gain_row = gain[...].astype(F32)
        ffn_own[part] = (unit * gain_row).astype(BF)
        scaled = grad * gain_row
        result = grad_output[part] + inverse * (
            scaled - unit * jnp.mean(scaled * unit, axis=-1, keepdims=True)
        )
        grad_middle[part] = result
        packet[part] = result.astype(BF)

    own_rows(buffers, rows, pl.ds(0, width), body)

    def place(index):
        return grads.at[index]

    copies.append(local.start(packet, place(t)))
    line = LineGather(wire, d, t, extent, lambda: packet, place)
    line.begin()
    router_part = transposed_dot(high, ffn_own[...]) + transposed_dot(low_part, ffn_own[...])
    small[0:16] = router_part[0:16]
    row = lax.broadcasted_iota(jnp.int32, (8, width), 0)
    gain_sum = jnp.sum(gain_part[...], axis=0, keepdims=True)
    small[16:24] = jnp.where(row == 1, gain_sum, 0.0)
    for step in range(1, extent):
        line.step(step)
    for copy in copies:
        copy.wait()
    for n, slot in enumerate(piece_slots):
        wire.arrive(slot, lambda: came[1 + n], (flip(d, 1 + n), t))
    wire.finish()


def leave(extent, partial, middle, grad_output, gates, chosen, gain, router, sources):
    rows, width = middle.shape
    tokens, grads, inner, active = sources
    units = active.shape[3]
    piece = jax.ShapeDtypeStruct((3, 2, units // 2, units // 2), BF)
    return pl.pallas_call(
        functools.partial(leave_kernel, extent),
        out_shape=[
            jax.ShapeDtypeStruct((rows, width), F32),
            jax.ShapeDtypeStruct((24, width), F32),
            jax.ShapeDtypeStruct((extent, rows, width), BF),
        ]
        + [piece] * 8,
        in_specs=[ANY, VM, VM, VM, VM, VM, VM] + [ANY] * 4,
        out_specs=[VM, VM] + [ANY] * 9,
        scratch_shapes=sum_scratch(extent, rows, width + 128)
        + [pltpu.VMEM((2,) + source.shape[2:], BF) for source in sources]
        + [
            pltpu.VMEM((width, 2 * units), F32),
            pltpu.VMEM((units, width), F32),
            pltpu.VMEM((8,) + piece.shape, BF),
            pltpu.VMEM((rows, width), BF),
            pltpu.VMEM((rows, 128), F32),
            pltpu.VMEM((8, width), F32),
            pltpu.VMEM((rows, width), BF),
        ]
        + dma_pair(120)
        + [pltpu.SemaphoreType.DMA((24,)), pltpu.SemaphoreType.DMA((4, 2))],
        compiler_params=kernel_params(5),
        cost_estimate=pl.CostEstimate(flops=0, bytes_accessed=350_000_000, transcendentals=0),
    )(partial, middle, grad_output, gates, chosen, gain, router, *sources)


def back_kernel(
    extent,
    grads,
    row_loss,
    hid_far,
    gain,
    qkv_far,
    o_weight,
    head_gain,
    cosine,
    sine,
    normed_far,
    units_far,
    low_far,
    probs_far,
    mixed,
    inverses,
    small,
    middle_far,
    grad_in,
    q_out,
    k_out,
    v_out,
    o_out,
    router_out,
    vectors_out,
    q_gain_out,
    k_gain_out,
    loss,
    low,
    probs,
    units,
    qkv_weight,
    normed,
    hid,
    grad_middle,
    load_sem,
    grad_mixed,
    scaled,
    raw_grad,
    sums,
    dots,
    outbox,
    inbox,
    gain_part,
    head_part,
    work,
    up_in,
    down_in,
    q_send,
    q_work,
    q_core,
    q_a,
    q_b,
    o_send,
    o_work,
    o_core,
    o_a,
    o_b,
    small_send,
    small_in,
    small_sum,
    small_last,
    send_sem,
    recv_sem,
):
    d, t = lax.axis_index("dp"), lax.axis_index("tensor")
    seq_len, width = hid.shape
    rows = seq_len // extent
    heads = head_gain.shape[0] // 2
    columns = heads * HD
    depth, o_width = q_out.shape[0], o_out.shape[1]
    peers = [(d, (t + k) % extent) for k in range(1, extent)]
    greet(line_peers(d, t, extent) + [(None, (flip(d, bits), t)) for bits in range(1, 8)])
    wire, local = Wire(send_sem, recv_sem), Local(load_sem)
    loads = [
        local.start(source, target)
        for source, target in (
            (low_far, low),
            (probs_far, probs),
            (units_far.at[pl.ds(0, seq_len), pl.ds(0, 2 * columns)], units),
            (normed_far, normed),
            (qkv_far, qkv_weight),
            (hid_far, hid),
            (middle_far, grad_middle),
        )
    ]
    to_x, to_y, to_c = (flip(d, 2), t), (flip(d, 4), t), (flip(d, 1), t)
    tile = 256
    root = math.sqrt(HD)
    turns = (3, 1, 2, 0)

    def mix(start):
        part = pl.ds(start, tile)
        grad_mixed[part] = dot_transposed(grads[part], o_weight[...]).astype(BF)

    rows_loop(seq_len, tile, mix)

    def o_slice(bits, target):
        start = pl.multiple_of(flip(d, bits) * o_width, o_width)
        target[...] = transposed_dot(mixed[...], grads[:, pl.ds(start, o_width)]).astype(BF)

    core_slots = {}
    for i in turns:
        o_slice(1 + 2 * i, o_send.at[i])
        core_slots["o", i] = wire.slot()
        wire.start(core_slots["o", i], lambda i=i: o_send.at[i], lambda i=i: o_core.at[i], to_c)
    for i in turns:
        o_slice(2 * i, o_work.at[i])
    sums[...] = jnp.zeros(sums.shape, F32)
    for load in loads:
        load.wait()

    def head(h, carry):
        section = pl.ds(pl.multiple_of(h * HD, HD), HD)
        key_section = pl.ds(pl.multiple_of(columns + h * HD, HD), HD)
        value_section = pl.ds(pl.multiple_of(2 * columns + h * HD, HD), HD)
        chance = probs[h]
        incoming = grad_mixed[:, section]
        raw_grad[:, value_section] = transposed_dot(chance.astype(BF), incoming).astype(BF)
        grad_probs = dot_transposed(incoming, low[:, value_section])
        grad_scores = (
            chance * (grad_probs - jnp.sum(grad_probs * chance, axis=-1, keepdims=True))
        ).astype(BF)
        pair = (
            jnp.dot(grad_scores, low[:, key_section], preferred_element_type=F32) / root,
            transposed_dot(grad_scores, low[:, section]) / root,
        )
        lane = lax.broadcasted_iota(jnp.int32, (seq_len, 128), 1)
        for n, where in enumerate((section, key_section)):
            value = turned(pair[n], cosine[...], sine[...], -1.0)
            unit = units[:, where]
            head_part[pl.ds(n * heads + h, 1)] = jnp.sum(value * unit, axis=0, keepdims=True)
            value = value * head_gain[pl.ds(n * heads + h, 1)]
            scaled[:, where] = value
            sums[...] += jnp.where(lane == n, jnp.sum(value * unit, axis=-1, keepdims=True), 0.0)
        return carry

    lax.fori_loop(0, heads, head, 0)
    outbox[...] = columns_to_rows(sums)
    outbox[2:3] = jnp.broadcast_to(jnp.sum(row_loss[:, 0:1], axis=0, keepdims=True), (1, seq_len))
    total = line_exchange(wire, t, d, extent, outbox, inbox)
    loss[...] = total[:, 0:128] / (2.0 * width * 8 * seq_len)
    dots[...] = rows_to_columns(total / width)

    def head_again(h, carry):
        for n in range(2):
            section = pl.ds(pl.multiple_of(n * columns + h * HD, HD), HD)
            raw_grad[:, section] = (
                inverses[:, n : n + 1]
                * (scaled[:, section] - units[:, section] * dots[:, n : n + 1])
            ).astype(BF)
        return carry

    lax.fori_loop(0, heads, head_again, 0)
    gain_part[...] = jnp.zeros(gain_part.shape, F32)
    order = plane_order(t)

    def input_block(k):
        part = pl.ds(pl.multiple_of(order[k] * rows, rows), rows)
        grad = dot_transposed(raw_grad[part], qkv_weight[...])
        value = hid[part].astype(F32)
        inverse = lax.rsqrt(jnp.mean(value * value, axis=-1, keepdims=True) + EPSILON)
        unit = value * inverse
        gain_part[...] += jnp.sum((grad * unit).reshape(rows // 8, 8, width), axis=0)
        change = grad * gain[...].astype(F32)
        work[order[k]] = (
            inverse * (change - unit * jnp.mean(change * unit, axis=-1, keepdims=True))
        ).astype(BF)

    def q_slice(bits, target):
        start = pl.multiple_of(flip(d, bits) * depth, depth)
        target[...] = transposed_dot(normed[:, pl.ds(start, depth)], raw_grad[...]).astype(BF)

    def q_core_send(i):
        q_slice(1 + 2 * i, q_send.at[i])
        core_slots["q", i] = wire.slot()
        wire.start(core_slots["q", i], lambda: q_send.at[i], lambda: q_core.at[i], to_c)

    line = LineSum(
        wire, d, t, extent, lambda index: work.at[index], up_in, down_in, rows, 2
    )

    def cut(ref, which):
        half = ref.shape[0] // 2
        return ref.at[pl.ds(which * half, half)]

    slots = {}
    routes_a = ((to_x, 3, 2, 0, 0), (to_y, 3, 1, 1, 1), (to_x, 1, 0, 0, 2), (to_y, 2, 0, 1, 3))
    routes_b = ((to_y, 2, 0, 0), (to_x, 1, 1, 1))
    tables = (("q", q_work, q_core, q_a, q_b), ("o", o_work, o_core, o_a, o_b))

    def core_add(i):
        for name, kept, core, unused, unused_too in tables:
            wire.arrive(core_slots[name, i], lambda: core.at[i], to_c)
            add_into(kept.at[i], core.at[i], kept.shape[1])

    def forward(stage, device, source, which, row):
        for name, kept, unused, first, second in tables:
            slots[name, stage, row] = wire.slot()
            inbox_ref = first if stage == "a" else second
            wire.start(
                slots[name, stage, row],
                lambda kept=kept: cut(kept.at[source], which),
                lambda inbox_ref=inbox_ref: inbox_ref.at[row],
                device,
            )

    q_core_send(3)
    q_core_send(1)
    input_block(0)
    line.step(0)
    q_core_send(2)
    q_core_send(0)
    for i in turns:
        q_slice(2 * i, q_work.at[i])
        core_add(i)
        for device, source, unused, which, row in routes_a:
            if source == i:
                forward("a", device, source, which, row)
    input_block(1)
    input_block(2)
    line.step(1)
    input_block(3)
    small_rows = small.shape[0]
    vector = jnp.sum(gain_part[...], axis=0, keepdims=True)
    row = lax.broadcasted_iota(jnp.int32, (small_rows, 128), 0)
    for number in range(width // 128):
        lanes = slice(number * 128, number * 128 + 128)
        small_send[number % 2, number // 2] = jnp.where(
            row == 16, vector[:, lanes], small[:, lanes]
        )
    small_slots = []
    for k, peer in enumerate(peers):
        slot = wire.slot()
        small_slots.append(slot)
        wire.start(
            slot,
            lambda k=k: small_send.at[((t + k + 1) % extent) // 2],
            lambda k=k: small_in.at[k],
            peer,
        )
    for device, source, target, which, row_number in routes_a:
        for name, kept, unused, first, second in tables:
            wire.arrive(slots[name, "a", row_number], lambda: first.at[row_number], device)
            add_into(cut(kept.at[target], which), first.at[row_number], first.shape[1])
        if row_number < 2:
            to, origin, part, b_row = routes_b[row_number]
            forward("b", to, origin, part, b_row)
    result = small_send[t // 2]
    for k, peer in enumerate(peers):
        wire.arrive(small_slots[k], lambda k=k: small_in.at[k], peer)
        result = result + small_in[k]
    small_sum[:, 0:small_rows] = result
    small_sum[:, small_rows : small_rows + 2 * heads] = jnp.broadcast_to(
        head_part[...][None], (8, 2 * heads, 128)
    )
    last_slots = {}
    for bits in range(1, 8):
        last_slots[bits] = wire.slot()
        wire.start(
            last_slots[bits],
            lambda bits=bits: small_sum.at[flip(d, bits)],
            lambda bits=bits: small_last.at[bits],
            (flip(d, bits), t),
        )
    line.step(2)
    for device, source, which, row_number in routes_b:
        for name, kept, unused, first, second in tables:
            came = second.at[row_number]
            wire.arrive(slots[name, "b", row_number], lambda: came, device)
            base = which * (kept.shape[1] // 2)

            def body(start, kept=kept, came=came, base=base, name=name):
                here = pl.ds(start, 16)
                there = pl.ds(pl.multiple_of(base + start, 16), 16)
                value = kept[0, there].astype(F32) + came[here].astype(F32)
                if name == "o":
                    o_out[there] = value
                else:
                    for n, target in enumerate((q_out, k_out, v_out)):
                        target[there] = value[:, n * columns : (n + 1) * columns]

            rows_loop(kept.shape[1] // 2, 16, body)
    line.last()
    mine = work.at[t]

    def finish(start):
        part = pl.ds(start, 16)
        grad_in[part] = grad_middle[part] + own_sum(
            mine, up_in.at[extent - 2], down_in.at[extent - 2], part, pl.ds(0, width)
        )

    rows_loop(rows, 16, finish)
    total = small_sum[d]
    for bits in range(1, 8):
        wire.arrive(
            last_slots[bits], lambda bits=bits: small_last.at[bits], (flip(d, bits), t)
        )
        total = total + small_last[bits]
    share = pltpu.roll(total, (128 - 64 * (t % 2)) % 128, 1)
    square = jnp.concatenate([share, jnp.zeros((128 - share.shape[0], 128), F32)], axis=0).T
    router_out[...] = square[0 : router_out.shape[0], 0:16]
    vectors_out[...] = share[16:24]
    head_width = q_gain_out.shape[1]
    gains = pltpu.roll(total, (128 - head_width * d) % 128, 1)
    q_gain_out[...] = gains[small_rows : small_rows + heads, 0:head_width]
    k_gain_out[...] = gains[small_rows + heads : small_rows + 2 * heads, 0:head_width]
    wire.finish()


def back(extent, *operands):
    seq_len, width = operands[0].shape
    rows = seq_len // extent
    head_gain, small = operands[6], operands[15]
    heads = head_gain.shape[0] // 2
    columns = heads * HD
    depth, o_width = width // 8, width // 8
    split = rows // 2
    shape = jax.ShapeDtypeStruct
    scratch = [
        pltpu.VMEM((seq_len, 3 * columns), BF),
        pltpu.VMEM((heads, seq_len, seq_len), F32),
        pltpu.VMEM((seq_len, 2 * columns), F32),
        pltpu.VMEM((width, 3 * columns), BF),
        pltpu.VMEM((seq_len, width), BF),
        pltpu.VMEM((seq_len, width), BF),
        pltpu.VMEM((rows, width), F32),
        pltpu.SemaphoreType.DMA((8,)),
        pltpu.VMEM((seq_len, columns), BF),
        pltpu.VMEM((seq_len, 2 * columns), F32),
        pltpu.VMEM((seq_len, 3 * columns), BF),
        pltpu.VMEM((seq_len, 128), F32),
        pltpu.VMEM((seq_len, 128), F32),
        pltpu.VMEM((8, seq_len), F32),
        pltpu.VMEM((extent - 1, 8, seq_len), F32),
        pltpu.VMEM((8, width), F32),
        pltpu.VMEM((2 * heads, HD), F32),
        pltpu.VMEM((extent, rows, width), BF),
        pltpu.VMEM((extent - 1, rows, width), BF),
        pltpu.VMEM((extent - 1, rows, width), BF),
    ]
    for tall, wide in ((depth, 3 * columns), (columns, o_width)):
        scratch += [
            pltpu.VMEM((4, tall, wide), BF),
            pltpu.VMEM((4, tall, wide), BF),
            pltpu.VMEM((4, tall, wide), BF),
            pltpu.VMEM((4, tall // 2, wide), BF),
            pltpu.VMEM((2, tall // 2, wide), BF),
        ]
    packed = small.shape[0] + 2 * heads
    scratch += [
        pltpu.VMEM((2, 8, small.shape[0], 128), F32),
        pltpu.VMEM((extent - 1, 8, small.shape[0], 128), F32),
        pltpu.VMEM((8, packed, 128), F32),
        pltpu.VMEM((8, packed, 128), F32),
    ]
    return pl.pallas_call(
        functools.partial(back_kernel, extent),
        out_shape=[
            shape((rows, width), F32),
            shape((depth, columns), F32),
            shape((depth, columns), F32),
            shape((depth, columns), F32),
            shape((columns, o_width), F32),
            shape((width // (8 * extent), 16), F32),
            shape((8, 128), F32),
            shape((heads, HD // 8), F32),
            shape((heads, HD // 8), F32),
            shape((8, 128), F32),
        ],
        in_specs=[ANY if n in (2, 4, 9, 10, 11, 12, 16) else VM for n in range(17)],
        out_specs=[VM] * 10,
        scratch_shapes=scratch + dma_pair(80),
        compiler_params=kernel_params(6),
        cost_estimate=pl.CostEstimate(flops=0, bytes_accessed=1_000_000, transcendentals=0),
    )(*operands)


def spread_kernel(*refs):
    pieces, large, (vectors, q_gain, k_gain, loss, router) = refs[:8], refs[8:13], refs[13:18]
    tables, large_out = refs[18:21], refs[21:26]
    loss_out, attn_out, ffn_out, q_gain_out, k_gain_out, router_out = refs[26:32]
    near, stage, *copies, in_sem, out_sem, large_sem = refs[32:]
    d = lax.axis_index("dp")
    slab = near.shape[3]
    moves = []
    for n, (source, middle, target) in enumerate(zip(large, copies, large_out)):
        moves.append(
            (
                pltpu.make_async_copy(source, middle, large_sem.at[0, n]),
                pltpu.make_async_copy(middle, target, large_sem.at[1, n]),
            )
        )
    loads = [
        pltpu.make_async_copy(pieces[bits], near.at[bits], in_sem.at[bits]) for bits in range(8)
    ]
    for bits in range(4):
        loads[bits].start()
    for first, second in moves:
        first.start()
    for bits in range(4, 8):
        loads[bits].start()
    loss_out[...] = loss[2:3, 0:1]
    attn_out[...] = vectors[0:1, 0 : attn_out.shape[1]]
    ffn_out[...] = vectors[1:2, 0 : ffn_out.shape[1]]
    q_gain_out[...] = q_gain[...]
    k_gain_out[...] = k_gain[...]
    router_out[...] = router[...]
    stores = []
    for bits in range(8):
        loads[bits].wait()
        begin = 2 * flip(d, bits)
        for place in range(3):
            for e in range(2):

                def body(start, bits=bits, place=place, e=e, begin=begin):
                    part = pl.ds(start, 64)
                    stage[place, begin + e, part] = near[bits, place, e, part].astype(F32)

                rows_loop(slab, 64, body)
            store = pltpu.make_async_copy(
                stage.at[place, pl.ds(begin, 2)],
                tables[place].at[pl.ds(begin, 2)],
                out_sem.at[bits, place],
            )
            store.start()
            stores.append(store)
        if bits == 3:
            for first, second in moves:
                first.wait()
                second.start()
    for first, second in moves:
        second.wait()
    for store in stores:
        store.wait()


def spread(pieces, large, small):
    table = jax.ShapeDtypeStruct((16,) + pieces[0].shape[2:], F32)
    vectors, q_gain, k_gain, loss, router = small
    shape = jax.ShapeDtypeStruct
    split = router.shape[0]
    same = lambda array: shape(array.shape, array.dtype)
    return pl.pallas_call(
        spread_kernel,
        out_shape=[table] * 3
        + [same(array) for array in large]
        + [
            shape((1, 1), F32),
            shape((1, split), F32),
            shape((1, split), F32),
            same(q_gain),
            same(k_gain),
            same(router),
        ],
        in_specs=[ANY] * 13 + [VM] * 5,
        out_specs=[ANY] * 8 + [VM] * 6,
        scratch_shapes=[
            pltpu.VMEM((8,) + pieces[0].shape, BF),
            pltpu.VMEM((3,) + table.shape, F32),
        ]
        + [pltpu.VMEM(array.shape, F32) for array in large]
        + [
            pltpu.SemaphoreType.DMA((8,)),
            pltpu.SemaphoreType.DMA((8, 3)),
            pltpu.SemaphoreType.DMA((2, 5)),
        ],
        compiler_params=pltpu.CompilerParams(vmem_limit_bytes=VMEM_LIMIT),
        cost_estimate=pl.CostEstimate(flops=0, bytes_accessed=20_000_000, transcendentals=0),
    )(*pieces, *large, *small)


def exchange(value, bits):
    if bits == 0:
        return value
    return lax.ppermute(value, "dp", [(i, i ^ bits) for i in range(8)])


def per_device_block(
    hidden_in,
    teacher,
    lengths,
    routes,
    attn_norm_gain,
    ffn_norm_gain,
    q_weight,
    k_weight,
    v_weight,
    q_gain,
    k_gain,
    o_weight,
    router_weight,
    gate_weight,
    up_weight,
    down_weight,
):
    extent = lax.axis_size("tensor")
    rows, width = hidden_in.shape
    seq_len = rows * extent
    angles = np.arange(seq_len)[:, None] * THETA ** (-np.arange(HD // 2) / (HD // 2))[None, :]
    cosine = jnp.asarray(np.concatenate([np.cos(angles)] * 2, axis=1), F32)
    sine = jnp.asarray(np.concatenate([-np.sin(angles), np.sin(angles)], axis=1), F32)
    (
        chosen,
        middle,
        gates,
        head_gain,
        inverses,
        hidden_bf,
        qkv_full,
        o_full,
        normed,
        units,
        low,
        probs,
        mixed,
        tokens,
        hidden,
        expert_partial,
        landed,
    ) = front(
        extent,
        lengths,
        hidden_in,
        q_weight,
        k_weight,
        v_weight,
        o_weight,
        q_gain,
        k_gain,
        gate_weight,
        up_weight,
        down_weight,
        attn_norm_gain[None, :],
        cosine,
        sine,
        ffn_norm_gain[None, :],
        router_weight.T,
        routes.T,
    )
    grad_output, row_loss, ffn_grad_partial, inner, active, grads = turn(
        extent,
        lengths,
        expert_partial,
        middle,
        teacher,
        tokens,
        hidden,
        landed,
        gate_weight,
        up_weight,
        down_weight,
    )
    grad_middle, small, attn_grad_rows, *came = leave(
        extent,
        ffn_grad_partial,
        middle,
        grad_output,
        gates,
        chosen,
        ffn_norm_gain[None, :],
        router_weight.T,
        (tokens, grads, inner, active),
    )
    expert_grads = came[:6] + [exchange(came[bits], bits) for bits in (6, 7)]
    (
        grad_in,
        grad_q,
        grad_k,
        grad_v,
        grad_o,
        grad_router,
        vectors,
        grad_q_gain,
        grad_k_gain,
        loss,
    ) = back(
        extent,
        attn_grad_rows.reshape(seq_len, width),
        row_loss,
        hidden_bf,
        attn_norm_gain[None, :],
        qkv_full,
        o_full,
        head_gain,
        cosine,
        sine,
        normed,
        units,
        low,
        probs,
        mixed,
        inverses,
        small,
        grad_middle,
    )
    (
        grad_gate,
        grad_up,
        grad_down,
        grad_in,
        grad_q,
        grad_k,
        grad_v,
        grad_o,
        loss,
        attn_part,
        ffn_part,
        grad_q_gain,
        grad_k_gain,
        grad_router,
    ) = spread(
        expert_grads,
        (grad_in, grad_q, grad_k, grad_v, grad_o),
        (vectors, grad_q_gain, grad_k_gain, loss, grad_router),
    )
    return (
        loss[0],
        grad_in,
        attn_part[0],
        ffn_part[0],
        grad_q,
        grad_k,
        grad_v,
        grad_q_gain,
        grad_k_gain,
        grad_o,
        grad_router,
        grad_gate,
        grad_up,
        grad_down,
    )


def solution(mesh):
    placed = (
        P(("dp", "tensor"), None),
        P(("dp", "tensor"), None),
        P(),
        P("dp", None),
        P(),
        P(),
        P("dp", "tensor"),
        P("dp", "tensor"),
        P("dp", "tensor"),
        P("tensor", "dp"),
        P("tensor", "dp"),
        P("tensor", "dp"),
        P(),
        P(None, "dp", "tensor"),
        P(None, "dp", "tensor"),
        P(None, "tensor", "dp"),
    )
    block = mesh.shape["dp"] == 8 and mesh.shape["tensor"] == 4
    return jax.shard_map(
        per_device_block if block else per_device,
        mesh=mesh,
        in_specs=placed,
        out_specs=(
            P("dp"),
            P(("dp", "tensor"), None),
            P(("dp", "tensor")),
            P(("dp", "tensor")),
            P("dp", "tensor"),
            P("dp", "tensor"),
            P("dp", "tensor"),
            P("tensor", "dp"),
            P("tensor", "dp"),
            P("tensor", "dp"),
            P(("dp", "tensor"), None),
            P(None, "dp", "tensor"),
            P(None, "dp", "tensor"),
            P(None, "tensor", "dp"),
        ),
        check_vma=False,
    )
```

```python
import functools
import math

import jax
import jax.numpy as jnp
import numpy as np
from jax import lax
from jax.experimental import pallas as pl
from jax.experimental.pallas import tpu as pltpu
from jax.sharding import PartitionSpec as P

HD = 128
TOK_DEV = 128
CAP = 68


EPSILON = 1e-05
THETA = 10000.0
HIGHEST = lax.Precision.HIGHEST


def inverse_rms(value):
    return lax.rsqrt(jnp.mean(value * value, axis=-1, keepdims=True) + EPSILON)


def rotate(value, cosine, sinus_table, direction):
    middle_index = value.shape[-1] // 2
    leading = value[..., :middle_index]
    trailing = value[..., middle_index:]
    return jnp.concatenate(
        [
            leading * cosine - direction * trailing * sinus_table,
            trailing * cosine + direction * leading * sinus_table,
        ],
        axis=-1,
    )


def norm_backward(grad_norm, unit_rows, inverse_rows, gain_row):
    scaled = grad_norm * gain_row
    return inverse_rows * (
        scaled - unit_rows * jnp.mean(scaled * unit_rows, axis=-1, keepdims=True)
    )


def fetch_attention(q_weight, k_weight, v_weight, o_weight, q_gain, k_gain):
    return (
        lax.all_gather(q_weight, "dp", axis=0, tiled=True),
        lax.all_gather(k_weight, "dp", axis=0, tiled=True),
        lax.all_gather(v_weight, "dp", axis=0, tiled=True),
        lax.all_gather(o_weight, "dp", axis=1, tiled=True),
        lax.all_gather(q_gain, "dp", axis=1, tiled=True),
        lax.all_gather(k_gain, "dp", axis=1, tiled=True),
    )


def fetch_experts(gate_weight, up_weight, down_weight):
    return (
        lax.all_gather(gate_weight, "dp", axis=1, tiled=True),
        lax.all_gather(up_weight, "dp", axis=1, tiled=True),
        lax.all_gather(down_weight, "dp", axis=2, tiled=True),
    )


def per_device(
    hidden_in,
    teacher,
    lengths,
    routes,
    attn_norm_gain,
    ffn_norm_gain,
    q_weight,
    k_weight,
    v_weight,
    q_gain,
    k_gain,
    o_weight,
    router_weight,
    gate_weight,
    up_weight,
    down_weight,
):
    dp_count = lax.axis_size("dp")
    tp_count = lax.axis_size("tensor")
    group_index = lax.axis_index("dp")
    member = lax.axis_index("tensor")
    row_count, model_width = hidden_in.shape
    seq_len = row_count * tp_count
    all_tokens = seq_len * dp_count
    length = lengths[group_index]
    total_count = jnp.sum(lengths).astype(jnp.float32)
    attn_gain = attn_norm_gain.astype(jnp.float32)
    ffn_gain = ffn_norm_gain.astype(jnp.float32)
    root_size = math.sqrt(HD)
    q_full, k_full, v_full, o_full, qgain_full, kgain_full = fetch_attention(
        q_weight, k_weight, v_weight, o_weight, q_gain, k_gain
    )
    local_heads = q_full.shape[1] // HD
    hidden_all = lax.all_gather(hidden_in, "tensor", axis=0, tiled=True).astype(jnp.float32)
    inverse_one = inverse_rms(hidden_all)
    unit_one = hidden_all * inverse_one
    normed = (unit_one * attn_gain).astype(jnp.bfloat16)
    query_raw = jnp.dot(normed, q_full, preferred_element_type=jnp.float32)
    key_raw = jnp.dot(normed, k_full, preferred_element_type=jnp.float32)
    value_low = jnp.dot(normed, v_full, preferred_element_type=jnp.float32).astype(jnp.bfloat16)
    query_sq, key_sq = lax.psum(
        (jnp.sum(query_raw * query_raw, axis=1), jnp.sum(key_raw * key_raw, axis=1)), "tensor"
    )
    query_inv = lax.rsqrt(query_sq / model_width + EPSILON)[:, None]
    key_inv = lax.rsqrt(key_sq / model_width + EPSILON)[:, None]
    query_unit = query_raw * query_inv
    key_unit = key_raw * key_inv
    query_gain = qgain_full.astype(jnp.float32).reshape(-1)
    key_gain = kgain_full.astype(jnp.float32).reshape(-1)
    positions = jnp.arange(seq_len)
    frequency = THETA ** (-jnp.arange(HD // 2).astype(jnp.float32) / (HD // 2))
    angles = positions.astype(jnp.float32)[:, None] * frequency[None, :]
    cosine = jnp.cos(angles)[:, None, :]
    sinus_table = jnp.sin(angles)[:, None, :]
    queries = rotate(
        (query_unit * query_gain).reshape(seq_len, local_heads, HD), cosine, sinus_table, 1.0
    ).astype(jnp.bfloat16)
    key_rows = rotate(
        (key_unit * key_gain).reshape(seq_len, local_heads, HD), cosine, sinus_table, 1.0
    ).astype(jnp.bfloat16)
    value_rows = value_low.reshape(seq_len, local_heads, HD)
    block_rows = min(512, seq_len)
    starts = jnp.arange(seq_len // block_rows) * block_rows

    def block_scores(start):
        query_block = lax.dynamic_slice_in_dim(queries, start, block_rows, 0)
        scores = (
            jnp.einsum("qhd,khd->hqk", query_block, key_rows, preferred_element_type=jnp.float32)
            / root_size
        )
        query_pos = start + jnp.arange(block_rows)
        allowed = (positions[None, :] <= query_pos[:, None]) & (positions[None, :] < length)
        return (query_block, jnp.where(allowed[None], scores, -1e30))

    def attend(start):
        unused_block, scores = block_scores(start)
        row_top = jnp.max(scores, axis=-1, keepdims=True)
        exponent = jnp.exp(scores - row_top)
        row_total = jnp.sum(exponent, axis=-1, keepdims=True)
        weights = (exponent / row_total).astype(jnp.bfloat16)
        mixed_block = jnp.einsum(
            "hqk,khd->qhd", weights, value_rows, preferred_element_type=jnp.float32
        )
        return (mixed_block.astype(jnp.bfloat16), (row_top + jnp.log(row_total))[..., 0])

    mixed_blocks, log_totals = lax.map(attend, starts)
    mixed = mixed_blocks.reshape(seq_len, local_heads * HD)
    attn_own = lax.psum_scatter(
        jnp.dot(mixed, o_full, preferred_element_type=jnp.float32).astype(jnp.bfloat16),
        "tensor",
        scatter_dimension=0,
        tiled=True,
    ).astype(jnp.float32)
    middle = hidden_in.astype(jnp.float32) + attn_own
    inverse_two = inverse_rms(middle)
    unit_two = middle * inverse_two
    ffn_own = (unit_two * ffn_gain).astype(jnp.bfloat16)
    gate_full, up_full, down_full = fetch_experts(gate_weight, up_weight, down_weight)
    ffn_all = lax.all_gather(ffn_own, "tensor", axis=0, tiled=True)
    expert_count = router_weight.shape[1]
    route_width = routes.shape[1]
    gate_probs = jax.nn.softmax(
        jnp.dot(ffn_all, router_weight, preferred_element_type=jnp.float32), axis=-1
    )
    picked = routes[:, :, None] == jnp.arange(expert_count)[None, None, :]
    route_gates = jnp.sum(jnp.where(picked, gate_probs[:, None, :], 0.0), axis=-1)
    block_count = seq_len // TOK_DEV
    per_expert = block_count * CAP
    picked_ints = picked.reshape(block_count, TOK_DEV * route_width, expert_count).astype(jnp.int32)
    slot_ranks = jnp.sum((jnp.cumsum(picked_ints, axis=1) - 1) * picked_ints, axis=-1).reshape(
        seq_len, route_width
    )
    block_ids = (positions // TOK_DEV)[:, None]
    slot_ids = (routes * per_expert + block_ids * CAP + slot_ranks).reshape(-1)
    slot_total = expert_count * per_expert
    token_ids = jnp.repeat(positions, route_width)
    group_width = 4
    turn_count = expert_count // group_width
    sources = (
        jnp.full((slot_total,), seq_len, jnp.int32)
        .at[slot_ids]
        .set(token_ids)
        .reshape(turn_count, group_width, per_expert)
    )
    slot_gates = (
        jnp.zeros((slot_total,), jnp.float32)
        .at[slot_ids]
        .set(route_gates.reshape(-1))
        .reshape(turn_count, group_width, per_expert, 1)
    )
    ffn_padded = jnp.concatenate([ffn_all, jnp.zeros((1, model_width), jnp.bfloat16)], axis=0)
    expert_running = jnp.zeros((seq_len + 1, model_width), jnp.float32)
    kept_values = []
    for turn_index in range(turn_count):
        lower = turn_index * group_width
        upper = lower + group_width
        expert_inputs = ffn_padded[sources[turn_index]]
        gate_value = jnp.einsum(
            "gpd,gdf->gpf",
            expert_inputs,
            gate_full[lower:upper],
            preferred_element_type=jnp.float32,
        )
        up_value = jnp.einsum(
            "gpd,gdf->gpf", expert_inputs, up_full[lower:upper], preferred_element_type=jnp.float32
        )
        active = (slot_gates[turn_index] * jax.nn.silu(gate_value) * up_value).astype(jnp.bfloat16)
        expert_outputs = jnp.einsum(
            "gpf,gfd->gpd", active, down_full[lower:upper], preferred_element_type=jnp.float32
        )
        expert_running = expert_running.at[sources[turn_index].reshape(-1)].add(
            expert_outputs.reshape(-1, model_width)
        )
        kept_values.append((gate_value, up_value, active))
    expert_own = lax.psum_scatter(
        expert_running[:seq_len].astype(jnp.bfloat16), "tensor", scatter_dimension=0, tiled=True
    ).astype(jnp.float32)
    output = middle + expert_own
    own_positions = member * row_count + jnp.arange(row_count)
    valid_rows = (own_positions < length)[:, None]
    mismatch = output - teacher.astype(jnp.float32)
    loss_own = jnp.sum(jnp.where(valid_rows, mismatch * mismatch, 0.0)) / (
        2.0 * model_width * total_count
    )
    grad_output = jnp.where(valid_rows, mismatch * (all_tokens / total_count), 0.0)
    grad_rows = lax.all_gather(grad_output.astype(jnp.bfloat16), "tensor", axis=0, tiled=True)
    gate_full, up_full, down_full = fetch_experts(gate_weight, up_weight, down_weight)
    grad_padded = jnp.concatenate([grad_rows, jnp.zeros((1, model_width), jnp.bfloat16)], axis=0)
    ffn_grad_running = jnp.zeros((seq_len + 1, model_width), jnp.float32)
    gate_grads = []
    up_grads = []
    down_grads = []
    slot_grads = []
    for turn_index in range(turn_count):
        gate_value, up_value, active = kept_values[turn_index]
        lower = turn_index * group_width
        upper = lower + group_width
        source_rows = sources[turn_index]
        expert_inputs = ffn_padded[source_rows]
        incoming = grad_padded[source_rows]
        grad_active = jnp.einsum(
            "gpd,gfd->gpf", incoming, down_full[lower:upper], preferred_element_type=jnp.float32
        )
        down_turn = jnp.einsum("gpf,gpd->gfd", active, incoming, preferred_element_type=jnp.float32)
        sigmoid_value = jax.nn.sigmoid(gate_value)
        silu_value = gate_value * sigmoid_value
        slot_grads.append(jnp.sum(grad_active * silu_value * up_value, axis=-1))
        grad_inner = grad_active * slot_gates[turn_index]
        grad_gate_value = (
            grad_inner * up_value * sigmoid_value * (1.0 + gate_value * (1.0 - sigmoid_value))
        ).astype(jnp.bfloat16)
        grad_up_value = (grad_inner * silu_value).astype(jnp.bfloat16)
        gate_turn = jnp.einsum(
            "gpd,gpf->gdf", expert_inputs, grad_gate_value, preferred_element_type=jnp.float32
        )
        up_turn = jnp.einsum(
            "gpd,gpf->gdf", expert_inputs, grad_up_value, preferred_element_type=jnp.float32
        )
        gate_grads.append(gate_turn)
        up_grads.append(up_turn)
        down_grads.append(down_turn)
        grad_inputs = jnp.einsum(
            "gpf,gdf->gpd",
            grad_gate_value,
            gate_full[lower:upper],
            preferred_element_type=jnp.float32,
        )
        grad_inputs = grad_inputs + jnp.einsum(
            "gpf,gdf->gpd", grad_up_value, up_full[lower:upper], preferred_element_type=jnp.float32
        )
        ffn_grad_running = ffn_grad_running.at[source_rows.reshape(-1)].add(
            grad_inputs.reshape(-1, model_width)
        )
    slot_grad_all = jnp.concatenate([entry.reshape(-1) for entry in slot_grads])
    route_grads = slot_grad_all[slot_ids].reshape(seq_len, route_width)
    grad_probs = jnp.sum(jnp.where(picked, route_grads[:, :, None], 0.0), axis=1)
    grad_logits = gate_probs * (
        grad_probs - jnp.sum(grad_probs * gate_probs, axis=-1, keepdims=True)
    )
    router_float = router_weight.astype(jnp.float32)
    ffn_grad_part = ffn_grad_running[:seq_len] + jnp.einsum(
        "se,de->sd", grad_logits, router_float, precision=HIGHEST
    )
    router_part = jnp.einsum(
        "sd,se->de", ffn_all, grad_logits, precision=HIGHEST, preferred_element_type=jnp.float32
    )
    ffn_grad_own = lax.psum_scatter(
        ffn_grad_part.astype(jnp.bfloat16), "tensor", scatter_dimension=0, tiled=True
    ).astype(jnp.float32)
    ffn_gain_part = jnp.sum(ffn_grad_own * unit_two, axis=0)
    grad_middle = grad_output + norm_backward(ffn_grad_own, unit_two, inverse_two, ffn_gain)
    attn_grad_rows = lax.all_gather(grad_middle.astype(jnp.bfloat16), "tensor", axis=0, tiled=True)
    q_full, k_full, v_full, o_full, qgain_full, kgain_full = fetch_attention(
        q_weight, k_weight, v_weight, o_weight, q_gain, k_gain
    )
    grad_o = jnp.einsum("sa,sb->ab", mixed, attn_grad_rows, preferred_element_type=jnp.float32)
    grad_mixed = (
        jnp.einsum("sb,ab->sa", attn_grad_rows, o_full, preferred_element_type=jnp.float32)
        .astype(jnp.bfloat16)
        .reshape(seq_len, local_heads, HD)
    )

    def attend_back(carry, inputs):
        key_running, value_running = carry
        start, log_total = inputs
        query_block, scores = block_scores(start)
        probs_float = jnp.exp(scores - log_total[..., None])
        probs_low = probs_float.astype(jnp.bfloat16)
        grad_block = lax.dynamic_slice_in_dim(grad_mixed, start, block_rows, 0)
        value_running = value_running + jnp.einsum(
            "hqk,qhd->khd", probs_low, grad_block, preferred_element_type=jnp.float32
        )
        grad_weights = jnp.einsum(
            "qhd,khd->hqk", grad_block, value_rows, preferred_element_type=jnp.float32
        )
        grad_scores = (
            probs_float
            * (grad_weights - jnp.sum(grad_weights * probs_float, axis=-1, keepdims=True))
        ).astype(jnp.bfloat16)
        query_grad_block = (
            jnp.einsum("hqk,khd->qhd", grad_scores, key_rows, preferred_element_type=jnp.float32)
            / root_size
        )
        key_running = (
            key_running
            + jnp.einsum(
                "hqk,qhd->khd", grad_scores, query_block, preferred_element_type=jnp.float32
            )
            / root_size
        )
        return ((key_running, value_running), query_grad_block)

    zero_heads = jnp.zeros((seq_len, local_heads, HD), jnp.float32)
    (key_grad_rot, value_grad), query_grad_blocks = lax.scan(
        attend_back, (zero_heads, zero_heads), (starts, log_totals)
    )
    query_grad = rotate(
        query_grad_blocks.reshape(seq_len, local_heads, HD), cosine, sinus_table, -1.0
    ).reshape(seq_len, local_heads * HD)
    key_grad = rotate(key_grad_rot, cosine, sinus_table, -1.0).reshape(seq_len, local_heads * HD)
    query_scaled = query_grad * query_gain
    key_scaled = key_grad * key_gain
    qgain_part = jnp.sum(query_grad * query_unit, axis=0)
    kgain_part = jnp.sum(key_grad * key_unit, axis=0)
    query_dot, key_dot, loss_group = lax.psum(
        (
            jnp.sum(query_scaled * query_unit, axis=1),
            jnp.sum(key_scaled * key_unit, axis=1),
            loss_own,
        ),
        "tensor",
    )
    query_raw_grad = (
        query_inv * (query_scaled - query_unit * (query_dot / model_width)[:, None])
    ).astype(jnp.bfloat16)
    key_raw_grad = (key_inv * (key_scaled - key_unit * (key_dot / model_width)[:, None])).astype(
        jnp.bfloat16
    )
    value_raw_grad = value_grad.reshape(seq_len, local_heads * HD).astype(jnp.bfloat16)
    grad_q = jnp.einsum("sd,sa->da", normed, query_raw_grad, preferred_element_type=jnp.float32)
    grad_k = jnp.einsum("sd,sa->da", normed, key_raw_grad, preferred_element_type=jnp.float32)
    grad_v = jnp.einsum("sd,sa->da", normed, value_raw_grad, preferred_element_type=jnp.float32)
    normed_grad = jnp.einsum(
        "sa,da->sd", query_raw_grad, q_full, preferred_element_type=jnp.float32
    )
    normed_grad = normed_grad + jnp.einsum(
        "sa,da->sd", key_raw_grad, k_full, preferred_element_type=jnp.float32
    )
    normed_grad = normed_grad + jnp.einsum(
        "sa,da->sd", value_raw_grad, v_full, preferred_element_type=jnp.float32
    )
    attn_gain_part = jnp.sum(normed_grad * unit_one, axis=0)
    input_part = norm_backward(normed_grad, unit_one, inverse_one, attn_gain)
    split_width = model_width // (dp_count * tp_count)
    input_own, attn_gain_share, ffn_gain_share, router_share = (
        lax.psum_scatter(
            input_part.astype(jnp.bfloat16), "tensor", scatter_dimension=0, tiled=True
        ).astype(jnp.float32),
        lax.psum_scatter(
            attn_gain_part.reshape(dp_count, tp_count, split_width).astype(jnp.bfloat16),
            "tensor",
            scatter_dimension=1,
            tiled=True,
        ).astype(jnp.float32),
        lax.psum_scatter(
            ffn_gain_part.reshape(dp_count, tp_count, split_width).astype(jnp.bfloat16),
            "tensor",
            scatter_dimension=1,
            tiled=True,
        ).astype(jnp.float32),
        lax.psum_scatter(
            router_part.reshape(dp_count, tp_count, split_width, expert_count).astype(jnp.bfloat16),
            "tensor",
            scatter_dimension=1,
            tiled=True,
        ).astype(jnp.float32),
    )
    grad_in = grad_middle + input_own
    (
        grad_q,
        grad_k,
        grad_v,
        grad_o,
        grad_qgain,
        grad_kgain,
        attn_gain_sum,
        ffn_gain_sum,
        router_sum,
    ) = (
        lax.psum_scatter(grad_q.astype(jnp.bfloat16), "dp", scatter_dimension=0, tiled=True).astype(
            jnp.float32
        ),
        lax.psum_scatter(grad_k.astype(jnp.bfloat16), "dp", scatter_dimension=0, tiled=True).astype(
            jnp.float32
        ),
        lax.psum_scatter(grad_v.astype(jnp.bfloat16), "dp", scatter_dimension=0, tiled=True).astype(
            jnp.float32
        ),
        lax.psum_scatter(grad_o.astype(jnp.bfloat16), "dp", scatter_dimension=1, tiled=True).astype(
            jnp.float32
        ),
        lax.psum_scatter(
            qgain_part.reshape(local_heads, HD).astype(jnp.bfloat16),
            "dp",
            scatter_dimension=1,
            tiled=True,
        ).astype(jnp.float32),
        lax.psum_scatter(
            kgain_part.reshape(local_heads, HD).astype(jnp.bfloat16),
            "dp",
            scatter_dimension=1,
            tiled=True,
        ).astype(jnp.float32),
        lax.psum_scatter(
            attn_gain_share.astype(jnp.bfloat16), "dp", scatter_dimension=0, tiled=True
        ).astype(jnp.float32),
        lax.psum_scatter(
            ffn_gain_share.astype(jnp.bfloat16), "dp", scatter_dimension=0, tiled=True
        ).astype(jnp.float32),
        lax.psum_scatter(
            router_share.astype(jnp.bfloat16), "dp", scatter_dimension=0, tiled=True
        ).astype(jnp.float32),
    )
    grad_gate, grad_up, grad_down = (
        lax.psum_scatter(
            jnp.concatenate(gate_grads, axis=0).astype(jnp.bfloat16),
            "dp",
            scatter_dimension=1,
            tiled=True,
        ).astype(jnp.float32),
        lax.psum_scatter(
            jnp.concatenate(up_grads, axis=0).astype(jnp.bfloat16),
            "dp",
            scatter_dimension=1,
            tiled=True,
        ).astype(jnp.float32),
        lax.psum_scatter(
            jnp.concatenate(down_grads, axis=0).astype(jnp.bfloat16),
            "dp",
            scatter_dimension=2,
            tiled=True,
        ).astype(jnp.float32),
    )
    return (
        loss_group.reshape(1),
        grad_in,
        attn_gain_sum.reshape(-1),
        ffn_gain_sum.reshape(-1),
        grad_q,
        grad_k,
        grad_v,
        grad_qgain,
        grad_kgain,
        grad_o,
        router_sum.reshape(-1, expert_count),
        grad_gate,
        grad_up,
        grad_down,
    )


MESH = pl.DeviceIdType.MESH
BF = jnp.bfloat16
F32 = jnp.float32
VMEM_LIMIT = 62 * 1024 * 1024
ANY = pl.BlockSpec(memory_space=pl.ANY)
VM = pl.BlockSpec(memory_space=pltpu.VMEM)


def flip(index, bits):
    for bit in (1, 2, 4):
        if bits & bit:
            index = index + bit * (1 - 2 * ((index // bit) % 2))
    return index


def both(first, second):
    return jnp.logical_and(first, second)


def under(condition, action):
    if condition is None:
        action()
    else:
        pl.when(condition)(action)


class Wire:
    def __init__(self, send_sem, recv_sem):
        self.send_sem, self.recv_sem, self.count, self.sent = send_sem, recv_sem, 0, []

    def slot(self):
        self.count += 1
        return self.count - 1

    def start(self, slot, source, target, device, condition=None):
        def make():
            return pltpu.make_async_remote_copy(
                src_ref=source(),
                dst_ref=target(),
                send_sem=self.send_sem.at[slot],
                recv_sem=self.recv_sem.at[slot],
                device_id=device,
                device_id_type=MESH,
            )

        under(condition, lambda: make().start())
        self.sent.append((condition, make))

    def arrive(self, slot, region, device, condition=None):
        copy = pltpu.make_async_remote_copy(
            src_ref=region(),
            dst_ref=region(),
            send_sem=self.send_sem.at[slot],
            recv_sem=self.recv_sem.at[slot],
            device_id=device,
            device_id_type=MESH,
        )
        under(condition, lambda: copy.wait_recv())

    def finish(self):
        for condition, make in self.sent:
            under(condition, lambda make=make: make().wait_send())
        self.sent = []


class Local:
    def __init__(self, sem):
        self.sem, self.count = sem, 0

    def start(self, source, target):
        copy = pltpu.make_async_copy(source, target, self.sem.at[self.count])
        self.count += 1
        copy.start()
        return copy


def greet(devices):
    barrier = pltpu.get_barrier_semaphore()
    for condition, device in devices:
        under(
            condition,
            lambda device=device: pl.semaphore_signal(
                barrier, inc=1, device_id=device, device_id_type=MESH
            ),
        )
    amount = sum(1 for condition, device in devices if condition is None)
    for condition, device in devices:
        if condition is not None:
            amount = amount + jnp.where(condition, 1, 0)
    pl.semaphore_wait(barrier, amount)


def line_devices(d, t, extent):
    return [(t < extent - 1, (d, t + 1)), (t > 0, (d, t - 1))]


def rows_loop(rows, step, body):
    def run(index, carry):
        body(pl.multiple_of(index * step, step))
        return carry

    lax.fori_loop(0, rows // step, run, 0)


def add_into(target, source, rows):
    def body(start):
        part = pl.ds(start, 16)
        target[part] = target[part] + source[part]

    rows_loop(rows, 16, body)


class LineGather:
    def __init__(self, wire, d, t, extent, own, place):
        self.wire, self.extent = wire, extent
        up = [wire.slot() for unused in range(extent - 1)]
        down = [wire.slot() for unused in range(extent - 1)]
        last = extent - 1
        above, below = (d, t + 1), (d, t - 1)
        self.first = (
            (up[0], own, lambda: place(t), above, t < last),
            (down[0], own, lambda: place(t), below, t > 0),
        )
        self.steps = {}
        for step in range(1, extent):
            from_below, from_above = t >= step, t <= last - step
            lower, upper = t - step, t + step
            self.steps[step] = (
                (
                    up,
                    lambda index=lower: place(index),
                    from_below,
                    both(from_below, t < last),
                    above,
                    below,
                ),
                (
                    down,
                    lambda index=upper: place(index),
                    from_above,
                    both(from_above, t > 0),
                    below,
                    above,
                ),
            )

    def begin(self):
        for slot, own, target, device, condition in self.first:
            self.wire.start(slot, own, target, device, condition)

    def step(self, step):
        for slots, region, valid, onward, to, source in self.steps[step]:
            self.wire.arrive(slots[step - 1], region, source, valid)
            if step < self.extent - 1:
                self.wire.start(slots[step], region, region, to, onward)


def arrival(t, turn):
    near = t - 1 + 2 * (1 - (t + 3) // 4)
    far = 3 * (1 - t // 2)
    choices = (t, near, 6 - t - near - far, far)
    if isinstance(turn, int):
        return choices[turn]
    result = choices[0]
    for number in range(1, 4):
        result = jnp.where(turn == number, choices[number], result)
    return result


LATE = 32


class PlaneGather:
    def __init__(self, wire, d, t, extent, own, place, bundle, rows):
        self.wire, self.place, self.bundle, self.own = wire, place, bundle, own
        self.early, self.half = rows - LATE, (rows - LATE) // 2
        self.to_x, self.to_y, self.to_c = (flip(d, 2), t), (flip(d, 4), t), (flip(d, 1), t)
        self.index = [arrival(t, turn) for turn in range(extent)]
        self.slots = {}
        late = lambda n: (self.early + n * (LATE // 2), LATE // 2)
        self.parts = {0: (0, self.half), 1: (self.half, self.half), 2: late(0), 3: late(1)}
        self.parts["early"], self.parts["late"] = (0, self.early), (self.early, LATE)
        self.send("gx", 0, self.source(0, "late"), self.spot(0, 0, 1, "late"), self.to_x)
        self.send("gy", 0, self.source(0, "late"), self.spot(0, 0, 2, "late"), self.to_y)
        here = self.index[0]
        self.line = LineGather(
            wire,
            d,
            t,
            extent,
            lambda: self.cut(own(), "early"),
            lambda j: self.cut(place(j, 0, 0), "early"),
        )
        self.late_line = LineGather(
            wire, d, t, extent, lambda: bundle(here, 0), lambda j: bundle(j, 0)
        )
        self.line.begin()
        self.stage_first(0)
        for name, i, which, onward, to, source in (
            ("gx", 1, 2, "gfy", self.to_y, self.to_x),
            ("gy", 2, 3, "gfx", self.to_x, self.to_y),
        ):
            self.wait(name, 0, self.spot(0, 0, i, "late"), source)
            self.send(onward, 0, self.spot(0, 0, i, which), self.spot(0, 0, 3, which), to)
        self.stage_second(0)

    def cut(self, ref, which):
        start, size = self.parts[which]
        return ref.at[pl.ds(start, size)]

    def send(self, name, turn, source, target, device):
        slot = self.wire.slot()
        self.slots[name, turn] = slot
        self.wire.start(slot, source, target, device)

    def wait(self, name, turn, region, device):
        self.wire.arrive(self.slots[name, turn], region, device)

    def spot(self, turn, c, i, which):
        return lambda: self.cut(self.place(self.index[turn], c, i), which)

    def source(self, turn, which):
        if turn == 0:
            return lambda: self.cut(self.own(), which)
        return self.spot(turn, 0, 0, which)

    def stage_first(self, turn):
        source, spot = self.source, self.spot
        self.send("x0", turn, source(turn, 0), spot(turn, 0, 1, 0), self.to_x)
        self.send("y1", turn, source(turn, 1), spot(turn, 0, 2, 1), self.to_y)

    def stage_second(self, turn):
        source, spot = self.source, self.spot
        self.send("x1", turn, source(turn, 1), spot(turn, 0, 1, 1), self.to_x)
        self.send("y0", turn, source(turn, 0), spot(turn, 0, 2, 0), self.to_y)
        self.send("c0", turn, source(turn, "early"), spot(turn, 1, 0, "early"), self.to_c)

    def stage(self, turn):
        self.stage_first(turn)
        self.stage_second(turn)

    def relay(self, turn):
        spot = self.spot
        self.wait("x0", turn, spot(turn, 0, 1, 0), self.to_x)
        self.send("fy", turn, spot(turn, 0, 1, 0), spot(turn, 0, 3, 0), self.to_y)
        self.wait("y1", turn, spot(turn, 0, 2, 1), self.to_y)
        self.send("fx", turn, spot(turn, 0, 2, 1), spot(turn, 0, 3, 1), self.to_x)
        self.wait("x1", turn, spot(turn, 0, 1, 1), self.to_x)
        self.send("c1", turn, spot(turn, 0, 1, "early"), spot(turn, 1, 1, "early"), self.to_c)
        self.wait("y0", turn, spot(turn, 0, 2, 0), self.to_y)
        self.send("c2", turn, spot(turn, 0, 2, "early"), spot(turn, 1, 2, "early"), self.to_c)

    def corner(self, turn):
        spot = self.spot
        self.wait("fy", turn, spot(turn, 0, 3, 0), self.to_y)
        self.wait("fx", turn, spot(turn, 0, 3, 1), self.to_x)
        self.send("c3", turn, spot(turn, 0, 3, "early"), spot(turn, 1, 3, "early"), self.to_c)

    def pass_bundle(self, turn):
        region = lambda c: (lambda: self.bundle(self.index[turn], c))
        self.send("cb", turn, region(0), region(1), self.to_c)

    def bundle_start(self, unused):
        spot = self.spot
        self.wait("gfy", 0, spot(0, 0, 3, 2), self.to_y)
        self.wait("gfx", 0, spot(0, 0, 3, 3), self.to_x)
        self.late_line.begin()
        self.pass_bundle(0)

    def bundle_step(self, step):
        self.late_line.step(step)
        self.pass_bundle(step)

    def other(self, turn):
        for i in range(4):
            self.wait("c%d" % i, turn, self.spot(turn, 1, i, "early"), self.to_c)
        self.wait("cb", turn, lambda: self.bundle(self.index[turn], 1), self.to_c)

    def actions(self):
        line, stage, relay, corner, other, late = (
            self.line.step,
            self.stage,
            self.relay,
            self.corner,
            self.other,
            self.bundle_step,
        )
        return (
            (
                (line, 1),
                (stage, 1),
                (self.bundle_start, 0),
                (relay, 0),
                (line, 2),
                (stage, 2),
                (corner, 0),
            ),
            ((relay, 1), (late, 1), (other, 0)),
            ((relay, 2), (line, 3), (stage, 3), (corner, 1)),
            ((other, 1),),
            ((late, 2), (corner, 2), (relay, 3)),
            ((other, 2),),
            ((late, 3), (corner, 3)),
            ((other, 3),),
        )


class LineSum:
    def __init__(self, wire, d, t, extent, block, up_in, down_in, rows, parts):
        self.wire, self.d, self.t, self.extent = wire, d, t, extent
        self.block, self.up_in, self.down_in = block, up_in, down_in
        self.rows, self.parts = rows // parts, parts
        self.up = [[wire.slot() for p in range(parts)] for s in range(extent - 1)]
        self.down = [[wire.slot() for p in range(parts)] for s in range(extent - 1)]

    def cut(self, ref, part):
        return ref.at[pl.ds(part * self.rows, self.rows)]

    def add(self, target, source):
        add_into(target, source, self.rows)

    def flow(self, step, part, near, index, slots, buffers, to_device, from_device):
        wire, extent = self.wire, self.extent
        block = lambda: self.cut(self.block(index), part)
        if step >= 1:
            source = lambda: self.cut(buffers.at[step - 1], part)
            active = both(both(near <= step, near < extent - 1), near >= 1)
            wire.arrive(slots[step - 1][part], source, from_device, active)
            under(active, lambda: self.add(block(), source()))
        wire.start(
            slots[step][part],
            block,
            lambda: self.cut(buffers.at[step], part),
            to_device,
            both(near <= step, near < extent - 1),
        )

    def step(self, step):
        d, t, extent = self.d, self.t, self.extent
        up, down = extent - 1 - step + t, step + t - (extent - 1)
        above, below = (d, t + 1), (d, t - 1)
        for part in range(self.parts):
            self.flow(step, part, t, up, self.up, self.up_in, above, below)
            self.flow(step, part, extent - 1 - t, down, self.down, self.down_in, below, above)

    def last(self):
        d, t, extent = self.d, self.t, self.extent
        for ready, missing, slots, buffers, device in (
            (t > 0, t == 0, self.up, self.up_in, (d, t - 1)),
            (t < extent - 1, t == extent - 1, self.down, self.down_in, (d, t + 1)),
        ):
            buffer = buffers.at[extent - 2]
            for part in range(self.parts):
                self.wire.arrive(
                    slots[extent - 2][part],
                    lambda part=part, buffer=buffer: self.cut(buffer, part),
                    device,
                    ready,
                )

            def clear(buffer=buffer):
                buffer[...] = jnp.zeros(buffer.shape, BF)

            under(missing, clear)


class BundleSum(LineSum):
    def cut(self, ref, part):
        return ref

    def add(self, target, source):
        for i in range(4):
            add_into(target.at[i], source.at[i], LATE)


def own_sum(block, up_in, down_in, part, columns):
    return (
        block[part, columns].astype(F32)
        + up_in[part, columns].astype(F32)
        + down_in[part, columns].astype(F32)
    )


def plane_order(t):
    top = t // 2
    inner = ((t + 1) // 2) % 2
    return (
        3 - 3 * top,
        2 - top,
        (1 - inner) * (1 - top) + (2 + inner) * top,
        inner * (1 - top) + (3 - inner) * top,
    )


def sum_plane(wire, local, d, t, extent, partial, buffers, rows, between=lambda turn: None):
    (
        work,
        own_in,
        a_in,
        b_in,
        up_in,
        down_in,
        late_up,
        late_down,
        late_a,
        late_b,
    ) = buffers
    order = plane_order(t)
    early, half = rows - LATE, (rows - LATE) // 2
    to_x, to_y, to_c = (flip(d, 2), t), (flip(d, 4), t), (flip(d, 1), t)
    turns = (3, 1, 2, 0)
    slots_c, slots_a, slots_b, loads = {}, {}, {}, {}

    def cut(ref, which):
        return ref.at[pl.ds(which * half, half)]

    def late_cut(ref, which):
        return ref.at[pl.ds(early + which * (LATE // 2), LATE // 2)]

    def begin(k):
        for i in turns:
            slots_c[k, i] = wire.slot()
            wire.start(
                slots_c[k, i],
                lambda i=i: partial.at[order[k], 1, i],
                lambda i=i: work.at[k, i],
                to_c,
            )
            loads[k, i] = local.start(partial.at[order[k], 0, i], own_in.at[k % 2, i])

    begin(0)

    def inverse(index):
        where = jnp.int32(0)
        for k in range(1, extent):
            where = where + k * jnp.where(order[k] == index, 1, 0)
        return where

    line = LineSum(
        wire,
        d,
        t,
        extent,
        lambda index: work.at[inverse(index), 0, pl.ds(0, early)],
        up_in,
        down_in,
        early,
        1,
    )
    late_line = BundleSum(
        wire,
        d,
        t,
        extent,
        lambda index: work.at[inverse(index), pl.ds(0, 4), pl.ds(early, LATE)],
        late_up,
        late_down,
        LATE,
        1,
    )
    routes_a = (
        (to_x, 3, 2, 0, 0),
        (to_y, 3, 1, 1, 1),
        (to_x, 1, 0, 0, 2),
        (to_y, 2, 0, 1, 3),
    )
    routes_b = ((to_y, 2, 0, 0), (to_x, 1, 1, 1))
    last = extent - 1

    def send_a(k, source, cutter, inbox):
        for device, origin, unused, which, row in routes_a:
            if origin == source:
                slots_a[inbox is a_in, k, row] = wire.slot()
                wire.start(
                    slots_a[inbox is a_in, k, row],
                    lambda origin=origin, which=which: cutter(work.at[k, origin], which),
                    lambda row=row: inbox.at[k, row] if inbox is a_in else inbox.at[row],
                    device,
                )

    def receive_a(k, cutter, inbox, second, size):
        for device, unused, target, which, row in routes_a:
            region = inbox.at[k, row] if inbox is a_in else inbox.at[row]
            wire.arrive(slots_a[inbox is a_in, k, row], lambda: region, device)
            add_into(cutter(work.at[k, target], which), region, size)
            if row < 2:
                to, origin, part, b_row = routes_b[row]
                slots_b[inbox is a_in, k, b_row] = wire.slot()
                wire.start(
                    slots_b[inbox is a_in, k, b_row],
                    lambda origin=origin, part=part: cutter(work.at[k, origin], part),
                    lambda b_row=b_row: second.at[k, b_row]
                    if inbox is a_in
                    else second.at[b_row],
                    to,
                )

    def receive_b(k, cutter, inbox, second, size):
        for device, unused, which, row in routes_b:
            region = second.at[k, row] if inbox is a_in else second.at[row]
            wire.arrive(slots_b[inbox is a_in, k, row], lambda: region, device)
            add_into(cutter(work.at[k, 0], which), region, size)

    for turn in range(extent + 2):
        if turn + 1 < extent:
            begin(turn + 1)
        if turn < extent:
            k = turn
            for i in turns:
                loads[k, i].wait()
                wire.arrive(slots_c[k, i], lambda k=k, i=i: work.at[k, i], to_c)
                add_into(work.at[k, i], own_in.at[k % 2, i], rows)
                send_a(k, i, cut, a_in)
            if k < last:
                late_line.step(k)
        if turn == extent:
            late_line.last()
            for i in turns:
                for inbox in (late_up, late_down):
                    add_into(
                        work.at[last, i, pl.ds(early, LATE)], inbox.at[last - 1, i], LATE
                    )
                send_a(last, i, late_cut, late_a)
        between(turn)
        if 1 <= turn <= extent:
            receive_a(turn - 1, cut, a_in, b_in, half)
        if turn == extent + 1:
            receive_a(last, late_cut, late_a, late_b, LATE // 2)
        if turn >= 2:
            k = turn - 2
            receive_b(k, cut, a_in, b_in, half)
            if k < last:
                line.step(k)
    between(extent + 2)
    receive_b(last, late_cut, late_a, late_b, LATE // 2)
    line.last()


def own_rows(buffers, rows, columns, body):
    work, up_in, down_in = buffers[0], buffers[4], buffers[5]
    mine = work.at[work.shape[0] - 1, 0]
    up_last, down_last = up_in.at[up_in.shape[0] - 1], down_in.at[down_in.shape[0] - 1]
    early = rows - LATE

    def first(start):
        part = pl.ds(start, 16)
        body(part, own_sum(mine, up_last, down_last, part, columns))

    def second(start):
        part = pl.ds(pl.multiple_of(early + start, 16), 16)
        body(part, mine[part, columns].astype(F32))

    rows_loop(early, 16, first)
    rows_loop(LATE, 16, second)


def sum_scratch(extent, rows, width):
    early = rows - LATE
    return [
        pltpu.VMEM((extent, 4, rows, width), BF),
        pltpu.VMEM((2, 4, rows, width), BF),
        pltpu.VMEM((extent, 4, early // 2, width), BF),
        pltpu.VMEM((extent, 2, early // 2, width), BF),
        pltpu.VMEM((extent - 1, early, width), BF),
        pltpu.VMEM((extent - 1, early, width), BF),
        pltpu.VMEM((extent - 1, 4, LATE, width), BF),
        pltpu.VMEM((extent - 1, 4, LATE, width), BF),
        pltpu.VMEM((4, LATE // 2, width), BF),
        pltpu.VMEM((2, LATE // 2, width), BF),
    ]


def plane_devices(d, t, extent):
    return line_devices(d, t, extent) + [(None, (flip(d, bits), t)) for bits in (1, 2, 4)]


def kernel_params(number):
    return pltpu.CompilerParams(
        collective_id=number, has_side_effects=True, vmem_limit_bytes=VMEM_LIMIT
    )


def dma_pair(count):
    return [pltpu.SemaphoreType.DMA((count,)), pltpu.SemaphoreType.DMA((count,))]


class Pieces:
    def __init__(self, d, in_weight, out_weight, sem, pieces, tables=None):
        self.copies = {}
        slab = out_weight.shape[0] // 2
        for bits, piece in enumerate(pieces):
            start = pl.multiple_of(flip(d, bits) * slab, slab)
            pairs = []
            for place in range(3):
                for e in range(2):
                    if place < 2:
                        column = (2 * place + e) * slab
                        whole = in_weight.at[pl.ds(start, slab), pl.ds(column, slab)]
                    else:
                        whole = out_weight.at[pl.ds(e * slab, slab), pl.ds(start, slab)]
                    if tables is not None and bits == 0:
                        part = tables[place].at[2 * d + e]
                    else:
                        part = piece.at[place, e]
                    pairs.append((part, whole, sem.at[bits * 6 + place * 2 + e]))
            self.copies[bits] = pairs

    def load(self, bits):
        for piece, whole, sem in self.copies[bits]:
            pltpu.make_async_copy(piece, whole, sem).start()

    def loaded(self, bits):
        for piece, whole, sem in self.copies[bits]:
            pltpu.make_async_copy(piece, whole, sem).wait()

    def store(self, bits):
        for piece, whole, sem in self.copies[bits]:
            pltpu.make_async_copy(whole, piece, sem).start()

    def stored(self, bits):
        for piece, whole, sem in self.copies[bits]:
            pltpu.make_async_copy(whole, piece, sem).wait()


def coefficients(columns, d, slab):
    values = columns.astype(F32)
    lane = lax.broadcasted_iota(jnp.int32, values.shape, 1)
    parts = []
    for e in range(2):
        wanted = jnp.logical_or(lane == 2 * d + e, lane == 16 + 2 * d + e)
        one = jnp.sum(jnp.where(wanted, values, 0.0), axis=-1, keepdims=True)
        parts.append(jnp.broadcast_to(one, (values.shape[0], slab)))
    return jnp.concatenate(parts, axis=1)


def line_exchange(wire, t, d, extent, outbox, inbox):
    peers = [(d, (t + k) % extent) for k in range(1, extent)]
    slots = []
    for k, peer in enumerate(peers):
        slot = wire.slot()
        slots.append(slot)
        wire.start(slot, lambda: outbox, lambda k=k: inbox.at[k], peer)
    result = outbox[...]
    for k, peer in enumerate(peers):
        wire.arrive(slots[k], lambda k=k: inbox.at[k], peer)
        result = result + inbox[k]
    return result


def columns_to_rows(ref):
    return ref[...].T[0:8]


def rows_to_columns(value):
    return jnp.concatenate([value, jnp.zeros((120, value.shape[1]), F32)], axis=0).T


def turned(value, cosine, sine, direction):
    return value * cosine + direction * pltpu.roll(value, HD // 2, 1) * sine


def line_peers(d, t, extent):
    return [(None, (d, (t + k) % extent)) for k in range(1, extent)]


def transposed_dot(left, right):
    return lax.dot_general(left, right, (((0,), (0,)), ((), ())), preferred_element_type=F32)


def dot_transposed(left, right):
    return lax.dot_general(left, right, (((1,), (1,)), ((), ())), preferred_element_type=F32)


def front_kernel(
    extent,
    lengths,
    hid,
    q_weight,
    k_weight,
    v_weight,
    o_weight,
    q_gain,
    k_gain,
    gate,
    up,
    down,
    attn_gain,
    cosine,
    sine,
    ffn_gain,
    router,
    routes,
    chosen,
    middle,
    gates,
    head_gain,
    inverses,
    hid_out,
    qkv_out,
    o_out,
    normed_out,
    raw_out,
    low_out,
    probs_out,
    mixed_out,
    tokens,
    hidden,
    out,
    landed,
    hid_all,
    qkv_all,
    o_all,
    gains_all,
    router_rows,
    normed,
    raw,
    low,
    probs,
    mixed,
    sums,
    outbox,
    inbox,
    gathered,
    work,
    up_in,
    down_in,
    in_weight,
    out_weight,
    hidden_stage,
    out_stage,
    send_sem,
    recv_sem,
    local_sem,
    weight_sem,
    stage_sem,
    token_sem,
    probs_sem,
):
    d, t = lax.axis_index("dp"), lax.axis_index("tensor")
    seq_len, width = hid_all.shape
    rows = seq_len // extent
    heads, head_width = q_gain.shape
    columns = heads * HD
    length = lengths[d]
    depth, o_rows, o_width = q_weight.shape[0], o_weight.shape[0], o_weight.shape[1]
    wire, local = Wire(send_sem, recv_sem), Local(local_sem)
    dx, dy, dxy = flip(d, 2), flip(d, 4), flip(d, 6)
    to_x, to_y, to_c = (dx, t), (dy, t), (flip(d, 1), t)

    def block(index):
        return hid_all.at[pl.ds(index * rows, rows)]

    def region(device, which):
        start = pl.multiple_of(device * o_width, o_width)
        if which is None:
            return [qkv_all.at[pl.ds(device * depth, depth)], o_all.at[:, pl.ds(start, o_width)]]
        return [
            qkv_all.at[pl.ds(device * depth + which * (depth // 2), depth // 2)],
            o_all.at[pl.ds(which * (o_rows // 2), o_rows // 2), pl.ds(start, o_width)],
        ]

    copies = [local.start(hid, block(t))]
    for n, weight in enumerate((q_weight, k_weight, v_weight)):
        target = qkv_all.at[pl.ds(d * depth, depth), pl.ds(n * columns, columns)]
        copies.append(local.start(weight, target))
    copies.append(local.start(o_weight, region(d, None)[1]))
    lane = lax.broadcasted_iota(jnp.int32, (heads, HD), 1)
    for n, source in enumerate((q_gain, k_gain)):
        value = source[...].astype(F32)
        spread_out = jnp.zeros((heads, HD), F32)
        for i in range(head_width):
            spread_out += jnp.where(lane == d * head_width + i, value[:, i : i + 1], 0.0)
        gains_all[0, n * heads : (n + 1) * heads] = spread_out
    router_rows[...] = jnp.zeros(router_rows.shape, BF)
    router_rows[0:16] = router[...]
    router_rows[16:32] = router[...]
    own_routes = routes[:, pl.ds(pl.multiple_of(t * rows, rows), rows)]
    expert = lax.broadcasted_iota(jnp.int32, (128, rows), 0)
    picked = jnp.zeros((128, rows), F32)
    for k in range(own_routes.shape[0]):
        match = both(own_routes[k : k + 1] == expert % 16, expert < 32)
        picked = jnp.where(match, 1.0, picked)
    chosen[...] = picked.T
    greet(line_peers(d, t, extent) + [(None, (flip(d, bits), t)) for bits in range(1, 8)])
    for copy in copies:
        copy.wait()

    def send(device, sources, targets):
        slots = []
        for source, target in zip(sources, targets):
            slot = wire.slot()
            wire.start(slot, lambda source=source: source, lambda target=target: target, device)
            slots.append(slot)
        return slots

    def arrive(slots, regions, device):
        for slot, part in zip(slots, regions):
            wire.arrive(slot, lambda: part, device)

    line = LineGather(wire, d, t, extent, lambda: block(t), block)
    line.begin()
    x_slots, y_slots, c_slots = {}, {}, {}
    for which, other in ((0, 1), (1, 0)):
        x_slots[which] = send(to_x, region(d, which), region(d, which))
        y_slots[other] = send(to_y, region(d, other), region(d, other))
    c_slots[1] = send(to_c, region(d, None), region(d, None))
    gain_slots = {}
    for bits in range(1, 8):
        gain_slots[bits] = wire.slot()
        wire.start(
            gain_slots[bits],
            lambda: gains_all.at[0],
            lambda bits=bits: gains_all.at[bits],
            (flip(d, bits), t),
        )
    weights = Pieces(
        d, in_weight, out_weight, weight_sem, [landed.at[bits] for bits in range(8)]
    )
    own_experts = Pieces(d, in_weight, out_weight, weight_sem, [None], (gate, up, down))
    own_experts.load(0)
    arrive(x_slots[0], region(dx, 0), to_x)
    over_y = send(to_y, region(dx, 0), region(dx, 0))
    arrive(y_slots[1], region(dy, 1), to_y)
    over_x = send(to_x, region(dy, 1), region(dy, 1))
    piece_slots = {}
    for bits in (2, 4, 1, 3, 5, 6, 7):
        first = 2 * flip(d, bits)
        piece_slots[bits] = send(
            (flip(d, bits), t),
            [weight.at[pl.ds(first, 2)] for weight in (gate, up, down)],
            [landed.at[bits, place] for place in range(3)],
        )
    line.step(1)
    arrive(x_slots[1], region(dx, 1), to_x)
    c_slots[3] = send(to_c, region(dx, None), region(dx, None))
    arrive(y_slots[0], region(dy, 0), to_y)
    c_slots[5] = send(to_c, region(dy, None), region(dy, None))
    for step in range(2, extent):
        line.step(step)
    arrive(over_y, region(dxy, 0), to_y)
    arrive(over_x, region(dxy, 1), to_x)
    c_slots[7] = send(to_c, region(dxy, None), region(dxy, None))
    for bits in range(1, 8):
        wire.arrive(
            gain_slots[bits], lambda bits=bits: gains_all.at[bits], (flip(d, bits), t)
        )
    total_gain = gains_all[0]
    for bits in range(1, 8):
        total_gain = total_gain + gains_all[bits]
    head_gain[...] = total_gain
    tile = 256

    def normalize(start):
        part = pl.ds(start, 64)
        value = hid_all[part].astype(F32)
        unit = value * lax.rsqrt(jnp.mean(value * value, axis=-1, keepdims=True) + EPSILON)
        normed[part] = (unit * attn_gain[0:1]).astype(BF)

    rows_loop(seq_len, 64, normalize)
    for bits in (1, 3, 5, 7):
        arrive(c_slots[bits], region(flip(d, bits), None), to_c)
    kept = [
        local.start(hid_all, hid_out),
        local.start(qkv_all, qkv_out),
        local.start(o_all, o_out),
        local.start(normed, normed_out),
    ]

    def project(start):
        part = pl.ds(start, tile)
        result = jnp.dot(normed[part], qkv_all[...], preferred_element_type=F32)
        raw[part] = result
        lane = lax.broadcasted_iota(jnp.int32, (tile, 128), 1)
        squares = [
            jnp.sum(jnp.square(result[:, n * columns : (n + 1) * columns]), axis=-1, keepdims=True)
            for n in range(2)
        ]
        sums[part] = jnp.where(lane == 0, squares[0], jnp.where(lane == 1, squares[1], 0.0))

    rows_loop(seq_len, tile, project)
    outbox[...] = columns_to_rows(sums)
    total = line_exchange(wire, t, d, extent, outbox, inbox)
    inverses[...] = rows_to_columns(lax.rsqrt(total / width + EPSILON))
    low[:, 2 * columns :] = raw[:, 2 * columns :].astype(BF)

    def turn_head(h, carry):
        for n in range(2):
            section = pl.ds(pl.multiple_of(n * columns + h * HD, HD), HD)
            unit = raw[:, section] * inverses[:, n : n + 1]
            raw[:, section] = unit
            scaled = unit * head_gain[pl.ds(n * heads + h, 1)]
            low[:, section] = turned(scaled, cosine[...], sine[...], 1.0).astype(BF)
        return carry

    lax.fori_loop(0, heads, turn_head, 0)
    kept += [local.start(raw, raw_out), local.start(low, low_out)]
    total_line = LineSum(
        wire, d, t, extent, lambda index: work.at[index], up_in, down_in, rows, 2
    )
    order = plane_order(t)

    def probs_copy(k):
        part = pl.ds(pl.multiple_of(order[k] * rows, rows), rows)
        return pltpu.make_async_copy(
            probs.at[k % 2], probs_out.at[pl.ds(0, heads), part], probs_sem.at[k % 2]
        )

    for k in range(extent):
        begin = pl.multiple_of(order[k] * rows, rows)
        part = pl.ds(begin, rows)
        if k >= 2:
            probs_copy(k - 2).wait()

        def head(h, carry, begin=begin, part=part, k=k):
            section = pl.ds(pl.multiple_of(h * HD, HD), HD)
            key_section = pl.ds(pl.multiple_of(columns + h * HD, HD), HD)
            value_section = pl.ds(pl.multiple_of(2 * columns + h * HD, HD), HD)
            scores = dot_transposed(low[part, section], low[:, key_section]) / math.sqrt(HD)
            row = begin + lax.broadcasted_iota(jnp.int32, scores.shape, 0)
            column = lax.broadcasted_iota(jnp.int32, scores.shape, 1)
            allowed = both(column <= row, column < length)
            scores = jnp.where(allowed, scores, -1e30)
            powers = jnp.exp(scores - jnp.max(scores, axis=-1, keepdims=True))
            result = powers / jnp.sum(powers, axis=-1, keepdims=True)
            probs[k % 2, h] = result
            mixed[part, section] = jnp.dot(
                result.astype(BF), low[:, value_section], preferred_element_type=F32
            ).astype(BF)
            return carry

        lax.fori_loop(0, heads, head, 0)
        probs_copy(k).start()
        work[order[k]] = jnp.dot(
            mixed[part], o_all[...], preferred_element_type=F32
        ).astype(BF)
        if k != 1:
            total_line.step(max(k - 1, 0))
    kept.append(local.start(mixed, mixed_out))
    total_line.last()
    mine = work.at[t]
    everything = pl.ds(0, width)
    packet = gathered.at[t, 0, 0]

    def body(start):
        part = pl.ds(start, 16)
        value = hid[part].astype(F32) + own_sum(
            mine, up_in.at[extent - 2], down_in.at[extent - 2], part, everything
        )
        middle[part] = value
        unit = value * lax.rsqrt(jnp.mean(value * value, axis=-1, keepdims=True) + EPSILON)
        packet[part, 0:width] = (unit * ffn_gain[1:2]).astype(BF)

    rows_loop(rows, 16, body)
    logits = dot_transposed(packet[:, 0:width], router_rows[...])
    lane = lax.broadcasted_iota(jnp.int32, logits.shape, 1)
    top = jnp.max(jnp.where(lane < 16, logits, -1e30), axis=-1, keepdims=True)
    powers = jnp.where(lane < 32, jnp.exp(logits - top), 0.0)
    chance = powers / jnp.sum(jnp.where(lane < 16, powers, 0.0), axis=-1, keepdims=True)
    gates[...] = chance
    coeff = chance * chosen[...]
    high = coeff.astype(BF).astype(F32)
    packet[:, width : width + 128] = jnp.where(lane < 16, high, coeff - high).astype(BF)

    def place(j, c, i):
        return gathered.at[j, c, i]

    def bundle(j, c):
        return gathered.at[j, c, pl.ds(0, 4), pl.ds(rows - LATE, LATE)]

    gather = PlaneGather(wire, d, t, extent, lambda: packet, place, bundle, rows)
    for bits in range(1, 8):
        arrive(
            piece_slots[bits], [landed.at[bits, place] for place in range(3)], (flip(d, bits), t)
        )
        weights.load(bits)
    own_experts.loaded(0)
    for bits in range(1, 8):
        weights.loaded(bits)
    units = out_weight.shape[0]

    def stage_copies(slot, j, c):
        return (
            pltpu.make_async_copy(hidden_stage.at[slot], hidden.at[j, c], stage_sem.at[0, slot]),
            pltpu.make_async_copy(out_stage.at[slot], out.at[j, c], stage_sem.at[1, slot]),
        )

    actions = gather.actions()

    def group(g, carry):
        for number, steps in enumerate(actions):

            @pl.when(g == number)
            def _():
                for action, argument in steps:
                    action(argument)

        j, c, slot = arrival(t, g // 2), g % 2, g % 2

        @pl.when(g >= 2)
        def _():
            for copy in stage_copies(slot, j, c):
                copy.wait()

        pltpu.make_async_copy(gathered.at[j, c], tokens.at[j, c], token_sem.at[g]).start()

        def some(first, carry):
            blocks, part = pl.ds(2 * first, 2), pl.ds(first * 2 * rows, 2 * rows)
            values = jnp.dot(
                gathered[j, c, blocks, :, 0:width].reshape(2 * rows, width),
                in_weight[...],
                preferred_element_type=F32,
            )
            hidden_stage[slot, part] = values.astype(BF)
            gate_value, up_value = values[:, :units], values[:, units:]
            coeff = coefficients(
                gathered[j, c, blocks, :, width : width + 128].reshape(2 * rows, 128),
                d,
                units // 2,
            )
            active = (coeff * (gate_value * jax.nn.sigmoid(gate_value)) * up_value).astype(BF)
            result = jnp.dot(active, out_weight[...], preferred_element_type=F32)
            out_stage[slot, blocks] = result.astype(BF).reshape(2, rows, width)
            return carry

        lax.fori_loop(0, 2, some, 0)
        for copy in stage_copies(slot, j, c):
            copy.start()
        return carry

    lax.fori_loop(0, 2 * extent, group, 0)
    for slot in range(2):
        for copy in stage_copies(slot, 0, slot):
            copy.wait()
    for g in range(2 * extent):
        pltpu.make_async_copy(
            gathered.at[arrival(t, g // 2), g % 2],
            tokens.at[arrival(t, g // 2), g % 2],
            token_sem.at[g],
        ).wait()
    for k in range(extent - 2, extent):
        probs_copy(k).wait()
    for copy in kept:
        copy.wait()
    wire.finish()


SMEM = pl.BlockSpec(memory_space=pltpu.SMEM)


def front(extent, lengths, hid, *rest):
    rows, width = hid.shape
    seq_len = rows * extent
    slab = rest[6].shape[1]
    heads = rest[4].shape[0]
    columns = heads * HD
    shape = jax.ShapeDtypeStruct
    kept = [
        shape((seq_len, width), BF),
        shape((width, 3 * columns), BF),
        shape((columns, width), BF),
        shape((seq_len, width), BF),
        shape((seq_len, 3 * columns), F32),
        shape((seq_len, 3 * columns), BF),
        shape((heads, seq_len, seq_len), F32),
        shape((seq_len, columns), BF),
    ]
    return pl.pallas_call(
        functools.partial(front_kernel, extent),
        out_shape=[
            shape((rows, 128), F32),
            shape((rows, width), F32),
            shape((rows, 128), F32),
            shape((2 * heads, HD), F32),
            shape((seq_len, 128), F32),
        ]
        + kept
        + [
            shape((extent, 2, 4, rows, width + 128), BF),
            shape((extent, 2, 4 * rows, 4 * slab), BF),
            shape((extent, 2, 4, rows, width), BF),
            shape((8, 3, 2, slab, slab), BF),
        ],
        in_specs=[SMEM, VM] + [ANY] * 4 + [VM] * 2 + [ANY] * 3 + [VM] * 6,
        out_specs=[VM] * 5 + [ANY] * 12,
        scratch_shapes=[
            pltpu.VMEM((seq_len, width), BF),
            pltpu.VMEM((width, 3 * columns), BF),
            pltpu.VMEM((columns, width), BF),
            pltpu.VMEM((8, 2 * heads, HD), F32),
            pltpu.VMEM((128, width), BF),
            pltpu.VMEM((seq_len, width), BF),
            pltpu.VMEM((seq_len, 3 * columns), F32),
            pltpu.VMEM((seq_len, 3 * columns), BF),
            pltpu.VMEM((2, heads, rows, seq_len), F32),
            pltpu.VMEM((seq_len, columns), BF),
            pltpu.VMEM((seq_len, 128), F32),
            pltpu.VMEM((8, seq_len), F32),
            pltpu.VMEM((extent - 1, 8, seq_len), F32),
            pltpu.VMEM((extent, 2, 4, rows, width + 128), BF),
            pltpu.VMEM((extent, rows, width), BF),
            pltpu.VMEM((extent - 1, rows, width), BF),
            pltpu.VMEM((extent - 1, rows, width), BF),
            pltpu.VMEM((width, 4 * slab), BF),
            pltpu.VMEM((2 * slab, width), BF),
            pltpu.VMEM((2, 4 * rows, 4 * slab), BF),
            pltpu.VMEM((2, 4, rows, width), BF),
        ]
        + dma_pair(180)
        + [
            pltpu.SemaphoreType.DMA((16,)),
            pltpu.SemaphoreType.DMA((48,)),
            pltpu.SemaphoreType.DMA((2, 2)),
            pltpu.SemaphoreType.DMA((2 * extent,)),
            pltpu.SemaphoreType.DMA((2,)),
        ],
        compiler_params=kernel_params(1),
        cost_estimate=pl.CostEstimate(flops=0, bytes_accessed=300_000_000, transcendentals=0),
    )(lengths, hid, *rest)


def turn_kernel(extent, lengths, partial, middle, teacher, tokens, hidden, *rest):
    landed, tables = rest[0], rest[1:4]
    grad_output, row_loss, out, inner_out, active_out, grads = rest[4:10]
    buffers = rest[10:20]
    (
        packet,
        in_weight,
        out_weight,
        coeff_tile,
        hidden_tile,
        factors,
        grad_tile,
        out_stage,
        active_tile,
        inner_tile,
        send_sem,
        recv_sem,
        local_sem,
        weight_sem,
        tile_sem,
        load_sem,
    ) = rest[20:]
    d, t = lax.axis_index("dp"), lax.axis_index("tensor")
    rows, width = middle.shape
    greet(plane_devices(d, t, extent))
    wire, local = Wire(send_sem, recv_sem), Local(local_sem)
    pieces = [landed.at[bits] for bits in range(8)]
    weights = Pieces(d, in_weight, out_weight, weight_sem, pieces, tables)
    units, slab = out_weight.shape[0], out_weight.shape[0] // 2
    count = 2 * extent

    def factor_loads(g):
        j, c, slot = g // 2, g % 2, g % 2
        part = (pl.ds(0, 4), pl.ds(0, rows), pl.ds(width, 128))
        return (
            pltpu.make_async_copy(
                tokens.at[(j, c) + part], coeff_tile.at[slot], load_sem.at[0, slot]
            ),
            pltpu.make_async_copy(hidden.at[j, c], hidden_tile.at[slot], load_sem.at[1, slot]),
        )

    def active_store(g):
        return pltpu.make_async_copy(
            active_tile.at[g % 2], active_out.at[g // 2, g % 2], load_sem.at[2, g % 2]
        )

    def prepare(g):
        if g + 1 < count:
            for copy in factor_loads(g + 1):
                copy.start()
        for copy in factor_loads(g):
            copy.wait()
        if g >= 2:
            active_store(g - 2).wait()
        slot = g % 2

        def some(first, carry):
            size = 2 * rows
            blocks, part = pl.ds(2 * first, 2), pl.ds(first * size, size)
            gate_value = hidden_tile[slot, part, 0:units].astype(F32)
            up_value = hidden_tile[slot, part, units : 2 * units].astype(F32)
            coeff = coefficients(coeff_tile[slot, blocks].reshape(size, 128), d, slab)
            sigmoid_value = jax.nn.sigmoid(gate_value)
            silu_value = gate_value * sigmoid_value
            slope = sigmoid_value * (1.0 + gate_value * (1.0 - sigmoid_value))
            direct = silu_value * up_value
            factors[g, part, 0:units] = (coeff * up_value * slope).astype(BF)
            factors[g, part, units : 2 * units] = (coeff * silu_value).astype(BF)
            factors[g, part, 2 * units : 3 * units] = direct.astype(BF)
            active_tile[slot, part] = (coeff * direct).astype(BF)
            return carry

        lax.fori_loop(0, 2, some, 0)
        active_store(g).start()

    for copy in factor_loads(0):
        copy.start()

    def between(turn_number):
        if turn_number == 1:
            for bits in range(8):
                weights.load(bits)
        if turn_number < extent:
            prepare(2 * turn_number)
            prepare(2 * turn_number + 1)

    sum_plane(wire, local, d, t, extent, partial, buffers, rows, between)
    for g in (count - 2, count - 1):
        active_store(g).wait()

    total_count = lengths[0]
    for n in range(1, lengths.shape[0]):
        total_count = total_count + lengths[n]
    length = lengths[d]

    def body(part, value):
        row = t * rows + part.start + lax.broadcasted_iota(jnp.int32, (16, 1), 0)
        count = jnp.broadcast_to(total_count, (16, 1)).astype(F32)
        weight = jnp.where(row < length, 8 * extent * rows / count, 0.0)
        output = middle[part] + value
        mismatch = output - teacher[part].astype(F32)
        scaled = mismatch * weight
        grad_output[part] = scaled
        packet[part] = scaled.astype(BF)
        row_loss[part] = jnp.broadcast_to(
            jnp.sum(scaled * mismatch, axis=-1, keepdims=True), (16, 128)
        )

    own_rows(buffers, rows, pl.ds(0, width), body)

    def place(j, c, i):
        return grads.at[j, c, i]

    def bundle(j, c):
        return grads.at[j, c, pl.ds(0, 4), pl.ds(rows - LATE, LATE)]

    own_copy = local.start(packet, place(t, 0, 0))
    gather = PlaneGather(wire, d, t, extent, lambda: packet, place, bundle, rows)
    own_copy.wait()
    for bits in range(8):
        weights.loaded(bits)
    actions = gather.actions()

    def out_copies(j, c):
        return (
            pltpu.make_async_copy(out_stage, out.at[j, c], tile_sem.at[1]),
            pltpu.make_async_copy(inner_tile, inner_out.at[j, c], tile_sem.at[2]),
        )

    def group(g, carry):
        j, c = arrival(t, g // 2), g % 2
        grad_copy = pltpu.make_async_copy(grads.at[j, c], grad_tile, tile_sem.at[0])
        for number, steps in enumerate(actions):

            @pl.when(g == number)
            def _():
                for action, argument in steps:
                    action(argument)

        grad_copy.start()

        @pl.when(g >= 1)
        def _():
            for copy in out_copies(j, c):
                copy.wait()

        grad_copy.wait()
        index = 2 * j + c

        def some(first, carry):
            size = 2 * rows
            blocks, part = pl.ds(2 * first, 2), pl.ds(first * size, size)
            grad_active = dot_transposed(
                grad_tile[blocks].reshape(size, width), out_weight[...]
            )
            product = grad_active * factors[index, part, 2 * units : 3 * units].astype(F32)
            lane = lax.broadcasted_iota(jnp.int32, (size, 128), 1)
            sums = jnp.zeros((size, 128), F32)
            for e in range(2):
                one = jnp.sum(product[:, e * slab : (e + 1) * slab], axis=-1, keepdims=True)
                sums = sums + jnp.where(lane == 2 * d + e, one, 0.0)
            out_stage[blocks, :, width : width + 128] = sums.astype(BF).reshape(2, rows, 128)
            for n in range(2):
                columns = pl.ds(n * units, units)
                inner_tile[part, columns] = (
                    grad_active * factors[index, part, columns].astype(F32)
                ).astype(BF)
            result = dot_transposed(inner_tile[part], in_weight[...]).astype(BF)
            out_stage[blocks, :, 0:width] = result.reshape(2, rows, width)
            return carry

        lax.fori_loop(0, 2, some, 0)
        for copy in out_copies(j, c):
            copy.start()
        return carry

    lax.fori_loop(0, 2 * extent, group, 0)
    for copy in out_copies(0, 0):
        copy.wait()
    wire.finish()


def turn(extent, lengths, partial, middle, teacher, tokens, hidden, landed, *tables):
    rows, width = middle.shape
    slab = landed.shape[3]
    return pl.pallas_call(
        functools.partial(turn_kernel, extent),
        out_shape=[
            jax.ShapeDtypeStruct((rows, width), F32),
            jax.ShapeDtypeStruct((rows, 128), F32),
            jax.ShapeDtypeStruct((extent, 2, 4, rows, width + 128), BF),
            jax.ShapeDtypeStruct((extent, 2, 4 * rows, 4 * slab), BF),
            jax.ShapeDtypeStruct((extent, 2, 4 * rows, 2 * slab), BF),
            jax.ShapeDtypeStruct((extent, 2, 4, rows, width), BF),
        ],
        in_specs=[SMEM, ANY, VM, VM] + [ANY] * 6,
        out_specs=[VM, VM] + [ANY] * 4,
        scratch_shapes=sum_scratch(extent, rows, width)
        + [
            pltpu.VMEM((rows, width), BF),
            pltpu.VMEM((width, 4 * slab), BF),
            pltpu.VMEM((2 * slab, width), BF),
            pltpu.VMEM((2, 4, rows, 128), BF),
            pltpu.VMEM((2, 4 * rows, 4 * slab), BF),
            pltpu.VMEM((2 * extent, 4 * rows, 6 * slab), BF),
            pltpu.VMEM((4, rows, width), BF),
            pltpu.VMEM((4, rows, width + 128), BF),
            pltpu.VMEM((2, 4 * rows, 2 * slab), BF),
            pltpu.VMEM((4 * rows, 4 * slab), BF),
        ]
        + dma_pair(150)
        + [
            pltpu.SemaphoreType.DMA((20,)),
            pltpu.SemaphoreType.DMA((48,)),
            pltpu.SemaphoreType.DMA((3,)),
            pltpu.SemaphoreType.DMA((3, 2)),
        ],
        compiler_params=kernel_params(4),
        cost_estimate=pl.CostEstimate(flops=0, bytes_accessed=450_000_000, transcendentals=0),
    )(lengths, partial, middle, teacher, tokens, hidden, landed, *tables)


class WeightGrads:
    def __init__(self, sources, tiles, totals, sem):
        self.sources, self.tiles, self.sem = sources, tiles, sem
        self.in_total, self.out_total = totals

    def copies(self, g):
        j, c, slot = g // 2, g % 2, g % 2
        return [
            pltpu.make_async_copy(source.at[j, c], tile.at[slot], self.sem.at[n, slot])
            for n, (source, tile) in enumerate(zip(self.sources, self.tiles))
        ]

    def start(self, g):
        for copy in self.copies(g):
            copy.start()

    def clear(self):
        self.in_total[...] = jnp.zeros(self.in_total.shape, F32)
        self.out_total[...] = jnp.zeros(self.out_total.shape, F32)

    def work(self, g, count):
        if g + 1 < count:
            self.start(g + 1)
        for copy in self.copies(g):
            copy.wait()
        slot = g % 2
        token_tile, grad_tile, inner_tile, active_tile = (tile.at[slot] for tile in self.tiles)
        size, width = inner_tile.shape[0], grad_tile.shape[2]

        def into_in(start):
            part = pl.ds(start, 256)
            left = token_tile[:, :, part].reshape(size, 256)
            self.in_total[part] += transposed_dot(left, inner_tile[...])

        rows_loop(width, 256, into_in)

        def into_out(start):
            part = pl.ds(start, 512)
            right = grad_tile[:, :, part].reshape(size, 512)
            self.out_total[:, part] += transposed_dot(active_tile[...], right)

        rows_loop(width, 512, into_out)

    def pieces(self, d, stage):
        slab = stage.shape[3]
        for bits in range(8):
            part = pl.ds(pl.multiple_of(flip(d, bits) * slab, slab), slab)
            for place in range(3):
                for e in range(2):
                    if place < 2:
                        column = (2 * place + e) * slab
                        value = self.in_total[part, column : column + slab]
                    else:
                        value = self.out_total[e * slab : (e + 1) * slab, part]
                    stage[bits, place, e] = value.astype(BF)


def leave_kernel(extent, partial, middle, grad_output, gates, chosen, gain, router, *rest):
    sources = rest[:4]
    grad_middle, small, grads = rest[4:7]
    came = rest[7:15]
    buffers = rest[15:25]
    tiles, totals = rest[25:29], rest[29:31]
    stage, packet, grad_logits, gain_part, ffn_own, send_sem, recv_sem, local_sem, tile_sem = rest[31:]
    d, t = lax.axis_index("dp"), lax.axis_index("tensor")
    rows, width = middle.shape
    greet(line_devices(d, t, extent) + [(None, (flip(d, bits), t)) for bits in range(1, 6)])
    wire, local = Wire(send_sem, recv_sem), Local(local_sem)
    weight_grads = WeightGrads(sources, tiles, totals, tile_sem)
    count = 2 * extent
    piece_slots, copies = [], []
    weight_grads.start(0)

    def between(turn_number):
        if turn_number == 0:
            weight_grads.clear()
        if turn_number < extent:
            weight_grads.work(2 * turn_number, count)
            weight_grads.work(2 * turn_number + 1, count)
        if turn_number == extent + 2:
            weight_grads.pieces(d, stage)
            for bits in range(1, 6):
                slot = wire.slot()
                piece_slots.append(slot)
                wire.start(
                    slot,
                    lambda bits=bits: stage.at[bits],
                    lambda bits=bits: came[bits],
                    (flip(d, bits), t),
                )
            for bits in (0, 6, 7):
                copies.append(local.start(stage.at[bits], came[bits]))

    sum_plane(wire, local, d, t, extent, partial, buffers, rows, between)

    def collect(part, value):
        grad_logits[part] = value

    own_rows(buffers, rows, pl.ds(width, 128), collect)
    coeff_grad = grad_logits[...] * chosen[...]
    lane = lax.broadcasted_iota(jnp.int32, coeff_grad.shape, 1)
    probs = jnp.where(lane < 16, gates[...], 0.0)
    coeff_grad = jnp.where(lane < 16, coeff_grad, 0.0)
    logit_grad = probs * (coeff_grad - jnp.sum(coeff_grad * probs, axis=-1, keepdims=True))
    grad_logits[...] = logit_grad
    high = logit_grad.astype(BF)
    low_part = (logit_grad - high.astype(F32)).astype(BF)
    for begin in range(0, width, 512):
        columns = slice(begin, begin + 512)
        grad_middle[:, columns] = jnp.dot(
            high[:, 0:16], router[:, columns], preferred_element_type=F32
        ) + jnp.dot(low_part[:, 0:16], router[:, columns], preferred_element_type=F32)
    gain_part[...] = jnp.zeros(gain_part.shape, F32)

    def body(part, value):
        grad = value + grad_middle[part]
        value = middle[part]
        inverse = lax.rsqrt(jnp.mean(value * value, axis=-1, keepdims=True) + EPSILON)
        unit = value * inverse
        product = grad * unit
        gain_part[...] += product[0:8] + product[8:16]
        gain_row = gain[1:2]
        ffn_own[part] = (unit * gain_row).astype(BF)
        scaled = grad * gain_row
        result = grad_output[part] + inverse * (
            scaled - unit * jnp.mean(scaled * unit, axis=-1, keepdims=True)
        )
        grad_middle[part] = result
        packet[part] = result.astype(BF)

    own_rows(buffers, rows, pl.ds(0, width), body)

    def place(index):
        return grads.at[index]

    copies.append(local.start(packet, place(t)))
    line = LineGather(wire, d, t, extent, lambda: packet, place)
    line.begin()
    router_part = transposed_dot(high, ffn_own[...]) + transposed_dot(low_part, ffn_own[...])
    small[0:16] = router_part[0:16]
    row = lax.broadcasted_iota(jnp.int32, (8, width), 0)
    gain_sum = jnp.sum(gain_part[...], axis=0, keepdims=True)
    small[16:24] = jnp.where(row == 1, gain_sum, 0.0)
    for step in range(1, extent):
        line.step(step)
    for copy in copies:
        copy.wait()
    for n, slot in enumerate(piece_slots):
        wire.arrive(slot, lambda: came[1 + n], (flip(d, 1 + n), t))
    wire.finish()


def leave(extent, partial, middle, grad_output, gates, chosen, gain, router, sources):
    rows, width = middle.shape
    tokens, grads, inner, active = sources
    units = active.shape[3]
    piece = jax.ShapeDtypeStruct((3, 2, units // 2, units // 2), BF)
    return pl.pallas_call(
        functools.partial(leave_kernel, extent),
        out_shape=[
            jax.ShapeDtypeStruct((rows, width), F32),
            jax.ShapeDtypeStruct((24, width), F32),
            jax.ShapeDtypeStruct((extent, rows, width), BF),
        ]
        + [piece] * 8,
        in_specs=[ANY, VM, VM, VM, VM, VM, VM] + [ANY] * 4,
        out_specs=[VM, VM] + [ANY] * 9,
        scratch_shapes=sum_scratch(extent, rows, width + 128)
        + [pltpu.VMEM((2,) + source.shape[2:], BF) for source in sources]
        + [
            pltpu.VMEM((width, 2 * units), F32),
            pltpu.VMEM((units, width), F32),
            pltpu.VMEM((8,) + piece.shape, BF),
            pltpu.VMEM((rows, width), BF),
            pltpu.VMEM((rows, 128), F32),
            pltpu.VMEM((8, width), F32),
            pltpu.VMEM((rows, width), BF),
        ]
        + dma_pair(120)
        + [pltpu.SemaphoreType.DMA((24,)), pltpu.SemaphoreType.DMA((4, 2))],
        compiler_params=kernel_params(5),
        cost_estimate=pl.CostEstimate(flops=0, bytes_accessed=350_000_000, transcendentals=0),
    )(partial, middle, grad_output, gates, chosen, gain, router, *sources)


def back_kernel(
    extent,
    grads,
    row_loss,
    hid_far,
    gain,
    qkv_far,
    o_weight,
    head_gain,
    cosine,
    sine,
    normed_far,
    units_far,
    low_far,
    probs_far,
    mixed,
    inverses,
    small,
    middle_far,
    grad_in,
    q_out,
    k_out,
    v_out,
    o_out,
    router_out,
    vectors_out,
    q_gain_out,
    k_gain_out,
    loss,
    low,
    probs,
    units,
    qkv_weight,
    normed,
    hid,
    grad_middle,
    load_sem,
    grad_mixed,
    scaled,
    raw_grad,
    sums,
    dots,
    outbox,
    inbox,
    gain_part,
    head_part,
    work,
    up_in,
    down_in,
    q_send,
    q_work,
    q_core,
    q_a,
    q_b,
    o_send,
    o_work,
    o_core,
    o_a,
    o_b,
    small_send,
    small_in,
    small_sum,
    small_last,
    send_sem,
    recv_sem,
):
    d, t = lax.axis_index("dp"), lax.axis_index("tensor")
    seq_len, width = hid.shape
    rows = seq_len // extent
    heads = head_gain.shape[0] // 2
    columns = heads * HD
    depth, o_width = q_out.shape[0], o_out.shape[1]
    peers = [(d, (t + k) % extent) for k in range(1, extent)]
    greet(line_peers(d, t, extent) + [(None, (flip(d, bits), t)) for bits in range(1, 8)])
    wire, local = Wire(send_sem, recv_sem), Local(load_sem)
    loads = [
        local.start(source, target)
        for source, target in (
            (low_far, low),
            (probs_far, probs),
            (units_far.at[pl.ds(0, seq_len), pl.ds(0, 2 * columns)], units),
            (normed_far, normed),
            (qkv_far, qkv_weight),
            (hid_far, hid),
            (middle_far, grad_middle),
        )
    ]
    to_x, to_y, to_c = (flip(d, 2), t), (flip(d, 4), t), (flip(d, 1), t)
    tile = 256
    root = math.sqrt(HD)
    turns = (3, 1, 2, 0)

    def mix(start):
        part = pl.ds(start, tile)
        grad_mixed[part] = dot_transposed(grads[part], o_weight[...]).astype(BF)

    rows_loop(seq_len, tile, mix)

    def o_slice(bits, target):
        start = pl.multiple_of(flip(d, bits) * o_width, o_width)
        target[...] = transposed_dot(mixed[...], grads[:, pl.ds(start, o_width)]).astype(BF)

    core_slots = {}
    for i in turns:
        o_slice(1 + 2 * i, o_send.at[i])
        core_slots["o", i] = wire.slot()
        wire.start(core_slots["o", i], lambda i=i: o_send.at[i], lambda i=i: o_core.at[i], to_c)
    for i in turns:
        o_slice(2 * i, o_work.at[i])
    sums[...] = jnp.zeros(sums.shape, F32)
    for load in loads:
        load.wait()

    def head(h, carry):
        section = pl.ds(pl.multiple_of(h * HD, HD), HD)
        key_section = pl.ds(pl.multiple_of(columns + h * HD, HD), HD)
        value_section = pl.ds(pl.multiple_of(2 * columns + h * HD, HD), HD)
        chance = probs[h]
        incoming = grad_mixed[:, section]
        raw_grad[:, value_section] = transposed_dot(chance.astype(BF), incoming).astype(BF)
        grad_probs = dot_transposed(incoming, low[:, value_section])
        grad_scores = (
            chance * (grad_probs - jnp.sum(grad_probs * chance, axis=-1, keepdims=True))
        ).astype(BF)
        pair = (
            jnp.dot(grad_scores, low[:, key_section], preferred_element_type=F32) / root,
            transposed_dot(grad_scores, low[:, section]) / root,
        )
        lane = lax.broadcasted_iota(jnp.int32, (seq_len, 128), 1)
        for n, where in enumerate((section, key_section)):
            value = turned(pair[n], cosine[...], sine[...], -1.0)
            unit = units[:, where]
            head_part[pl.ds(n * heads + h, 1)] = jnp.sum(value * unit, axis=0, keepdims=True)
            value = value * head_gain[pl.ds(n * heads + h, 1)]
            scaled[:, where] = value
            sums[...] += jnp.where(lane == n, jnp.sum(value * unit, axis=-1, keepdims=True), 0.0)
        return carry

    lax.fori_loop(0, heads, head, 0)
    outbox[...] = columns_to_rows(sums)
    outbox[2:3] = jnp.broadcast_to(jnp.sum(row_loss[:, 0:1], axis=0, keepdims=True), (1, seq_len))
    total = line_exchange(wire, t, d, extent, outbox, inbox)
    loss[...] = total[:, 0:128] / (2.0 * width * 8 * seq_len)
    dots[...] = rows_to_columns(total / width)

    def head_again(h, carry):
        for n in range(2):
            section = pl.ds(pl.multiple_of(n * columns + h * HD, HD), HD)
            raw_grad[:, section] = (
                inverses[:, n : n + 1]
                * (scaled[:, section] - units[:, section] * dots[:, n : n + 1])
            ).astype(BF)
        return carry

    lax.fori_loop(0, heads, head_again, 0)
    gain_part[...] = jnp.zeros(gain_part.shape, F32)
    order = plane_order(t)

    def input_block(k):
        part = pl.ds(pl.multiple_of(order[k] * rows, rows), rows)
        grad = dot_transposed(raw_grad[part], qkv_weight[...])
        value = hid[part].astype(F32)
        inverse = lax.rsqrt(jnp.mean(value * value, axis=-1, keepdims=True) + EPSILON)
        unit = value * inverse
        gain_part[...] += jnp.sum((grad * unit).reshape(rows // 8, 8, width), axis=0)
        change = grad * gain[0:1]
        work[order[k]] = (
            inverse * (change - unit * jnp.mean(change * unit, axis=-1, keepdims=True))
        ).astype(BF)

    def q_slice(bits, target):
        start = pl.multiple_of(flip(d, bits) * depth, depth)
        target[...] = transposed_dot(normed[:, pl.ds(start, depth)], raw_grad[...]).astype(BF)

    def q_core_send(i):
        q_slice(1 + 2 * i, q_send.at[i])
        core_slots["q", i] = wire.slot()
        wire.start(core_slots["q", i], lambda: q_send.at[i], lambda: q_core.at[i], to_c)

    line = LineSum(
        wire, d, t, extent, lambda index: work.at[index], up_in, down_in, rows, 2
    )

    def cut(ref, which):
        half = ref.shape[0] // 2
        return ref.at[pl.ds(which * half, half)]

    slots = {}
    routes_a = ((to_x, 3, 2, 0, 0), (to_y, 3, 1, 1, 1), (to_x, 1, 0, 0, 2), (to_y, 2, 0, 1, 3))
    routes_b = ((to_y, 2, 0, 0), (to_x, 1, 1, 1))
    tables = (("q", q_work, q_core, q_a, q_b), ("o", o_work, o_core, o_a, o_b))

    def core_add(i):
        for name, kept, core, unused, unused_too in tables:
            wire.arrive(core_slots[name, i], lambda: core.at[i], to_c)
            add_into(kept.at[i], core.at[i], kept.shape[1])

    def forward(stage, device, source, which, row):
        for name, kept, unused, first, second in tables:
            slots[name, stage, row] = wire.slot()
            inbox_ref = first if stage == "a" else second
            wire.start(
                slots[name, stage, row],
                lambda kept=kept: cut(kept.at[source], which),
                lambda inbox_ref=inbox_ref: inbox_ref.at[row],
                device,
            )

    q_core_send(3)
    input_block(0)
    line.step(0)
    q_core_send(1)
    q_core_send(2)
    q_core_send(0)
    for i in turns:
        q_slice(2 * i, q_work.at[i])
        core_add(i)
        for device, source, unused, which, row in routes_a:
            if source == i:
                forward("a", device, source, which, row)
    input_block(1)
    input_block(2)
    line.step(1)
    input_block(3)
    small_rows = small.shape[0]
    vector = jnp.sum(gain_part[...], axis=0, keepdims=True)
    row = lax.broadcasted_iota(jnp.int32, (small_rows, 128), 0)
    for number in range(width // 128):
        lanes = slice(number * 128, number * 128 + 128)
        small_send[number % 2, number // 2] = jnp.where(
            row == 16, vector[:, lanes], small[:, lanes]
        )
    small_slots = []
    for k, peer in enumerate(peers):
        slot = wire.slot()
        small_slots.append(slot)
        wire.start(
            slot,
            lambda k=k: small_send.at[((t + k + 1) % extent) // 2],
            lambda k=k: small_in.at[k],
            peer,
        )
    for device, source, target, which, row_number in routes_a:
        for name, kept, unused, first, second in tables:
            wire.arrive(slots[name, "a", row_number], lambda: first.at[row_number], device)
            add_into(cut(kept.at[target], which), first.at[row_number], first.shape[1])
        if row_number < 2:
            to, origin, part, b_row = routes_b[row_number]
            forward("b", to, origin, part, b_row)
        if row_number == 1:
            line.step(2)
    result = small_send[t // 2]
    for k, peer in enumerate(peers):
        wire.arrive(small_slots[k], lambda k=k: small_in.at[k], peer)
        result = result + small_in[k]
    small_sum[:, 0:small_rows] = result
    small_sum[:, small_rows : small_rows + 2 * heads] = jnp.broadcast_to(
        head_part[...][None], (8, 2 * heads, 128)
    )
    last_slots = {}
    for bits in range(1, 8):
        last_slots[bits] = wire.slot()
        wire.start(
            last_slots[bits],
            lambda bits=bits: small_sum.at[flip(d, bits)],
            lambda bits=bits: small_last.at[bits],
            (flip(d, bits), t),
        )
    for device, source, which, row_number in routes_b:
        for name, kept, unused, first, second in tables:
            came = second.at[row_number]
            wire.arrive(slots[name, "b", row_number], lambda: came, device)
            base = which * (kept.shape[1] // 2)

            def body(start, kept=kept, came=came, base=base, name=name):
                here = pl.ds(start, 16)
                there = pl.ds(pl.multiple_of(base + start, 16), 16)
                value = kept[0, there].astype(F32) + came[here].astype(F32)
                if name == "o":
                    o_out[there] = value
                else:
                    for n, target in enumerate((q_out, k_out, v_out)):
                        target[there] = value[:, n * columns : (n + 1) * columns]

            rows_loop(kept.shape[1] // 2, 16, body)
    line.last()
    mine = work.at[t]

    def finish(start):
        part = pl.ds(start, 16)
        grad_in[part] = grad_middle[part] + own_sum(
            mine, up_in.at[extent - 2], down_in.at[extent - 2], part, pl.ds(0, width)
        )

    rows_loop(rows, 16, finish)
    total = small_sum[d]
    for bits in range(1, 8):
        wire.arrive(
            last_slots[bits], lambda bits=bits: small_last.at[bits], (flip(d, bits), t)
        )
        total = total + small_last[bits]
    share = pltpu.roll(total, (128 - 64 * (t % 2)) % 128, 1)
    router_out[...] = share[0:16, 0 : router_out.shape[1]]
    vectors_out[...] = share[16:24]
    head_width = q_gain_out.shape[1]
    gains = pltpu.roll(total, (128 - head_width * d) % 128, 1)
    q_gain_out[...] = gains[small_rows : small_rows + heads, 0:head_width]
    k_gain_out[...] = gains[small_rows + heads : small_rows + 2 * heads, 0:head_width]
    wire.finish()


def back(extent, *operands):
    seq_len, width = operands[0].shape
    rows = seq_len // extent
    head_gain, small = operands[6], operands[15]
    heads = head_gain.shape[0] // 2
    columns = heads * HD
    depth, o_width = width // 8, width // 8
    split = rows // 2
    shape = jax.ShapeDtypeStruct
    scratch = [
        pltpu.VMEM((seq_len, 3 * columns), BF),
        pltpu.VMEM((heads, seq_len, seq_len), F32),
        pltpu.VMEM((seq_len, 2 * columns), F32),
        pltpu.VMEM((width, 3 * columns), BF),
        pltpu.VMEM((seq_len, width), BF),
        pltpu.VMEM((seq_len, width), BF),
        pltpu.VMEM((rows, width), F32),
        pltpu.SemaphoreType.DMA((8,)),
        pltpu.VMEM((seq_len, columns), BF),
        pltpu.VMEM((seq_len, 2 * columns), F32),
        pltpu.VMEM((seq_len, 3 * columns), BF),
        pltpu.VMEM((seq_len, 128), F32),
        pltpu.VMEM((seq_len, 128), F32),
        pltpu.VMEM((8, seq_len), F32),
        pltpu.VMEM((extent - 1, 8, seq_len), F32),
        pltpu.VMEM((8, width), F32),
        pltpu.VMEM((2 * heads, HD), F32),
        pltpu.VMEM((extent, rows, width), BF),
        pltpu.VMEM((extent - 1, rows, width), BF),
        pltpu.VMEM((extent - 1, rows, width), BF),
    ]
    for tall, wide in ((depth, 3 * columns), (columns, o_width)):
        scratch += [
            pltpu.VMEM((4, tall, wide), BF),
            pltpu.VMEM((4, tall, wide), BF),
            pltpu.VMEM((4, tall, wide), BF),
            pltpu.VMEM((4, tall // 2, wide), BF),
            pltpu.VMEM((2, tall // 2, wide), BF),
        ]
    packed = small.shape[0] + 2 * heads
    scratch += [
        pltpu.VMEM((2, 8, small.shape[0], 128), F32),
        pltpu.VMEM((extent - 1, 8, small.shape[0], 128), F32),
        pltpu.VMEM((8, packed, 128), F32),
        pltpu.VMEM((8, packed, 128), F32),
    ]
    return pl.pallas_call(
        functools.partial(back_kernel, extent),
        out_shape=[
            shape((rows, width), F32),
            shape((depth, columns), F32),
            shape((depth, columns), F32),
            shape((depth, columns), F32),
            shape((columns, o_width), F32),
            shape((16, width // (8 * extent)), F32),
            shape((8, 128), F32),
            shape((heads, HD // 8), F32),
            shape((heads, HD // 8), F32),
            shape((8, 128), F32),
        ],
        in_specs=[ANY if n in (2, 4, 9, 10, 11, 12, 16) else VM for n in range(17)],
        out_specs=[VM] * 10,
        scratch_shapes=scratch + dma_pair(80),
        compiler_params=kernel_params(6),
        cost_estimate=pl.CostEstimate(flops=0, bytes_accessed=1_000_000, transcendentals=0),
    )(*operands)


def spread_kernel(*refs):
    pieces, large, (vectors, q_gain, k_gain, loss, router) = refs[:8], refs[8:13], refs[13:18]
    tables, large_out = refs[18:21], refs[21:26]
    loss_out, attn_out, ffn_out, q_gain_out, k_gain_out, router_out = refs[26:32]
    near, stage, *copies, in_sem, out_sem, large_sem = refs[32:]
    d = lax.axis_index("dp")
    slab = near.shape[3]
    moves = []
    for n, (source, middle, target) in enumerate(zip(large, copies, large_out)):
        moves.append(
            (
                pltpu.make_async_copy(source, middle, large_sem.at[0, n]),
                pltpu.make_async_copy(middle, target, large_sem.at[1, n]),
            )
        )
    loads = [
        pltpu.make_async_copy(pieces[bits], near.at[bits], in_sem.at[bits]) for bits in range(8)
    ]
    for bits in range(4):
        loads[bits].start()
    for first, second in moves:
        first.start()
    for bits in range(4, 8):
        loads[bits].start()
    loss_out[...] = loss[2:3, 0:1]
    attn_out[...] = vectors[0:1, 0 : attn_out.shape[1]]
    ffn_out[...] = vectors[1:2, 0 : ffn_out.shape[1]]
    q_gain_out[...] = q_gain[...]
    k_gain_out[...] = k_gain[...]
    router_out[...] = router[...]
    stores = []
    for bits in range(8):
        loads[bits].wait()
        begin = 2 * flip(d, bits)
        for place in range(3):
            for e in range(2):

                def body(start, bits=bits, place=place, e=e, begin=begin):
                    part = pl.ds(start, 64)
                    stage[place, begin + e, part] = near[bits, place, e, part].astype(F32)

                rows_loop(slab, 64, body)
            store = pltpu.make_async_copy(
                stage.at[place, pl.ds(begin, 2)],
                tables[place].at[pl.ds(begin, 2)],
                out_sem.at[bits, place],
            )
            store.start()
            stores.append(store)
        if bits == 3:
            for first, second in moves:
                first.wait()
                second.start()
    for first, second in moves:
        second.wait()
    for store in stores:
        store.wait()


def spread(pieces, large, small):
    table = jax.ShapeDtypeStruct((16,) + pieces[0].shape[2:], F32)
    vectors, q_gain, k_gain, loss, router = small
    shape = jax.ShapeDtypeStruct
    split = router.shape[1]
    same = lambda array: shape(array.shape, array.dtype)
    return pl.pallas_call(
        spread_kernel,
        out_shape=[table] * 3
        + [same(array) for array in large]
        + [
            shape((1, 1), F32),
            shape((1, split), F32),
            shape((1, split), F32),
            same(q_gain),
            same(k_gain),
            same(router),
        ],
        in_specs=[ANY] * 13 + [VM] * 5,
        out_specs=[ANY] * 8 + [VM] * 6,
        scratch_shapes=[
            pltpu.VMEM((8,) + pieces[0].shape, BF),
            pltpu.VMEM((3,) + table.shape, F32),
        ]
        + [pltpu.VMEM(array.shape, F32) for array in large]
        + [
            pltpu.SemaphoreType.DMA((8,)),
            pltpu.SemaphoreType.DMA((8, 3)),
            pltpu.SemaphoreType.DMA((2, 5)),
        ],
        compiler_params=pltpu.CompilerParams(vmem_limit_bytes=VMEM_LIMIT),
        cost_estimate=pl.CostEstimate(flops=0, bytes_accessed=20_000_000, transcendentals=0),
    )(*pieces, *large, *small)


def exchange(value, bits):
    if bits == 0:
        return value
    return lax.ppermute(value, "dp", [(i, i ^ bits) for i in range(8)])


def per_device_block(
    hidden_in,
    teacher,
    lengths,
    routes,
    attn_norm_gain,
    ffn_norm_gain,
    q_weight,
    k_weight,
    v_weight,
    q_gain,
    k_gain,
    o_weight,
    router_weight,
    gate_weight,
    up_weight,
    down_weight,
):
    extent = lax.axis_size("tensor")
    rows, width = hidden_in.shape
    seq_len = rows * extent
    norm_gains = jnp.stack([attn_norm_gain, ffn_norm_gain]).astype(F32)
    angles = np.arange(seq_len)[:, None] * THETA ** (-np.arange(HD // 2) / (HD // 2))[None, :]
    cosine = jnp.asarray(np.concatenate([np.cos(angles)] * 2, axis=1), F32)
    sine = jnp.asarray(np.concatenate([-np.sin(angles), np.sin(angles)], axis=1), F32)
    (
        chosen,
        middle,
        gates,
        head_gain,
        inverses,
        hidden_bf,
        qkv_full,
        o_full,
        normed,
        units,
        low,
        probs,
        mixed,
        tokens,
        hidden,
        expert_partial,
        landed,
    ) = front(
        extent,
        lengths,
        hidden_in,
        q_weight,
        k_weight,
        v_weight,
        o_weight,
        q_gain,
        k_gain,
        gate_weight,
        up_weight,
        down_weight,
        norm_gains,
        cosine,
        sine,
        norm_gains,
        router_weight.T,
        routes.T,
    )
    grad_output, row_loss, ffn_grad_partial, inner, active, grads = turn(
        extent,
        lengths,
        expert_partial,
        middle,
        teacher,
        tokens,
        hidden,
        landed,
        gate_weight,
        up_weight,
        down_weight,
    )
    grad_middle, small, attn_grad_rows, *came = leave(
        extent,
        ffn_grad_partial,
        middle,
        grad_output,
        gates,
        chosen,
        norm_gains,
        router_weight.T,
        (tokens, grads, inner, active),
    )
    expert_grads = came[:6] + [exchange(came[bits], bits) for bits in (6, 7)]
    (
        grad_in,
        grad_q,
        grad_k,
        grad_v,
        grad_o,
        grad_router,
        vectors,
        grad_q_gain,
        grad_k_gain,
        loss,
    ) = back(
        extent,
        attn_grad_rows.reshape(seq_len, width),
        row_loss,
        hidden_bf,
        norm_gains,
        qkv_full,
        o_full,
        head_gain,
        cosine,
        sine,
        normed,
        units,
        low,
        probs,
        mixed,
        inverses,
        small,
        grad_middle,
    )
    (
        grad_gate,
        grad_up,
        grad_down,
        grad_in,
        grad_q,
        grad_k,
        grad_v,
        grad_o,
        loss,
        attn_part,
        ffn_part,
        grad_q_gain,
        grad_k_gain,
        grad_router,
    ) = spread(
        expert_grads,
        (grad_in, grad_q, grad_k, grad_v, grad_o),
        (vectors, grad_q_gain, grad_k_gain, loss, grad_router),
    )
    return (
        loss[0],
        grad_in,
        attn_part[0],
        ffn_part[0],
        grad_q,
        grad_k,
        grad_v,
        grad_q_gain,
        grad_k_gain,
        grad_o,
        grad_router.T,
        grad_gate,
        grad_up,
        grad_down,
    )


def solution(mesh):
    placed = (
        P(("dp", "tensor"), None),
        P(("dp", "tensor"), None),
        P(),
        P("dp", None),
        P(),
        P(),
        P("dp", "tensor"),
        P("dp", "tensor"),
        P("dp", "tensor"),
        P("tensor", "dp"),
        P("tensor", "dp"),
        P("tensor", "dp"),
        P(),
        P(None, "dp", "tensor"),
        P(None, "dp", "tensor"),
        P(None, "tensor", "dp"),
    )
    block = mesh.shape["dp"] == 8 and mesh.shape["tensor"] == 4
    return jax.shard_map(
        per_device_block if block else per_device,
        mesh=mesh,
        in_specs=placed,
        out_specs=(
            P("dp"),
            P(("dp", "tensor"), None),
            P(("dp", "tensor")),
            P(("dp", "tensor")),
            P("dp", "tensor"),
            P("dp", "tensor"),
            P("dp", "tensor"),
            P("tensor", "dp"),
            P("tensor", "dp"),
            P("tensor", "dp"),
            P(("dp", "tensor"), None),
            P(None, "dp", "tensor"),
            P(None, "dp", "tensor"),
            P(None, "tensor", "dp"),
        ),
        check_vma=False,
    )
```
